32 devices in a mesh: seq: 8 (over y, x, core), exp: 4 (over z).
Axes of the slice: x: 2, y: 2, z: 4, core: 2. Of those that a mesh axis runs over, the one named last changes fastest.
Arguments:
- tokens: bfloat16 [4, 1024, 1152], P('exp', 'seq'), may hold values from -6 to 6
- segment_ids: int32 [4, 1024], P('exp', 'seq'), may hold values from 0 to 1, as said below
- routes: int32 [4, 1024, 1], P('exp', 'seq'), may hold values from 0 to 3; in each aligned block of 128 rows (0 to 127, 128 to 255, ..., all dimensions but the last counted through in order) at most 64 rows name the same one
- cotangent: bfloat16 [4, 1024, 1152], P('exp', 'seq'), may hold values from -6 to 6
- norm_gain: bfloat16 [1152], P('exp'), may hold values from 0.5 to 1.5
- in_proj: bfloat16 [1152, 4608], P('exp'), may hold values from -0.1875 to 0.1875
- conv_weight: bfloat16 [4, 2304], P(None, 'exp'), may hold values from -3 to 3
- conv_bias: bfloat16 [2304], P('exp'), may hold values from -3 to 3
- x_proj: bfloat16 [2304, 104], P('exp'), may hold values from -0.125 to 0.125
- dt_proj: bfloat16 [72, 2304], P(None, 'exp'), may hold values from -0.75 to 0.75
- dt_bias: bfloat16 [2304], P('exp'), may hold values from -12 to -1
- a_log: bfloat16 [16, 2304], P(None, 'exp'), may hold values from -1 to 1.5
- d_skip: bfloat16 [2304], P('exp'), may hold values from 0.5 to 1.5
- out_proj: bfloat16 [2304, 1152], P('exp'), may hold values from -0.5 to 0.5
- moe_gain: bfloat16 [1152], P('exp'), may hold values from 0.5 to 1.5
- router: bfloat16 [1152, 4], P('exp'), may hold values from -0.09375 to 0.09375
- up_proj: bfloat16 [4, 1152, 3072], P('exp'), may hold values from -0.1875 to 0.1875
- down_proj: bfloat16 [4, 3072, 1152], P('exp'), may hold values from -0.875 to 0.875
Outputs:
- output: bfloat16 [4, 1024, 1152], P('exp', 'seq')
- grad_tokens: float32 [4, 1024, 1152], P('exp', 'seq')
- grad_norm_gain: float32 [1152], P('exp')
- grad_in_proj: float32 [1152, 4608], P('exp')
- grad_conv_weight: float32 [4, 2304], P(None, 'exp')
- grad_conv_bias: float32 [2304], P('exp')
- grad_x_proj: float32 [2304, 104], P('exp')
- grad_dt_proj: float32 [72, 2304], P(None, 'exp')
- grad_dt_bias: float32 [2304], P('exp')
- grad_a_log: float32 [16, 2304], P(None, 'exp')
- grad_d_skip: float32 [2304], P('exp')
- grad_out_proj: float32 [2304, 1152], P('exp')
- grad_moe_gain: float32 [1152], P('exp')
- grad_router: float32 [1152, 4], P('exp')
- grad_up_proj: float32 [4, 1152, 3072], P('exp', 'seq')
- grad_down_proj: float32 [4, 3072, 1152], P('exp', 'seq')
The draws below stay inside these ranges and needn't reach their ends.
Inputs may be any that keep to these rules, and one draw needn't show every extreme that they name: `segment_ids`: along each row the ids start at 0 and rise by 0 or 1 from one position to the next. `routes`: at most 64 tokens of one device go to one expert, and some expert takes exactly 64 tokens of some device.
All inputs are finite; a program needn't handle non-finite values.
Results may differ from the reference program's by a relative error of at most 0.015.
Values may be sent and summed in bfloat16 or wider, within the bound.
A program may use at most 640 MiB of HBM per device.

```python
import math
import jax
import jax.numpy as jnp
import numpy as np
from jax import lax

D = 1152
DI = 2304
N = 16
R = 72
KW = 4
FF = 3072
TOK_DEV = 128
EXPERTS = 4
XW = 104
STREAMS = 4
LEN = 1024
CAP = 64


def draw_segment_ids(key, part):
    subkeys = jax.random.split(jax.random.fold_in(key, 7), 3)
    slot_len = 4 * TOK_DEV
    doc_count = LEN // slot_len
    order = jnp.arange(1, doc_count, dtype=jnp.int32)[None, :]
    spread = 3 * slot_len // 8
    wide_jitter = jax.random.randint(subkeys[0], (STREAMS, doc_count - 1), -spread, spread + 1).astype(jnp.int32)
    border_jitter = (TOK_DEV * jax.random.randint(subkeys[1], (STREAMS, doc_count - 1), -1, 2)).astype(jnp.int32)
    jitter = jnp.where(order % 2 == 1, border_jitter, wide_jitter)
    cuts = (order * slot_len + jitter).astype(jnp.int32)
    whole_row = jax.random.randint(subkeys[2], (), 0, STREAMS).astype(jnp.int32)
    keep_cuts = (jnp.arange(STREAMS, dtype=jnp.int32) != whole_row)[:, None, None]
    positions = jnp.arange(LEN, dtype=jnp.int32)[None, None, :]
    crossed = (positions >= cuts[:, :, None]) & keep_cuts
    return jnp.sum(crossed.astype(jnp.int32), axis=1).astype(jnp.int32)


def block_scale(own_key, dims, pieces, low, high):
    def one(axis_at, parts):
        steps = jax.random.uniform(jax.random.fold_in(jax.random.fold_in(own_key, 6), axis_at), (parts,), jnp.float32, low / len(pieces), high / len(pieces))
        return jnp.repeat(jnp.exp(steps), dims[axis_at] // parts).reshape((-1,) + (1,) * (len(dims) - axis_at - 1))

    gain = one(*pieces[0])
    for cut in pieces[1:]:
        gain = gain * one(*cut)
    return gain


def deal_out(key, own, number, rows, amount, top, bound, lean):
    sequence = jax.random.permutation(key, amount)
    packed, usual = load_shares(amount, rows * top, bound, lean, True), load_shares(amount, rows * top, bound, lean, False)
    places = jnp.arange(amount)

    def named(sizes, rotation):
        used = int((sizes > 0).sum())
        fixed = max(1, used // 4)
        moved = fixed + (places - fixed + rotation * (used - fixed)) % max(1, amount - fixed)
        return jnp.zeros((amount,), jnp.int32).at[sequence[jnp.where(places < fixed, places, moved)]].set(jnp.asarray(sizes, jnp.int32))

    sizes = jnp.where(number % 4 == 0, named(packed, number // 4), named(usual, number - number // 4 - 1))
    mixed = jax.random.permutation(jax.random.fold_in(own, 3), amount)
    giver, taker = mixed[0:amount // 2 * 2:2], mixed[1:amount // 2 * 2:2]
    slack = jnp.minimum(sizes[giver] - 1, bound - sizes[taker]) // 2
    slack = jnp.where((giver == sequence[0]) | (taker == sequence[0]) | (sizes[taker] == 0), 0, jnp.maximum(slack, 0))
    moved = jax.random.randint(jax.random.fold_in(own, 4), (amount // 2,), 0, 1 << 20) % (slack + 1)
    sizes = sizes.at[giver].add(-moved).at[taker].add(moved)
    members = jnp.searchsorted(jnp.cumsum(sizes), jnp.arange(rows * top), side="right").astype(jnp.int32)
    grid = members.reshape(top, rows).T
    grid = grid[jax.random.permutation(jax.random.fold_in(own, 1), rows)]
    rotation = jax.random.randint(jax.random.fold_in(own, 2), (rows, 1), 0, top)
    return jnp.take_along_axis(grid, (jnp.arange(top)[None, :] + rotation) % top, axis=1)


def load_shares(amount, total, most, skew, full):
    portions = [(1 << 20) // math.isqrt(grade ** skew) + 1 for grade in range(1, amount + 1)]
    largest = most if full else min(most, max(-(-total // amount), total * portions[0] // sum(portions)))
    least = 1 if total - largest >= amount - 1 else 0
    holding, spare = [largest] + [least] * (amount - 1), total - largest - least * (amount - 1)
    while spare > 0:
        candidates = [i for i in range(1, amount) if holding[i] < largest] or [i for i in range(1, amount) if holding[i] < most]
        whole, remaining = sum([portions[i] for i in candidates]), spare
        for i in candidates:
            extra = min(most - holding[i], max(1, remaining * portions[i] // whole), spare)
            holding[i] = holding[i] + extra
            spare = spare - extra
    return np.array(holding)


def normal_values(key, shape, deviation, limit, cuts=(), kind=jnp.bfloat16):
    level = block_scale(key, shape, cuts, -0.22, 0.18) if cuts else 1.0
    values = jax.random.normal(key, shape, jnp.float32) * deviation * level
    return jnp.minimum(jnp.maximum(values, -limit), limit).astype(kind)


def setup_inputs(seed: int = 0) -> dict:
    keys = jax.random.split(jax.random.key(seed), 19)
    tokens = normal_values(keys[0], (STREAMS, LEN, D), 1.0, 6.0, ((0, 4), (1, 8)))
    segment_ids = draw_segment_ids(jax.random.fold_in(keys[18], 71), 0)
    routes_keys = jax.random.split(jax.random.fold_in(keys[2], 1), STREAMS * LEN // TOK_DEV)
    routes_turns = jax.random.permutation(jax.random.fold_in(keys[2], 3), STREAMS * LEN // TOK_DEV)
    routes = jax.vmap(lambda own, number: deal_out(jax.random.fold_in(keys[2], 2), own, number, TOK_DEV, EXPERTS, 1, CAP, 2))(routes_keys, routes_turns).reshape((STREAMS, LEN, 1))
    cotangent = normal_values(keys[3], (STREAMS, LEN, D), 1.0, 6.0, ((0, 4), (1, 8)))
    norm_gain = jnp.clip(1.0 + 0.1 * jax.random.normal(keys[4], (D,), jnp.float32), 0.5, 1.5).astype(jnp.bfloat16)
    in_proj = normal_values(keys[5], (D, 2 * DI), D ** -0.5, 0.1875, ((0, 4),))
    conv_weight = normal_values(keys[6], (KW, DI), 0.5, 3.0, ((1, 4),))
    conv_bias = normal_values(keys[7], (DI,), 0.5, 3.0, ((0, 4),))
    x_proj = normal_values(keys[8], (DI, XW), DI ** -0.5, 0.125, ((0, 4),))
    dt_proj = normal_values(keys[9], (R, DI), R ** -0.5, 0.75, ((1, 4),))
    dt_bias = jnp.clip(-12.0 + 11.0 * jax.random.uniform(keys[10], (DI,), jnp.float32) ** block_scale(keys[10], (DI,), ((0, 4),), -0.2, 0.2), -12.0, -1.0).astype(jnp.bfloat16)
    a_log = jnp.clip(-1.0 + 2.5 * jax.random.uniform(keys[11], (N, DI), jnp.float32) ** block_scale(keys[11], (N, DI), ((1, 4),), -0.2, 0.2), -1.0, 1.5).astype(jnp.bfloat16)
    d_skip = jnp.clip(0.5 + 1.0 * jax.random.uniform(keys[12], (DI,), jnp.float32) ** block_scale(keys[12], (DI,), ((0, 4),), -0.2, 0.2), 0.5, 1.5).astype(jnp.bfloat16)
    out_proj = normal_values(keys[13], (DI, D), (DI // 16) ** -0.5, 0.5, ((0, 4),))
    moe_gain = jnp.clip(1.0 + 0.1 * jax.random.normal(keys[14], (D,), jnp.float32), 0.5, 1.5).astype(jnp.bfloat16)
    router = normal_values(keys[15], (D, EXPERTS), (4 * D) ** -0.5, 0.09375, ((0, 4),))
    up_proj = normal_values(keys[16], (EXPERTS, D, FF), D ** -0.5, 0.1875, ((0, 4),))
    down_proj = normal_values(keys[17], (EXPERTS, FF, D), (FF // 64) ** -0.5, 0.875, ((0, 4),))
    return {"tokens": tokens, "segment_ids": segment_ids, "routes": routes, "cotangent": cotangent, "norm_gain": norm_gain, "in_proj": in_proj, "conv_weight": conv_weight, "conv_bias": conv_bias, "x_proj": x_proj, "dt_proj": dt_proj, "dt_bias": dt_bias, "a_log": a_log, "d_skip": d_skip, "out_proj": out_proj, "moe_gain": moe_gain, "router": router, "up_proj": up_proj, "down_proj": down_proj}


EPSILON = 1e-05
TOP_PRECISION = lax.Precision.HIGHEST

@jax.custom_vjp
def low(v):
    return lax.optimization_barrier(v.astype(jnp.bfloat16)).astype(jnp.float32)

@jax.custom_vjp
def low_back(v):
    return v

def low_keep(v):
    return (low(v), None)

def low_pass(kept, grad):
    return (grad,)

def back_keep(v):
    return (v, None)

def back_low(kept, grad):
    return (low(grad),)
low.defvjp(low_keep, low_pass)
low_back.defvjp(back_keep, back_low)

def matmul(first_op, second_op):
    return jnp.dot(first_op, second_op, precision=TOP_PRECISION, preferred_element_type=jnp.float32)

def rms_apply(residual, gain_vec):
    return residual * lax.rsqrt(lax.optimization_barrier(jnp.mean(residual * residual, axis=-1, keepdims=True)) + EPSILON) * gain_vec

def state_block(hidden, inputs, rates):

    def advance(current, row_items):
        step_row, in_row, out_row, signal_row, carry_row = row_items
        current = jnp.exp(step_row[None, :] * rates) * carry_row * current + (step_row * signal_row)[None, :] * in_row[:, None]
        return (current, lax.optimization_barrier(jnp.sum(out_row[:, None] * current, axis=0)))
    return lax.scan(advance, hidden, inputs)

def selective_scan(step_size, in_coef, out_coef, signal, carry_on, rates):
    length = step_size.shape[0]
    blocks = length // TOK_DEV

    def to_blocks(array_in):
        return array_in.reshape((blocks, TOK_DEV) + array_in.shape[1:])

    def one_block(hidden, inputs):
        return state_block(hidden, inputs, rates)
    initial = jnp.zeros(rates.shape, jnp.float32)
    sectioned = tuple((to_blocks(array_in) for array_in in (step_size, in_coef, out_coef, signal, carry_on)))
    _, outputs = lax.scan(jax.checkpoint(one_block), initial, sectioned)
    return outputs.reshape(length, -1)

def layer_forward(residual, seg_row, route_row, params):
    norm_gain, in_proj, conv_weight, conv_bias, x_proj, dt_proj, dt_bias, a_log, d_skip, out_proj, moe_gain, router, up_proj, down_proj = params
    length = residual.shape[0]
    inner = dt_proj.shape[1]
    dt_rank = dt_proj.shape[0]
    state_count = a_log.shape[0]
    tap_count = conv_weight.shape[0]
    experts = router.shape[1]
    normed = low(rms_apply(residual, norm_gain))
    projected = low_back(matmul(normed, in_proj))
    conv_in = projected[:, :inner]
    gate_in = projected[:, inner:]
    padded = jnp.concatenate([jnp.zeros((tap_count - 1, inner), jnp.float32), conv_in], axis=0)
    padded_seg = jnp.concatenate([jnp.zeros((tap_count - 1,), jnp.int32), seg_row], axis=0)
    conv_out = conv_bias[None, :] + sum((conv_weight[offset][None, :] * padded[offset:offset + length] * (padded_seg[offset:offset + length] == seg_row).astype(jnp.float32)[:, None] for offset in range(tap_count)))
    signal = low(jax.nn.silu(conv_out))
    mixed_proj = low_back(matmul(signal, x_proj))
    dt_low = low(mixed_proj[:, :dt_rank])
    in_coef = mixed_proj[:, dt_rank:dt_rank + state_count]
    out_coef = mixed_proj[:, dt_rank + state_count:]
    step_size = jax.nn.softplus(low_back(matmul(dt_low, dt_proj)) + dt_bias)
    carry_on = (padded_seg[tap_count - 2:tap_count - 2 + length] == seg_row).astype(jnp.float32)
    rates = -jnp.exp(a_log)
    scanned = selective_scan(step_size, in_coef, out_coef, signal, carry_on, rates) + d_skip * signal
    gated = low(scanned * jax.nn.silu(gate_in))
    resid_mid = residual + low_back(matmul(gated, out_proj))
    moe_in = low(rms_apply(resid_mid, moe_gain))
    chances = jax.nn.softmax(matmul(moe_in, router), axis=-1)
    choose = route_row[:, None] == jnp.arange(experts, dtype=jnp.int32)[None, :]
    gating = lax.optimization_barrier(jnp.sum(chances * choose.astype(jnp.float32), axis=-1))
    choose_int = choose.astype(jnp.int32)
    blocks = length // TOK_DEV
    counted = jnp.cumsum(choose_int.reshape(blocks, TOK_DEV, experts), axis=1).astype(jnp.int32).reshape(length, experts)
    slot_rank = (lax.optimization_barrier(jnp.sum(counted * choose_int, axis=1)) - 1).astype(jnp.int32)
    slot_ids = (jnp.arange(length, dtype=jnp.int32) // TOK_DEV * CAP + slot_rank).astype(jnp.int32)
    dispatched_in = low_back(moe_in)
    buffers = jnp.zeros((experts, blocks * CAP, residual.shape[1]), jnp.float32).at[route_row, slot_ids].set(dispatched_in)
    expert_pre = low_back(jnp.einsum('esd,edf->esf', buffers, up_proj, precision=TOP_PRECISION, preferred_element_type=jnp.float32))
    hidden = low(jax.nn.gelu(expert_pre, approximate=False))
    results = low(low_back(jnp.einsum('esf,efd->esd', hidden, down_proj, precision=TOP_PRECISION, preferred_element_type=jnp.float32)))
    expert_out = results[route_row, slot_ids]
    return resid_mid + gating[:, None] * expert_out

def reference(tokens, segment_ids, routes, cotangent, norm_gain, in_proj, conv_weight, conv_bias, x_proj, dt_proj, dt_bias, a_log, d_skip, out_proj, moe_gain, router, up_proj, down_proj):
    params = tuple((weight.astype(jnp.float32) for weight in (norm_gain, in_proj, conv_weight, conv_bias, x_proj, dt_proj, dt_bias, a_log, d_skip, out_proj, moe_gain, router, up_proj, down_proj)))

    def per_stream(totals, inputs):
        token_row, seg_row, route_row, cot_row = inputs

        def forward_fn(residual, weights):
            return layer_forward(residual, seg_row, route_row, weights)
        result, pullback = jax.vjp(forward_fn, token_row.astype(jnp.float32), params)
        token_grad, weight_grads = pullback(cot_row.astype(jnp.float32))
        totals = tuple((total + update for total, update in zip(totals, weight_grads)))
        return (totals, (result.astype(jnp.bfloat16), token_grad))
    zeros = tuple((jnp.zeros_like(weight) for weight in params))
    totals, (outputs, token_grads) = lax.scan(per_stream, zeros, (tokens, segment_ids, routes[:, :, 0], cotangent))
    return (outputs, token_grads) + totals
```

```python
import functools
import math

import jax
import jax.numpy as jnp
from jax import lax
from jax.experimental import pallas as pl
from jax.experimental.pallas import tpu as pltpu
from jax.sharding import PartitionSpec as P

EPSILON = 1e-05
LOG2E = math.log2(math.e)
LN2 = math.log(2.0)
CLOSED = 1e30
LANES = 128
SUB = 8
F32 = jnp.float32
BF16 = jnp.bfloat16
VMEM_LIMIT = 56 * 1024 * 1024


def mm(a, b):
    return lax.dot_general(a, b, (((1,), (0,)), ((), ())), preferred_element_type=F32)


def mm_nt(a, b):
    return lax.dot_general(a, b, (((1,), (1,)), ((), ())), preferred_element_type=F32)


def mm_tn(a, b):
    return lax.dot_general(a, b, (((0,), (0,)), ((), ())), preferred_element_type=F32)


def split_hi_lo(value):
    high = value.astype(BF16)
    return high, (value - high.astype(F32)).astype(BF16)


def sigmoid(v):
    return 1.0 / (1.0 + jnp.exp(-v))


def softplus(v):
    e = jnp.exp(-jnp.abs(v))
    small = e * (1.0 - e * (0.5 - e * (1.0 / 3.0 - e * 0.25)))
    return jnp.maximum(v, 0.0) + jnp.where(e < 0.01, small, jnp.log(1.0 + e))


def rms_scale(v):
    return lax.rsqrt(jnp.mean(v * v, axis=-1, keepdims=True) + EPSILON)


def rms_back(resid, gain, grad):
    s = rms_scale(resid)
    v = gain * grad
    out = s * v - resid * (s * s * s) * jnp.mean(resid * v, axis=-1, keepdims=True)
    return out, jnp.sum(grad * resid * s, axis=0, keepdims=True)


def block(shape, index):
    return pl.BlockSpec(shape, index)


def whole(shape):
    zeros = (0,) * len(shape)
    return pl.BlockSpec(shape, lambda *_: zeros)


def call(body, name, grid, ins, in_specs, outs, out_specs, scratch, cost=None):
    return pl.pallas_call(
        body,
        name=name,
        grid=grid,
        in_specs=in_specs,
        out_specs=out_specs,
        out_shape=outs,
        scratch_shapes=scratch,
        cost_estimate=cost,
        compiler_params=pltpu.CompilerParams(vmem_limit_bytes=VMEM_LIMIT),
    )(*ins)


def sds(shape, dtype):
    return jax.ShapeDtypeStruct(shape, dtype)


def pick(total, options):
    for o in options:
        if total % o == 0:
            return o
    return total


CONV_W, CONV_B, DT_B, SKIP, A_LOG = 0, 4, 5, 6, 8


class Sizes:
    def __init__(self, tokens, in_proj, dt_proj, x_proj, a_log, up_proj, exp_count):
        self.T = tokens.shape[1]
        self.D = tokens.shape[2]
        self.DI = in_proj.shape[1] // 2
        self.N = a_log.shape[0]
        self.R = dt_proj.shape[0]
        self.XW = x_proj.shape[1]
        self.FF = up_proj.shape[2]
        self.E = exp_count
        self.CAP = 2 * self.T // exp_count
        self.J = self.T // SUB
        self.DT0 = A_LOG + self.N
        self.X0 = self.DT0 + self.R
        self.SMALL = self.X0 + self.XW


def front(z, tokens, halo, masks, gpack, w_conv, w_gate, small):
    T, D, DI, J = z.T, z.D, z.DI, z.J
    H = halo.shape[0]
    cb = pick(DI, (384, 256, 128))
    steps = DI // cb

    def body(tok, hal, msk, gp, wc, wg, sm, normed_o, conv_o, hconv_o, gate_o, sig_o, mixed_o, nrm):
        i = pl.program_id(0)

        @pl.when(i == 0)
        def _():
            gain = gp[0:1, :]
            t = tok[...].astype(F32)
            nt = (t * rms_scale(t) * gain).astype(BF16)
            h = hal[...].astype(F32)
            nrm[0:T, :] = nt
            nrm[T : T + H, :] = (h * rms_scale(h) * gain).astype(BF16)
            normed_o[...] = nt
            mixed_o[...] = jnp.zeros_like(mixed_o)

        conv = mm(nrm[...], wc[...])
        gate_o[...] = mm(nrm[0:T, :], wg[...])
        main, edge = conv[:T], conv[T:]
        conv_o[...] = main
        hconv_o[...] = edge
        xpad = padded_rows(main, edge, J, cb)
        out = jnp.broadcast_to(sm[CONV_B : CONV_B + 1, :], (T, cb))
        for o in range(4):
            m = jnp.broadcast_to(msk[:, o : o + 1], (T, cb))
            out = out + sm[CONV_W + o : CONV_W + o + 1, :] * xpad[o : o + J].reshape(T, cb) * m
        sig = (out * sigmoid(out)).astype(BF16)
        sig_o[...] = sig
        mixed_o[...] += mm_nt(sig, sm[z.X0 : z.X0 + z.XW, :].astype(BF16))

    col = lambda r: block((r, cb), lambda i: (0, i))
    return call(
        body,
        "front",
        (steps,),
        (tokens, halo, masks, gpack, w_conv, w_gate, small),
        [
            whole(tokens.shape),
            whole(halo.shape),
            whole(masks.shape),
            whole(gpack.shape),
            col(D),
            col(D),
            col(z.SMALL),
        ],
        [
            sds((T, D), BF16),
            sds((T, DI), F32),
            sds((H, DI), F32),
            sds((T, DI), F32),
            sds((T, DI), BF16),
            sds((T, z.XW), F32),
        ],
        [whole((T, D)), col(T), col(H), col(T), col(T), whole((T, z.XW))],
        [pltpu.VMEM((T + H, D), BF16)],
    )


def expand_columns(z, src, col0, dst):
    def one(j, carry):
        rows = src[pl.ds(pl.multiple_of(j * SUB, SUB), SUB), :]
        for n in range(z.N):
            at = pl.multiple_of((j * z.N + n) * SUB, SUB)
            dst[pl.ds(at, SUB), :] = jnp.broadcast_to(
                rows[:, col0 + n : col0 + n + 1], (SUB, LANES)
            )
        return carry

    lax.fori_loop(0, z.J, one, 0)


def expand_closed(z, masks, dst):
    dst[...] = jnp.broadcast_to((1.0 - masks[:, 2:3]) * CLOSED, (z.T, LANES))


def tile_groups(cb):
    return 2 if cb % (2 * LANES) == 0 else 1


def lane_at(p, tg, k):
    return pl.ds(pl.multiple_of(p * tg * LANES, LANES) + k * LANES, LANES)


def row8(j):
    return pl.ds(pl.multiple_of(j * SUB, SUB), SUB)


def shift_down(v, d):
    rows = lax.broadcasted_iota(jnp.int32, v.shape, 0)
    return jnp.where(rows >= d, pltpu.roll(v, d, 0), 0.0)


def shift_up(v, d):
    rows = lax.broadcasted_iota(jnp.int32, v.shape, 0)
    return jnp.where(rows < SUB - d, pltpu.roll(v, SUB - d, 0), 0.0)


def summary(z, mixed, sig, masks, small):
    T, DI, N, J = z.T, z.DI, z.N, z.J
    cb = pick(DI, (768, 384, 256, 128))
    tg = tile_groups(cb)
    ng = 8

    def body(mix, sg, msk, sm, dt_o, pre_o, hdev_o, stot_o, dwin_o, bx, cl, u_s, hd, rates_s):
        i = pl.program_id(0)

        @pl.when(i == 0)
        def _():
            expand_columns(z, mix, z.R, bx)
            expand_closed(z, msk, cl)

        low = mix[:, 0 : z.R].astype(BF16)
        pre = mm(low, sm[z.DT0 : z.DT0 + z.R, :].astype(BF16)) + sm[DT_B : DT_B + 1, :]
        step = softplus(pre)
        dt_o[...] = step
        u_s[...] = step * sg[...].astype(F32)
        rates_s[...] = -jnp.exp(sm[A_LOG : A_LOG + N, :]) * LOG2E

        def pair(p, carry):
            totals = []
            for k in range(tg):
                tot = jnp.zeros((SUB, LANES), F32)
                for j in range(J):
                    tot = tot + (dt_o[j * SUB : j * SUB + SUB, lane_at(p, tg, k)] + cl[j * SUB : j * SUB + SUB, :])
                totals.append(tot)
            wins = []
            for k in range(tg):
                w1 = totals[k]
                w2 = w1 + shift_down(w1, 1)
                w4 = w2 + shift_down(w2, 2)
                w8 = w4 + shift_down(w4, 4)
                wins.append((w1, w2, w4))
                dwin_o[0:SUB, lane_at(p, tg, k)] = w1
                dwin_o[SUB : 2 * SUB, lane_at(p, tg, k)] = shift_down(w8, 1)
                stot_o[:, lane_at(p, tg, k)] = w8[SUB - 1 : SUB, :]
            for g in range(0, N, ng):
                rr = [
                    [
                        jnp.broadcast_to(rates_s[g + n : g + n + 1, lane_at(p, tg, k)], (SUB, LANES))
                        for k in range(tg)
                    ]
                    for n in range(ng)
                ]

                def step_j(j, hs):
                    dts = [dt_o[row8(j), lane_at(p, tg, k)] + cl[row8(j), :] for k in range(tg)]
                    us = [u_s[row8(j), lane_at(p, tg, k)] for k in range(tg)]
                    new = []
                    for n in range(ng):
                        b = bx[row8(j * N + g + n), :]
                        for k in range(tg):
                            new.append(
                                jnp.exp2(dts[k] * rr[n][k]) * hs[n * tg + k] + us[k] * b
                            )
                    return tuple(new)

                hs = lax.fori_loop(
                    0, J, step_j, tuple(jnp.zeros((SUB, LANES), F32) for _ in range(ng * tg)), unroll=2
                )
                for n in range(ng):
                    for k in range(tg):
                        h = hs[n * tg + k]
                        w1, w2, w4 = wins[k]
                        r = rr[n][k]
                        h = h + jnp.exp2(r * w1) * shift_down(h, 1)
                        h = h + jnp.exp2(r * w2) * shift_down(h, 2)
                        h = h + jnp.exp2(r * w4) * shift_down(h, 4)
                        at = (g + n) * SUB
                        pre_o[at : at + SUB, lane_at(p, tg, k)] = shift_down(h, 1)
                        hd[g + n : g + n + 1, lane_at(p, tg, k)] = h[SUB - 1 : SUB, :]
            return carry

        lax.fori_loop(0, cb // (tg * LANES), pair, 0)
        hdev_o[...] = hd[...].astype(BF16)

    col = lambda r: block((r, cb), lambda i: (0, i))
    return call(
        body,
        "summary",
        (DI // cb,),
        (mixed, sig, masks, small),
        [whole(mixed.shape), col(T), whole(masks.shape), col(z.SMALL)],
        [
            sds((T, DI), F32),
            sds((N * SUB, DI), F32),
            sds((N, DI), BF16),
            sds((1, DI), F32),
            sds((2 * SUB, DI), F32),
        ],
        [col(T), col(N * SUB), col(N), col(1), col(2 * SUB)],
        [
            pltpu.VMEM((J * N * SUB, LANES), F32),
            pltpu.VMEM((T, LANES), F32),
            pltpu.VMEM((T, cb), F32),
            pltpu.VMEM((N, cb), F32),
            pltpu.VMEM((N, cb), F32),
        ],
    )


def chain_states(count, mine, order, sums, heads, rates2):
    state = jnp.zeros_like(rates2)
    for k in range(count):
        at = order(k)
        new = jnp.exp2(rates2 * sums(at)) * state + heads(at).astype(F32)
        state = jnp.where(mine(at), new, state)
    return state


def scan_forward(z, where, mixed, dt, sig, gate, masks, small, pre, dwin, h_all, s_all, w_out,
                 tokens, gpack, router, table):
    T, D, DI, N, J, E = z.T, z.D, z.DI, z.N, z.J, z.E
    cb = pick(DI, (768, 384, 256, 128))
    tg = tile_groups(cb)
    ng = 8
    S = h_all.shape[0]
    slots = table.shape[1]
    steps = DI // cb

    def body(wh, mix, dt_r, sg, gt, msk, sm, pr, dw, ha, sa, wo, tok, gp, rt, tb,
             st_o, y_o, mid_o, moe_o, ch_o, out_o, bx, cx, cl, u_s, rates_s, hin, acc):
        i = pl.program_id(0)

        @pl.when(i == 0)
        def _():
            expand_columns(z, mix, z.R, bx)
            expand_columns(z, mix, z.R + N, cx)
            expand_closed(z, msk, cl)
            acc[...] = jnp.zeros_like(acc)

        me = wh[0]
        rates2 = -jnp.exp(sm[A_LOG : A_LOG + N, :]) * LOG2E
        rates_s[...] = rates2
        hin[...] = chain_states(
            S - 1, lambda k: k < me, lambda k: k, lambda k: sa[k], lambda k: ha[k], rates2
        )
        u_s[...] = dt_r[...] * sg[...].astype(F32)

        def pair(p, carry):
            lanes = [lane_at(p, tg, k) for k in range(tg)]
            for g in range(0, N, ng):
                rr = [
                    [jnp.broadcast_to(rates_s[g + n : g + n + 1, lanes[k]], (SUB, LANES)) for k in range(tg)]
                    for n in range(ng)
                ]
                init = []
                for n in range(ng):
                    for k in range(tg):
                        at = (g + n) * SUB
                        init.append(
                            pr[at : at + SUB, lanes[k]]
                            + jnp.exp2(rr[n][k] * dw[SUB : 2 * SUB, lanes[k]])
                            * jnp.broadcast_to(hin[g + n : g + n + 1, lanes[k]], (SUB, LANES))
                        )

                def keep(j, hs):
                    for n in range(0, ng, 2):
                        for k in range(tg):
                            two = jnp.concatenate([hs[n * tg + k], hs[(n + 1) * tg + k]], axis=0)
                            at = pl.multiple_of(j * N * SUB + (g + n) * SUB, 2 * SUB)
                            st_o[pl.ds(at, 2 * SUB), lanes[k]] = two.astype(BF16)

                keep(0, init)

                def step_j(j, hs):
                    dts = [dt_r[row8(j), lanes[k]] + cl[row8(j), :] for k in range(tg)]
                    us = [u_s[row8(j), lanes[k]] for k in range(tg)]
                    if g == 0:
                        ys = [jnp.zeros((SUB, LANES), F32) for k in range(tg)]
                    else:
                        ys = [y_o[row8(j), lanes[k]] for k in range(tg)]
                    new = []
                    for n in range(ng):
                        b = bx[row8(j * N + g + n), :]
                        c = cx[row8(j * N + g + n), :]
                        for k in range(tg):
                            h = jnp.exp2(dts[k] * rr[n][k]) * hs[n * tg + k] + us[k] * b
                            ys[k] = ys[k] + h * c
                            new.append(h)
                    for k in range(tg):
                        y_o[row8(j), lanes[k]] = ys[k]
                    keep(j + 1, new)
                    return tuple(new)

                lax.fori_loop(0, J, step_j, tuple(init), unroll=2)
            return carry

        lax.fori_loop(0, cb // (tg * LANES), pair, 0)
        y = y_o[...] + sm[SKIP : SKIP + 1, :] * sg[...].astype(F32)
        y_o[...] = y
        g_in = gt[...]
        gated = (y * (g_in * sigmoid(g_in))).astype(BF16)
        acc[...] += mm(gated, wo[...])

        @pl.when(i == steps - 1)
        def _():
            mid = tok[...].astype(F32) + acc[...]
            mid_o[...] = mid
            moe = (mid * rms_scale(mid) * gp[1:2, :]).astype(BF16)
            moe_o[...] = moe
            logits = mm_nt(moe, rt[...])
            ch_o[...] = router_softmax(logits, E)
            out_o[...] = mm_tn(tb[...], moe).astype(BF16)

    col = lambda r: block((r, cb), lambda i: (0, i))
    return call(
        body,
        "scan_forward",
        (steps,),
        (where, mixed, dt, sig, gate, masks, small, pre, dwin, h_all, s_all, w_out, tokens, gpack, router, table),
        [
            pl.BlockSpec(memory_space=pltpu.SMEM),
            whole(mixed.shape),
            col(T),
            col(T),
            col(T),
            whole(masks.shape),
            col(z.SMALL),
            col(N * SUB),
            col(2 * SUB),
            block((S, N, cb), lambda i: (0, 0, i)),
            block((S, 1, cb), lambda i: (0, 0, i)),
            block((cb, D), lambda i: (i, 0)),
            whole(tokens.shape),
            whole(gpack.shape),
            whole(router.shape),
            whole(table.shape),
        ],
        [
            sds(((J + 1) * N * SUB, DI), BF16),
            sds((T, DI), F32),
            sds((T, D), F32),
            sds((T, D), BF16),
            sds((T, LANES), F32),
            sds((slots, D), BF16),
        ],
        [
            col((J + 1) * N * SUB),
            col(T),
            whole((T, D)),
            whole((T, D)),
            whole((T, LANES)),
            whole((slots, D)),
        ],
        [
            pltpu.VMEM((J * N * SUB, LANES), F32),
            pltpu.VMEM((J * N * SUB, LANES), F32),
            pltpu.VMEM((T, LANES), F32),
            pltpu.VMEM((T, cb), F32),
            pltpu.VMEM((N, cb), F32),
            pltpu.VMEM((N, cb), F32),
            pltpu.VMEM((T, D), F32),
        ],
    )


def router_softmax(logits, experts):
    lane = lax.broadcasted_iota(jnp.int32, logits.shape, 1)
    logits = jnp.where(lane < experts, logits, -1e30)
    top = jnp.max(logits, axis=-1, keepdims=True)
    e = jnp.where(lane < experts, jnp.exp(logits - top), 0.0)
    return e / jnp.sum(e, axis=-1, keepdims=True)


def expert(z, where, x, cot, router, up, down):
    D, FF, E = z.D, z.FF, z.E
    M = x.shape[0]
    fb = pick(FF, (512, 256, 128))
    steps = FF // fb

    def body(wh, x_r, c_r, rt, up_r, dn_r, ret_o, gg_o, dwu_o, dwd_o, g_s, out_s, dx_s):
        i = pl.program_id(0)

        @pl.when(i == 0)
        def _():
            ch = router_softmax(mm_nt(x_r[...], rt[...]), E)
            lane = lax.broadcasted_iota(jnp.int32, ch.shape, 1)
            gating = jnp.sum(jnp.where(lane == wh[1], ch, 0.0), axis=-1, keepdims=True)
            g_s[...] = (gating * c_r[...].astype(F32)).astype(BF16)
            out_s[...] = jnp.zeros_like(out_s)
            dx_s[...] = jnp.zeros_like(dx_s)

        xv, gv = x_r[...], g_s[...]
        upv, dnv = up_r[...], dn_r[...]
        pre = mm(xv, upv)
        cdf = 0.5 * (1.0 + lax.erf(pre * (2.0 ** -0.5)))
        hidden = (pre * cdf).astype(BF16)
        slope = cdf + pre * jnp.exp(-0.5 * pre * pre) * (1.0 / math.sqrt(2.0 * math.pi))
        out_s[...] += mm(hidden, dnv)
        pg = (mm_nt(gv, dnv) * slope).astype(BF16)
        dx_s[...] += mm_nt(pg, upv)
        dwd_o[...] = mm_tn(hidden, gv).astype(BF16)
        dwu_o[...] = mm_tn(xv, pg).astype(BF16)

        @pl.when(i == steps - 1)
        def _():
            out = out_s[...].astype(BF16)
            ret_o[0] = out
            ret_o[1] = dx_s[...].astype(BF16)
            gg_o[...] = jnp.broadcast_to(
                jnp.sum(out.astype(F32) * c_r[...].astype(F32), axis=-1, keepdims=True), gg_o.shape
            )

    return call(
        body,
        "expert",
        (steps,),
        (where, x, cot, router, up, down),
        [
            pl.BlockSpec(memory_space=pltpu.SMEM),
            whole(x.shape),
            whole(cot.shape),
            whole(router.shape),
            block((D, fb), lambda i: (0, i)),
            block((fb, D), lambda i: (i, 0)),
        ],
        [
            sds((2, M, D), BF16),
            sds((M, LANES), F32),
            sds((D, FF), BF16),
            sds((FF, D), BF16),
        ],
        [
            whole((2, M, D)),
            whole((M, LANES)),
            block((D, fb), lambda i: (0, i)),
            block((fb, D), lambda i: (i, 0)),
        ],
        [pltpu.VMEM((M, D), BF16), pltpu.VMEM((M, D), F32), pltpu.VMEM((M, D), F32)],
    )


def middle(z, ret_out, ret_dx, table, choose, chances, mid, moe, cot, gpack, router, gate, y, sig,
           small, w_out, mixed, dt, masks, normed):
    T, D, DI, N, J, E = z.T, z.D, z.DI, z.N, z.J, z.E
    cb = pick(DI, (384, 256, 128))
    tg = 1 if cb % 256 else 2
    tg = 3 if cb == 384 else tg
    ng = 4
    steps = DI // cb
    G = gpack.shape[0]

    def body(ro, rd, tb, cho, chn, md, me_r, ct, gp, rt, gt, yr, sg, sm, wo, mix, dt_r, msk, nm,
             out_o, mg_o, gg_o, yg_o, gi_o, dwo_o, dwg_o, fdev_o, suf_o, skip_o,
             cx, cl, rates_s, br, fd):
        i = pl.program_id(0)

        @pl.when(i == 0)
        def _():
            expand_columns(z, mix, z.R + N, cx)
            expand_closed(z, msk, cl)
            tbv = tb[...]
            eo = mm(tbv, ro[...])
            grad = ct[...].astype(F32)
            ch = chn[...]
            pick_e = cho[...]
            gating = jnp.sum(ch * pick_e, axis=-1, keepdims=True)
            out_o[...] = (md[...] + gating * eo).astype(BF16)
            gate_grad = jnp.sum(grad * eo, axis=-1, keepdims=True)
            lg = ch * (gate_grad * pick_e - gate_grad * gating)
            hi, lo = split_hi_lo(lg)
            rtv = rt[...]
            mig = mm(tbv, rd[...]) + mm(hi, rtv) + mm(lo, rtv)
            mev = me_r[...]
            rg = mm_tn(hi, mev) + mm_tn(lo, mev)
            d, gain_g = rms_back(md[...], gp[1:2, :], mig)
            total = grad + d
            mg_o[...] = total
            br[...] = total.astype(BF16)
            gg_o[...] = jnp.zeros_like(gg_o)
            gg_o[1:2, :] = gain_g
            gg_o[2 : 2 + E, :] = rg[0:E, :]

        gg = mm_nt(br[...], wo[...])
        g_in = gt[...]
        s = sigmoid(g_in)
        act = g_in * s
        yv = yr[...]
        yg = gg * act
        yg_o[...] = yg
        gi = (gg * yv * (s * (1.0 + g_in * (1.0 - s)))).astype(BF16)
        gi_o[...] = gi
        gated = (yv * act).astype(BF16)
        dwo_o[...] = mm_tn(gated, br[...]).astype(BF16)
        dwg_o[...] = mm_tn(nm[...], gi).astype(BF16)
        skip_o[...] = jnp.sum(yg * sg[...].astype(F32), axis=0, keepdims=True)
        rates_s[...] = -jnp.exp(sm[A_LOG : A_LOG + N, :]) * LOG2E

        lanes = [slice(k * LANES, (k + 1) * LANES) for k in range(tg)]
        for p in range(cb // (tg * LANES)):
            wins = []
            for k in range(tg):
                tot = jnp.zeros((SUB, LANES), F32)
                for j in range(J):
                    tot = tot + (dt_r[j * SUB : j * SUB + SUB, lanes[k]] + cl[j * SUB : j * SUB + SUB, :])
                w1 = tot
                w2 = w1 + shift_up(w1, 1)
                w4 = w2 + shift_up(w2, 2)
                w8 = w4 + shift_up(w4, 4)
                wins.append((w1, w2, w4))
                suf_o[N * SUB : (N + 1) * SUB, lanes[k]] = shift_up(w8, 1)
            for g in range(0, N, ng):
                rr = [
                    [jnp.broadcast_to(rates_s[g + n : g + n + 1, lanes[k]], (SUB, LANES)) for k in range(tg)]
                    for n in range(ng)
                ]

                def step_j(jj, fs):
                    j = J - 1 - jj
                    dts = [dt_r[row8(j), lanes[k]] + cl[row8(j), :] for k in range(tg)]
                    ygs = [yg_o[row8(j), lanes[k]] for k in range(tg)]
                    new = []
                    for n in range(ng):
                        c = cx[row8(j * N + g + n), :]
                        for k in range(tg):
                            new.append(
                                jnp.exp2(dts[k] * rr[n][k]) * (fs[n * tg + k] + ygs[k] * c)
                            )
                    return tuple(new)

                fs = lax.fori_loop(
                    0, J, step_j, tuple(jnp.zeros((SUB, LANES), F32) for _ in range(ng * tg)), unroll=2
                )
                for n in range(ng):
                    for k in range(tg):
                        f = fs[n * tg + k]
                        w1, w2, w4 = wins[k]
                        r = rr[n][k]
                        f = f + jnp.exp2(r * w1) * shift_up(f, 1)
                        f = f + jnp.exp2(r * w2) * shift_up(f, 2)
                        f = f + jnp.exp2(r * w4) * shift_up(f, 4)
                        at = (g + n) * SUB
                        suf_o[at : at + SUB, lanes[k]] = shift_up(f, 1)
                        fd[g + n : g + n + 1, lanes[k]] = f[0:1, :]
        fdev_o[...] = fd[...].astype(BF16)

    assert cb == tg * LANES
    col = lambda r: block((r, cb), lambda i: (0, i))
    row = lambda c: block((cb, c), lambda i: (i, 0))
    return call(
        body,
        "middle",
        (steps,),
        (ret_out, ret_dx, table, choose, chances, mid, moe, cot, gpack, router, gate, y, sig, small,
         w_out, mixed, dt, masks, normed),
        [
            whole(ret_out.shape),
            whole(ret_dx.shape),
            whole(table.shape),
            whole(choose.shape),
            whole(chances.shape),
            whole(mid.shape),
            whole(moe.shape),
            whole(cot.shape),
            whole(gpack.shape),
            whole(router.shape),
            col(T),
            col(T),
            col(T),
            col(z.SMALL),
            row(D),
            whole(mixed.shape),
            col(T),
            whole(masks.shape),
            whole(normed.shape),
        ],
        [
            sds((T, D), BF16),
            sds((T, D), F32),
            sds((G, D), F32),
            sds((T, DI), F32),
            sds((T, DI), BF16),
            sds((DI, D), BF16),
            sds((D, DI), BF16),
            sds((N, DI), BF16),
            sds(((N + 1) * SUB, DI), F32),
            sds((1, DI), F32),
        ],
        [
            whole((T, D)),
            whole((T, D)),
            whole((G, D)),
            col(T),
            col(T),
            row(D),
            col(D),
            col(N),
            col((N + 1) * SUB),
            col(1),
        ],
        [
            pltpu.VMEM((J * N * SUB, LANES), F32),
            pltpu.VMEM((T, LANES), F32),
            pltpu.VMEM((N, cb), F32),
            pltpu.VMEM((T, D), BF16),
            pltpu.VMEM((N, cb), F32),
        ],
    )


def scan_backward(z, where, mixed, dt, sig, yg, masks, small, suf, f_all, s_all, states):
    T, DI, N, J = z.T, z.DI, z.N, z.J
    cb = pick(DI, (768, 384, 256, 128))
    tg = tile_groups(cb)
    ng = 4
    S = f_all.shape[0]
    steps = DI // cb

    def body(wh, mix, dt_r, sg, yr, msk, sm, sf, fa, sa, st, ssg_o, dpl_o, mg_o, gs_o,
             bx, cx, cl, u_s, rates_s, fin, dg_s, rs_s, ia, oa, rt_s, low_s):
        i = pl.program_id(0)

        @pl.when(i == 0)
        def _():
            expand_columns(z, mix, z.R, bx)
            expand_columns(z, mix, z.R + N, cx)
            expand_closed(z, msk, cl)
            ia[...] = jnp.zeros_like(ia)
            oa[...] = jnp.zeros_like(oa)
            low_s[...] = jnp.zeros_like(low_s)

        me = wh[0]
        rates2 = -jnp.exp(sm[A_LOG : A_LOG + N, :]) * LOG2E
        rates_s[...] = rates2
        fin[...] = chain_states(
            S - 1, lambda k: k > me, lambda k: S - 1 - k, lambda k: sa[k], lambda k: fa[k], rates2
        )
        sigf = sg[...].astype(F32)
        u_s[...] = dt_r[...] * sigf

        def pair(p, carry):
            lanes = [lane_at(p, tg, k) for k in range(tg)]
            for g in range(0, N, ng):
                rr = [
                    [jnp.broadcast_to(rates_s[g + n : g + n + 1, lanes[k]], (SUB, LANES)) for k in range(tg)]
                    for n in range(ng)
                ]
                flow = []
                for n in range(ng):
                    for k in range(tg):
                        at = (g + n) * SUB
                        flow.append(
                            sf[at : at + SUB, lanes[k]]
                            + jnp.exp2(rr[n][k] * sf[N * SUB : (N + 1) * SUB, lanes[k]])
                            * jnp.broadcast_to(fin[g + n : g + n + 1, lanes[k]], (SUB, LANES))
                        )

                def load(j):
                    got = [[None] * tg for _ in range(ng)]
                    for n in range(0, ng, 2):
                        for k in range(tg):
                            at = pl.multiple_of(j * N * SUB + (g + n) * SUB, 2 * SUB)
                            two = st[pl.ds(at, 2 * SUB), lanes[k]].astype(F32)
                            got[n][k] = two[0:SUB]
                            got[n + 1][k] = two[SUB : 2 * SUB]
                    return [got[n][k] for n in range(ng) for k in range(tg)]

                def step_j(jj, carry):
                    fs, hs, rts = carry
                    j = J - 1 - jj
                    dtp = [dt_r[row8(j), lanes[k]] for k in range(tg)]
                    dts = [dtp[k] + cl[row8(j), :] for k in range(tg)]
                    us = [u_s[row8(j), lanes[k]] for k in range(tg)]
                    ygs = [yr[row8(j), lanes[k]] for k in range(tg)]
                    before = load(j)
                    if g == 0:
                        dgs = [jnp.zeros((SUB, LANES), F32) for k in range(tg)]
                        rss = [jnp.zeros((SUB, LANES), F32) for k in range(tg)]
                    else:
                        dgs = [dg_s[row8(j), lanes[k]] for k in range(tg)]
                        rss = [rs_s[row8(j), lanes[k]] for k in range(tg)]
                    nf, nr = [], []
                    for n in range(ng):
                        at = row8(j * N + g + n)
                        b = bx[at, :]
                        c = cx[at, :]
                        ig = jnp.zeros((SUB, LANES), F32)
                        og = jnp.zeros((SUB, LANES), F32)
                        for k in range(tg):
                            q = n * tg + k
                            grad = ygs[k] * c + fs[q]
                            f = jnp.exp2(dts[k] * rr[n][k]) * grad
                            rt = f * before[q]
                            rss[k] = rss[k] + rt * rr[n][k]
                            dgs[k] = dgs[k] + grad * b
                            nr.append(rts[q] + rt * dtp[k])
                            ig = ig + grad * us[k]
                            og = og + hs[q] * ygs[k]
                            nf.append(f)
                        ia[at, :] += ig
                        oa[at, :] += og
                    for k in range(tg):
                        dg_s[row8(j), lanes[k]] = dgs[k]
                        rs_s[row8(j), lanes[k]] = rss[k]
                    return tuple(nf), tuple(before), tuple(nr)

                zero = tuple(jnp.zeros((SUB, LANES), F32) for _ in range(ng * tg))
                _, _, rts = lax.fori_loop(
                    0, J, step_j, (tuple(flow), tuple(load(J)), zero), unroll=2
                )
                for n in range(ng):
                    for k in range(tg):
                        rt_s[g + n : g + n + 1, lanes[k]] = jnp.sum(rts[n * tg + k], axis=0, keepdims=True)
            return carry

        lax.fori_loop(0, cb // (tg * LANES), pair, 0)
        dg = dg_s[...]
        ssg_o[...] = dg * dt_r[...] + yr[...] * sm[SKIP : SKIP + 1, :]
        step_grad = rs_s[...] * LN2 + dg * sigf
        low = mix[:, 0 : z.R].astype(BF16)
        dtw = sm[z.DT0 : z.DT0 + z.R, :].astype(BF16)
        pre = mm(low, dtw) + sm[DT_B : DT_B + 1, :]
        dpg = step_grad * sigmoid(pre)
        dpl = dpg.astype(BF16)
        dpl_o[...] = dpl
        gs_o[...] = jnp.zeros_like(gs_o)
        gs_o[DT_B : DT_B + 1, :] = jnp.sum(dpg, axis=0, keepdims=True)
        gs_o[A_LOG : A_LOG + N, :] = rt_s[...] * (rates2 * LN2)
        gs_o[z.DT0 : z.DT0 + z.R, :] = mm_tn(low, dpl)
        low_s[...] += mm_nt(dpl, dtw)

        @pl.when(i == steps - 1)
        def _():
            mg_o[:, 0 : z.R] = low_s[...].astype(BF16)
            lane = lax.broadcasted_iota(jnp.int32, (SUB, LANES), 1)

            def gather(j, carry):
                both = jnp.zeros((SUB, LANES), F32)
                for n in range(N):
                    at = row8(j * N + n)
                    both = jnp.where(lane == n, jnp.sum(ia[at, :], axis=1, keepdims=True), both)
                    both = jnp.where(lane == N + n, jnp.sum(oa[at, :], axis=1, keepdims=True), both)
                cl[row8(j), :] = both
                return carry

            lax.fori_loop(0, J, gather, 0)
            mg_o[:, z.R : z.R + 2 * N] = cl[:, 0 : 2 * N].astype(BF16)

    col = lambda r: block((r, cb), lambda i: (0, i))
    wide = lambda: pltpu.VMEM((J * N * SUB, LANES), F32)
    return call(
        body,
        "scan_backward",
        (steps,),
        (where, mixed, dt, sig, yg, masks, small, suf, f_all, s_all, states),
        [
            pl.BlockSpec(memory_space=pltpu.SMEM),
            whole(mixed.shape),
            col(T),
            col(T),
            col(T),
            whole(masks.shape),
            col(z.SMALL),
            col((N + 1) * SUB),
            block((S, N, cb), lambda i: (0, 0, i)),
            block((S, 1, cb), lambda i: (0, 0, i)),
            col((J + 1) * N * SUB),
        ],
        [sds((T, DI), F32), sds((T, DI), BF16), sds((T, z.XW), BF16), sds((z.X0, DI), F32)],
        [col(T), col(T), whole((T, z.XW)), col(z.X0)],
        [
            wide(),
            wide(),
            pltpu.VMEM((T, LANES), F32),
            pltpu.VMEM((T, cb), F32),
            pltpu.VMEM((N, cb), F32),
            pltpu.VMEM((N, cb), F32),
            pltpu.VMEM((T, cb), F32),
            pltpu.VMEM((T, cb), F32),
            wide(),
            wide(),
            pltpu.VMEM((N, cb), F32),
            pltpu.VMEM((T, z.R), F32),
        ],
    )


def padded_rows(main, edge, J, cb):
    H = edge.shape[0]
    m3 = main.reshape(J, SUB, cb)
    first = lax.broadcasted_iota(jnp.int32, (SUB, cb), 0) == 0
    tail = jnp.stack(
        [
            jnp.where(
                first,
                jnp.broadcast_to(edge[H - 3 + k : H - 2 + k, :], (SUB, cb)),
                pltpu.roll(m3[J - 3 + k], 1, 0),
            )
            for k in range(3)
        ]
    )
    return jnp.concatenate([tail, m3], axis=0)


def conv_backward(z, mixed_grad, sig, ssg, conv_in, hconv, masks, small, skip):
    T, DI, J = z.T, z.DI, z.J
    H = hconv.shape[0]
    cb = pick(DI, (384, 256, 128))
    steps = DI // cb

    def body(mg, sg, ss, ci, hc, msk, sm, sk, cig_o, edge_o, gt_o, gx_o):
        mgv = mg[...]
        sgv = sg[...]
        xw = sm[z.X0 : z.X0 + z.XW, :].astype(BF16)
        gx_o[...] = mm_tn(mgv, sgv)
        sgrad = ss[...] + mm(mgv, xw)
        xpad = padded_rows(ci[...], hc[...], J, cb)
        valid = [jnp.broadcast_to(msk[:, o : o + 1], (T, cb)) for o in range(4)]
        out = jnp.broadcast_to(sm[CONV_B : CONV_B + 1, :], (T, cb))
        for o in range(4):
            out = out + sm[CONV_W + o : CONV_W + o + 1, :] * xpad[o : o + J].reshape(T, cb) * valid[o]
        s = sigmoid(out)
        cg = sgrad * (s * (1.0 + out * (1.0 - s)))
        gt_o[CONV_B : CONV_B + 1, :] = jnp.sum(cg, axis=0, keepdims=True)
        gt_o[DT_B : DT_B + 1, :] = jnp.zeros((1, cb), F32)
        gt_o[SKIP : SKIP + 1, :] = sk[...]
        gt_o[SKIP + 1 : SKIP + 2, :] = jnp.zeros((1, cb), F32)
        total = jnp.zeros((J, SUB, cb), F32)
        last = lax.broadcasted_iota(jnp.int32, (SUB, cb), 0) == SUB - 1
        edges = [jnp.zeros((1, cb), F32) for _ in range(3)]
        for o in range(4):
            masked = cg * valid[o]
            gt_o[CONV_W + o : CONV_W + o + 1, :] = jnp.sum(
                masked * xpad[o : o + J].reshape(T, cb), axis=0, keepdims=True
            )
            c3 = (sm[CONV_W + o : CONV_W + o + 1, :] * masked).reshape(J, SUB, cb)
            k = 3 - o
            if k == 0:
                total = total + c3
            else:
                wrap = jnp.stack(
                    [jnp.where(last, 0.0, pltpu.roll(c3[t], SUB - 1, 0)) for t in range(k)]
                )
                total = total + jnp.concatenate([c3[k:], wrap], axis=0)
                for i in range(o, 3):
                    edges[i] = edges[i] + c3[i - o, 0:1, :]
        cig_o[...] = total.reshape(T, cb)
        edge_o[...] = jnp.zeros_like(edge_o)
        for i in range(3):
            edge_o[i : i + 1, :] = edges[i]

    col = lambda r: block((r, cb), lambda i: (0, i))
    return call(
        body,
        "conv_backward",
        (steps,),
        (mixed_grad, sig, ssg, conv_in, hconv, masks, small, skip),
        [
            whole(mixed_grad.shape),
            col(T),
            col(T),
            col(T),
            col(H),
            whole(masks.shape),
            col(z.SMALL),
            col(1),
        ],
        [sds((T, DI), F32), sds((SUB, DI), F32), sds((SUB, DI), F32), sds((z.XW, DI), F32)],
        [col(T), col(SUB), col(SUB), col(z.XW)],
        [],
    )


def last(z, cig, edge, gate_grad, normed, w_conv, w_gate, tokens, mid_grad, gpack, ggrad):
    T, D, DI, J = z.T, z.D, z.DI, z.J
    cb = pick(DI, (384, 256, 128))
    steps = DI // cb
    G = gpack.shape[0]

    def body(cg, eg, gg, nm, wc, wg, tok, mg, gp, gpre, dw_o, tg_o, gn_o, acc):
        i = pl.program_id(0)

        @pl.when(i == 0)
        def _():
            acc[...] = jnp.zeros_like(acc)

        c3 = cg[...].reshape(J, SUB, cb)
        is_last = lax.broadcasted_iota(jnp.int32, (SUB, cb), 0) == SUB - 1
        fixed = jnp.stack(
            [
                c3[J - 3 + k]
                + jnp.where(is_last, jnp.broadcast_to(eg[k : k + 1, :], (SUB, cb)), 0.0)
                for k in range(3)
            ]
        )
        pc = jnp.concatenate([c3[: J - 3], fixed], axis=0).reshape(T, cb).astype(BF16)
        dw_o[...] = mm_tn(nm[...], pc).astype(BF16)
        acc[...] += mm_nt(pc, wc[...]) + mm_nt(gg[...], wg[...])

        @pl.when(i == steps - 1)
        def _():
            d, gain_g = rms_back(tok[...].astype(F32), gp[0:1, :], acc[...])
            tg_o[...] = mg[...] + d
            gn_o[...] = gpre[...]
            gn_o[0:1, :] = gain_g

    col = lambda r: block((r, cb), lambda i: (0, i))
    return call(
        body,
        "last",
        (steps,),
        (cig, edge, gate_grad, normed, w_conv, w_gate, tokens, mid_grad, gpack, ggrad),
        [
            col(T),
            col(SUB),
            col(T),
            whole(normed.shape),
            col(D),
            col(D),
            whole(tokens.shape),
            whole(mid_grad.shape),
            whole(gpack.shape),
            whole(ggrad.shape),
        ],
        [sds((D, DI), BF16), sds((T, D), F32), sds((G, D), F32)],
        [col(D), whole((T, D)), whole((G, D))],
        [pltpu.VMEM((T, D), F32)],
    )


def to_chunks(a, J):
    return a.reshape((SUB, J) + a.shape[1:]).swapaxes(0, 1).reshape(a.shape)


def from_chunks(a, J):
    return a.reshape((J, SUB) + a.shape[1:]).swapaxes(0, 1).reshape(a.shape)


def from_behind(block_in, axis, distance):
    devices = range(lax.axis_size(axis))
    route = [(i - distance, i) for i in devices if i - distance in devices]
    return lax.ppermute(block_in, axis, route)


def on_device(
    tokens, segment_ids, routes, cotangent, norm_gain, in_proj, conv_weight, conv_bias, x_proj,
    dt_proj, dt_bias, a_log, d_skip, out_proj, moe_gain, router, up_proj, down_proj,
):
    E = lax.axis_size("exp")
    S = lax.axis_size("seq")
    z = Sizes(tokens, in_proj, dt_proj, x_proj, a_log, up_proj, E)
    T, D, DI, N, J, CAP = z.T, z.D, z.DI, z.N, z.J, z.CAP
    me_s, me_e = lax.axis_index("seq"), lax.axis_index("exp")
    where = jnp.stack([me_s, me_e]).astype(jnp.int32)
    halo = from_behind(tokens[0, T - J :], "seq", 1)
    seg = segment_ids[0]
    seg_tail = from_behind(seg[T - 3 :], "seq", 1)

    own = in_proj.shape[1] // 2
    cw = dt_proj.shape[1]
    zero = jnp.zeros((1, cw), BF16)
    small_own = jnp.concatenate(
        [conv_weight, conv_bias[None], dt_bias[None], d_skip[None], zero, a_log, dt_proj, x_proj.T], axis=0
    )
    gr = 8 * -(-(2 + E) // 8)
    g_own = jnp.concatenate(
        [norm_gain[None], moe_gain[None], router.T, jnp.zeros((gr - 2 - E, router.shape[0]), BF16)], axis=0
    )
    w_in = lax.all_gather(in_proj, "exp", axis=0, tiled=True)
    w_out = lax.all_gather(out_proj, "exp", axis=0, tiled=True)
    small = lax.all_gather(small_own, "exp", axis=1, tiled=True).astype(F32)
    gpack_low = lax.all_gather(g_own, "exp", axis=1, tiled=True)
    gpack = gpack_low.astype(F32)
    router_t = jnp.zeros((LANES, D), BF16).at[0:E].set(gpack_low[2 : 2 + E])
    w_conv, w_gate = w_in[:, :DI], w_in[:, DI:]

    padded_seg = jnp.concatenate([seg_tail, seg])
    masks = jnp.stack([(padded_seg[o : o + T] == seg).astype(F32) for o in range(4)] + [seg * 0.0] * 4, axis=1)
    masks = to_chunks(masks, J)
    tok = to_chunks(tokens[0], J)
    cot = to_chunks(cotangent[0], J)
    route = to_chunks(routes[0, :, 0], J)
    choose = route[:, None] == jnp.arange(E)[None, :]
    upto = (jnp.arange(T)[None, :] <= jnp.arange(T)[:, None]).astype(BF16)
    counts = jnp.dot(upto, choose.astype(BF16), preferred_element_type=F32)
    rank = jnp.sum(counts * choose, axis=-1).astype(jnp.int32) - 1
    table = ((route * CAP + rank)[:, None] == jnp.arange(E * CAP)[None, :]).astype(BF16)
    choose_wide = (route[:, None] == jnp.arange(LANES)[None, :]).astype(F32)
    cot_slots = lax.dot_general(table, cot, (((0,), (0,)), ((), ())), preferred_element_type=F32).astype(BF16)

    def trade(a):
        return lax.all_to_all(a.reshape(E, CAP, -1), "exp", split_axis=0, concat_axis=0, tiled=True).reshape(a.shape)

    cot_here = trade(cot_slots)

    normed, conv_in, hconv, gate, sig, mixed = front(z, tok, halo, masks, gpack, w_conv, w_gate, small)
    dt, pre, hdev, stot, dwin = summary(z, mixed, sig, masks, small)
    h_all = lax.all_gather(hdev, "seq")
    s_all = lax.all_gather(stot, "seq")
    states, y, mid, moe, chances, outbound = scan_forward(
        z, where, mixed, dt, sig, gate, masks, small, pre, dwin, h_all, s_all, w_out, tok, gpack, router_t, table
    )
    arrived = trade(outbound)
    ret, _, dwu, dwd = expert(z, where, arrived, cot_here, router_t, up_proj[0], down_proj[0])
    up_part = lax.psum_scatter(dwu, "seq", scatter_dimension=0, tiled=True).astype(F32)
    down_part = lax.psum_scatter(dwd, "seq", scatter_dimension=0, tiled=True).astype(F32)
    ret_dx = trade(ret[1])
    ret_out = trade(ret[0])
    output, mid_grad, ggrad, yg, gate_grad, dw_out, dw_gate, fdev, suf, skip = middle(
        z, ret_out, ret_dx, table, choose_wide, chances, mid, moe, cot, gpack, router_t, gate, y, sig, small,
        w_out, mixed, dt, masks, normed
    )
    f_all = lax.all_gather(fdev, "seq")
    ssg, dpl, mixed_grad, gs = scan_backward(
        z, where, mixed, dt, sig, yg, masks, small, suf, f_all, s_all, states
    )
    cig, edge, gtop, gx = conv_backward(z, mixed_grad, sig, ssg, conv_in, hconv, masks, small, skip)
    edge_in = from_behind(edge, "seq", -1)
    dw_conv, token_grad, ggrad = last(
        z, cig, edge_in, gate_grad, normed, w_conv, w_gate, tok, mid_grad, gpack, ggrad
    )
    gsmall = jnp.concatenate([gtop + gs[0:8], gs[8:], gx], axis=0)

    def reduce_rows(g):
        part = lax.psum_scatter(g, "exp", scatter_dimension=0, tiled=True)
        return lax.psum(part, "seq").astype(F32)

    dw_in = reduce_rows(jnp.concatenate([dw_conv, dw_gate], axis=1))
    dw_out = reduce_rows(dw_out)
    gsmall = lax.psum(gsmall, ("seq", "exp"))
    gsmall = lax.dynamic_slice_in_dim(gsmall, me_e * cw, cw, axis=1)
    ggrad = lax.psum(ggrad, ("seq", "exp"))
    dwid = norm_gain.shape[0]
    ggrad = lax.dynamic_slice_in_dim(ggrad, me_e * dwid, dwid, axis=1)
    return (
        from_chunks(output, J)[None],
        from_chunks(token_grad, J)[None],
        ggrad[0],
        dw_in,
        gsmall[CONV_W : CONV_W + 4],
        gsmall[CONV_B],
        gsmall[z.X0 :].T,
        gsmall[z.DT0 : z.X0],
        gsmall[DT_B],
        gsmall[A_LOG : A_LOG + N],
        gsmall[SKIP],
        dw_out,
        ggrad[1],
        ggrad[2 : 2 + E].T,
        up_part[None],
        down_part[None],
    )


def solution(mesh):
    row = P("exp", "seq", None)
    in_specs = (
        row, P("exp", "seq"), row, row, P("exp"), P("exp", None), P(None, "exp"), P("exp"), P("exp", None),
        P(None, "exp"), P("exp"), P(None, "exp"), P("exp"), P("exp", None), P("exp"), P("exp", None),
        P("exp", None, None), P("exp", None, None),
    )
    out_specs = (
        row, row, P("exp"), P("exp", None), P(None, "exp"), P("exp"), P("exp", None), P(None, "exp"), P("exp"),
        P(None, "exp"), P("exp"), P("exp", None), P("exp"), P("exp", None), row, row,
    )
    return jax.shard_map(on_device, mesh=mesh, in_specs=in_specs, out_specs=out_specs, check_vma=False)
```

```python
import functools
import math

import jax
import jax.numpy as jnp
from jax import lax
from jax.experimental import pallas as pl
from jax.experimental.pallas import tpu as pltpu
from jax.sharding import PartitionSpec as P

EPSILON = 1e-05
LOG2E = math.log2(math.e)
LN2 = math.log(2.0)
CLOSED = 1e30
LANES = 128
SUB = 8
F32 = jnp.float32
BF16 = jnp.bfloat16
VMEM_LIMIT = 56 * 1024 * 1024


def mm(a, b):
    return lax.dot_general(a, b, (((1,), (0,)), ((), ())), preferred_element_type=F32)


def mm_nt(a, b):
    return lax.dot_general(a, b, (((1,), (1,)), ((), ())), preferred_element_type=F32)


def mm_tn(a, b):
    return lax.dot_general(a, b, (((0,), (0,)), ((), ())), preferred_element_type=F32)


def split_hi_lo(value):
    high = value.astype(BF16)
    return high, (value - high.astype(F32)).astype(BF16)


def sigmoid(v):
    return 1.0 / (1.0 + jnp.exp(-v))


def softplus(v):
    e = jnp.exp(-jnp.abs(v))
    small = e * (1.0 - e * (0.5 - e * (1.0 / 3.0 - e * 0.25)))
    return jnp.maximum(v, 0.0) + jnp.where(e < 0.01, small, jnp.log(1.0 + e))


def rms_scale(v):
    return lax.rsqrt(jnp.mean(v * v, axis=-1, keepdims=True) + EPSILON)


def rms_back(resid, gain, grad):
    s = rms_scale(resid)
    v = gain * grad
    out = s * v - resid * (s * s * s) * jnp.mean(resid * v, axis=-1, keepdims=True)
    return out, jnp.sum(grad * resid * s, axis=0, keepdims=True)


def block(shape, index):
    return pl.BlockSpec(shape, index)


def whole(shape):
    zeros = (0,) * len(shape)
    return pl.BlockSpec(shape, lambda *_: zeros)


def call(body, name, grid, ins, in_specs, outs, out_specs, scratch, cost=None):
    return pl.pallas_call(
        body,
        name=name,
        grid=grid,
        in_specs=in_specs,
        out_specs=out_specs,
        out_shape=outs,
        scratch_shapes=scratch,
        cost_estimate=cost,
        compiler_params=pltpu.CompilerParams(vmem_limit_bytes=VMEM_LIMIT),
    )(*ins)


def sds(shape, dtype):
    return jax.ShapeDtypeStruct(shape, dtype)


def pick(total, options):
    for o in options:
        if total % o == 0:
            return o
    return total


CONV_W, CONV_B, DT_B, SKIP, A_LOG = 0, 4, 5, 6, 8


class Sizes:
    def __init__(self, tokens, in_proj, dt_proj, x_proj, a_log, up_proj, exp_count):
        self.T = tokens.shape[1]
        self.D = tokens.shape[2]
        self.DI = in_proj.shape[1] // 2
        self.N = a_log.shape[0]
        self.R = dt_proj.shape[0]
        self.XW = x_proj.shape[1]
        self.FF = up_proj.shape[2]
        self.E = exp_count
        self.CAP = 2 * self.T // exp_count
        self.J = self.T // SUB
        self.DT0 = A_LOG + self.N
        self.X0 = self.DT0 + self.R
        self.SMALL = self.X0 + self.XW


MESH = pl.DeviceIdType.MESH
ANY = pl.BlockSpec(memory_space=pl.ANY)


def greet(peers):
    barrier = pltpu.get_barrier_semaphore()
    for peer in peers:
        pl.semaphore_signal(barrier, inc=1, device_id=peer, device_id_type=MESH)
    pl.semaphore_wait(barrier, len(peers))


def exchange(axis, count, arrays, spread, cid):
    n = len(arrays)
    blocks = [a.shape[1:] if not s else a.shape for a, s in zip(arrays, spread)]

    def body(*refs):
        xs, os = refs[:n], refs[n : 2 * n]
        send, recv, own = refs[2 * n :]
        me = lax.axis_index(axis)
        peers = [lax.rem(me + k, count) for k in range(1, count)]
        greet([{axis: p} for p in peers])
        copies = []
        for a in range(n):
            for k, p in enumerate(peers):
                c = pltpu.make_async_remote_copy(
                    xs[a] if spread[a] else xs[a].at[p],
                    os[a].at[me],
                    send.at[a, k],
                    recv.at[a, k],
                    device_id={axis: p},
                    device_id_type=MESH,
                )
                c.start()
                copies.append(c)
        locals_ = []
        for a in range(n):
            c = pltpu.make_async_copy(xs[a] if spread[a] else xs[a].at[me], os[a].at[me], own.at[a])
            c.start()
            locals_.append(c)
        for c in locals_ + copies:
            c.wait()

    outs = [sds((count,) + tuple(b), a.dtype) for a, b in zip(arrays, blocks)]
    return pl.pallas_call(
        body,
        name="exchange_" + axis,
        in_specs=[ANY] * n,
        out_specs=[ANY] * n,
        out_shape=outs,
        scratch_shapes=[
            pltpu.SemaphoreType.DMA((n, count - 1)),
            pltpu.SemaphoreType.DMA((n, count - 1)),
            pltpu.SemaphoreType.DMA((n,)),
        ],
        compiler_params=pltpu.CompilerParams(collective_id=cid, has_side_effects=True),
    )(*arrays)


def gather_weights(E, arrays, regions, cid):
    n = len(arrays)
    offsets = [d for k in range(1, E) for d in (-k, k)]

    def slot(d):
        return 2 * (abs(d) - 1) + (1 if d > 0 else 0)

    def body(*refs):
        xs, os = refs[:n], refs[n : 2 * n]
        zs, zr, ps, pr, cs, cr, own = refs[2 * n :]
        s, me = lax.axis_index("seq"), lax.axis_index("exp")
        chip, core = s // 2, lax.rem(s, 2)
        sib = chip * 2 + (1 - core)
        chips = [
            chip + 1 - 2 * lax.rem(chip, 2),
            chip + 2 - 4 * (chip // 2),
            3 - chip,
        ]
        right, left = lax.rem(me + 1, E), lax.rem(me + E - 1, E)
        greet(
            [{"seq": s, "exp": right}, {"seq": s, "exp": left}, {"seq": sib, "exp": me}]
            + [{"seq": q * 2 + core, "exp": me} for q in chips]
        )
        owns = [pltpu.make_async_copy(xs[a], os[a].at[me], own.at[a]) for a in range(n)]
        for c in owns:
            c.start()

        def part(a, region, q):
            rows = arrays[a].shape[0] // 2
            r = pl.ds(pl.multiple_of(core * rows, 16), rows)
            whole_cols, each = regions[a]
            if region == 0:
                return (r, slice(None)) if whole_cols == arrays[a].shape[1] else (r, pl.ds(0, whole_cols))
            return (r, pl.ds(pl.multiple_of(whole_cols + q * each, LANES), each))

        def kinds(a):
            return [1, 0] if regions[a][1] else [0]

        def z_copy(a, region, d, to_right):
            at = part(a, region, chip)
            src = xs[a].at[at] if d == 0 else os[a].at[(me + d,) + at]
            there = slot(d - 1 if to_right else d + 1)
            return pltpu.make_async_remote_copy(
                src, os[a].at[(me + d,) + at], zs.at[a, region, there], zr.at[a, region, there],
                device_id={"seq": s, "exp": right if to_right else left}, device_id_type=MESH,
            )

        def z_arrival(a, region, d):
            at = part(a, region, chip)
            ref = os[a].at[(me + d,) + at]
            return pltpu.make_async_remote_copy(
                ref, ref, zs.at[a, region, slot(d)], zr.at[a, region, slot(d)],
                device_id={"seq": s, "exp": right}, device_id_type=MESH,
            )

        def plane_copy(a, k, d):
            ref = os[a].at[(me + d,) + part(a, 1, chip)]
            return pltpu.make_async_remote_copy(
                ref, ref, ps.at[a, k, slot(d)], pr.at[a, k, slot(d)],
                device_id={"seq": chips[k] * 2 + core, "exp": me}, device_id_type=MESH,
            )

        def plane_arrival(a, k, d):
            ref = os[a].at[(me + d,) + part(a, 1, chips[k])]
            return pltpu.make_async_remote_copy(
                ref, ref, ps.at[a, k, slot(d)], pr.at[a, k, slot(d)],
                device_id={"seq": chips[k] * 2 + core, "exp": me}, device_id_type=MESH,
            )

        def sib_copy(a, which, d):
            at = part(a, 0, chip) if which == 0 else part(a, 1, chip if which == 1 else chips[which - 2])
            ref = os[a].at[(me + d,) + at]
            return pltpu.make_async_remote_copy(
                ref, ref, cs.at[a, which, slot(d)], cr.at[a, which, slot(d)],
                device_id={"seq": sib, "exp": me}, device_id_type=MESH,
            )

        def sib_arrival(a, which, d):
            rows = arrays[a].shape[0] // 2
            at = part(a, 0, chip) if which == 0 else part(a, 1, chip if which == 1 else chips[which - 2])
            ref = os[a].at[(me + d, pl.ds(pl.multiple_of((1 - core) * rows, 16), rows), at[1])]
            return pltpu.make_async_remote_copy(
                ref, ref, cs.at[a, which, slot(d)], cr.at[a, which, slot(d)],
                device_id={"seq": sib, "exp": me}, device_id_type=MESH,
            )

        def exists(d):
            return (me + d >= 0) & (me + d < E)

        def z_starts(a, region, d):
            if d <= 0:
                @pl.when(exists(d) & (me < E - 1))
                def _():
                    z_copy(a, region, d, True).start()
            if d >= 0:
                @pl.when(exists(d) & (me > 0))
                def _():
                    z_copy(a, region, d, False).start()

        order = [(a, r) for a in range(n) for r in kinds(a)]
        for a, r in order:
            z_starts(a, r, 0)

        def arrivals(k):
            for a, r in order:
                for d in (-k, k):
                    @pl.when(exists(d))
                    def _():
                        z_arrival(a, r, d).wait_recv()
                    if k < E - 1:
                        z_starts(a, r, d)

                    @pl.when(exists(d))
                    def _():
                        if r == 1:
                            for j in range(3):
                                plane_copy(a, j, d).start()
                        sib_copy(a, r, d).start()

        def plane(k):
            for a in range(n):
                if regions[a][1]:
                    for d in (-k, k):
                        @pl.when(exists(d))
                        def _():
                            for j in range(3):
                                plane_arrival(a, j, d).wait_recv()
                                sib_copy(a, 2 + j, d).start()

        for k in range(1, E):
            arrivals(k)
            if k > 1:
                plane(k - 1)
        plane(E - 1)
        for a in range(n):
            whiches = [0] + ([1, 2, 3, 4] if regions[a][1] else [])
            for d in offsets:
                @pl.when(exists(d))
                def _():
                    for w in whiches:
                        sib_arrival(a, w, d).wait_recv()
                        sib_copy(a, w, d).wait_send()
                    if regions[a][1]:
                        for j in range(3):
                            plane_copy(a, j, d).wait_send()
        for a, r in order:
            for d in [0] + offsets:
                if d <= 0 and abs(d) < E - 1:
                    @pl.when(exists(d) & (me < E - 1))
                    def _():
                        z_copy(a, r, d, True).wait_send()
                if d >= 0 and abs(d) < E - 1:
                    @pl.when(exists(d) & (me > 0))
                    def _():
                        z_copy(a, r, d, False).wait_send()
        for c in owns:
            c.wait()

    slots = 2 * (E - 1)
    sem = lambda *dims: pltpu.SemaphoreType.DMA(dims)
    return pl.pallas_call(
        body,
        name="gather_weights",
        in_specs=[ANY] * n,
        out_specs=[ANY] * n,
        out_shape=[sds((E,) + a.shape, a.dtype) for a in arrays],
        scratch_shapes=[
            sem(n, 2, slots), sem(n, 2, slots), sem(n, 3, slots), sem(n, 3, slots),
            sem(n, 5, slots), sem(n, 5, slots), sem(n),
        ],
        compiler_params=pltpu.CompilerParams(collective_id=cid, has_side_effects=True),
    )(*arrays)


def gather_chain(E, arrays, cid):
    n = len(arrays)

    def slot(d):
        return 2 * (abs(d) - 1) + (1 if d > 0 else 0)

    def body(*refs):
        xs, os = refs[:n], refs[n : 2 * n]
        zs, zr, own = refs[2 * n :]
        me = lax.axis_index("exp")
        right, left = lax.rem(me + 1, E), lax.rem(me + E - 1, E)
        greet([{"exp": right}, {"exp": left}])

        def exists(d):
            return (me + d >= 0) & (me + d < E)

        def copy(a, d, to_right):
            there = slot(d - 1 if to_right else d + 1)
            return pltpu.make_async_remote_copy(
                xs[a] if d == 0 else os[a].at[me + d], os[a].at[me + d], zs.at[a, there], zr.at[a, there],
                device_id={"exp": right if to_right else left}, device_id_type=MESH,
            )

        def arrival(a, d):
            ref = os[a].at[me + d]
            return pltpu.make_async_remote_copy(
                ref, ref, zs.at[a, slot(d)], zr.at[a, slot(d)],
                device_id={"exp": right}, device_id_type=MESH,
            )

        def each(a, d, act):
            if d <= 0:
                @pl.when(exists(d) & (me < E - 1))
                def _():
                    act(copy(a, d, True))
            if d >= 0:
                @pl.when(exists(d) & (me > 0))
                def _():
                    act(copy(a, d, False))

        for a in range(n):
            each(a, 0, lambda c: c.start())
        owns = [pltpu.make_async_copy(xs[a], os[a].at[me], own.at[a]) for a in range(n)]
        for c in owns:
            c.start()
        for k in range(1, E):
            for a in range(n):
                for d in (-k, k):
                    @pl.when(exists(d))
                    def _():
                        arrival(a, d).wait_recv()
                    if k < E - 1:
                        each(a, d, lambda c: c.start())
        for a in range(n):
            for k in range(0, E - 1):
                for d in (-k, k) if k else (0,):
                    each(a, d, lambda c: c.wait_send())
        for c in owns:
            c.wait()

    slots = 2 * (E - 1)
    return pl.pallas_call(
        body,
        name="gather_chain",
        in_specs=[ANY] * n,
        out_specs=[ANY] * n,
        out_shape=[sds((E,) + a.shape, a.dtype) for a in arrays],
        scratch_shapes=[
            pltpu.SemaphoreType.DMA((n, slots)),
            pltpu.SemaphoreType.DMA((n, slots)),
            pltpu.SemaphoreType.DMA((n,)),
        ],
        compiler_params=pltpu.CompilerParams(collective_id=cid, has_side_effects=True),
    )(*arrays)


def reduce_plane(E, p_in, p_out, p_small, cid):
    RI, CI = p_in.shape
    ri, ci = RI // 2, CI // 4
    _, ro, co = p_out.shape
    _, rs8, cs = p_small.shape
    rs = rs8 // 8
    p_small = p_small.reshape(E, 4, 2, rs, cs)
    p_out = p_out.reshape(4, 2, ro, co)

    def body(xi, xo, xs, oi, oo, os, a_i, b_i, a_o, b_o, a_s, b_s, t_i, t_o, t_s, z_s, r_i, r_o, r_s,
             lsem, c_send, c_recv, q_send, q_recv, z_send, z_recv, g_send, g_recv, f_send, f_recv):
        s, me = lax.axis_index("seq"), lax.axis_index("exp")
        chip, core = s // 2, lax.rem(s, 2)
        other = 1 - core
        sib = {"seq": chip * 2 + other, "exp": me}
        chips = [chip + 1 - 2 * lax.rem(chip, 2), chip + 2 - 4 * (chip // 2), 3 - chip]
        there = [{"seq": q * 2 + core, "exp": me} for q in chips]
        zs = [lax.rem(me + k, E) for k in range(1, E)]
        greet([sib] + there + [{"seq": s, "exp": p} for p in zs])

        def remote(src, dst, send, recv, to):
            return pltpu.make_async_remote_copy(src, dst, send, recv, device_id=to, device_id_type=MESH)

        half = lambda c: pl.ds(pl.multiple_of(c * ri, 16), ri)
        first = [
            remote(xi.at[half(other)], b_i, c_send.at[0], c_recv.at[0], sib),
            remote(xo.at[:, other], b_o, c_send.at[1], c_recv.at[1], sib),
            remote(xs.at[:, :, other], b_s, c_send.at[2], c_recv.at[2], sib),
        ]
        for c in first:
            c.start()
        mine = [
            pltpu.make_async_copy(xi.at[half(core)], a_i, lsem.at[0]),
            pltpu.make_async_copy(xo.at[:, core], a_o, lsem.at[1]),
            pltpu.make_async_copy(xs.at[:, :, core], a_s, lsem.at[2]),
        ]
        for c in mine:
            c.start()
        adds = lambda a, b: (a.astype(F32) + b.astype(F32)).astype(BF16)
        cols = lambda q: pl.ds(pl.multiple_of(q * ci, LANES), ci)
        second = []
        for w in (0, 1, 2):
            mine[w].wait()
            first[w].wait()
            if w == 0:
                a_i[...] = adds(a_i[...], b_i[...])
            elif w == 1:
                a_o[...] = adds(a_o[...], b_o[...])
            else:
                a_s[...] = adds(a_s[...], b_s[...])
            for k in range(3):
                src = [a_i.at[:, cols(chips[k])], a_o.at[chips[k]], a_s.at[:, chips[k]]][w]
                dst = [t_i, t_o, t_s][w].at[k]
                c = remote(src, dst, q_send.at[w, k], q_recv.at[w, k], there[k])
                c.start()
                second.append(c)

        def total(own, parts):
            out = own.astype(F32)
            for k in range(3):
                out = out + parts[k].astype(F32)
            return out.astype(BF16)

        for c in second[6:9]:
            c.wait()
        a_s[:, chip] = total(a_s[:, chip], t_s)
        third = []
        for k, p in enumerate(zs):
            c = remote(a_s.at[p, chip], z_s.at[me], z_send.at[k], z_recv.at[k], {"seq": s, "exp": p})
            c.start()
            third.append(c)

        gathers = []

        def spread(w, ref):
            for k in range(3):
                c = remote(ref, ref, g_send.at[w, k], g_recv.at[w, k], there[k])
                c.start()
                gathers.append(c)
            c = remote(ref, ref, f_send.at[w, 3], f_recv.at[w, 3], sib)
            c.start()
            gathers.append(c)

        for c in second[0:3]:
            c.wait()
        r_i[core, chip] = total(a_i[:, cols(chip)], t_i)
        spread(0, r_i.at[core, chip])
        for c in second[3:6]:
            c.wait()
        r_o[core, chip] = total(a_o[chip], t_o)
        spread(1, r_o.at[core, chip])
        for c in third:
            c.wait()
        out = a_s[me, chip].astype(F32)
        for k, p in enumerate(zs):
            out = out + z_s[p].astype(F32)
        r_s[core, chip] = out.astype(BF16)
        spread(2, r_s.at[core, chip])

        def landed(w, c, q):
            return [r_i, r_o, r_s][w].at[c, q]

        passed = []
        for w in (0, 1, 2):
            for k in range(3):
                ref = landed(w, core, chips[k])
                remote(ref, ref, g_send.at[w, k], g_recv.at[w, k], there[k]).wait_recv()
                c = remote(ref, ref, f_send.at[w, k], f_recv.at[w, k], sib)
                c.start()
                passed.append(c)
        for c in gathers:
            c.wait_send()
        for c in passed:
            c.wait_send()
        for w in (0, 1, 2):
            for k in range(4):
                ref = landed(w, other, chips[k] if k < 3 else chip)
                remote(ref, ref, f_send.at[w, k], f_recv.at[w, k], sib).wait_recv()
        writes = []
        for c in range(2):
            for q in range(4):
                writes.append(
                    pltpu.make_async_copy(
                        r_i.at[c, q], oi.at[c * ri : (c + 1) * ri, q * ci : (q + 1) * ci], lsem.at[3 + c * 4 + q]
                    )
                )
                writes.append(pltpu.make_async_copy(r_o.at[c, q], oo.at[q, c], lsem.at[11 + c * 4 + q]))
                writes.append(pltpu.make_async_copy(r_s.at[c, q], os.at[q, c], lsem.at[19 + c * 4 + q]))
        for c in writes:
            c.start()
        for c in writes:
            c.wait()

    v = lambda *dims: pltpu.VMEM(dims, BF16)
    sem = lambda *dims: pltpu.SemaphoreType.DMA(dims)
    oi, oo, os = pl.pallas_call(
        body,
        name="reduce_plane",
        in_specs=[ANY] * 3,
        out_specs=[ANY] * 3,
        out_shape=[sds((RI, CI), BF16), sds((4, 2, ro, co), BF16), sds((4, 2, rs, cs), BF16)],
        scratch_shapes=[
            v(ri, CI), v(ri, CI), v(4, ro, co), v(4, ro, co), v(E, 4, rs, cs), v(E, 4, rs, cs),
            v(3, ri, ci), v(3, ro, co), v(3, E, rs, cs), v(E, rs, cs),
            v(2, 4, ri, ci), v(2, 4, ro, co), v(2, 4, rs, cs),
            sem(27), sem(3), sem(3), sem(3, 3), sem(3, 3), sem(E - 1), sem(E - 1),
            sem(3, 3), sem(3, 3), sem(3, 4), sem(3, 4),
        ],
        compiler_params=pltpu.CompilerParams(
            collective_id=cid, has_side_effects=True, vmem_limit_bytes=VMEM_LIMIT
        ),
    )(p_in, p_out, p_small)
    return oi, oo.reshape(8, ro, co), os.reshape(8 * rs, cs)


def front(z, tokens, halo, masks, gpack, w_in, small):
    T, D, DI, J = z.T, z.D, z.DI, z.J
    H = halo.shape[0]
    cb = pick(DI, (384, 256, 128))
    steps = DI // cb

    def body(tok, hal, msk, gp, wc, wg, sm, normed_o, conv_o, hconv_o, gate_o, sig_o, mixed_o, nrm):
        i = pl.program_id(0)

        @pl.when(i == 0)
        def _():
            gain = gp[0:1, :]
            t = tok[...].astype(F32)
            nt = (t * rms_scale(t) * gain).astype(BF16)
            h = hal[...].astype(F32)
            nrm[0:T, :] = nt
            nrm[T : T + H, :] = (h * rms_scale(h) * gain).astype(BF16)
            normed_o[...] = nt
            mixed_o[...] = jnp.zeros_like(mixed_o)

        conv = mm(nrm[...], wc[...])
        gate_o[...] = mm(nrm[0:T, :], wg[...])
        main, edge = conv[:T], conv[T:]
        conv_o[...] = main
        hconv_o[...] = edge
        xpad = padded_rows(main, edge, J, cb)
        out = jnp.broadcast_to(sm[CONV_B : CONV_B + 1, :], (T, cb))
        for o in range(4):
            m = jnp.broadcast_to(msk[:, o : o + 1], (T, cb))
            out = out + sm[CONV_W + o : CONV_W + o + 1, :] * xpad[o : o + J].reshape(T, cb) * m
        sig = (out * sigmoid(out)).astype(BF16)
        sig_o[...] = sig
        mixed_o[...] += mm_nt(sig, sm[z.X0 : z.X0 + z.XW, :].astype(BF16))

    col = lambda r: block((r, cb), lambda i: (0, i))
    return call(
        body,
        "front",
        (steps,),
        (tokens, halo, masks, gpack, w_in, w_in, small),
        [
            whole(tokens.shape),
            whole(halo.shape),
            whole(masks.shape),
            whole(gpack.shape),
            col(D),
            block((D, cb), lambda i: (0, i + steps)),
            col(z.SMALL),
        ],
        [
            sds((T, D), BF16),
            sds((T, DI), F32),
            sds((H, DI), F32),
            sds((T, DI), F32),
            sds((T, DI), BF16),
            sds((T, z.XW), F32),
        ],
        [whole((T, D)), col(T), col(H), col(T), col(T), whole((T, z.XW))],
        [pltpu.VMEM((T + H, D), BF16)],
    )


def expand_columns(z, src, col0, dst):
    def one(j, carry):
        rows = src[pl.ds(pl.multiple_of(j * SUB, SUB), SUB), :]
        for n in range(z.N):
            at = pl.multiple_of((j * z.N + n) * SUB, SUB)
            dst[pl.ds(at, SUB), :] = jnp.broadcast_to(
                rows[:, col0 + n : col0 + n + 1], (SUB, LANES)
            )
        return carry

    lax.fori_loop(0, z.J, one, 0)


def expand_closed(z, masks, dst):
    dst[...] = jnp.broadcast_to((1.0 - masks[:, 2:3]) * CLOSED, (z.T, LANES))


def tile_groups(cb):
    return 2 if cb % (2 * LANES) == 0 else 1


def lane_at(p, tg, k):
    return pl.ds(pl.multiple_of(p * tg * LANES, LANES) + k * LANES, LANES)


def row8(j):
    return pl.ds(pl.multiple_of(j * SUB, SUB), SUB)


def shift_down(v, d):
    rows = lax.broadcasted_iota(jnp.int32, v.shape, 0)
    return jnp.where(rows >= d, pltpu.roll(v, d, 0), 0.0)


def shift_up(v, d):
    rows = lax.broadcasted_iota(jnp.int32, v.shape, 0)
    return jnp.where(rows < SUB - d, pltpu.roll(v, SUB - d, 0), 0.0)


def summary(z, mixed, sig, masks, small):
    T, DI, N, J = z.T, z.DI, z.N, z.J
    cb = pick(DI, (768, 384, 256, 128))
    tg = tile_groups(cb)
    ng = 8

    def body(mix, sg, msk, sm, dt_o, pre_o, hdev_o, stot_o, dwin_o, bx, cl, u_s, hd, rates_s):
        i = pl.program_id(0)

        @pl.when(i == 0)
        def _():
            expand_columns(z, mix, z.R, bx)
            expand_closed(z, msk, cl)

        low = mix[:, 0 : z.R].astype(BF16)
        pre = mm(low, sm[z.DT0 : z.DT0 + z.R, :].astype(BF16)) + sm[DT_B : DT_B + 1, :]
        step = softplus(pre)
        dt_o[...] = step
        u_s[...] = step * sg[...].astype(F32)
        rates_s[...] = -jnp.exp(sm[A_LOG : A_LOG + N, :]) * LOG2E

        def pair(p, carry):
            totals = []
            for k in range(tg):
                tot = jnp.zeros((SUB, LANES), F32)
                for j in range(J):
                    tot = tot + (dt_o[j * SUB : j * SUB + SUB, lane_at(p, tg, k)] + cl[j * SUB : j * SUB + SUB, :])
                totals.append(tot)
            wins = []
            for k in range(tg):
                w1 = totals[k]
                w2 = w1 + shift_down(w1, 1)
                w4 = w2 + shift_down(w2, 2)
                w8 = w4 + shift_down(w4, 4)
                wins.append((w1, w2, w4))
                dwin_o[0:SUB, lane_at(p, tg, k)] = w1
                dwin_o[SUB : 2 * SUB, lane_at(p, tg, k)] = shift_down(w8, 1)
                stot_o[:, lane_at(p, tg, k)] = w8[SUB - 1 : SUB, :]
            for g in range(0, N, ng):
                rr = [
                    [
                        jnp.broadcast_to(rates_s[g + n : g + n + 1, lane_at(p, tg, k)], (SUB, LANES))
                        for k in range(tg)
                    ]
                    for n in range(ng)
                ]

                def step_j(j, hs):
                    dts = [dt_o[row8(j), lane_at(p, tg, k)] + cl[row8(j), :] for k in range(tg)]
                    us = [u_s[row8(j), lane_at(p, tg, k)] for k in range(tg)]
                    new = []
                    for n in range(ng):
                        b = bx[row8(j * N + g + n), :]
                        for k in range(tg):
                            new.append(
                                jnp.exp2(dts[k] * rr[n][k]) * hs[n * tg + k] + us[k] * b
                            )
                    return tuple(new)

                hs = lax.fori_loop(
                    0, J, step_j, tuple(jnp.zeros((SUB, LANES), F32) for _ in range(ng * tg)), unroll=2
                )
                for n in range(ng):
                    for k in range(tg):
                        h = hs[n * tg + k]
                        w1, w2, w4 = wins[k]
                        r = rr[n][k]
                        h = h + jnp.exp2(r * w1) * shift_down(h, 1)
                        h = h + jnp.exp2(r * w2) * shift_down(h, 2)
                        h = h + jnp.exp2(r * w4) * shift_down(h, 4)
                        at = (g + n) * SUB
                        pre_o[at : at + SUB, lane_at(p, tg, k)] = shift_down(h, 1)
                        hd[g + n : g + n + 1, lane_at(p, tg, k)] = h[SUB - 1 : SUB, :]
            return carry

        lax.fori_loop(0, cb // (tg * LANES), pair, 0)
        hdev_o[...] = hd[...].astype(BF16)

    col = lambda r: block((r, cb), lambda i: (0, i))
    return call(
        body,
        "summary",
        (DI // cb,),
        (mixed, sig, masks, small),
        [whole(mixed.shape), col(T), whole(masks.shape), col(z.SMALL)],
        [
            sds((T, DI), F32),
            sds((N * SUB, DI), F32),
            sds((N, DI), BF16),
            sds((1, DI), F32),
            sds((2 * SUB, DI), F32),
        ],
        [col(T), col(N * SUB), col(N), col(1), col(2 * SUB)],
        [
            pltpu.VMEM((J * N * SUB, LANES), F32),
            pltpu.VMEM((T, LANES), F32),
            pltpu.VMEM((T, cb), F32),
            pltpu.VMEM((N, cb), F32),
            pltpu.VMEM((N, cb), F32),
        ],
    )


def chain_states(count, mine, order, sums, heads, rates2):
    state = jnp.zeros_like(rates2)
    for k in range(count):
        at = order(k)
        new = jnp.exp2(rates2 * sums(at)) * state + heads(at).astype(F32)
        state = jnp.where(mine(at), new, state)
    return state


def scan_forward(z, where, mixed, dt, sig, gate, masks, small, pre, dwin, h_all, s_all, w_out,
                 tokens, gpack, router, table):
    T, D, DI, N, J, E = z.T, z.D, z.DI, z.N, z.J, z.E
    cb = pick(DI, (768, 384, 256, 128))
    tg = tile_groups(cb)
    ng = 8
    S = h_all.shape[0]
    slots = table.shape[1]
    steps = DI // cb

    def body(wh, mix, dt_r, sg, gt, msk, sm, pr, dw, ha, sa, wo, tok, gp, rt, tb,
             st_o, y_o, mid_o, moe_o, ch_o, out_o, bx, cx, cl, u_s, rates_s, hin, acc):
        i = pl.program_id(0)

        @pl.when(i == 0)
        def _():
            expand_columns(z, mix, z.R, bx)
            expand_columns(z, mix, z.R + N, cx)
            expand_closed(z, msk, cl)
            acc[...] = jnp.zeros_like(acc)

        me = wh[0]
        rates2 = -jnp.exp(sm[A_LOG : A_LOG + N, :]) * LOG2E
        rates_s[...] = rates2
        hin[...] = chain_states(
            S - 1, lambda k: k < me, lambda k: k, lambda k: sa[k], lambda k: ha[k], rates2
        )
        u_s[...] = dt_r[...] * sg[...].astype(F32)

        def pair(p, carry):
            lanes = [lane_at(p, tg, k) for k in range(tg)]
            for g in range(0, N, ng):
                rr = [
                    [jnp.broadcast_to(rates_s[g + n : g + n + 1, lanes[k]], (SUB, LANES)) for k in range(tg)]
                    for n in range(ng)
                ]
                init = []
                for n in range(ng):
                    for k in range(tg):
                        at = (g + n) * SUB
                        init.append(
                            pr[at : at + SUB, lanes[k]]
                            + jnp.exp2(rr[n][k] * dw[SUB : 2 * SUB, lanes[k]])
                            * jnp.broadcast_to(hin[g + n : g + n + 1, lanes[k]], (SUB, LANES))
                        )

                def keep(j, hs):
                    for n in range(0, ng, 2):
                        for k in range(tg):
                            two = jnp.concatenate([hs[n * tg + k], hs[(n + 1) * tg + k]], axis=0)
                            at = pl.multiple_of(j * N * SUB + (g + n) * SUB, 2 * SUB)
                            st_o[pl.ds(at, 2 * SUB), lanes[k]] = two.astype(BF16)

                keep(0, init)

                def step_j(j, hs):
                    dts = [dt_r[row8(j), lanes[k]] + cl[row8(j), :] for k in range(tg)]
                    us = [u_s[row8(j), lanes[k]] for k in range(tg)]
                    if g == 0:
                        ys = [jnp.zeros((SUB, LANES), F32) for k in range(tg)]
                    else:
                        ys = [y_o[row8(j), lanes[k]] for k in range(tg)]
                    new = []
                    for n in range(ng):
                        b = bx[row8(j * N + g + n), :]
                        c = cx[row8(j * N + g + n), :]
                        for k in range(tg):
                            h = jnp.exp2(dts[k] * rr[n][k]) * hs[n * tg + k] + us[k] * b
                            ys[k] = ys[k] + h * c
                            new.append(h)
                    for k in range(tg):
                        y_o[row8(j), lanes[k]] = ys[k]
                    keep(j + 1, new)
                    return tuple(new)

                lax.fori_loop(0, J, step_j, tuple(init), unroll=2)
            return carry

        lax.fori_loop(0, cb // (tg * LANES), pair, 0)
        y = y_o[...] + sm[SKIP : SKIP + 1, :] * sg[...].astype(F32)
        y_o[...] = y
        g_in = gt[...]
        gated = (y * (g_in * sigmoid(g_in))).astype(BF16)
        acc[...] += mm(gated, wo[...])

        @pl.when(i == steps - 1)
        def _():
            mid = tok[...].astype(F32) + acc[...]
            mid_o[...] = mid
            moe = (mid * rms_scale(mid) * gp[1:2, :]).astype(BF16)
            moe_o[...] = moe
            logits = mm_nt(moe, rt[...])
            ch_o[...] = router_softmax(logits, E)
            out_o[...] = mm_tn(tb[...], moe).astype(BF16)

    col = lambda r: block((r, cb), lambda i: (0, i))
    return call(
        body,
        "scan_forward",
        (steps,),
        (where, mixed, dt, sig, gate, masks, small, pre, dwin, h_all, s_all, w_out, tokens, gpack, router, table),
        [
            pl.BlockSpec(memory_space=pltpu.SMEM),
            whole(mixed.shape),
            col(T),
            col(T),
            col(T),
            whole(masks.shape),
            col(z.SMALL),
            col(N * SUB),
            col(2 * SUB),
            block((S, N, cb), lambda i: (0, 0, i)),
            block((S, 1, cb), lambda i: (0, 0, i)),
            block((cb, D), lambda i: (i, 0)),
            whole(tokens.shape),
            whole(gpack.shape),
            whole(router.shape),
            whole(table.shape),
        ],
        [
            sds(((J + 1) * N * SUB, DI), BF16),
            sds((T, DI), F32),
            sds((T, D), F32),
            sds((T, D), BF16),
            sds((T, LANES), F32),
            sds((slots, D), BF16),
        ],
        [
            col((J + 1) * N * SUB),
            col(T),
            whole((T, D)),
            whole((T, D)),
            whole((T, LANES)),
            whole((slots, D)),
        ],
        [
            pltpu.VMEM((J * N * SUB, LANES), F32),
            pltpu.VMEM((J * N * SUB, LANES), F32),
            pltpu.VMEM((T, LANES), F32),
            pltpu.VMEM((T, cb), F32),
            pltpu.VMEM((N, cb), F32),
            pltpu.VMEM((N, cb), F32),
            pltpu.VMEM((T, D), F32),
        ],
    )


def router_softmax(logits, experts):
    lane = lax.broadcasted_iota(jnp.int32, logits.shape, 1)
    logits = jnp.where(lane < experts, logits, -1e30)
    top = jnp.max(logits, axis=-1, keepdims=True)
    e = jnp.where(lane < experts, jnp.exp(logits - top), 0.0)
    return e / jnp.sum(e, axis=-1, keepdims=True)


def expert(z, where, x, cot, router, up, down):
    D, FF, E = z.D, z.FF, z.E
    M = x.shape[0]
    fb = pick(FF, (512, 256, 128))
    steps = FF // fb

    def body(wh, x_r, c_r, rt, up_r, dn_r, ret_o, rdx_o, dwu_o, dwd_o, g_s, out_s, dx_s):
        i = pl.program_id(0)

        @pl.when(i == 0)
        def _():
            ch = router_softmax(mm_nt(x_r[...], rt[...]), E)
            lane = lax.broadcasted_iota(jnp.int32, ch.shape, 1)
            gating = jnp.sum(jnp.where(lane == wh[1], ch, 0.0), axis=-1, keepdims=True)
            g_s[...] = (gating * c_r[...].astype(F32)).astype(BF16)
            out_s[...] = jnp.zeros_like(out_s)
            dx_s[...] = jnp.zeros_like(dx_s)

        xv, gv = x_r[...], g_s[...]
        upv, dnv = up_r[...], dn_r[...]
        pre = mm(xv, upv)
        cdf = 0.5 * (1.0 + lax.erf(pre * (2.0 ** -0.5)))
        hidden = (pre * cdf).astype(BF16)
        slope = cdf + pre * jnp.exp(-0.5 * pre * pre) * (1.0 / math.sqrt(2.0 * math.pi))
        out_s[...] += mm(hidden, dnv)
        pg = (mm_nt(gv, dnv) * slope).astype(BF16)
        dx_s[...] += mm_nt(pg, upv)
        dwd_o[...] = mm_tn(hidden, gv).astype(BF16)
        dwu_o[...] = mm_tn(xv, pg).astype(BF16)

        @pl.when(i == steps - 1)
        def _():
            out = out_s[...].astype(BF16)
            ret_o[...] = out
            rdx_o[:, 0:D] = dx_s[...].astype(BF16)
            gg = jnp.sum(out.astype(F32) * c_r[...].astype(F32), axis=-1, keepdims=True)
            hi, lo = split_hi_lo(gg)
            lane = lax.broadcasted_iota(jnp.int32, (M, LANES), 1)
            both = jnp.where(lane == 0, hi.astype(F32), jnp.where(lane == 1, lo.astype(F32), 0.0))
            rdx_o[:, D : D + LANES] = both.astype(BF16)

    return call(
        body,
        "expert",
        (steps,),
        (where, x, cot, router, up, down),
        [
            pl.BlockSpec(memory_space=pltpu.SMEM),
            whole(x.shape),
            whole(cot.shape),
            whole(router.shape),
            block((D, fb), lambda i: (0, i)),
            block((fb, D), lambda i: (i, 0)),
        ],
        [
            sds((M, D), BF16),
            sds((M, D + LANES), BF16),
            sds((D, FF), BF16),
            sds((FF, D), BF16),
        ],
        [
            whole((M, D)),
            whole((M, D + LANES)),
            block((D, fb), lambda i: (0, i)),
            block((fb, D), lambda i: (i, 0)),
        ],
        [pltpu.VMEM((M, D), BF16), pltpu.VMEM((M, D), F32), pltpu.VMEM((M, D), F32)],
    )


def middle(z, ret_dx, table, choose, chances, mid, moe, cot, gpack, router, gate, y, sig,
           small, w_out, mixed, dt, masks):
    T, D, DI, N, J, E = z.T, z.D, z.DI, z.N, z.J, z.E
    cb = pick(DI, (384, 256, 128))
    tg = 1 if cb % 256 else 2
    tg = 3 if cb == 384 else tg
    ng = 4
    steps = DI // cb
    G = gpack.shape[0]

    def body(rd, tb, cho, chn, md, me_r, ct, gp, rt, gt, yr, sg, sm, wo, mix, dt_r, msk,
             mg_o, br, gg_o, yg_o, gi_o, gd_o, fdev_o, suf_o, skip_o,
             cx, cl, rates_s, fd):
        i = pl.program_id(0)

        @pl.when(i == 0)
        def _():
            expand_columns(z, mix, z.R + N, cx)
            expand_closed(z, msk, cl)
            tbv = tb[...]
            back = mm(tbv, rd[...])
            grad = ct[...].astype(F32)
            ch = chn[...]
            pick_e = cho[...]
            gating = jnp.sum(ch * pick_e, axis=-1, keepdims=True)
            gate_grad = back[:, D : D + 1] + back[:, D + 1 : D + 2]
            lg = ch * (gate_grad * pick_e - gate_grad * gating)
            hi, lo = split_hi_lo(lg)
            rtv = rt[...]
            mig = back[:, 0:D] + mm(hi, rtv) + mm(lo, rtv)
            mev = me_r[...]
            rg = mm_tn(hi, mev) + mm_tn(lo, mev)
            d, gain_g = rms_back(md[...], gp[1:2, :], mig)
            total = grad + d
            mg_o[...] = total
            br[...] = total.astype(BF16)
            gg_o[...] = jnp.zeros_like(gg_o)
            gg_o[1:2, :] = gain_g
            gg_o[2 : 2 + E, :] = rg[0:E, :]

        gg = mm_nt(br[...], wo[...])
        g_in = gt[...]
        s = sigmoid(g_in)
        act = g_in * s
        yv = yr[...]
        yg = gg * act
        yg_o[...] = yg
        gi = (gg * yv * (s * (1.0 + g_in * (1.0 - s)))).astype(BF16)
        gi_o[...] = gi
        gd_o[...] = (yv * act).astype(BF16)
        skip_o[...] = jnp.sum(yg * sg[...].astype(F32), axis=0, keepdims=True)
        rates_s[...] = -jnp.exp(sm[A_LOG : A_LOG + N, :]) * LOG2E

        lanes = [slice(k * LANES, (k + 1) * LANES) for k in range(tg)]
        for p in range(cb // (tg * LANES)):
            wins = []
            for k in range(tg):
                tot = jnp.zeros((SUB, LANES), F32)
                for j in range(J):
                    tot = tot + (dt_r[j * SUB : j * SUB + SUB, lanes[k]] + cl[j * SUB : j * SUB + SUB, :])
                w1 = tot
                w2 = w1 + shift_up(w1, 1)
                w4 = w2 + shift_up(w2, 2)
                w8 = w4 + shift_up(w4, 4)
                wins.append((w1, w2, w4))
                suf_o[N * SUB : (N + 1) * SUB, lanes[k]] = shift_up(w8, 1)
            for g in range(0, N, ng):
                rr = [
                    [jnp.broadcast_to(rates_s[g + n : g + n + 1, lanes[k]], (SUB, LANES)) for k in range(tg)]
                    for n in range(ng)
                ]

                def step_j(jj, fs):
                    j = J - 1 - jj
                    dts = [dt_r[row8(j), lanes[k]] + cl[row8(j), :] for k in range(tg)]
                    ygs = [yg_o[row8(j), lanes[k]] for k in range(tg)]
                    new = []
                    for n in range(ng):
                        c = cx[row8(j * N + g + n), :]
                        for k in range(tg):
                            new.append(
                                jnp.exp2(dts[k] * rr[n][k]) * (fs[n * tg + k] + ygs[k] * c)
                            )
                    return tuple(new)

                fs = lax.fori_loop(
                    0, J, step_j, tuple(jnp.zeros((SUB, LANES), F32) for _ in range(ng * tg)), unroll=2
                )
                for n in range(ng):
                    for k in range(tg):
                        f = fs[n * tg + k]
                        w1, w2, w4 = wins[k]
                        r = rr[n][k]
                        f = f + jnp.exp2(r * w1) * shift_up(f, 1)
                        f = f + jnp.exp2(r * w2) * shift_up(f, 2)
                        f = f + jnp.exp2(r * w4) * shift_up(f, 4)
                        at = (g + n) * SUB
                        suf_o[at : at + SUB, lanes[k]] = shift_up(f, 1)
                        fd[g + n : g + n + 1, lanes[k]] = f[0:1, :]
        fdev_o[...] = fd[...].astype(BF16)

    assert cb == tg * LANES
    col = lambda r: block((r, cb), lambda i: (0, i))
    row = lambda c: block((cb, c), lambda i: (i, 0))
    return call(
        body,
        "middle",
        (steps,),
        (ret_dx, table, choose, chances, mid, moe, cot, gpack, router, gate, y, sig, small,
         w_out, mixed, dt, masks),
        [
            whole(ret_dx.shape),
            whole(table.shape),
            whole(choose.shape),
            whole(chances.shape),
            whole(mid.shape),
            whole(moe.shape),
            whole(cot.shape),
            whole(gpack.shape),
            whole(router.shape),
            col(T),
            col(T),
            col(T),
            col(z.SMALL),
            row(D),
            whole(mixed.shape),
            col(T),
            whole(masks.shape),
        ],
        [
            sds((T, D), F32),
            sds((T, D), BF16),
            sds((G, D), F32),
            sds((T, DI), F32),
            sds((T, DI), BF16),
            sds((T, DI), BF16),
            sds((N, DI), BF16),
            sds(((N + 1) * SUB, DI), F32),
            sds((1, DI), F32),
        ],
        [
            whole((T, D)),
            whole((T, D)),
            whole((G, D)),
            col(T),
            col(T),
            col(T),
            col(N),
            col((N + 1) * SUB),
            col(1),
        ],
        [
            pltpu.VMEM((J * N * SUB, LANES), F32),
            pltpu.VMEM((T, LANES), F32),
            pltpu.VMEM((N, cb), F32),
            pltpu.VMEM((N, cb), F32),
        ],
    )


def scan_backward(z, where, mixed, dt, sig, yg, masks, small, suf, f_all, s_all, states):
    T, DI, N, J = z.T, z.DI, z.N, z.J
    cb = pick(DI, (768, 384, 256, 128))
    tg = tile_groups(cb)
    ng = 4
    S = f_all.shape[0]
    steps = DI // cb

    def body(wh, mix, dt_r, sg, yr, msk, sm, sf, fa, sa, st, ssg_o, dpl_o, mg_o, gs_o,
             bx, cx, cl, u_s, rates_s, fin, dg_s, rs_s, ia, oa, rt_s, low_s):
        i = pl.program_id(0)

        @pl.when(i == 0)
        def _():
            expand_columns(z, mix, z.R, bx)
            expand_columns(z, mix, z.R + N, cx)
            expand_closed(z, msk, cl)
            ia[...] = jnp.zeros_like(ia)
            oa[...] = jnp.zeros_like(oa)
            low_s[...] = jnp.zeros_like(low_s)

        me = wh[0]
        rates2 = -jnp.exp(sm[A_LOG : A_LOG + N, :]) * LOG2E
        rates_s[...] = rates2
        fin[...] = chain_states(
            S - 1, lambda k: k > me, lambda k: S - 1 - k, lambda k: sa[k], lambda k: fa[k], rates2
        )
        sigf = sg[...].astype(F32)
        u_s[...] = dt_r[...] * sigf

        def pair(p, carry):
            lanes = [lane_at(p, tg, k) for k in range(tg)]
            for g in range(0, N, ng):
                rr = [
                    [jnp.broadcast_to(rates_s[g + n : g + n + 1, lanes[k]], (SUB, LANES)) for k in range(tg)]
                    for n in range(ng)
                ]
                flow = []
                for n in range(ng):
                    for k in range(tg):
                        at = (g + n) * SUB
                        flow.append(
                            sf[at : at + SUB, lanes[k]]
                            + jnp.exp2(rr[n][k] * sf[N * SUB : (N + 1) * SUB, lanes[k]])
                            * jnp.broadcast_to(fin[g + n : g + n + 1, lanes[k]], (SUB, LANES))
                        )

                def load(j):
                    got = [[None] * tg for _ in range(ng)]
                    for n in range(0, ng, 2):
                        for k in range(tg):
                            at = pl.multiple_of(j * N * SUB + (g + n) * SUB, 2 * SUB)
                            two = st[pl.ds(at, 2 * SUB), lanes[k]].astype(F32)
                            got[n][k] = two[0:SUB]
                            got[n + 1][k] = two[SUB : 2 * SUB]
                    return [got[n][k] for n in range(ng) for k in range(tg)]

                def step_j(jj, carry):
                    fs, hs, rts = carry
                    j = J - 1 - jj
                    dtp = [dt_r[row8(j), lanes[k]] for k in range(tg)]
                    dts = [dtp[k] + cl[row8(j), :] for k in range(tg)]
                    us = [u_s[row8(j), lanes[k]] for k in range(tg)]
                    ygs = [yr[row8(j), lanes[k]] for k in range(tg)]
                    before = load(j)
                    if g == 0:
                        dgs = [jnp.zeros((SUB, LANES), F32) for k in range(tg)]
                        rss = [jnp.zeros((SUB, LANES), F32) for k in range(tg)]
                    else:
                        dgs = [dg_s[row8(j), lanes[k]] for k in range(tg)]
                        rss = [rs_s[row8(j), lanes[k]] for k in range(tg)]
                    nf, nr = [], []
                    for n in range(ng):
                        at = row8(j * N + g + n)
                        b = bx[at, :]
                        c = cx[at, :]
                        ig = jnp.zeros((SUB, LANES), F32)
                        og = jnp.zeros((SUB, LANES), F32)
                        for k in range(tg):
                            q = n * tg + k
                            grad = ygs[k] * c + fs[q]
                            f = jnp.exp2(dts[k] * rr[n][k]) * grad
                            rt = f * before[q]
                            rss[k] = rss[k] + rt * rr[n][k]
                            dgs[k] = dgs[k] + grad * b
                            nr.append(rts[q] + rt * dtp[k])
                            ig = ig + grad * us[k]
                            og = og + hs[q] * ygs[k]
                            nf.append(f)
                        ia[at, :] += ig
                        oa[at, :] += og
                    for k in range(tg):
                        dg_s[row8(j), lanes[k]] = dgs[k]
                        rs_s[row8(j), lanes[k]] = rss[k]
                    return tuple(nf), tuple(before), tuple(nr)

                zero = tuple(jnp.zeros((SUB, LANES), F32) for _ in range(ng * tg))
                _, _, rts = lax.fori_loop(
                    0, J, step_j, (tuple(flow), tuple(load(J)), zero), unroll=2
                )
                for n in range(ng):
                    for k in range(tg):
                        rt_s[g + n : g + n + 1, lanes[k]] = jnp.sum(rts[n * tg + k], axis=0, keepdims=True)
            return carry

        lax.fori_loop(0, cb // (tg * LANES), pair, 0)
        dg = dg_s[...]
        ssg_o[...] = dg * dt_r[...] + yr[...] * sm[SKIP : SKIP + 1, :]
        step_grad = rs_s[...] * LN2 + dg * sigf
        low = mix[:, 0 : z.R].astype(BF16)
        dtw = sm[z.DT0 : z.DT0 + z.R, :].astype(BF16)
        pre = mm(low, dtw) + sm[DT_B : DT_B + 1, :]
        dpg = step_grad * sigmoid(pre)
        dpl = dpg.astype(BF16)
        dpl_o[...] = dpl
        gs_o[...] = jnp.zeros_like(gs_o)
        gs_o[DT_B : DT_B + 1, :] = jnp.sum(dpg, axis=0, keepdims=True)
        gs_o[A_LOG : A_LOG + N, :] = rt_s[...] * (rates2 * LN2)
        gs_o[z.DT0 : z.DT0 + z.R, :] = mm_tn(low, dpl)
        low_s[...] += mm_nt(dpl, dtw)

        @pl.when(i == steps - 1)
        def _():
            mg_o[:, 0 : z.R] = low_s[...].astype(BF16)
            lane = lax.broadcasted_iota(jnp.int32, (SUB, LANES), 1)

            def gather(j, carry):
                both = jnp.zeros((SUB, LANES), F32)
                for n in range(N):
                    at = row8(j * N + n)
                    both = jnp.where(lane == n, jnp.sum(ia[at, :], axis=1, keepdims=True), both)
                    both = jnp.where(lane == N + n, jnp.sum(oa[at, :], axis=1, keepdims=True), both)
                cl[row8(j), :] = both
                return carry

            lax.fori_loop(0, J, gather, 0)
            mg_o[:, z.R : z.R + 2 * N] = cl[:, 0 : 2 * N].astype(BF16)

    col = lambda r: block((r, cb), lambda i: (0, i))
    wide = lambda: pltpu.VMEM((J * N * SUB, LANES), F32)
    return call(
        body,
        "scan_backward",
        (steps,),
        (where, mixed, dt, sig, yg, masks, small, suf, f_all, s_all, states),
        [
            pl.BlockSpec(memory_space=pltpu.SMEM),
            whole(mixed.shape),
            col(T),
            col(T),
            col(T),
            whole(masks.shape),
            col(z.SMALL),
            col((N + 1) * SUB),
            block((S, N, cb), lambda i: (0, 0, i)),
            block((S, 1, cb), lambda i: (0, 0, i)),
            col((J + 1) * N * SUB),
        ],
        [sds((T, DI), F32), sds((T, DI), BF16), sds((T, z.XW), BF16), sds((z.X0, DI), F32)],
        [col(T), col(T), whole((T, z.XW)), col(z.X0)],
        [
            wide(),
            wide(),
            pltpu.VMEM((T, LANES), F32),
            pltpu.VMEM((T, cb), F32),
            pltpu.VMEM((N, cb), F32),
            pltpu.VMEM((N, cb), F32),
            pltpu.VMEM((T, cb), F32),
            pltpu.VMEM((T, cb), F32),
            wide(),
            wide(),
            pltpu.VMEM((N, cb), F32),
            pltpu.VMEM((T, z.R), F32),
        ],
    )


def padded_rows(main, edge, J, cb):
    H = edge.shape[0]
    m3 = main.reshape(J, SUB, cb)
    first = lax.broadcasted_iota(jnp.int32, (SUB, cb), 0) == 0
    tail = jnp.stack(
        [
            jnp.where(
                first,
                jnp.broadcast_to(edge[H - 3 + k : H - 2 + k, :], (SUB, cb)),
                pltpu.roll(m3[J - 3 + k], 1, 0),
            )
            for k in range(3)
        ]
    )
    return jnp.concatenate([tail, m3], axis=0)


def conv_backward(z, mixed_grad, sig, ssg, conv_in, hconv, masks, small, skip):
    T, DI, J = z.T, z.DI, z.J
    H = hconv.shape[0]
    cb = pick(DI, (384, 256, 128))
    steps = DI // cb

    def body(mg, sg, ss, ci, hc, msk, sm, sk, cig_o, edge_o, gt_o, gx_o):
        mgv = mg[...]
        sgv = sg[...]
        xw = sm[z.X0 : z.X0 + z.XW, :].astype(BF16)
        gx_o[...] = mm_tn(mgv, sgv)
        sgrad = ss[...] + mm(mgv, xw)
        xpad = padded_rows(ci[...], hc[...], J, cb)
        valid = [jnp.broadcast_to(msk[:, o : o + 1], (T, cb)) for o in range(4)]
        out = jnp.broadcast_to(sm[CONV_B : CONV_B + 1, :], (T, cb))
        for o in range(4):
            out = out + sm[CONV_W + o : CONV_W + o + 1, :] * xpad[o : o + J].reshape(T, cb) * valid[o]
        s = sigmoid(out)
        cg = sgrad * (s * (1.0 + out * (1.0 - s)))
        gt_o[CONV_B : CONV_B + 1, :] = jnp.sum(cg, axis=0, keepdims=True)
        gt_o[DT_B : DT_B + 1, :] = jnp.zeros((1, cb), F32)
        gt_o[SKIP : SKIP + 1, :] = sk[...]
        gt_o[SKIP + 1 : SKIP + 2, :] = jnp.zeros((1, cb), F32)
        total = jnp.zeros((J, SUB, cb), F32)
        last = lax.broadcasted_iota(jnp.int32, (SUB, cb), 0) == SUB - 1
        edges = [jnp.zeros((1, cb), F32) for _ in range(3)]
        for o in range(4):
            masked = cg * valid[o]
            gt_o[CONV_W + o : CONV_W + o + 1, :] = jnp.sum(
                masked * xpad[o : o + J].reshape(T, cb), axis=0, keepdims=True
            )
            c3 = (sm[CONV_W + o : CONV_W + o + 1, :] * masked).reshape(J, SUB, cb)
            k = 3 - o
            if k == 0:
                total = total + c3
            else:
                wrap = jnp.stack(
                    [jnp.where(last, 0.0, pltpu.roll(c3[t], SUB - 1, 0)) for t in range(k)]
                )
                total = total + jnp.concatenate([c3[k:], wrap], axis=0)
                for i in range(o, 3):
                    edges[i] = edges[i] + c3[i - o, 0:1, :]
        cig_o[...] = total.reshape(T, cb)
        edge_o[...] = jnp.zeros_like(edge_o)
        for i in range(3):
            edge_o[i : i + 1, :] = edges[i]

    col = lambda r: block((r, cb), lambda i: (0, i))
    return call(
        body,
        "conv_backward",
        (steps,),
        (mixed_grad, sig, ssg, conv_in, hconv, masks, small, skip),
        [
            whole(mixed_grad.shape),
            col(T),
            col(T),
            col(T),
            col(H),
            whole(masks.shape),
            col(z.SMALL),
            col(1),
        ],
        [sds((T, DI), F32), sds((SUB, DI), F32), sds((SUB, DI), F32), sds((z.XW, DI), F32)],
        [col(T), col(SUB), col(SUB), col(z.XW)],
        [],
    )


def last(z, cig, edge, gate_grad, w_in, tokens, mid_grad, gpack, ggrad):
    T, D, DI, J = z.T, z.D, z.DI, z.J
    cb = pick(DI, (384, 256, 128))
    steps = DI // cb
    G = gpack.shape[0]

    def body(cg, eg, gg, wc, wg, tok, mg, gp, gpre, pc_o, tg_o, gn_o, acc):
        i = pl.program_id(0)

        @pl.when(i == 0)
        def _():
            acc[...] = jnp.zeros_like(acc)

        c3 = cg[...].reshape(J, SUB, cb)
        is_last = lax.broadcasted_iota(jnp.int32, (SUB, cb), 0) == SUB - 1
        fixed = jnp.stack(
            [
                c3[J - 3 + k]
                + jnp.where(is_last, jnp.broadcast_to(eg[k : k + 1, :], (SUB, cb)), 0.0)
                for k in range(3)
            ]
        )
        pc = jnp.concatenate([c3[: J - 3], fixed], axis=0).reshape(T, cb).astype(BF16)
        pc_o[...] = pc
        acc[...] += mm_nt(pc, wc[...]) + mm_nt(gg[...], wg[...])

        @pl.when(i == steps - 1)
        def _():
            d, gain_g = rms_back(tok[...].astype(F32), gp[0:1, :], acc[...])
            tg_o[...] = mg[...] + d
            gn_o[...] = gpre[...]
            gn_o[0:1, :] = gain_g

    col = lambda r: block((r, cb), lambda i: (0, i))
    return call(
        body,
        "last",
        (steps,),
        (cig, edge, gate_grad, w_in, w_in, tokens, mid_grad, gpack, ggrad),
        [
            col(T),
            col(SUB),
            col(T),
            col(D),
            block((D, cb), lambda i: (0, i + steps)),
            whole(tokens.shape),
            whole(mid_grad.shape),
            whole(gpack.shape),
            whole(ggrad.shape),
        ],
        [sds((T, DI), BF16), sds((T, D), F32), sds((G, D), F32)],
        [col(T), whole((T, D)), whole((G, D))],
        [pltpu.VMEM((T, D), F32)],
    )


def to_chunks(a, J):
    return a.reshape((SUB, J) + a.shape[1:]).swapaxes(0, 1).reshape(a.shape)


def from_chunks(a, J):
    return a.reshape((J, SUB) + a.shape[1:]).swapaxes(0, 1).reshape(a.shape)


def from_behind(block_in, axis, distance):
    devices = range(lax.axis_size(axis))
    route = [(i - distance, i) for i in devices if i - distance in devices]
    return lax.ppermute(block_in, axis, route)


def on_device(
    tokens, segment_ids, routes, cotangent, norm_gain, in_proj, conv_weight, conv_bias, x_proj,
    dt_proj, dt_bias, a_log, d_skip, out_proj, moe_gain, router, up_proj, down_proj,
):
    E = lax.axis_size("exp")
    S = lax.axis_size("seq")
    z = Sizes(tokens, in_proj, dt_proj, x_proj, a_log, up_proj, E)
    T, D, DI, N, J, CAP = z.T, z.D, z.DI, z.N, z.J, z.CAP
    me_s, me_e = lax.axis_index("seq"), lax.axis_index("exp")
    where = jnp.stack([me_s, me_e]).astype(jnp.int32)
    halo = from_behind(tokens[0, T - J :], "seq", 1)
    seg = segment_ids[0]
    seg_tail = from_behind(seg[T - 3 :], "seq", 1)

    cw = dt_proj.shape[1]
    dw = norm_gain.shape[0]
    plane = S == 8 and dw % 32 == 0
    small_own = jnp.concatenate(
        [conv_weight, conv_bias[None], dt_bias[None], d_skip[None], jnp.zeros((1, cw), BF16), a_log, dt_proj,
         x_proj.T, jnp.zeros((-z.SMALL % 32, cw), BF16)], axis=0
    )
    g_own = jnp.concatenate(
        [norm_gain[None], moe_gain[None], router.T, jnp.zeros((32 - 2 - E, dw), BF16)], axis=0
    )
    owned = [in_proj, out_proj, small_own, g_own]
    if plane:
        each = lambda cols, most: (cols - 4 * most * LANES, most * LANES)
        tiles_in, tiles_out = 2 * DI // LANES, D // LANES
        regions = [
            each(2 * DI, max(1, tiles_in * 5 // 36)), each(D, max(1, tiles_out * 2 // 9)), (cw, 0), (dw, 0)
        ]
        w_in, w_out, small, gpack_low = gather_weights(E, owned, regions, 1)
    else:
        w_in, w_out, small, gpack_low = [lax.all_gather(a, "exp") for a in owned]
    w_in = w_in.reshape(D, 2 * DI)
    w_out = w_out.reshape(DI, D)
    join = lambda a: a.swapaxes(0, 1).reshape(a.shape[1], -1)
    small = join(small[:, : z.SMALL]).astype(F32)
    gpack_low = join(gpack_low[:, : 2 + E])
    gr = 8 * -(-(2 + E) // 8)
    gpack = jnp.zeros((gr, D), F32).at[: 2 + E].set(gpack_low.astype(F32))
    router_t = jnp.zeros((LANES, D), BF16).at[0:E].set(gpack_low[2 : 2 + E])

    padded_seg = jnp.concatenate([seg_tail, seg])
    masks = jnp.stack([(padded_seg[o : o + T] == seg).astype(F32) for o in range(4)] + [seg * 0.0] * 4, axis=1)
    masks = to_chunks(masks, J)
    tok = to_chunks(tokens[0], J)
    cot = to_chunks(cotangent[0], J)
    route = to_chunks(routes[0, :, 0], J)
    choose = route[:, None] == jnp.arange(E)[None, :]
    upto = (jnp.arange(T)[None, :] <= jnp.arange(T)[:, None]).astype(BF16)
    counts = jnp.dot(upto, choose.astype(BF16), preferred_element_type=F32)
    rank = jnp.sum(counts * choose, axis=-1).astype(jnp.int32) - 1
    table = ((route * CAP + rank)[:, None] == jnp.arange(E * CAP)[None, :]).astype(BF16)
    choose_wide = (route[:, None] == jnp.arange(LANES)[None, :]).astype(F32)
    cot_slots = lax.dot_general(table, cot, (((0,), (0,)), ((), ())), preferred_element_type=F32).astype(BF16)

    def trade(a):
        return lax.all_to_all(a, "exp", split_axis=0, concat_axis=0, tiled=True)

    def columns(a):
        return a.reshape(T, E, -1).swapaxes(0, 1)

    cot_here = trade(cot_slots.reshape(E, CAP, D)).reshape(E * CAP, D)

    normed, conv_in, hconv, gate, sig, mixed = front(z, tok, halo, masks, gpack, w_in, small)
    normed_z = trade(columns(normed)).reshape(E * T, -1)
    dt, pre, hdev, stot, dwin = summary(z, mixed, sig, masks, small)
    h_all, s_all = exchange("seq", S, [hdev, stot], [True, True], 2)
    states, y, mid, moe, chances, outbound = scan_forward(
        z, where, mixed, dt, sig, gate, masks, small, pre, dwin, h_all, s_all, w_out, tok, gpack, router_t, table
    )
    (arrived,) = exchange("exp", E, [outbound.reshape(E, CAP, D)], [False], 3)
    ret_out, ret_dx, dwu, dwd = expert(
        z, where, arrived.reshape(E * CAP, D), cot_here, router_t, up_proj[0], down_proj[0]
    )
    (back_dx,) = exchange("exp", E, [ret_dx.reshape(E, CAP, -1)], [False], 4)
    up_part, down_part = scatter_plane(dwu, dwd, S)
    back_out = trade(ret_out.reshape(E, CAP, D)).reshape(E * CAP, D)
    mid_grad, branch, ggrad, yg, gate_grad, gated, fdev, suf, skip = middle(
        z, back_dx.reshape(E * CAP, -1), table, choose_wide, chances, mid, moe, cot, gpack, router_t, gate, y, sig,
        small, w_out, mixed, dt, masks
    )
    (f_all,) = exchange("seq", S, [fdev], [True], 5)
    gated_z = trade(columns(gated)).reshape(E * T, -1)
    branch_all = lax.all_gather(branch, "exp", tiled=True)
    gate_all = lax.all_gather(gate_grad, "exp", tiled=True)
    out_rows = contract(gated_z, branch_all).astype(BF16)
    gate_cols = contract(normed_z, gate_all).astype(BF16)
    gating = jnp.sum(chances * choose_wide, axis=-1, keepdims=True)
    output = (mid + gating * jnp.dot(table, back_out, preferred_element_type=F32)).astype(BF16)
    ssg, dpl, mixed_grad, gs = scan_backward(
        z, where, mixed, dt, sig, yg, masks, small, suf, f_all, s_all, states
    )
    cig, edge, gtop, gx = conv_backward(z, mixed_grad, sig, ssg, conv_in, hconv, masks, small, skip)
    edge_in = from_behind(edge, "seq", -1)
    conv_grad, token_grad, ggrad = last(z, cig, edge_in, gate_grad, w_in, tok, mid_grad, gpack, ggrad)
    (conv_all,) = gather_chain(E, [conv_grad], 6)
    conv_cols = contract(normed_z, conv_all.reshape(E * T, DI)).astype(BF16)

    gsmall = jnp.concatenate([gtop + gs[0:8], gs[8:], gx], axis=0)
    blocks = lambda a: a.reshape(a.shape[0], E, -1).swapaxes(0, 1)
    gpart = jnp.pad(blocks(ggrad), ((0, 0), (0, 0), (0, cw - dw)))
    rows = z.SMALL + gr
    pad = -rows % 128
    smalls = jnp.concatenate(
        [blocks(gsmall), gpart, jnp.zeros((E, pad, cw), F32)], axis=1
    ).astype(BF16)
    cols = jnp.concatenate([conv_cols, gate_cols], axis=1)
    if plane:
        each = cw // 8
        each_pad = 16 * -(-each // 16)
        padded = jnp.pad(out_rows.reshape(8, each, D), ((0, 0), (0, each_pad - each), (0, 0)))
        dw_in, dw_out, gsum = reduce_plane(E, cols, padded, smalls, 7)
        dw_out = dw_out[:, :each].reshape(cw, D)
    else:
        dw_in, dw_out = lax.psum(cols, "seq"), lax.psum(out_rows, "seq")
        gsum = lax.psum_scatter(lax.psum(smalls, "seq"), "exp", scatter_dimension=0, tiled=True)[0]
    gsum = gsum.astype(F32)
    return (
        from_chunks(output, J)[None],
        from_chunks(token_grad, J)[None],
        gsum[z.SMALL, :dw],
        dw_in.astype(F32),
        gsum[CONV_W : CONV_W + 4],
        gsum[CONV_B],
        gsum[z.X0 : z.SMALL].T,
        gsum[z.DT0 : z.X0],
        gsum[DT_B],
        gsum[A_LOG : A_LOG + N],
        gsum[SKIP],
        dw_out.astype(F32),
        gsum[z.SMALL + 1, :dw],
        gsum[z.SMALL + 2 : z.SMALL + 2 + E, :dw].T,
        up_part[None],
        down_part[None],
    )


def contract(a, b):
    return lax.dot_general(a, b, (((0,), (0,)), ((), ())), preferred_element_type=F32)


def scatter_plane(a, b, S):
    if S != 8:
        return [lax.psum_scatter(v, "seq", scatter_dimension=0, tiled=True).astype(F32) for v in (a, b)]
    s = lax.axis_index("seq")
    place = {1: lax.rem(s, 2), 2: lax.rem(s // 2, 2), 4: s // 4}

    def halve(v, axis, bit):
        keep = lax.dynamic_index_in_dim(v, place[bit], axis, keepdims=False)
        give = lax.dynamic_index_in_dim(v, 1 - place[bit], axis, keepdims=False)
        got = lax.ppermute(give, "seq", [(i, i ^ bit) for i in range(8)])
        return keep.astype(F32) + got.astype(F32)

    split = lambda v: v.reshape((2, 2, 2, v.shape[0] // 8) + v.shape[1:])
    a, b = split(a), split(b)
    a, b = halve(a, 2, 1).astype(BF16), halve(b, 2, 1).astype(BF16)
    a, b = halve(a, 1, 2).astype(BF16), halve(b, 0, 4).astype(BF16)
    return halve(a, 0, 4), halve(b, 0, 2)


def solution(mesh):
    row = P("exp", "seq", None)
    in_specs = (
        row, P("exp", "seq"), row, row, P("exp"), P("exp", None), P(None, "exp"), P("exp"), P("exp", None),
        P(None, "exp"), P("exp"), P(None, "exp"), P("exp"), P("exp", None), P("exp"), P("exp", None),
        P("exp", None, None), P("exp", None, None),
    )
    out_specs = (
        row, row, P("exp"), P("exp", None), P(None, "exp"), P("exp"), P("exp", None), P(None, "exp"), P("exp"),
        P(None, "exp"), P("exp"), P("exp", None), P("exp"), P("exp", None), row, row,
    )
    return jax.shard_map(on_device, mesh=mesh, in_specs=in_specs, out_specs=out_specs, check_vma=False)
```

```python
import functools
import math

import jax
import jax.numpy as jnp
from jax import lax
from jax.experimental import pallas as pl
from jax.experimental.pallas import tpu as pltpu
from jax.sharding import PartitionSpec as P

EPSILON = 1e-05
LOG2E = math.log2(math.e)
LN2 = math.log(2.0)
CLOSED = 1e30
LANES = 128
SUB = 8
F32 = jnp.float32
BF16 = jnp.bfloat16
VMEM_LIMIT = 56 * 1024 * 1024


def mm(a, b):
    return lax.dot_general(a, b, (((1,), (0,)), ((), ())), preferred_element_type=F32)


def mm_nt(a, b):
    return lax.dot_general(a, b, (((1,), (1,)), ((), ())), preferred_element_type=F32)


def mm_tn(a, b):
    return lax.dot_general(a, b, (((0,), (0,)), ((), ())), preferred_element_type=F32)


def split_hi_lo(value):
    high = value.astype(BF16)
    return high, (value - high.astype(F32)).astype(BF16)


def sigmoid(v):
    return 1.0 / (1.0 + jnp.exp(-v))


def softplus(v):
    e = jnp.exp(-jnp.abs(v))
    small = e * (1.0 - e * (0.5 - e * (1.0 / 3.0 - e * 0.25)))
    return jnp.maximum(v, 0.0) + jnp.where(e < 0.01, small, jnp.log(1.0 + e))


def rms_scale(v):
    return lax.rsqrt(jnp.mean(v * v, axis=-1, keepdims=True) + EPSILON)


def rms_back(resid, gain, grad):
    s = rms_scale(resid)
    v = gain * grad
    out = s * v - resid * (s * s * s) * jnp.mean(resid * v, axis=-1, keepdims=True)
    return out, jnp.sum(grad * resid * s, axis=0, keepdims=True)


def block(shape, index):
    return pl.BlockSpec(shape, index)


def whole(shape):
    zeros = (0,) * len(shape)
    return pl.BlockSpec(shape, lambda *_: zeros)


def call(body, name, grid, ins, in_specs, outs, out_specs, scratch, cost=None):
    return pl.pallas_call(
        body,
        name=name,
        grid=grid,
        in_specs=in_specs,
        out_specs=out_specs,
        out_shape=outs,
        scratch_shapes=scratch,
        cost_estimate=cost,
        compiler_params=pltpu.CompilerParams(vmem_limit_bytes=VMEM_LIMIT),
    )(*ins)


def sds(shape, dtype):
    return jax.ShapeDtypeStruct(shape, dtype)


def pick(total, options):
    for o in options:
        if total % o == 0:
            return o
    return total


CONV_W, CONV_B, DT_B, SKIP, A_LOG = 0, 4, 5, 6, 8


class Sizes:
    def __init__(self, tokens, in_proj, dt_proj, x_proj, a_log, up_proj, exp_count):
        self.T = tokens.shape[1]
        self.D = tokens.shape[2]
        self.DI = in_proj.shape[1] // 2
        self.N = a_log.shape[0]
        self.R = dt_proj.shape[0]
        self.XW = x_proj.shape[1]
        self.FF = up_proj.shape[2]
        self.E = exp_count
        self.CAP = 2 * self.T // exp_count
        self.J = self.T // SUB
        self.DT0 = A_LOG + self.N
        self.X0 = self.DT0 + self.R
        self.SMALL = self.X0 + self.XW


MESH = pl.DeviceIdType.MESH
ANY = pl.BlockSpec(memory_space=pl.ANY)


def greet(peers):
    barrier = pltpu.get_barrier_semaphore()
    for peer in peers:
        pl.semaphore_signal(barrier, inc=1, device_id=peer, device_id_type=MESH)
    pl.semaphore_wait(barrier, len(peers))


def exchange(axis, count, arrays, spread, cid):
    n = len(arrays)
    blocks = [a.shape[1:] if not s else a.shape for a, s in zip(arrays, spread)]

    def body(*refs):
        xs, os = refs[:n], refs[n : 2 * n]
        send, recv, own = refs[2 * n : 2 * n + 3]
        held = refs[2 * n + 3 :]
        me = lax.axis_index(axis)
        ins = [
            pltpu.make_async_copy(xs[a] if spread[a] else xs[a].at[me], held[a], own.at[a]) for a in range(n)
        ]
        for c in ins:
            c.start()
        peers = [lax.rem(me + k, count) for k in range(1, count)]
        greet([{axis: p} for p in peers])
        copies = []
        for a in range(n):
            for k, p in enumerate(peers):
                c = pltpu.make_async_remote_copy(
                    xs[a] if spread[a] else xs[a].at[p],
                    os[a].at[me],
                    send.at[a, k],
                    recv.at[a, k],
                    device_id={axis: p},
                    device_id_type=MESH,
                )
                c.start()
                copies.append(c)
        locals_ = []
        for a in range(n):
            ins[a].wait()
            c = pltpu.make_async_copy(held[a], os[a].at[me], own.at[a])
            c.start()
            locals_.append(c)
        for c in locals_ + copies:
            c.wait()

    outs = [sds((count,) + tuple(b), a.dtype) for a, b in zip(arrays, blocks)]
    return pl.pallas_call(
        body,
        name="exchange_" + axis,
        in_specs=[ANY] * n,
        out_specs=[ANY] * n,
        out_shape=outs,
        scratch_shapes=[
            pltpu.SemaphoreType.DMA((n, count - 1)),
            pltpu.SemaphoreType.DMA((n, count - 1)),
            pltpu.SemaphoreType.DMA((n,)),
        ]
        + [pltpu.VMEM(b, a.dtype) for a, b in zip(arrays, blocks)],
        compiler_params=pltpu.CompilerParams(collective_id=cid, has_side_effects=True),
    )(*arrays)


def gather_weights(E, arrays, regions, cid):
    n = len(arrays)
    offsets = [d for k in range(1, E) for d in (-k, k)]

    def slot(d):
        return 2 * (abs(d) - 1) + (1 if d > 0 else 0)

    def body(*refs):
        xs, os = refs[:n], refs[n : 2 * n]
        zs, zr, ps, pr, cs, cr, own = refs[2 * n : 2 * n + 7]
        held = refs[2 * n + 7 :]
        s, me = lax.axis_index("seq"), lax.axis_index("exp")
        chip, core = s // 2, lax.rem(s, 2)
        sib = chip * 2 + (1 - core)
        chips = [
            chip + 1 - 2 * lax.rem(chip, 2),
            chip + 2 - 4 * (chip // 2),
            3 - chip,
        ]
        right, left = lax.rem(me + 1, E), lax.rem(me + E - 1, E)
        greet(
            [{"seq": s, "exp": right}, {"seq": s, "exp": left}, {"seq": sib, "exp": me}]
            + [{"seq": q * 2 + core, "exp": me} for q in chips]
        )
        ins = [pltpu.make_async_copy(xs[a], held[a], own.at[a]) for a in range(n)]
        owns = [pltpu.make_async_copy(held[a], os[a].at[me], own.at[a]) for a in range(n)]
        for c in ins:
            c.start()

        def part(a, region, q):
            rows = arrays[a].shape[0] // 2
            r = pl.ds(pl.multiple_of(core * rows, 16), rows)
            whole_cols, each = regions[a]
            if region == 0:
                return (r, slice(None)) if whole_cols == arrays[a].shape[1] else (r, pl.ds(0, whole_cols))
            return (r, pl.ds(pl.multiple_of(whole_cols + q * each, LANES), each))

        def kinds(a):
            return [1, 0] if regions[a][1] else [0]

        def z_copy(a, region, d, to_right):
            at = part(a, region, chip)
            src = xs[a].at[at] if d == 0 else os[a].at[(me + d,) + at]
            there = slot(d - 1 if to_right else d + 1)
            return pltpu.make_async_remote_copy(
                src, os[a].at[(me + d,) + at], zs.at[a, region, there], zr.at[a, region, there],
                device_id={"seq": s, "exp": right if to_right else left}, device_id_type=MESH,
            )

        def z_arrival(a, region, d):
            at = part(a, region, chip)
            ref = os[a].at[(me + d,) + at]
            return pltpu.make_async_remote_copy(
                ref, ref, zs.at[a, region, slot(d)], zr.at[a, region, slot(d)],
                device_id={"seq": s, "exp": right}, device_id_type=MESH,
            )

        def plane_copy(a, k, d):
            ref = os[a].at[(me + d,) + part(a, 1, chip)]
            return pltpu.make_async_remote_copy(
                ref, ref, ps.at[a, k, slot(d)], pr.at[a, k, slot(d)],
                device_id={"seq": chips[k] * 2 + core, "exp": me}, device_id_type=MESH,
            )

        def plane_arrival(a, k, d):
            ref = os[a].at[(me + d,) + part(a, 1, chips[k])]
            return pltpu.make_async_remote_copy(
                ref, ref, ps.at[a, k, slot(d)], pr.at[a, k, slot(d)],
                device_id={"seq": chips[k] * 2 + core, "exp": me}, device_id_type=MESH,
            )

        def sib_copy(a, which, d):
            at = part(a, 0, chip) if which == 0 else part(a, 1, chip if which == 1 else chips[which - 2])
            ref = os[a].at[(me + d,) + at]
            return pltpu.make_async_remote_copy(
                ref, ref, cs.at[a, which, slot(d)], cr.at[a, which, slot(d)],
                device_id={"seq": sib, "exp": me}, device_id_type=MESH,
            )

        def sib_arrival(a, which, d):
            rows = arrays[a].shape[0] // 2
            at = part(a, 0, chip) if which == 0 else part(a, 1, chip if which == 1 else chips[which - 2])
            ref = os[a].at[(me + d, pl.ds(pl.multiple_of((1 - core) * rows, 16), rows), at[1])]
            return pltpu.make_async_remote_copy(
                ref, ref, cs.at[a, which, slot(d)], cr.at[a, which, slot(d)],
                device_id={"seq": sib, "exp": me}, device_id_type=MESH,
            )

        def exists(d):
            return (me + d >= 0) & (me + d < E)

        def z_starts(a, region, d):
            if d <= 0:
                @pl.when(exists(d) & (me < E - 1))
                def _():
                    z_copy(a, region, d, True).start()
            if d >= 0:
                @pl.when(exists(d) & (me > 0))
                def _():
                    z_copy(a, region, d, False).start()

        order = [(a, r) for a in range(n) for r in kinds(a)]
        for a, r in order:
            z_starts(a, r, 0)

        for a in range(n):
            ins[a].wait()
            owns[a].start()

        def arrivals(k):
            for a, r in order:
                for d in (-k, k):
                    @pl.when(exists(d))
                    def _():
                        z_arrival(a, r, d).wait_recv()
                    if k < E - 1:
                        z_starts(a, r, d)

                    @pl.when(exists(d))
                    def _():
                        if r == 1:
                            for j in range(3):
                                plane_copy(a, j, d).start()
                        sib_copy(a, r, d).start()

        def plane(k):
            for a in range(n):
                if regions[a][1]:
                    for d in (-k, k):
                        @pl.when(exists(d))
                        def _():
                            for j in range(3):
                                plane_arrival(a, j, d).wait_recv()
                                sib_copy(a, 2 + j, d).start()

        for k in range(1, E):
            arrivals(k)
            if k > 1:
                plane(k - 1)
        plane(E - 1)
        for a in range(n):
            whiches = [0] + ([1, 2, 3, 4] if regions[a][1] else [])
            for d in offsets:
                @pl.when(exists(d))
                def _():
                    for w in whiches:
                        sib_arrival(a, w, d).wait_recv()
                        sib_copy(a, w, d).wait_send()
                    if regions[a][1]:
                        for j in range(3):
                            plane_copy(a, j, d).wait_send()
        for a, r in order:
            for d in [0] + offsets:
                if d <= 0 and abs(d) < E - 1:
                    @pl.when(exists(d) & (me < E - 1))
                    def _():
                        z_copy(a, r, d, True).wait_send()
                if d >= 0 and abs(d) < E - 1:
                    @pl.when(exists(d) & (me > 0))
                    def _():
                        z_copy(a, r, d, False).wait_send()
        for c in owns:
            c.wait()

    slots = 2 * (E - 1)
    sem = lambda *dims: pltpu.SemaphoreType.DMA(dims)
    return pl.pallas_call(
        body,
        name="gather_weights",
        in_specs=[ANY] * n,
        out_specs=[ANY] * n,
        out_shape=[sds((E,) + a.shape, a.dtype) for a in arrays],
        scratch_shapes=[
            sem(n, 2, slots), sem(n, 2, slots), sem(n, 3, slots), sem(n, 3, slots),
            sem(n, 5, slots), sem(n, 5, slots), sem(n),
        ]
        + [pltpu.VMEM(a.shape, a.dtype) for a in arrays],
        compiler_params=pltpu.CompilerParams(
            collective_id=cid, has_side_effects=True, vmem_limit_bytes=VMEM_LIMIT
        ),
    )(*arrays)


def reduce_plane(E, p_in, p_out, p_small, cid):
    RI, CI = p_in.shape
    ri, ci = RI // 2, CI // 4
    _, ro, co = p_out.shape
    _, rs8, cs = p_small.shape
    rs = rs8 // 8
    p_small = p_small.reshape(E, 4, 2, rs, cs)
    p_out = p_out.reshape(4, 2, ro, co)

    def body(xi, xo, xs, oi, oo, os, a_i, b_i, a_o, b_o, a_s, b_s, t_i, t_o, t_s, z_s, r_i, r_o, r_s,
             lsem, c_send, c_recv, q_send, q_recv, z_send, z_recv, g_send, g_recv, f_send, f_recv):
        s, me = lax.axis_index("seq"), lax.axis_index("exp")
        chip, core = s // 2, lax.rem(s, 2)
        other = 1 - core
        sib = {"seq": chip * 2 + other, "exp": me}
        chips = [chip + 1 - 2 * lax.rem(chip, 2), chip + 2 - 4 * (chip // 2), 3 - chip]
        there = [{"seq": q * 2 + core, "exp": me} for q in chips]
        zs = [lax.rem(me + k, E) for k in range(1, E)]
        greet([sib] + there + [{"seq": s, "exp": p} for p in zs])

        def remote(src, dst, send, recv, to):
            return pltpu.make_async_remote_copy(src, dst, send, recv, device_id=to, device_id_type=MESH)

        half = lambda c: pl.ds(pl.multiple_of(c * ri, 16), ri)
        first = [
            remote(xi.at[half(other)], b_i, c_send.at[0], c_recv.at[0], sib),
            remote(xo.at[:, other], b_o, c_send.at[1], c_recv.at[1], sib),
            remote(xs.at[:, :, other], b_s, c_send.at[2], c_recv.at[2], sib),
        ]
        for c in first:
            c.start()
        mine = [
            pltpu.make_async_copy(xi.at[half(core)], a_i, lsem.at[0]),
            pltpu.make_async_copy(xo.at[:, core], a_o, lsem.at[1]),
            pltpu.make_async_copy(xs.at[:, :, core], a_s, lsem.at[2]),
        ]
        for c in mine:
            c.start()
        adds = lambda a, b: (a.astype(F32) + b.astype(F32)).astype(BF16)
        cols = lambda q: pl.ds(pl.multiple_of(q * ci, LANES), ci)
        second = []
        for w in (0, 1, 2):
            mine[w].wait()
            first[w].wait()
            if w == 0:
                a_i[...] = adds(a_i[...], b_i[...])
            elif w == 1:
                a_o[...] = adds(a_o[...], b_o[...])
            else:
                a_s[...] = adds(a_s[...], b_s[...])
            for k in range(3):
                src = [a_i.at[:, cols(chips[k])], a_o.at[chips[k]], a_s.at[:, chips[k]]][w]
                dst = [t_i, t_o, t_s][w].at[k]
                c = remote(src, dst, q_send.at[w, k], q_recv.at[w, k], there[k])
                c.start()
                second.append(c)

        def total(own, parts):
            out = own.astype(F32)
            for k in range(3):
                out = out + parts[k].astype(F32)
            return out.astype(BF16)

        for c in second[6:9]:
            c.wait()
        a_s[:, chip] = total(a_s[:, chip], t_s)
        third = []
        for k, p in enumerate(zs):
            c = remote(a_s.at[p, chip], z_s.at[me], z_send.at[k], z_recv.at[k], {"seq": s, "exp": p})
            c.start()
            third.append(c)

        gathers = []

        def spread(w, ref):
            for k in range(3):
                c = remote(ref, ref, g_send.at[w, k], g_recv.at[w, k], there[k])
                c.start()
                gathers.append(c)
            c = remote(ref, ref, f_send.at[w, 3], f_recv.at[w, 3], sib)
            c.start()
            gathers.append(c)

        for c in second[0:3]:
            c.wait()
        r_i[core, chip] = total(a_i[:, cols(chip)], t_i)
        spread(0, r_i.at[core, chip])
        for c in second[3:6]:
            c.wait()
        r_o[core, chip] = total(a_o[chip], t_o)
        spread(1, r_o.at[core, chip])
        for c in third:
            c.wait()
        out = a_s[me, chip].astype(F32)
        for k, p in enumerate(zs):
            out = out + z_s[p].astype(F32)
        r_s[core, chip] = out.astype(BF16)
        spread(2, r_s.at[core, chip])

        def landed(w, c, q):
            return [r_i, r_o, r_s][w].at[c, q]

        passed = []
        for w in (0, 1, 2):
            for k in range(3):
                ref = landed(w, core, chips[k])
                remote(ref, ref, g_send.at[w, k], g_recv.at[w, k], there[k]).wait_recv()
                c = remote(ref, ref, f_send.at[w, k], f_recv.at[w, k], sib)
                c.start()
                passed.append(c)
        for c in gathers:
            c.wait_send()
        for c in passed:
            c.wait_send()
        for w in (0, 1, 2):
            for k in range(4):
                ref = landed(w, other, chips[k] if k < 3 else chip)
                remote(ref, ref, f_send.at[w, k], f_recv.at[w, k], sib).wait_recv()
        writes = []
        for c in range(2):
            for q in range(4):
                writes.append(
                    pltpu.make_async_copy(
                        r_i.at[c, q], oi.at[c * ri : (c + 1) * ri, q * ci : (q + 1) * ci], lsem.at[3 + c * 4 + q]
                    )
                )
                writes.append(pltpu.make_async_copy(r_o.at[c, q], oo.at[q, c], lsem.at[11 + c * 4 + q]))
                writes.append(pltpu.make_async_copy(r_s.at[c, q], os.at[q, c], lsem.at[19 + c * 4 + q]))
        for c in writes:
            c.start()
        for c in writes:
            c.wait()

    v = lambda *dims: pltpu.VMEM(dims, BF16)
    sem = lambda *dims: pltpu.SemaphoreType.DMA(dims)
    oi, oo, os = pl.pallas_call(
        body,
        name="reduce_plane",
        in_specs=[ANY] * 3,
        out_specs=[ANY] * 3,
        out_shape=[sds((RI, CI), BF16), sds((4, 2, ro, co), BF16), sds((4, 2, rs, cs), BF16)],
        scratch_shapes=[
            v(ri, CI), v(ri, CI), v(4, ro, co), v(4, ro, co), v(E, 4, rs, cs), v(E, 4, rs, cs),
            v(3, ri, ci), v(3, ro, co), v(3, E, rs, cs), v(E, rs, cs),
            v(2, 4, ri, ci), v(2, 4, ro, co), v(2, 4, rs, cs),
            sem(27), sem(3), sem(3), sem(3, 3), sem(3, 3), sem(E - 1), sem(E - 1),
            sem(3, 3), sem(3, 3), sem(3, 4), sem(3, 4),
        ],
        compiler_params=pltpu.CompilerParams(
            collective_id=cid, has_side_effects=True, vmem_limit_bytes=VMEM_LIMIT
        ),
    )(p_in, p_out, p_small)
    return oi, oo.reshape(8, ro, co), os.reshape(8 * rs, cs)


def front(z, tokens, halo, masks, gpack, w_in, small):
    T, D, DI, J = z.T, z.D, z.DI, z.J
    H = halo.shape[0]
    cb = pick(DI, (384, 256, 128))
    steps = DI // cb

    def body(tok, hal, msk, gp, wc, wg, sm, normed_o, conv_o, hconv_o, gate_o, sig_o, mixed_o, nrm):
        i = pl.program_id(0)

        @pl.when(i == 0)
        def _():
            gain = gp[0:1, :]
            t = tok[...].astype(F32)
            nt = (t * rms_scale(t) * gain).astype(BF16)
            h = hal[...].astype(F32)
            nrm[0:T, :] = nt
            nrm[T : T + H, :] = (h * rms_scale(h) * gain).astype(BF16)
            normed_o[...] = nt
            mixed_o[...] = jnp.zeros_like(mixed_o)

        conv = mm(nrm[...], wc[...])
        gate_o[...] = mm(nrm[0:T, :], wg[...])
        main, edge = conv[:T], conv[T:]
        conv_o[...] = main
        hconv_o[...] = edge
        xpad = padded_rows(main, edge, J, cb)
        out = jnp.broadcast_to(sm[CONV_B : CONV_B + 1, :], (T, cb))
        for o in range(4):
            m = jnp.broadcast_to(msk[:, o : o + 1], (T, cb))
            out = out + sm[CONV_W + o : CONV_W + o + 1, :] * xpad[o : o + J].reshape(T, cb) * m
        sig = (out * sigmoid(out)).astype(BF16)
        sig_o[...] = sig
        mixed_o[...] += mm_nt(sig, sm[z.X0 : z.X0 + z.XW, :].astype(BF16))

    col = lambda r: block((r, cb), lambda i: (0, i))
    return call(
        body,
        "front",
        (steps,),
        (tokens, halo, masks, gpack, w_in, w_in, small),
        [
            whole(tokens.shape),
            whole(halo.shape),
            whole(masks.shape),
            whole(gpack.shape),
            col(D),
            block((D, cb), lambda i: (0, i + steps)),
            col(z.SMALL),
        ],
        [
            sds((T, D), BF16),
            sds((T, DI), F32),
            sds((H, DI), F32),
            sds((T, DI), F32),
            sds((T, DI), BF16),
            sds((T, z.XW), F32),
        ],
        [whole((T, D)), col(T), col(H), col(T), col(T), whole((T, z.XW))],
        [pltpu.VMEM((T + H, D), BF16)],
    )


def expand_columns(z, src, col0, dst):
    def one(j, carry):
        rows = src[pl.ds(pl.multiple_of(j * SUB, SUB), SUB), :]
        for n in range(z.N):
            at = pl.multiple_of((j * z.N + n) * SUB, SUB)
            dst[pl.ds(at, SUB), :] = jnp.broadcast_to(
                rows[:, col0 + n : col0 + n + 1], (SUB, LANES)
            )
        return carry

    lax.fori_loop(0, z.J, one, 0)


def expand_closed(z, masks, dst):
    dst[...] = jnp.broadcast_to((1.0 - masks[:, 2:3]) * CLOSED, (z.T, LANES))


def tile_groups(cb):
    return 2 if cb % (2 * LANES) == 0 else 1


def lane_at(p, tg, k):
    return pl.ds(pl.multiple_of(p * tg * LANES, LANES) + k * LANES, LANES)


def row8(j):
    return pl.ds(pl.multiple_of(j * SUB, SUB), SUB)


def shift_down(v, d):
    rows = lax.broadcasted_iota(jnp.int32, v.shape, 0)
    return jnp.where(rows >= d, pltpu.roll(v, d, 0), 0.0)


def shift_up(v, d):
    rows = lax.broadcasted_iota(jnp.int32, v.shape, 0)
    return jnp.where(rows < SUB - d, pltpu.roll(v, SUB - d, 0), 0.0)


def summary(z, mixed, sig, masks, small):
    T, DI, N, J = z.T, z.DI, z.N, z.J
    cb = pick(DI, (768, 384, 256, 128))
    tg = tile_groups(cb)
    ng = 8

    def body(mix, sg, msk, sm, dt_o, pre_o, hdev_o, stot_o, dwin_o, bx, cl, u_s, hd, rates_s):
        i = pl.program_id(0)

        @pl.when(i == 0)
        def _():
            expand_columns(z, mix, z.R, bx)
            expand_closed(z, msk, cl)

        low = mix[:, 0 : z.R].astype(BF16)
        pre = mm(low, sm[z.DT0 : z.DT0 + z.R, :].astype(BF16)) + sm[DT_B : DT_B + 1, :]
        step = softplus(pre)
        dt_o[...] = step
        u_s[...] = step * sg[...].astype(F32)
        rates_s[...] = -jnp.exp(sm[A_LOG : A_LOG + N, :]) * LOG2E

        def pair(p, carry):
            totals = []
            for k in range(tg):
                tot = jnp.zeros((SUB, LANES), F32)
                for j in range(J):
                    tot = tot + (dt_o[j * SUB : j * SUB + SUB, lane_at(p, tg, k)] + cl[j * SUB : j * SUB + SUB, :])
                totals.append(tot)
            wins = []
            for k in range(tg):
                w1 = totals[k]
                w2 = w1 + shift_down(w1, 1)
                w4 = w2 + shift_down(w2, 2)
                w8 = w4 + shift_down(w4, 4)
                wins.append((w1, w2, w4))
                dwin_o[0:SUB, lane_at(p, tg, k)] = w1
                dwin_o[SUB : 2 * SUB, lane_at(p, tg, k)] = shift_down(w8, 1)
                stot_o[:, lane_at(p, tg, k)] = w8[SUB - 1 : SUB, :]
            for g in range(0, N, ng):
                rr = [
                    [
                        jnp.broadcast_to(rates_s[g + n : g + n + 1, lane_at(p, tg, k)], (SUB, LANES))
                        for k in range(tg)
                    ]
                    for n in range(ng)
                ]

                def step_j(j, hs):
                    dts = [dt_o[row8(j), lane_at(p, tg, k)] + cl[row8(j), :] for k in range(tg)]
                    us = [u_s[row8(j), lane_at(p, tg, k)] for k in range(tg)]
                    new = []
                    for n in range(ng):
                        b = bx[row8(j * N + g + n), :]
                        for k in range(tg):
                            new.append(
                                jnp.exp2(dts[k] * rr[n][k]) * hs[n * tg + k] + us[k] * b
                            )
                    return tuple(new)

                hs = lax.fori_loop(
                    0, J, step_j, tuple(jnp.zeros((SUB, LANES), F32) for _ in range(ng * tg)), unroll=2
                )
                for n in range(ng):
                    for k in range(tg):
                        h = hs[n * tg + k]
                        w1, w2, w4 = wins[k]
                        r = rr[n][k]
                        h = h + jnp.exp2(r * w1) * shift_down(h, 1)
                        h = h + jnp.exp2(r * w2) * shift_down(h, 2)
                        h = h + jnp.exp2(r * w4) * shift_down(h, 4)
                        at = (g + n) * SUB
                        pre_o[at : at + SUB, lane_at(p, tg, k)] = shift_down(h, 1)
                        hd[g + n : g + n + 1, lane_at(p, tg, k)] = h[SUB - 1 : SUB, :]
            return carry

        lax.fori_loop(0, cb // (tg * LANES), pair, 0)
        hdev_o[...] = hd[...].astype(BF16)

    col = lambda r: block((r, cb), lambda i: (0, i))
    return call(
        body,
        "summary",
        (DI // cb,),
        (mixed, sig, masks, small),
        [whole(mixed.shape), col(T), whole(masks.shape), col(z.SMALL)],
        [
            sds((T, DI), F32),
            sds((N * SUB, DI), F32),
            sds((N, DI), BF16),
            sds((1, DI), F32),
            sds((2 * SUB, DI), F32),
        ],
        [col(T), col(N * SUB), col(N), col(1), col(2 * SUB)],
        [
            pltpu.VMEM((J * N * SUB, LANES), F32),
            pltpu.VMEM((T, LANES), F32),
            pltpu.VMEM((T, cb), F32),
            pltpu.VMEM((N, cb), F32),
            pltpu.VMEM((N, cb), F32),
        ],
    )


def chain_states(count, mine, order, sums, heads, rates2):
    state = jnp.zeros_like(rates2)
    for k in range(count):
        at = order(k)
        new = jnp.exp2(rates2 * sums(at)) * state + heads(at).astype(F32)
        state = jnp.where(mine(at), new, state)
    return state


def scan_forward(z, where, mixed, dt, sig, gate, masks, small, pre, dwin, h_all, s_all, w_out,
                 tokens, gpack, router, table):
    T, D, DI, N, J, E = z.T, z.D, z.DI, z.N, z.J, z.E
    cb = pick(DI, (768, 384, 256, 128))
    tg = tile_groups(cb)
    ng = 8
    S = h_all.shape[0]
    slots = table.shape[1]
    steps = DI // cb

    def body(wh, mix, dt_r, sg, gt, msk, sm, pr, dw, ha, sa, wo, tok, gp, rt, tb,
             st_o, y_o, mid_o, moe_o, ch_o, out_o, bx, cx, cl, u_s, rates_s, hin, acc):
        i = pl.program_id(0)

        @pl.when(i == 0)
        def _():
            expand_columns(z, mix, z.R, bx)
            expand_columns(z, mix, z.R + N, cx)
            expand_closed(z, msk, cl)
            acc[...] = jnp.zeros_like(acc)

        me = wh[0]
        rates2 = -jnp.exp(sm[A_LOG : A_LOG + N, :]) * LOG2E
        rates_s[...] = rates2
        hin[...] = chain_states(
            S - 1, lambda k: k < me, lambda k: k, lambda k: sa[k], lambda k: ha[k], rates2
        )
        u_s[...] = dt_r[...] * sg[...].astype(F32)

        def pair(p, carry):
            lanes = [lane_at(p, tg, k) for k in range(tg)]
            for g in range(0, N, ng):
                rr = [
                    [jnp.broadcast_to(rates_s[g + n : g + n + 1, lanes[k]], (SUB, LANES)) for k in range(tg)]
                    for n in range(ng)
                ]
                init = []
                for n in range(ng):
                    for k in range(tg):
                        at = (g + n) * SUB
                        init.append(
                            pr[at : at + SUB, lanes[k]]
                            + jnp.exp2(rr[n][k] * dw[SUB : 2 * SUB, lanes[k]])
                            * jnp.broadcast_to(hin[g + n : g + n + 1, lanes[k]], (SUB, LANES))
                        )

                def keep(j, hs):
                    for n in range(0, ng, 2):
                        for k in range(tg):
                            two = jnp.concatenate([hs[n * tg + k], hs[(n + 1) * tg + k]], axis=0)
                            at = pl.multiple_of(j * N * SUB + (g + n) * SUB, 2 * SUB)
                            st_o[pl.ds(at, 2 * SUB), lanes[k]] = two.astype(BF16)

                keep(0, init)

                def step_j(j, hs):
                    dts = [dt_r[row8(j), lanes[k]] + cl[row8(j), :] for k in range(tg)]
                    us = [u_s[row8(j), lanes[k]] for k in range(tg)]
                    if g == 0:
                        ys = [jnp.zeros((SUB, LANES), F32) for k in range(tg)]
                    else:
                        ys = [y_o[row8(j), lanes[k]] for k in range(tg)]
                    new = []
                    for n in range(ng):
                        b = bx[row8(j * N + g + n), :]
                        c = cx[row8(j * N + g + n), :]
                        for k in range(tg):
                            h = jnp.exp2(dts[k] * rr[n][k]) * hs[n * tg + k] + us[k] * b
                            ys[k] = ys[k] + h * c
                            new.append(h)
                    for k in range(tg):
                        y_o[row8(j), lanes[k]] = ys[k]
                    keep(j + 1, new)
                    return tuple(new)

                lax.fori_loop(0, J, step_j, tuple(init), unroll=2)
            return carry

        lax.fori_loop(0, cb // (tg * LANES), pair, 0)
        y = y_o[...] + sm[SKIP : SKIP + 1, :] * sg[...].astype(F32)
        y_o[...] = y
        g_in = gt[...]
        gated = (y * (g_in * sigmoid(g_in))).astype(BF16)
        acc[...] += mm(gated, wo[...])

        @pl.when(i == steps - 1)
        def _():
            mid = tok[...].astype(F32) + acc[...]
            mid_o[...] = mid
            moe = (mid * rms_scale(mid) * gp[1:2, :]).astype(BF16)
            moe_o[...] = moe
            logits = mm_nt(moe, rt[...])
            ch_o[...] = router_softmax(logits, E)
            out_o[...] = mm_tn(tb[...], moe).astype(BF16)

    col = lambda r: block((r, cb), lambda i: (0, i))
    return call(
        body,
        "scan_forward",
        (steps,),
        (where, mixed, dt, sig, gate, masks, small, pre, dwin, h_all, s_all, w_out, tokens, gpack, router, table),
        [
            pl.BlockSpec(memory_space=pltpu.SMEM),
            whole(mixed.shape),
            col(T),
            col(T),
            col(T),
            whole(masks.shape),
            col(z.SMALL),
            col(N * SUB),
            col(2 * SUB),
            block((S, N, cb), lambda i: (0, 0, i)),
            block((S, 1, cb), lambda i: (0, 0, i)),
            block((cb, D), lambda i: (i, 0)),
            whole(tokens.shape),
            whole(gpack.shape),
            whole(router.shape),
            whole(table.shape),
        ],
        [
            sds(((J + 1) * N * SUB, DI), BF16),
            sds((T, DI), F32),
            sds((T, D), F32),
            sds((T, D), BF16),
            sds((T, LANES), F32),
            sds((slots, D), BF16),
        ],
        [
            col((J + 1) * N * SUB),
            col(T),
            whole((T, D)),
            whole((T, D)),
            whole((T, LANES)),
            whole((slots, D)),
        ],
        [
            pltpu.VMEM((J * N * SUB, LANES), F32),
            pltpu.VMEM((J * N * SUB, LANES), F32),
            pltpu.VMEM((T, LANES), F32),
            pltpu.VMEM((T, cb), F32),
            pltpu.VMEM((N, cb), F32),
            pltpu.VMEM((N, cb), F32),
            pltpu.VMEM((T, D), F32),
        ],
    )


def router_softmax(logits, experts):
    lane = lax.broadcasted_iota(jnp.int32, logits.shape, 1)
    logits = jnp.where(lane < experts, logits, -1e30)
    top = jnp.max(logits, axis=-1, keepdims=True)
    e = jnp.where(lane < experts, jnp.exp(logits - top), 0.0)
    return e / jnp.sum(e, axis=-1, keepdims=True)


def expert(z, where, x, cot, router, up, down):
    D, FF, E = z.D, z.FF, z.E
    M = x.shape[0]
    fb = FF // 8
    steps = 4

    def body(wh, x_r, c_r, rt, up_r, dn_r, ret_o, rdx_o, dwu_o, dwd_o, g_s, out_s, dx_s):
        i = pl.program_id(0)

        @pl.when(i == 0)
        def _():
            ch = router_softmax(mm_nt(x_r[...], rt[...]), E)
            lane = lax.broadcasted_iota(jnp.int32, ch.shape, 1)
            gating = jnp.sum(jnp.where(lane == wh[1], ch, 0.0), axis=-1, keepdims=True)
            g_s[...] = (gating * c_r[...].astype(F32)).astype(BF16)
            out_s[...] = jnp.zeros_like(out_s)
            dx_s[...] = jnp.zeros_like(dx_s)

        xv, gv = x_r[...], g_s[...]
        upv, dnv = up_r[...], dn_r[...]
        pre = mm(xv, upv)
        cdf = 0.5 * (1.0 + lax.erf(pre * (2.0 ** -0.5)))
        hidden = (pre * cdf).astype(BF16)
        slope = cdf + pre * jnp.exp(-0.5 * pre * pre) * (1.0 / math.sqrt(2.0 * math.pi))
        out_s[...] += mm(hidden, dnv)
        pg = (mm_nt(gv, dnv) * slope).astype(BF16)
        dx_s[...] += mm_nt(pg, upv)
        dwd_o[...] = mm_tn(hidden, gv).astype(BF16)
        dwu_o[...] = mm_tn(xv, pg).astype(BF16)

        @pl.when(i == steps - 1)
        def _():
            out = out_s[...]
            ret_o[...] = out.astype(BF16)
            rdx_o[:, 0:D] = dx_s[...].astype(BF16)
            gg = jnp.sum(out * c_r[...].astype(F32), axis=-1, keepdims=True)
            hi, lo = split_hi_lo(gg)
            lane = lax.broadcasted_iota(jnp.int32, (M, LANES), 1)
            both = jnp.where(lane == 0, hi.astype(F32), jnp.where(lane == 1, lo.astype(F32), 0.0))
            rdx_o[:, D : D + LANES] = both.astype(BF16)

    whole_ = lambda shape: pl.BlockSpec(shape, lambda i, w: (0,) * len(shape))
    return pl.pallas_call(
        body,
        name="expert",
        grid_spec=pltpu.PrefetchScalarGridSpec(
            num_scalar_prefetch=1,
            grid=(steps,),
            in_specs=[
                whole_(x.shape),
                whole_(cot.shape),
                whole_(router.shape),
                pl.BlockSpec((D, fb), lambda i, w: (0, 2 * i + w[2])),
                pl.BlockSpec((fb, D), lambda i, w: (2 * i + w[2], 0)),
            ],
            out_specs=[
                whole_((M, D)),
                whole_((M, D + LANES)),
                pl.BlockSpec((D, fb), lambda i, w: (0, i)),
                pl.BlockSpec((fb, D), lambda i, w: (i, 0)),
            ],
            scratch_shapes=[pltpu.VMEM((M, D), BF16), pltpu.VMEM((M, D), F32), pltpu.VMEM((M, D), F32)],
        ),
        out_shape=[
            sds((M, D), BF16),
            sds((M, D + LANES), BF16),
            sds((D, steps * fb), BF16),
            sds((steps * fb, D), BF16),
        ],
        compiler_params=pltpu.CompilerParams(vmem_limit_bytes=VMEM_LIMIT),
    )(where, x, cot, router, up, down)


def padded_rows(main, edge, J, cb):
    H = edge.shape[0]
    m3 = main.reshape(J, SUB, cb)
    first = lax.broadcasted_iota(jnp.int32, (SUB, cb), 0) == 0
    tail = jnp.stack(
        [
            jnp.where(
                first,
                jnp.broadcast_to(edge[H - 3 + k : H - 2 + k, :], (SUB, cb)),
                pltpu.roll(m3[J - 3 + k], 1, 0),
            )
            for k in range(3)
        ]
    )
    return jnp.concatenate([tail, m3], axis=0)


def at_cols(i, cb):
    return pl.ds(pl.multiple_of(i * cb, LANES), cb)


def lanes_of(i, cb, p, tg, k):
    return pl.ds(pl.multiple_of(i * cb + p * tg * LANES, LANES) + k * LANES, LANES)


class Chain:
    def __init__(self, E, src, dst, send, recv, own):
        self.E, self.src, self.dst, self.send, self.recv, self.own = E, src, dst, send, recv, own
        self.me = lax.axis_index("exp")
        self.right, self.left = lax.rem(self.me + 1, E), lax.rem(self.me + E - 1, E)

    def slot(self, d):
        return 2 * (abs(d) - 1) + (1 if d > 0 else 0)

    def exists(self, d):
        return (self.me + d >= 0) & (self.me + d < self.E)

    def each(self, d, act):
        for to_right in (True, False):
            if (d <= 0) if to_right else (d >= 0):
                edge = self.me < self.E - 1 if to_right else self.me > 0
                there = self.slot(d - 1 if to_right else d + 1)

                @pl.when(self.exists(d) & edge)
                def _():
                    act(
                        pltpu.make_async_remote_copy(
                            self.src if d == 0 else self.dst.at[self.me + d],
                            self.dst.at[self.me + d],
                            self.send.at[there],
                            self.recv.at[there],
                            device_id={"exp": self.right if to_right else self.left},
                            device_id_type=MESH,
                        )
                    )

    def local(self):
        return pltpu.make_async_copy(self.src, self.dst.at[self.me], self.own)

    def start(self):
        self.each(0, lambda c: c.start())
        self.local().start()

    def hop(self, k):
        for d in (-k, k):
            ref = self.dst.at[self.me + d]

            @pl.when(self.exists(d))
            def _():
                pltpu.make_async_remote_copy(
                    ref, ref, self.send.at[self.slot(d)], self.recv.at[self.slot(d)],
                    device_id={"exp": self.right}, device_id_type=MESH,
                ).wait_recv()

            if k < self.E - 1:
                self.each(d, lambda c: c.start())

    def finish(self):
        for k in range(self.E - 1):
            for d in (-k, k) if k else (0,):
                self.each(d, lambda c: c.wait_send())
        self.local().wait()


def backward(z, S, plane, dxp, outp, dwu, dwd, states, w_out, w_in, table, choose, chances, mid, moe, cot, gpack,
             router, gate, y, sig, small, mixed, dt, masks, conv_in, hconv, s_all, tok, cid):
    T, D, DI, N, J, E, CAP = z.T, z.D, z.DI, z.N, z.J, z.E, z.CAP
    M = E * CAP
    G = gpack.shape[0]
    H = hconv.shape[0]
    DZ = DI // E
    cb_m = pick(DI, (384, 256, 128))
    cb_s = pick(DI, (768, 384, 256, 128))
    steps_s = DI // cb_s
    tg_s = tile_groups(cb_s)
    ng_s = 4
    uq, uc = dwu.shape[0] // 4, dwu.shape[1]
    dq, dc = dwd.shape[0] // 4, dwd.shape[1]
    ST = (J + 1) * N * SUB
    rows_big = max(ST, 2 * D)
    chain_slots = 2 * (E - 1)

    def body(
        dxp, outp, dwu, dwd, states, w_out, w_in, table, choose, chances, mid, moe, cot, gp, router, gate, y, sig,
        small, mixed, dt, masks, conv_in, hconv, s_all, tok,
        tg_o, gs_o, gg_o, back_o, gate_o, pc_o, br_o, gz_o, up_o, down_o,
        big, wo_v, dx_a, dx_b, out_a, out_b, dx_z, yg, gi, gd, gz, br, mg, fdev, f_all, suf, ssg, dpl, cig, cg_edge,
        edge_in, pc, bx, cx, ia, oa, cl, u_s, rates_s, fin, dg_s, rs_s, rt_s, low_s, mxg, acc, fd,
        ua, ub, ub2, uf, da, db, db2,
        ld, sw_s, sw_r, dz_s, dz_r, oz_s, oz_r, f_s, f_r, e_s, e_r, g_s, g_r, p_s, p_r, b_s, b_r, a_s, a_r, x_s, x_r,
    ):
        s, me = lax.axis_index("seq"), lax.axis_index("exp")
        core = lax.rem(s, 2)
        other = 1 - core
        sib = {"seq": s + 1 - 2 * core}
        seqs = [lax.rem(s + k, S) for k in range(1, S)]
        zs = [lax.rem(me + k, E) for k in range(1, E)]
        greet([{"seq": p} for p in seqs] + [{"exp": p} for p in zs])

        def remote(src, dst, send, recv, to):
            return pltpu.make_async_remote_copy(src, dst, send, recv, device_id=to, device_id_type=MESH)

        swaps = [
            remote(dxp.at[other], dx_b, sw_s.at[0], sw_r.at[0], sib),
            remote(outp.at[other], out_b, sw_s.at[1], sw_r.at[1], sib),
        ]
        for c in swaps:
            c.start()
        loads = [
            pltpu.make_async_copy(dxp.at[core], dx_a, ld.at[0]),
            pltpu.make_async_copy(outp.at[core], out_a, ld.at[1]),
            pltpu.make_async_copy(w_out, wo_v, ld.at[2]),
        ]
        for c in loads:
            c.start()

        def state_load(i):
            half = pl.ds((i % 2) * cb_s, cb_s)
            return pltpu.make_async_copy(
                states.at[:, i * cb_s : (i + 1) * cb_s], big.at[0:ST, half], ld.at[3 + i % 2]
            )

        state_load(0).start()
        if plane:
            chip = s // 2
            xx, yy = lax.rem(chip, 2), chip // 2
            to_x = {"seq": s + 2 - 4 * xx}
            to_y = {"seq": s + 4 - 8 * yy}
            u4 = lambda ref, v, w: ref.at[pl.ds(pl.multiple_of((2 * v + w) * uq, 16), uq)]
            up1 = [
                remote(u4(dwu, v, 1 - xx), ub.at[v], a_s.at[v], a_r.at[v], to_x) for v in range(2)
            ]
            d_half = lambda v: pl.ds(pl.multiple_of(v * 2 * dq, 16), 2 * dq)
            down1 = remote(dwd.at[d_half(1 - yy)], db, a_s.at[2], a_r.at[2], to_y)
            for c in up1 + [down1]:
                c.start()
            mine = [pltpu.make_async_copy(u4(dwu, v, xx), ua.at[v], ld.at[5 + v]) for v in range(2)]
            mine.append(pltpu.make_async_copy(dwd.at[d_half(yy)], da, ld.at[7]))
            for c in mine:
                c.start()

        adds = lambda a, b: (a.astype(F32) + b.astype(F32)).astype(BF16)
        loads[0].wait()
        swaps[0].wait()
        dx_a[...] = adds(dx_a[...], dx_b[...])
        block_of = lambda ref, p: ref.at[pl.ds(pl.multiple_of(p * CAP, 16), CAP)]
        dx_moves = [
            remote(block_of(dx_a, p), block_of(dx_z, me), dz_s.at[k], dz_r.at[k], {"exp": p})
            for k, p in enumerate(zs)
        ]
        for c in dx_moves:
            c.start()
        here = pl.ds(pl.multiple_of(me * CAP, 16), CAP)
        dx_z[here, :] = dx_a[here, :]
        loads[1].wait()
        swaps[1].wait()
        out_a[...] = adds(out_a[...], out_b[...])
        out_moves = [
            remote(block_of(out_a, p), block_of(back_o, me), oz_s.at[k], oz_r.at[k], {"exp": p})
            for k, p in enumerate(zs)
        ]
        for c in out_moves:
            c.start()
        back_own = pltpu.make_async_copy(block_of(out_a, me), block_of(back_o, me), ld.at[8])
        back_own.start()
        expand_columns(z, mixed, z.R, bx)
        expand_columns(z, mixed, z.R + N, cx)
        expand_closed(z, masks, cl)
        for c in dx_moves:
            c.wait()

        back = mm(table[...], dx_z[...])
        grad = cot[...].astype(F32)
        ch = chances[...]
        pick_e = choose[...]
        gating = jnp.sum(ch * pick_e, axis=-1, keepdims=True)
        gate_grad = back[:, D : D + 1] + back[:, D + 1 : D + 2]
        lg = ch * (gate_grad * pick_e - gate_grad * gating)
        hi, lo = split_hi_lo(lg)
        rtv = router[...]
        mig = back[:, 0:D] + mm(hi, rtv) + mm(lo, rtv)
        mev = moe[...]
        rg = mm_tn(hi, mev) + mm_tn(lo, mev)
        d, gain_g = rms_back(mid[...], gp[1:2, :], mig)
        mg[...] = grad + d
        br[...] = mg[...].astype(BF16)
        gg_o[...] = jnp.zeros_like(gg_o)
        gg_o[1:2, :] = gain_g
        gg_o[2 : 2 + E, :] = rg[0:E, :]
        chain_b = Chain(E, br, br_o, b_s, b_r, ld.at[9])
        loads[2].wait()

        def middle_block(i, carry):
            C = at_cols(i, cb_m)
            gg = mm_nt(br[...], wo_v[C, :])
            g_in = gate[:, C]
            sg = sigmoid(g_in)
            act = g_in * sg
            yv = y[:, C]
            ygv = gg * act
            yg[:, C] = ygv
            gi[:, C] = (gg * yv * (sg * (1.0 + g_in * (1.0 - sg)))).astype(BF16)
            gd[:, C] = (yv * act).astype(BF16)
            gs_o[SKIP : SKIP + 1, C] = jnp.sum(ygv * sig[:, C].astype(F32), axis=0, keepdims=True)
            return carry

        lax.fori_loop(0, DI // cb_m, middle_block, 0)
        chain_g = Chain(E, gi, gate_o, g_s, g_r, ld.at[10])
        chain_g.start()
        chain_b.start()

        tg, ng = 2 if DI % 256 == 0 else 1, 8
        wide = tg * LANES

        def flow_block(i, carry):
            lanes = [pl.ds(pl.multiple_of(i * wide, LANES) + k * LANES, LANES) for k in range(tg)]
            both = pl.ds(pl.multiple_of(i * wide, LANES), wide)
            rates = -jnp.exp(small[A_LOG : A_LOG + N, both]) * LOG2E
            wins = []
            for k in range(tg):
                w1 = jnp.zeros((SUB, LANES), F32)
                for j in range(J):
                    w1 = w1 + (dt[j * SUB : j * SUB + SUB, lanes[k]] + cl[j * SUB : j * SUB + SUB, :])
                w2 = w1 + shift_up(w1, 1)
                w4 = w2 + shift_up(w2, 2)
                w8 = w4 + shift_up(w4, 4)
                wins.append((w1, w2, w4))
                suf[N * SUB : (N + 1) * SUB, lanes[k]] = shift_up(w8, 1)
            for g in range(0, N, ng):
                rr = [
                    [
                        jnp.broadcast_to(rates[g + n : g + n + 1, k * LANES : (k + 1) * LANES], (SUB, LANES))
                        for k in range(tg)
                    ]
                    for n in range(ng)
                ]

                def step_j(jj, fs):
                    j = J - 1 - jj
                    dts = [dt[row8(j), lanes[k]] + cl[row8(j), :] for k in range(tg)]
                    ygs = [yg[row8(j), lanes[k]] for k in range(tg)]
                    new = []
                    for n in range(ng):
                        c = cx[row8(j * N + g + n), :]
                        for k in range(tg):
                            new.append(jnp.exp2(dts[k] * rr[n][k]) * (fs[n * tg + k] + ygs[k] * c))
                    return tuple(new)

                fs = lax.fori_loop(
                    0, J, step_j, tuple(jnp.zeros((SUB, LANES), F32) for _ in range(ng * tg)), unroll=2
                )
                for n in range(ng):
                    for k in range(tg):
                        f = fs[n * tg + k]
                        w1, w2, w4 = wins[k]
                        r = rr[n][k]
                        f = f + jnp.exp2(r * w1) * shift_up(f, 1)
                        f = f + jnp.exp2(r * w2) * shift_up(f, 2)
                        f = f + jnp.exp2(r * w4) * shift_up(f, 4)
                        suf[(g + n) * SUB : (g + n + 1) * SUB, lanes[k]] = shift_up(f, 1)
                        fd[g + n : g + n + 1, lanes[k]] = f[0:1, :]
            return carry

        lax.fori_loop(0, DI // wide, flow_block, 0)
        fdev[...] = fd[...].astype(BF16)
        f_moves = [
            remote(fdev, f_all.at[s], f_s.at[k], f_r.at[k], {"seq": p}) for k, p in enumerate(seqs)
        ]
        for c in f_moves:
            c.start()
        f_all[s] = fdev[...]
        for e in range(E):
            gz[e] = gd[:, e * DZ : (e + 1) * DZ]
        gz_moves = [remote(gz.at[p], gz_o.at[me], x_s.at[k], x_r.at[k], {"exp": p}) for k, p in enumerate(zs)]
        for c in gz_moves:
            c.start()
        gz_own = pltpu.make_async_copy(gz.at[me], gz_o.at[me], ld.at[11])
        gz_own.start()
        chain_g.hop(1)
        chain_b.hop(1)
        if plane:
            for c in mine + up1 + [down1]:
                c.wait()
            ua[...] = adds(ua[...], ub[...])
            da[...] = adds(da[...], db[...])
            up2 = remote(ua.at[1 - yy], ub2, a_s.at[3], a_r.at[3], to_y)
            down2 = remote(
                da.at[pl.ds(pl.multiple_of((1 - xx) * dq, 16), dq)], db2, a_s.at[4], a_r.at[4], to_x
            )
            up2.start()
            down2.start()
        for c in f_moves:
            c.wait()

        ia[...] = jnp.zeros_like(ia)
        oa[...] = jnp.zeros_like(oa)
        low_s[...] = jnp.zeros_like(low_s)
        for i in range(steps_s):
            state_load(i).wait()
            if i + 1 < steps_s:
                state_load(i + 1).start()
            C = slice(i * cb_s, (i + 1) * cb_s)
            base = (i % 2) * cb_s
            rates2 = -jnp.exp(small[A_LOG : A_LOG + N, C]) * LOG2E
            rates_s[...] = rates2
            fin[...] = chain_states(
                S - 1, lambda k: k > s, lambda k: S - 1 - k, lambda k: s_all[k, :, C], lambda k: f_all[k, :, C],
                rates2,
            )
            sigf = sig[:, C].astype(F32)
            u_s[...] = dt[:, C] * sigf

            def pair(p, carry):
                lanes = [lanes_of(i, cb_s, p, tg_s, k) for k in range(tg_s)]
                near = [lane_at(p, tg_s, k) for k in range(tg_s)]
                held = [
                    pl.ds(base + pl.multiple_of(p * tg_s * LANES, LANES) + k * LANES, LANES) for k in range(tg_s)
                ]
                for g in range(0, N, ng_s):
                    rr = [
                        [
                            jnp.broadcast_to(rates_s[g + n : g + n + 1, near[k]], (SUB, LANES))
                            for k in range(tg_s)
                        ]
                        for n in range(ng_s)
                    ]
                    flow = []
                    for n in range(ng_s):
                        for k in range(tg_s):
                            at = (g + n) * SUB
                            flow.append(
                                suf[at : at + SUB, lanes[k]]
                                + jnp.exp2(rr[n][k] * suf[N * SUB : (N + 1) * SUB, lanes[k]])
                                * jnp.broadcast_to(fin[g + n : g + n + 1, near[k]], (SUB, LANES))
                            )

                    def load(j):
                        got = [[None] * tg_s for _ in range(ng_s)]
                        for n in range(0, ng_s, 2):
                            for k in range(tg_s):
                                at = pl.multiple_of(j * N * SUB + (g + n) * SUB, 2 * SUB)
                                two = big[pl.ds(at, 2 * SUB), held[k]].astype(F32)
                                got[n][k] = two[0:SUB]
                                got[n + 1][k] = two[SUB : 2 * SUB]
                        return [got[n][k] for n in range(ng_s) for k in range(tg_s)]

                    def step_j(jj, carry):
                        fs, hs, rts = carry
                        j = J - 1 - jj
                        dtp = [dt[row8(j), lanes[k]] for k in range(tg_s)]
                        dts = [dtp[k] + cl[row8(j), :] for k in range(tg_s)]
                        us = [u_s[row8(j), near[k]] for k in range(tg_s)]
                        ygs = [yg[row8(j), lanes[k]] for k in range(tg_s)]
                        before = load(j)
                        if g == 0:
                            dgs = [jnp.zeros((SUB, LANES), F32) for k in range(tg_s)]
                            rss = [jnp.zeros((SUB, LANES), F32) for k in range(tg_s)]
                        else:
                            dgs = [dg_s[row8(j), near[k]] for k in range(tg_s)]
                            rss = [rs_s[row8(j), near[k]] for k in range(tg_s)]
                        nf, nr = [], []
                        for n in range(ng_s):
                            at = row8(j * N + g + n)
                            b = bx[at, :]
                            c = cx[at, :]
                            ig = jnp.zeros((SUB, LANES), F32)
                            og = jnp.zeros((SUB, LANES), F32)
                            for k in range(tg_s):
                                q = n * tg_s + k
                                gr = ygs[k] * c + fs[q]
                                f = jnp.exp2(dts[k] * rr[n][k]) * gr
                                rt = f * before[q]
                                rss[k] = rss[k] + rt * rr[n][k]
                                dgs[k] = dgs[k] + gr * b
                                nr.append(rts[q] + rt * dtp[k])
                                ig = ig + gr * us[k]
                                og = og + hs[q] * ygs[k]
                                nf.append(f)
                            ia[at, :] += ig
                            oa[at, :] += og
                        for k in range(tg_s):
                            dg_s[row8(j), near[k]] = dgs[k]
                            rs_s[row8(j), near[k]] = rss[k]
                        return tuple(nf), tuple(before), tuple(nr)

                    zero = tuple(jnp.zeros((SUB, LANES), F32) for _ in range(ng_s * tg_s))
                    _, _, rts = lax.fori_loop(
                        0, J, step_j, (tuple(flow), tuple(load(J)), zero), unroll=2
                    )
                    for n in range(ng_s):
                        for k in range(tg_s):
                            rt_s[g + n : g + n + 1, near[k]] = jnp.sum(rts[n * tg_s + k], axis=0, keepdims=True)
                return carry

            lax.fori_loop(0, cb_s // (tg_s * LANES), pair, 0)
            dg = dg_s[...]
            ssg[:, C] = dg * dt[:, C] + yg[:, C] * small[SKIP : SKIP + 1, C]
            step_grad = rs_s[...] * LN2 + dg * sigf
            low = mixed[:, 0 : z.R].astype(BF16)
            dtw = small[z.DT0 : z.DT0 + z.R, C].astype(BF16)
            pre = mm(low, dtw) + small[DT_B : DT_B + 1, C]
            dpg = step_grad * sigmoid(pre)
            dpl = dpg.astype(BF16)
            gs_o[DT_B : DT_B + 1, C] = jnp.sum(dpg, axis=0, keepdims=True)
            gs_o[SKIP + 1 : SKIP + 2, C] = jnp.zeros((1, cb_s), F32)
            gs_o[A_LOG : A_LOG + N, C] = rt_s[...] * (rates2 * LN2)
            gs_o[z.DT0 : z.DT0 + z.R, C] = mm_tn(low, dpl)
            low_s[...] += mm_nt(dpl, dtw)
            if i + 2 <= E - 1:
                chain_g.hop(i + 2)
                chain_b.hop(i + 2)
        for k in range(steps_s + 2, E):
            chain_g.hop(k)
            chain_b.hop(k)

        mxg[:, 0 : z.R] = low_s[...].astype(BF16)
        lane = lax.broadcasted_iota(jnp.int32, (SUB, LANES), 1)

        def gather(j, carry):
            both = jnp.zeros((SUB, LANES), F32)
            for n in range(N):
                at = row8(j * N + n)
                both = jnp.where(lane == n, jnp.sum(ia[at, :], axis=1, keepdims=True), both)
                both = jnp.where(lane == N + n, jnp.sum(oa[at, :], axis=1, keepdims=True), both)
            cl[row8(j), :] = both
            return carry

        lax.fori_loop(0, J, gather, 0)
        mxg[:, z.R : z.R + 2 * N] = cl[:, 0 : 2 * N].astype(BF16)

        def weight_load(i):
            half = pl.ds((i % 2) * cb_s, cb_s)
            return [
                pltpu.make_async_copy(
                    w_in.at[:, h * DI + i * cb_s : h * DI + (i + 1) * cb_s], big.at[h * D : (h + 1) * D, half],
                    ld.at[12 + 2 * (i % 2) + h],
                )
                for h in range(2)
            ]

        for c in weight_load(0):
            c.start()

        def conv_block(i, carry):
            C = at_cols(i, cb_m)
            mgv = mxg[...]
            sgv = sig[:, C]
            xw = small[z.X0 : z.X0 + z.XW, C].astype(BF16)
            gs_o[z.X0 : z.X0 + z.XW, C] = mm_tn(mgv, sgv)
            sgrad = ssg[:, C] + mm(mgv, xw)
            xpad = padded_rows(conv_in[:, C], hconv[:, C], J, cb_m)
            valid = [jnp.broadcast_to(masks[:, o : o + 1], (T, cb_m)) for o in range(4)]
            out = jnp.broadcast_to(small[CONV_B : CONV_B + 1, C], (T, cb_m))
            for o in range(4):
                w = small[CONV_W + o : CONV_W + o + 1, C]
                out = out + w * xpad[o : o + J].reshape(T, cb_m) * valid[o]
            sv = sigmoid(out)
            cg = sgrad * (sv * (1.0 + out * (1.0 - sv)))
            gs_o[CONV_B : CONV_B + 1, C] = jnp.sum(cg, axis=0, keepdims=True)
            total = jnp.zeros((J, SUB, cb_m), F32)
            final = lax.broadcasted_iota(jnp.int32, (SUB, cb_m), 0) == SUB - 1
            edges = [jnp.zeros((1, cb_m), F32) for _ in range(3)]
            for o in range(4):
                masked = cg * valid[o]
                gs_o[CONV_W + o : CONV_W + o + 1, C] = jnp.sum(
                    masked * xpad[o : o + J].reshape(T, cb_m), axis=0, keepdims=True
                )
                c3 = (small[CONV_W + o : CONV_W + o + 1, C] * masked).reshape(J, SUB, cb_m)
                k = 3 - o
                if k == 0:
                    total = total + c3
                else:
                    wrap = jnp.stack(
                        [jnp.where(final, 0.0, pltpu.roll(c3[t], SUB - 1, 0)) for t in range(k)]
                    )
                    total = total + jnp.concatenate([c3[k:], wrap], axis=0)
                    for i2 in range(o, 3):
                        edges[i2] = edges[i2] + c3[i2 - o, 0:1, :]
            cig[:, C] = total.reshape(T, cb_m)
            cg_edge[:, C] = jnp.concatenate(edges + [jnp.zeros((SUB - 3, cb_m), F32)], axis=0)
            return carry

        lax.fori_loop(0, DI // cb_m, conv_block, 0)
        back_edge = remote(cg_edge, edge_in, e_s, e_r, {"seq": lax.rem(s + S - 1, S)})
        back_edge.start()
        if plane:
            up2.wait()
            down2.wait()
            uf[...] = adds(ua[yy], ub2[...])
            half_u = uq // 2
            rows_u = lambda c: pl.ds(pl.multiple_of(c * half_u, 16), half_u)
            up3 = remote(uf.at[rows_u(other)], up_o.at[core], a_s.at[5], a_r.at[5], sib)
            up3.start()
            up_own = pltpu.make_async_copy(uf.at[rows_u(core)], up_o.at[core], ld.at[16])
            up_own.start()
            down_o[...] = da[pl.ds(pl.multiple_of(xx * dq, 16), dq), :].astype(F32) + db2[...].astype(F32)
        else:
            down_o[...] = jnp.zeros_like(down_o)
        back_edge.wait()
        live = jnp.where(s < S - 1, 1.0, 0.0)

        def fix_block(i, carry):
            C = at_cols(i, cb_m)
            c3 = cig[:, C].reshape(J, SUB, cb_m)
            final = lax.broadcasted_iota(jnp.int32, (SUB, cb_m), 0) == SUB - 1
            fixed = jnp.stack(
                [
                    c3[J - 3 + k]
                    + jnp.where(final, jnp.broadcast_to(edge_in[k : k + 1, C] * live, (SUB, cb_m)), 0.0)
                    for k in range(3)
                ]
            )
            pc[:, C] = jnp.concatenate([c3[: J - 3], fixed], axis=0).reshape(T, cb_m).astype(BF16)
            return carry

        lax.fori_loop(0, DI // cb_m, fix_block, 0)
        chain_p = Chain(E, pc, pc_o, p_s, p_r, ld.at[17])
        chain_p.start()
        acc[...] = jnp.zeros_like(acc)
        for i in range(steps_s):
            for c in weight_load(i):
                c.wait()
            if i + 1 < steps_s:
                for c in weight_load(i + 1):
                    c.start()
            C = slice(i * cb_s, (i + 1) * cb_s)
            half = slice((i % 2) * cb_s, (i % 2 + 1) * cb_s)
            acc[...] += mm_nt(pc[:, C], big[0:D, half]) + mm_nt(gi[:, C], big[D : 2 * D, half])
        d, gain_g = rms_back(tok[...].astype(F32), gp[0:1, :], acc[...])
        tg_o[...] = mg[...] + d
        gg_o[0:1, :] = gain_g
        for k in range(1, E):
            chain_p.hop(k)
        for c in out_moves + gz_moves:
            c.wait()
        back_own.wait()
        gz_own.wait()
        if plane:
            up3.wait()
            up_own.wait()
        for ch_ in (chain_g, chain_b, chain_p):
            ch_.finish()

    v = pltpu.VMEM
    sem = lambda *dims: pltpu.SemaphoreType.DMA(dims)
    vm = pl.BlockSpec(memory_space=pltpu.VMEM)
    up_shape = (2, uq // 2, uc) if plane else (1, 16, LANES)
    down_shape = (dq, dc) if plane else (16, LANES)
    u_shape = (2, uq, uc) if plane else (2, 16, LANES)
    d_shape = (2 * dq, dc) if plane else (32, LANES)
    ins = (dxp, outp, dwu, dwd, states, w_out, w_in, table, choose, chances, mid, moe, cot, gpack, router, gate, y,
           sig, small, mixed, dt, masks, conv_in, hconv, s_all, tok)
    return pl.pallas_call(
        body,
        name="backward",
        in_specs=[ANY] * 7 + [vm] * (len(ins) - 7),
        out_specs=[vm] * 3 + [ANY] * 5 + [ANY, vm],
        out_shape=[
            sds((T, D), F32),
            sds((z.SMALL, DI), F32),
            sds((G, D), F32),
            sds((M, D), BF16),
            sds((E, T, DI), BF16),
            sds((E, T, DI), BF16),
            sds((E, T, D), BF16),
            sds((E, T, DZ), BF16),
            sds(up_shape, BF16),
            sds(down_shape, F32),
        ],
        scratch_shapes=[
            v((rows_big, 2 * cb_s), BF16),
            v((DI, D), BF16),
            v((M, D + LANES), BF16), v((M, D + LANES), BF16), v((M, D), BF16), v((M, D), BF16),
            v((M, D + LANES), BF16),
            v((T, DI), F32), v((T, DI), BF16), v((T, DI), BF16), v((E, T, DZ), BF16),
            v((T, D), BF16), v((T, D), F32),
            v((N, DI), BF16), v((S, N, DI), BF16), v(((N + 1) * SUB, DI), F32),
            v((T, DI), F32), v((SUB, LANES), F32), v((T, DI), F32), v((SUB, DI), F32), v((SUB, DI), F32),
            v((T, DI), BF16),
            v((J * N * SUB, LANES), F32), v((J * N * SUB, LANES), F32),
            v((J * N * SUB, LANES), F32), v((J * N * SUB, LANES), F32),
            v((T, LANES), F32), v((T, cb_s), F32), v((N, cb_s), F32), v((N, cb_s), F32),
            v((T, cb_s), F32), v((T, cb_s), F32), v((N, cb_s), F32), v((T, z.R), F32), v((T, z.XW), BF16),
            v((T, D), F32), v((N, DI), F32),
            v(u_shape, BF16), v(u_shape, BF16), v(u_shape[1:], BF16), v(u_shape[1:], BF16),
            v(d_shape, BF16), v(d_shape, BF16), v((d_shape[0] // 2, d_shape[1]), BF16),
            sem(18), sem(2), sem(2), sem(E - 1), sem(E - 1), sem(E - 1), sem(E - 1), sem(S - 1), sem(S - 1),
            pltpu.SemaphoreType.DMA, pltpu.SemaphoreType.DMA,
            sem(chain_slots), sem(chain_slots), sem(chain_slots), sem(chain_slots), sem(chain_slots), sem(chain_slots),
            sem(6), sem(6), sem(E - 1), sem(E - 1),
        ],
        compiler_params=pltpu.CompilerParams(
            collective_id=cid, has_side_effects=True, vmem_limit_bytes=60 * 1024 * 1024
        ),
    )(*ins)


def dispatch(E, S, outbound, cid):
    CAP, D = outbound.shape[1:]

    def body(x, o, zs_s, zs_r, c_s, c_r, own):
        s, me = lax.axis_index("seq"), lax.axis_index("exp")
        core = lax.rem(s, 2)
        sib = {"seq": s + 1 - 2 * core}
        zs = [lax.rem(me + k, E) for k in range(1, E)]
        greet([sib] + [{"exp": p} for p in zs])
        sends = [
            pltpu.make_async_remote_copy(
                x.at[p], o.at[core, me], zs_s.at[k], zs_r.at[k], device_id={"exp": p}, device_id_type=MESH
            )
            for k, p in enumerate(zs)
        ]
        for c in sends:
            c.start()
        local = pltpu.make_async_copy(x.at[me], o.at[core, me], own)
        local.start()
        passes = [
            pltpu.make_async_remote_copy(
                x.at[me], o.at[core, me], c_s.at[0], c_r.at[0], device_id=sib, device_id_type=MESH
            )
        ]
        passes[0].start()
        for k in range(1, E):
            frm = lax.rem(me + E - k, E)
            ref = o.at[core, frm]
            pltpu.make_async_remote_copy(
                ref, ref, zs_s.at[k - 1], zs_r.at[k - 1], device_id={"exp": frm}, device_id_type=MESH
            ).wait_recv()
            c = pltpu.make_async_remote_copy(
                ref, ref, c_s.at[k], c_r.at[k], device_id=sib, device_id_type=MESH
            )
            c.start()
            passes.append(c)
        local.wait()
        for c in sends:
            c.wait_send()
        for c in passes:
            c.wait_send()
        for k in range(E):
            ref = o.at[1 - core, lax.rem(me + E - k, E)]
            pltpu.make_async_remote_copy(
                ref, ref, c_s.at[k], c_r.at[k], device_id=sib, device_id_type=MESH
            ).wait_recv()

    vm = pl.BlockSpec(memory_space=pltpu.VMEM)
    return pl.pallas_call(
        body,
        name="dispatch",
        in_specs=[vm],
        out_specs=vm,
        out_shape=sds((2, E, CAP, D), outbound.dtype),
        scratch_shapes=[
            pltpu.SemaphoreType.DMA((E - 1,)), pltpu.SemaphoreType.DMA((E - 1,)),
            pltpu.SemaphoreType.DMA((E,)), pltpu.SemaphoreType.DMA((E,)), pltpu.SemaphoreType.DMA,
        ],
        compiler_params=pltpu.CompilerParams(collective_id=cid, has_side_effects=True),
    )(outbound)


def to_chunks(a, J):
    return a.reshape((SUB, J) + a.shape[1:]).swapaxes(0, 1).reshape(a.shape)


def from_chunks(a, J):
    return a.reshape((J, SUB) + a.shape[1:]).swapaxes(0, 1).reshape(a.shape)


def from_behind(block_in, axis, distance):
    devices = range(lax.axis_size(axis))
    route = [(i - distance, i) for i in devices if i - distance in devices]
    return lax.ppermute(block_in, axis, route)


def on_device(
    tokens, segment_ids, routes, cotangent, norm_gain, in_proj, conv_weight, conv_bias, x_proj,
    dt_proj, dt_bias, a_log, d_skip, out_proj, moe_gain, router, up_proj, down_proj,
):
    E = lax.axis_size("exp")
    S = lax.axis_size("seq")
    z = Sizes(tokens, in_proj, dt_proj, x_proj, a_log, up_proj, E)
    T, D, DI, N, J, CAP = z.T, z.D, z.DI, z.N, z.J, z.CAP
    me_s, me_e = lax.axis_index("seq"), lax.axis_index("exp")
    core = lax.rem(me_s, 2)
    where = jnp.stack([me_s, me_e, core]).astype(jnp.int32)
    halo = from_behind(tokens[0, T - J :], "seq", 1)
    seg = segment_ids[0]
    seg_tail = from_behind(seg[T - 3 :], "seq", 1)

    cw = dt_proj.shape[1]
    dw = norm_gain.shape[0]
    plane = S == 8 and dw % 32 == 0
    small_own = jnp.concatenate(
        [conv_weight, conv_bias[None], dt_bias[None], d_skip[None], jnp.zeros((1, cw), BF16), a_log, dt_proj,
         x_proj.T, jnp.zeros((-z.SMALL % 32, cw), BF16)], axis=0
    )
    g_own = jnp.concatenate(
        [norm_gain[None], moe_gain[None], router.T, jnp.zeros((32 - 2 - E, dw), BF16)], axis=0
    )
    owned = [in_proj, out_proj, small_own, g_own]
    if plane:
        each = lambda cols, most: (cols - 4 * most * LANES, most * LANES)
        tiles_in, tiles_out = 2 * DI // LANES, D // LANES
        regions = [
            each(2 * DI, max(1, tiles_in * 5 // 36)), each(D, max(1, tiles_out * 2 // 9)), (cw, 0), (dw, 0)
        ]
        w_in, w_out, small, gpack_low = gather_weights(E, owned, regions, 1)
    else:
        w_in, w_out, small, gpack_low = [lax.all_gather(a, "exp") for a in owned]
    w_in = w_in.reshape(D, 2 * DI)
    w_out = w_out.reshape(DI, D)
    join = lambda a: a.swapaxes(0, 1).reshape(a.shape[1], -1)
    small = join(small[:, : z.SMALL]).astype(F32)
    gpack_low = join(gpack_low[:, : 2 + E])
    gr = 8 * -(-(2 + E) // 8)
    gpack = jnp.zeros((gr, D), F32).at[: 2 + E].set(gpack_low.astype(F32))
    router_t = jnp.zeros((LANES, D), BF16).at[0:E].set(gpack_low[2 : 2 + E])

    padded_seg = jnp.concatenate([seg_tail, seg])
    masks = jnp.stack([(padded_seg[o : o + T] == seg).astype(F32) for o in range(4)] + [seg * 0.0] * 4, axis=1)
    masks = to_chunks(masks, J)
    tok = to_chunks(tokens[0], J)
    cot = to_chunks(cotangent[0], J)
    route = to_chunks(routes[0, :, 0], J)
    choose = route[:, None] == jnp.arange(E)[None, :]
    upto = (jnp.arange(T)[None, :] <= jnp.arange(T)[:, None]).astype(BF16)
    counts = jnp.dot(upto, choose.astype(BF16), preferred_element_type=F32)
    rank = jnp.sum(counts * choose, axis=-1).astype(jnp.int32) - 1
    table = ((route * CAP + rank)[:, None] == jnp.arange(E * CAP)[None, :]).astype(BF16)
    choose_wide = (route[:, None] == jnp.arange(LANES)[None, :]).astype(F32)
    cot_slots = lax.dot_general(table, cot, (((0,), (0,)), ((), ())), preferred_element_type=F32).astype(BF16)

    def trade(a):
        return lax.all_to_all(a, "exp", split_axis=0, concat_axis=0, tiled=True)

    def columns(a):
        return a.reshape(T, E, -1).swapaxes(0, 1)

    cot_here = trade(cot_slots.reshape(E, CAP, D)).reshape(E * CAP, D)
    cot_there = lax.ppermute(cot_here, "seq", [(i, i ^ 1) for i in range(S)])
    cot_pair = jnp.where(
        core == 0, jnp.concatenate([cot_here, cot_there]), jnp.concatenate([cot_there, cot_here])
    )

    normed, conv_in, hconv, gate, sig, mixed = front(z, tok, halo, masks, gpack, w_in, small)
    normed_z = trade(columns(normed)).reshape(E * T, -1)
    dt, pre, hdev, stot, dwin = summary(z, mixed, sig, masks, small)
    h_all, s_all = exchange("seq", S, [hdev, stot], [True, True], 2)
    states, y, mid, moe, chances, outbound = scan_forward(
        z, where, mixed, dt, sig, gate, masks, small, pre, dwin, h_all, s_all, w_out, tok, gpack, router_t, table
    )
    arrived = dispatch(E, S, outbound.reshape(E, CAP, D), 3)
    outp, dxp, dwu, dwd = expert(
        z, where, arrived.reshape(2 * E * CAP, D), cot_pair, router_t, up_proj[0], down_proj[0]
    )
    token_grad, gsmall, ggrad, back_out, gate_all, conv_all, branch_all, gated_z, up_sum, down_part = backward(
        z, S, plane, dxp.reshape(2, E * CAP, -1), outp.reshape(2, E * CAP, D), dwu, dwd, states, w_out, w_in, table,
        choose_wide, chances, mid, moe, cot, gpack, router_t, gate, y, sig, small, mixed, dt, masks, conv_in, hconv,
        s_all, tok, 4
    )
    fb = z.FF // 8
    if plane:
        up_part = up_sum.reshape(2, D // 8, 4, fb).transpose(1, 2, 0, 3).reshape(D // 8, z.FF).astype(F32)
    else:
        up_full = jnp.zeros((D, 4, 2, fb), BF16)
        up_full = lax.dynamic_update_slice_in_dim(up_full, dwu.reshape(D, 4, 1, fb), core, axis=2)
        down_full = jnp.zeros((4, 2, fb, D), BF16)
        down_full = lax.dynamic_update_slice_in_dim(down_full, dwd.reshape(4, 1, fb, D), core, axis=1)
        up_part, down_part = [
            lax.psum_scatter(v, "seq", scatter_dimension=0, tiled=True).astype(F32)
            for v in (up_full.reshape(D, z.FF), down_full.reshape(z.FF, D))
        ]
    out_rows = contract(gated_z.reshape(E * T, -1), branch_all.reshape(E * T, D)).astype(BF16)
    gate_cols = contract(normed_z, gate_all.reshape(E * T, DI)).astype(BF16)
    conv_cols = contract(normed_z, conv_all.reshape(E * T, DI)).astype(BF16)
    gating = jnp.sum(chances * choose_wide, axis=-1, keepdims=True)
    output = (mid + gating * jnp.dot(table, back_out, preferred_element_type=F32)).astype(BF16)

    blocks = lambda a: a.reshape(a.shape[0], E, -1).swapaxes(0, 1)
    gpart = jnp.pad(blocks(ggrad), ((0, 0), (0, 0), (0, cw - dw)))
    rows = z.SMALL + gr
    pad = -rows % 128
    smalls = jnp.concatenate(
        [blocks(gsmall), gpart, jnp.zeros((E, pad, cw), F32)], axis=1
    ).astype(BF16)
    cols = jnp.concatenate([conv_cols, gate_cols], axis=1)
    if plane:
        each = cw // 8
        each_pad = 16 * -(-each // 16)
        padded = jnp.pad(out_rows.reshape(8, each, D), ((0, 0), (0, each_pad - each), (0, 0)))
        dw_in, dw_out, gsum = reduce_plane(E, cols, padded, smalls, 7)
        dw_out = dw_out[:, :each].reshape(cw, D)
    else:
        dw_in, dw_out = lax.psum(cols, "seq"), lax.psum(out_rows, "seq")
        gsum = lax.psum_scatter(lax.psum(smalls, "seq"), "exp", scatter_dimension=0, tiled=True)[0]
    gsum = gsum.astype(F32)
    return (
        from_chunks(output, J)[None],
        from_chunks(token_grad, J)[None],
        gsum[z.SMALL, :dw],
        dw_in.astype(F32),
        gsum[CONV_W : CONV_W + 4],
        gsum[CONV_B],
        gsum[z.X0 : z.SMALL].T,
        gsum[z.DT0 : z.X0],
        gsum[DT_B],
        gsum[A_LOG : A_LOG + N],
        gsum[SKIP],
        dw_out.astype(F32),
        gsum[z.SMALL + 1, :dw],
        gsum[z.SMALL + 2 : z.SMALL + 2 + E, :dw].T,
        up_part[None],
        down_part[None],
    )


def contract(a, b):
    return lax.dot_general(a, b, (((0,), (0,)), ((), ())), preferred_element_type=F32)


def solution(mesh):
    row = P("exp", "seq", None)
    in_specs = (
        row, P("exp", "seq"), row, row, P("exp"), P("exp", None), P(None, "exp"), P("exp"), P("exp", None),
        P(None, "exp"), P("exp"), P(None, "exp"), P("exp"), P("exp", None), P("exp"), P("exp", None),
        P("exp", None, None), P("exp", None, None),
    )
    out_specs = (
        row, row, P("exp"), P("exp", None), P(None, "exp"), P("exp"), P("exp", None), P(None, "exp"), P("exp"),
        P(None, "exp"), P("exp"), P("exp", None), P("exp"), P("exp", None), row, row,
    )
    return jax.shard_map(on_device, mesh=mesh, in_specs=in_specs, out_specs=out_specs, check_vma=False)
```

```python
import functools
import math

import jax
import jax.numpy as jnp
from jax import lax
from jax.experimental import pallas as pl
from jax.experimental.pallas import tpu as pltpu
from jax.sharding import PartitionSpec as P

EPSILON = 1e-05
LOG2E = math.log2(math.e)
LN2 = math.log(2.0)
CLOSED = 1e30
LANES = 128
SUB = 8
F32 = jnp.float32
BF16 = jnp.bfloat16
VMEM_LIMIT = 56 * 1024 * 1024


def mm(a, b):
    return lax.dot_general(a, b, (((1,), (0,)), ((), ())), preferred_element_type=F32)


def mm_nt(a, b):
    return lax.dot_general(a, b, (((1,), (1,)), ((), ())), preferred_element_type=F32)


def mm_tn(a, b):
    return lax.dot_general(a, b, (((0,), (0,)), ((), ())), preferred_element_type=F32)


def split_hi_lo(value):
    high = value.astype(BF16)
    return high, (value - high.astype(F32)).astype(BF16)


def sigmoid(v):
    return 1.0 / (1.0 + jnp.exp(-v))


def softplus(v):
    e = jnp.exp(-jnp.abs(v))
    small = e * (1.0 - e * (0.5 - e * (1.0 / 3.0 - e * 0.25)))
    return jnp.maximum(v, 0.0) + jnp.where(e < 0.01, small, jnp.log(1.0 + e))


def rms_scale(v):
    return lax.rsqrt(jnp.mean(v * v, axis=-1, keepdims=True) + EPSILON)


def rms_back(resid, gain, grad):
    s = rms_scale(resid)
    v = gain * grad
    out = s * v - resid * (s * s * s) * jnp.mean(resid * v, axis=-1, keepdims=True)
    return out, jnp.sum(grad * resid * s, axis=0, keepdims=True)


def block(shape, index):
    return pl.BlockSpec(shape, index)


def whole(shape):
    zeros = (0,) * len(shape)
    return pl.BlockSpec(shape, lambda *_: zeros)


def call(body, name, grid, ins, in_specs, outs, out_specs, scratch, cost=None):
    return pl.pallas_call(
        body,
        name=name,
        grid=grid,
        in_specs=in_specs,
        out_specs=out_specs,
        out_shape=outs,
        scratch_shapes=scratch,
        cost_estimate=cost,
        compiler_params=pltpu.CompilerParams(vmem_limit_bytes=VMEM_LIMIT),
    )(*ins)


def sds(shape, dtype):
    return jax.ShapeDtypeStruct(shape, dtype)


def pick(total, options):
    for o in options:
        if total % o == 0:
            return o
    return total


CONV_W, CONV_B, DT_B, SKIP, A_LOG = 0, 4, 5, 6, 8


class Sizes:
    def __init__(self, tokens, in_proj, dt_proj, x_proj, a_log, up_proj, exp_count):
        self.T = tokens.shape[1]
        self.D = tokens.shape[2]
        self.DI = in_proj.shape[1] // 2
        self.N = a_log.shape[0]
        self.R = dt_proj.shape[0]
        self.XW = x_proj.shape[1]
        self.FF = up_proj.shape[2]
        self.E = exp_count
        self.CAP = 2 * self.T // exp_count
        self.J = self.T // SUB
        self.DT0 = A_LOG + self.N
        self.X0 = self.DT0 + self.R
        self.SMALL = self.X0 + self.XW


MESH = pl.DeviceIdType.MESH
ANY = pl.BlockSpec(memory_space=pl.ANY)


def greet(peers):
    barrier = pltpu.get_barrier_semaphore()
    for peer in peers:
        pl.semaphore_signal(barrier, inc=1, device_id=peer, device_id_type=MESH)
    pl.semaphore_wait(barrier, len(peers))


def reduce_plane(E, p_in, p_out, p_small, cid):
    RI, CI = p_in.shape
    ri, ci = RI // 2, CI // 4
    _, ro, co = p_out.shape
    _, rs8, cs = p_small.shape
    rs = rs8 // 8
    p_small = p_small.reshape(E, 4, 2, rs, cs)
    p_out = p_out.reshape(4, 2, ro, co)

    def body(xi, xo, xs, oi, oo, os, a_i, b_i, a_o, b_o, a_s, b_s, t_i, t_o, t_s, z_s, r_i, r_o, r_s,
             lsem, c_send, c_recv, q_send, q_recv, z_send, z_recv, g_send, g_recv, f_send, f_recv):
        s, me = lax.axis_index("seq"), lax.axis_index("exp")
        chip, core = s // 2, lax.rem(s, 2)
        other = 1 - core
        sib = {"seq": chip * 2 + other, "exp": me}
        chips = [chip + 1 - 2 * lax.rem(chip, 2), chip + 2 - 4 * (chip // 2), 3 - chip]
        there = [{"seq": q * 2 + core, "exp": me} for q in chips]
        zs = [lax.rem(me + k, E) for k in range(1, E)]
        greet([sib] + there + [{"seq": s, "exp": p} for p in zs])

        def remote(src, dst, send, recv, to):
            return pltpu.make_async_remote_copy(src, dst, send, recv, device_id=to, device_id_type=MESH)

        half = lambda c: pl.ds(pl.multiple_of(c * ri, 16), ri)
        first = [
            remote(xi.at[half(other)], b_i, c_send.at[0], c_recv.at[0], sib),
            remote(xo.at[:, other], b_o, c_send.at[1], c_recv.at[1], sib),
            remote(xs.at[:, :, other], b_s, c_send.at[2], c_recv.at[2], sib),
        ]
        for c in first:
            c.start()
        mine = [
            pltpu.make_async_copy(xi.at[half(core)], a_i, lsem.at[0]),
            pltpu.make_async_copy(xo.at[:, core], a_o, lsem.at[1]),
            pltpu.make_async_copy(xs.at[:, :, core], a_s, lsem.at[2]),
        ]
        for c in mine:
            c.start()
        adds = lambda a, b: (a.astype(F32) + b.astype(F32)).astype(BF16)
        cols = lambda q: pl.ds(pl.multiple_of(q * ci, LANES), ci)
        second = []
        for w in (0, 1, 2):
            mine[w].wait()
            first[w].wait()
            if w == 0:
                a_i[...] = adds(a_i[...], b_i[...])
            elif w == 1:
                a_o[...] = adds(a_o[...], b_o[...])
            else:
                a_s[...] = adds(a_s[...], b_s[...])
            for k in range(3):
                src = [a_i.at[:, cols(chips[k])], a_o.at[chips[k]], a_s.at[:, chips[k]]][w]
                dst = [t_i, t_o, t_s][w].at[k]
                c = remote(src, dst, q_send.at[w, k], q_recv.at[w, k], there[k])
                c.start()
                second.append(c)

        def total(own, parts):
            out = own.astype(F32)
            for k in range(3):
                out = out + parts[k].astype(F32)
            return out.astype(BF16)

        for c in second[6:9]:
            c.wait()
        a_s[:, chip] = total(a_s[:, chip], t_s)
        third = []
        for k, p in enumerate(zs):
            c = remote(a_s.at[p, chip], z_s.at[me], z_send.at[k], z_recv.at[k], {"seq": s, "exp": p})
            c.start()
            third.append(c)

        gathers = []

        def spread(w, ref):
            for k in range(3):
                c = remote(ref, ref, g_send.at[w, k], g_recv.at[w, k], there[k])
                c.start()
                gathers.append(c)
            c = remote(ref, ref, f_send.at[w, 3], f_recv.at[w, 3], sib)
            c.start()
            gathers.append(c)

        for c in second[0:3]:
            c.wait()
        r_i[core, chip] = total(a_i[:, cols(chip)], t_i)
        spread(0, r_i.at[core, chip])
        for c in second[3:6]:
            c.wait()
        r_o[core, chip] = total(a_o[chip], t_o)
        spread(1, r_o.at[core, chip])
        for c in third:
            c.wait()
        out = a_s[me, chip].astype(F32)
        for k, p in enumerate(zs):
            out = out + z_s[p].astype(F32)
        r_s[core, chip] = out.astype(BF16)
        spread(2, r_s.at[core, chip])

        def landed(w, c, q):
            return [r_i, r_o, r_s][w].at[c, q]

        passed = []
        for w in (0, 1, 2):
            for k in range(3):
                ref = landed(w, core, chips[k])
                remote(ref, ref, g_send.at[w, k], g_recv.at[w, k], there[k]).wait_recv()
                c = remote(ref, ref, f_send.at[w, k], f_recv.at[w, k], sib)
                c.start()
                passed.append(c)
        for c in gathers:
            c.wait_send()
        for c in passed:
            c.wait_send()
        for w in (0, 1, 2):
            for k in range(4):
                ref = landed(w, other, chips[k] if k < 3 else chip)
                remote(ref, ref, f_send.at[w, k], f_recv.at[w, k], sib).wait_recv()
        writes = []
        for c in range(2):
            for q in range(4):
                writes.append(
                    pltpu.make_async_copy(
                        r_i.at[c, q], oi.at[c * ri : (c + 1) * ri, q * ci : (q + 1) * ci], lsem.at[3 + c * 4 + q]
                    )
                )
                writes.append(pltpu.make_async_copy(r_o.at[c, q], oo.at[q, c], lsem.at[11 + c * 4 + q]))
                writes.append(pltpu.make_async_copy(r_s.at[c, q], os.at[q, c], lsem.at[19 + c * 4 + q]))
        for c in writes:
            c.start()
        for c in writes:
            c.wait()

    v = lambda *dims: pltpu.VMEM(dims, BF16)
    sem = lambda *dims: pltpu.SemaphoreType.DMA(dims)
    oi, oo, os = pl.pallas_call(
        body,
        name="reduce_plane",
        in_specs=[ANY] * 3,
        out_specs=[ANY] * 3,
        out_shape=[sds((RI, CI), BF16), sds((4, 2, ro, co), BF16), sds((4, 2, rs, cs), BF16)],
        scratch_shapes=[
            v(ri, CI), v(ri, CI), v(4, ro, co), v(4, ro, co), v(E, 4, rs, cs), v(E, 4, rs, cs),
            v(3, ri, ci), v(3, ro, co), v(3, E, rs, cs), v(E, rs, cs),
            v(2, 4, ri, ci), v(2, 4, ro, co), v(2, 4, rs, cs),
            sem(27), sem(3), sem(3), sem(3, 3), sem(3, 3), sem(E - 1), sem(E - 1),
            sem(3, 3), sem(3, 3), sem(3, 4), sem(3, 4),
        ],
        compiler_params=pltpu.CompilerParams(
            collective_id=cid, has_side_effects=True, vmem_limit_bytes=VMEM_LIMIT
        ),
    )(p_in, p_out, p_small)
    return oi, oo.reshape(8, ro, co), os.reshape(8 * rs, cs)


def expand_columns(z, src, col0, dst):
    def one(j, carry):
        rows = src[pl.ds(pl.multiple_of(j * SUB, SUB), SUB), :]
        for n in range(z.N):
            at = pl.multiple_of((j * z.N + n) * SUB, SUB)
            dst[pl.ds(at, SUB), :] = jnp.broadcast_to(
                rows[:, col0 + n : col0 + n + 1], (SUB, LANES)
            )
        return carry

    lax.fori_loop(0, z.J, one, 0)


def expand_closed(z, masks, dst):
    dst[...] = jnp.broadcast_to((1.0 - masks[:, 2:3]) * CLOSED, (z.T, LANES))


def tile_groups(cb):
    return 2 if cb % (2 * LANES) == 0 else 1


def lane_at(p, tg, k):
    return pl.ds(pl.multiple_of(p * tg * LANES, LANES) + k * LANES, LANES)


def row8(j):
    return pl.ds(pl.multiple_of(j * SUB, SUB), SUB)


def shift_down(v, d):
    rows = lax.broadcasted_iota(jnp.int32, v.shape, 0)
    return jnp.where(rows >= d, pltpu.roll(v, d, 0), 0.0)


def shift_up(v, d):
    rows = lax.broadcasted_iota(jnp.int32, v.shape, 0)
    return jnp.where(rows < SUB - d, pltpu.roll(v, SUB - d, 0), 0.0)


def chain_states(count, mine, order, sums, heads, rates2):
    state = jnp.zeros_like(rates2)
    for k in range(count):
        at = order(k)
        new = jnp.exp2(rates2 * sums(at)) * state + heads(at).astype(F32)
        state = jnp.where(mine(at), new, state)
    return state


def router_softmax(logits, experts):
    lane = lax.broadcasted_iota(jnp.int32, logits.shape, 1)
    logits = jnp.where(lane < experts, logits, -1e30)
    top = jnp.max(logits, axis=-1, keepdims=True)
    e = jnp.where(lane < experts, jnp.exp(logits - top), 0.0)
    return e / jnp.sum(e, axis=-1, keepdims=True)


def expert(z, where, x, cot, router, up, down):
    D, FF, E = z.D, z.FF, z.E
    M = x.shape[0]
    fb = FF // 8
    steps = 4

    def body(wh, x_r, c_r, rt, up_r, dn_r, ret_o, rdx_o, dwu_o, dwd_o, g_s, out_s, dx_s):
        i = pl.program_id(0)

        @pl.when(i == 0)
        def _():
            ch = router_softmax(mm_nt(x_r[...], rt[...]), E)
            lane = lax.broadcasted_iota(jnp.int32, ch.shape, 1)
            gating = jnp.sum(jnp.where(lane == wh[1], ch, 0.0), axis=-1, keepdims=True)
            g_s[...] = (gating * c_r[...].astype(F32)).astype(BF16)
            out_s[...] = jnp.zeros_like(out_s)
            dx_s[...] = jnp.zeros_like(dx_s)

        xv, gv = x_r[...], g_s[...]
        upv, dnv = up_r[...], dn_r[...]
        pre = mm(xv, upv)
        cdf = 0.5 * (1.0 + lax.erf(pre * (2.0 ** -0.5)))
        hidden = (pre * cdf).astype(BF16)
        slope = cdf + pre * jnp.exp(-0.5 * pre * pre) * (1.0 / math.sqrt(2.0 * math.pi))
        out_s[...] += mm(hidden, dnv)
        pg = (mm_nt(gv, dnv) * slope).astype(BF16)
        dx_s[...] += mm_nt(pg, upv)
        dwd_o[...] = mm_tn(hidden, gv).astype(BF16)
        dwu_o[...] = mm_tn(xv, pg).astype(BF16)

        @pl.when(i == steps - 1)
        def _():
            out = out_s[...]
            ret_o[...] = out.astype(BF16)
            rdx_o[:, 0:D] = dx_s[...].astype(BF16)
            gg = jnp.sum(out * c_r[...].astype(F32), axis=-1, keepdims=True)
            hi, lo = split_hi_lo(gg)
            lane = lax.broadcasted_iota(jnp.int32, (M, LANES), 1)
            both = jnp.where(lane == 0, hi.astype(F32), jnp.where(lane == 1, lo.astype(F32), 0.0))
            rdx_o[:, D : D + LANES] = both.astype(BF16)

    whole_ = lambda shape: pl.BlockSpec(shape, lambda i, w: (0,) * len(shape))
    return pl.pallas_call(
        body,
        name="expert",
        grid_spec=pltpu.PrefetchScalarGridSpec(
            num_scalar_prefetch=1,
            grid=(steps,),
            in_specs=[
                whole_(x.shape),
                whole_(cot.shape),
                whole_(router.shape),
                pl.BlockSpec((D, fb), lambda i, w: (0, 2 * i + w[2])),
                pl.BlockSpec((fb, D), lambda i, w: (2 * i + w[2], 0)),
            ],
            out_specs=[
                whole_((M, D)),
                whole_((M, D + LANES)),
                pl.BlockSpec((D, fb), lambda i, w: (0, i)),
                pl.BlockSpec((fb, D), lambda i, w: (i, 0)),
            ],
            scratch_shapes=[pltpu.VMEM((M, D), BF16), pltpu.VMEM((M, D), F32), pltpu.VMEM((M, D), F32)],
        ),
        out_shape=[
            sds((M, D), BF16),
            sds((M, D + LANES), BF16),
            sds((D, steps * fb), BF16),
            sds((steps * fb, D), BF16),
        ],
        compiler_params=pltpu.CompilerParams(vmem_limit_bytes=VMEM_LIMIT),
    )(where, x, cot, router, up, down)


def padded_rows(main, edge, J, cb):
    H = edge.shape[0]
    m3 = main.reshape(J, SUB, cb)
    first = lax.broadcasted_iota(jnp.int32, (SUB, cb), 0) == 0
    tail = jnp.stack(
        [
            jnp.where(
                first,
                jnp.broadcast_to(edge[H - 3 + k : H - 2 + k, :], (SUB, cb)),
                pltpu.roll(m3[J - 3 + k], 1, 0),
            )
            for k in range(3)
        ]
    )
    return jnp.concatenate([tail, m3], axis=0)


def at_cols(i, cb):
    return pl.ds(pl.multiple_of(i * cb, LANES), cb)


def lanes_of(i, cb, p, tg, k):
    return pl.ds(pl.multiple_of(i * cb + p * tg * LANES, LANES) + k * LANES, LANES)


class Chain:
    def __init__(self, E, src, dst, send, recv, own):
        self.E, self.src, self.dst, self.send, self.recv, self.own = E, src, dst, send, recv, own
        self.me = lax.axis_index("exp")
        self.right, self.left = lax.rem(self.me + 1, E), lax.rem(self.me + E - 1, E)

    def slot(self, d):
        return 2 * (abs(d) - 1) + (1 if d > 0 else 0)

    def exists(self, d):
        return (self.me + d >= 0) & (self.me + d < self.E)

    def each(self, d, act):
        for to_right in (True, False):
            if (d <= 0) if to_right else (d >= 0):
                edge = self.me < self.E - 1 if to_right else self.me > 0
                there = self.slot(d - 1 if to_right else d + 1)

                @pl.when(self.exists(d) & edge)
                def _():
                    act(
                        pltpu.make_async_remote_copy(
                            self.src if d == 0 else self.dst.at[self.me + d],
                            self.dst.at[self.me + d],
                            self.send.at[there],
                            self.recv.at[there],
                            device_id={"exp": self.right if to_right else self.left},
                            device_id_type=MESH,
                        )
                    )

    def local(self):
        return pltpu.make_async_copy(self.src, self.dst.at[self.me], self.own)

    def start(self):
        self.each(0, lambda c: c.start())
        self.local().start()

    def hop(self, k):
        for d in (-k, k):
            ref = self.dst.at[self.me + d]

            @pl.when(self.exists(d))
            def _():
                pltpu.make_async_remote_copy(
                    ref, ref, self.send.at[self.slot(d)], self.recv.at[self.slot(d)],
                    device_id={"exp": self.right}, device_id_type=MESH,
                ).wait_recv()

            if k < self.E - 1:
                self.each(d, lambda c: c.start())

    def finish(self):
        for k in range(self.E - 1):
            for d in (-k, k) if k else (0,):
                self.each(d, lambda c: c.wait_send())
        self.local().wait()


class Spread:
    def __init__(self, E, src, col0, dst, cols, whole_cols, each, sems):
        self.E, self.src, self.col0, self.dst, self.cols = E, src, col0, dst, cols
        self.whole_cols, self.each_cols = whole_cols, each
        self.zs, self.zr, self.ps, self.pr, self.cs, self.cr = sems
        self.rows = src.shape[0]
        s, self.me = lax.axis_index("seq"), lax.axis_index("exp")
        self.chip, self.core = s // 2, lax.rem(s, 2)
        self.sib = {"seq": s + 1 - 2 * self.core}
        self.chips = [self.chip + 1 - 2 * lax.rem(self.chip, 2), self.chip + 2 - 4 * (self.chip // 2), 3 - self.chip]
        self.right, self.left = lax.rem(self.me + 1, E), lax.rem(self.me + E - 1, E)
        self.regions = [1, 0] if each else [0]
        self.offsets = [d for k in range(1, E) for d in (-k, k)]

    def slot(self, d):
        return 2 * (abs(d) - 1) + (1 if d > 0 else 0)

    def exists(self, d):
        return (self.me + d >= 0) & (self.me + d < self.E)

    def span(self, region, q):
        if region == 0:
            return 0, self.whole_cols
        return pl.multiple_of(self.whole_cols + q * self.each_cols, LANES), self.each_cols

    def there(self, d, region, q, core):
        half = self.rows // 2
        start, width = self.span(region, q)
        at = pl.ds(pl.multiple_of((self.me + d) * self.rows + core * half, 16), half)
        return self.dst.at[at] if width == self.cols else self.dst.at[at, pl.ds(start, width)]

    def own(self, region):
        half = self.rows // 2
        start, width = self.span(region, self.chip)
        at = pl.ds(pl.multiple_of(self.core * half, 16), half)
        if width == self.src.shape[1]:
            return self.src.at[at]
        return self.src.at[at, pl.ds(pl.multiple_of(self.col0 + start, LANES), width)]

    def local(self, sem):
        at = pl.ds(pl.multiple_of(self.me * self.rows, 16), self.rows)
        src = self.src if self.cols == self.src.shape[1] else self.src.at[:, self.col0 : self.col0 + self.cols]
        return pltpu.make_async_copy(src, self.dst.at[at], sem)

    def z_each(self, region, d, act):
        for to_right in (True, False):
            if (d <= 0) if to_right else (d >= 0):
                edge = self.me < self.E - 1 if to_right else self.me > 0
                slot = self.slot(d - 1 if to_right else d + 1)

                @pl.when(self.exists(d) & edge)
                def _():
                    act(
                        pltpu.make_async_remote_copy(
                            self.own(region) if d == 0 else self.there(d, region, self.chip, self.core),
                            self.there(d, region, self.chip, self.core),
                            self.zs.at[region, slot],
                            self.zr.at[region, slot],
                            device_id={"exp": self.right if to_right else self.left},
                            device_id_type=MESH,
                        )
                    )

    def start(self):
        for r in self.regions:
            self.z_each(r, 0, lambda c: c.start())

    def plane_copy(self, k, d):
        ref = self.there(d, 1, self.chip, self.core)
        return pltpu.make_async_remote_copy(
            ref, ref, self.ps.at[k, self.slot(d)], self.pr.at[k, self.slot(d)],
            device_id={"seq": self.chips[k] * 2 + self.core}, device_id_type=MESH,
        )

    def piece(self, which, d, core):
        if which == 0:
            return self.there(d, 0, self.chip, core)
        return self.there(d, 1, self.chip if which == 1 else self.chips[which - 2], core)

    def sib_copy(self, which, d, core):
        ref = self.piece(which, d, core)
        return pltpu.make_async_remote_copy(
            ref, ref, self.cs.at[which, self.slot(d)], self.cr.at[which, self.slot(d)],
            device_id=self.sib, device_id_type=MESH,
        )

    def hop(self, k):
        for r in self.regions:
            for d in (-k, k):
                @pl.when(self.exists(d))
                def _():
                    ref = self.there(d, r, self.chip, self.core)
                    pltpu.make_async_remote_copy(
                        ref, ref, self.zs.at[r, self.slot(d)], self.zr.at[r, self.slot(d)],
                        device_id={"exp": self.right}, device_id_type=MESH,
                    ).wait_recv()

                if k < self.E - 1:
                    self.z_each(r, d, lambda c: c.start())

                @pl.when(self.exists(d))
                def _():
                    if r == 1:
                        for j in range(3):
                            self.plane_copy(j, d).start()
                    self.sib_copy(r, d, self.core).start()

    def plane(self, k):
        if not self.each_cols:
            return
        for d in (-k, k):
            @pl.when(self.exists(d))
            def _():
                for j in range(3):
                    ref = self.there(d, 1, self.chips[j], self.core)
                    pltpu.make_async_remote_copy(
                        ref, ref, self.ps.at[j, self.slot(d)], self.pr.at[j, self.slot(d)],
                        device_id=self.sib, device_id_type=MESH,
                    ).wait_recv()
                    self.sib_copy(2 + j, d, self.core).start()

    def landed(self):
        for d in self.offsets:
            @pl.when(self.exists(d))
            def _():
                for w in range(5 if self.each_cols else 1):
                    self.sib_copy(w, d, 1 - self.core).wait_recv()

    def finish(self):
        for d in self.offsets:
            @pl.when(self.exists(d))
            def _():
                for w in range(5 if self.each_cols else 1):
                    self.sib_copy(w, d, self.core).wait_send()
                if self.each_cols:
                    for j in range(3):
                        self.plane_copy(j, d).wait_send()
        for r in self.regions:
            for k in range(self.E - 1):
                for d in (-k, k) if k else (0,):
                    self.z_each(r, d, lambda c: c.wait_send())


def forward(z, S, plane, tok, tail, seg_tail, seg_head, cot, route, masks, in_proj, out_proj, small_own, g_own, gr, cid):
    T, D, DI, N, J, E, CAP = z.T, z.D, z.DI, z.N, z.J, z.E, z.CAP
    H = tail.shape[0]
    M = E * CAP
    DZ, NZ = DI // E, D // E
    rs, rg = small_own.shape[0], g_own.shape[0]
    if not plane:
        rs, rg = rs // E, rg // E
    cb = pick(DI, (384, 256, 128))
    cs = pick(DI, (768, 384, 256, 128))
    tg = tile_groups(cs)
    wide = tg * LANES
    ng = 8
    steps = DI // cs
    ST = (J + 1) * N * SUB
    tiles, tiles_o = DI // LANES, D // LANES
    split = (tiles // 4 - (0 if tiles % 4 else 1)) * LANES
    split_o = max(1, tiles_o * 2 // 9) * LANES

    def body(
        tok, tail, seg_t, seg_h, cot, route, msk_in, in_p, out_p, sm_p, g_p,
        sm, gp, rt, table, choose, masks, conv_in, hconv, gate, sig, mixed, dt, y, mid, moe, ch_o, s_all,
        st_o, win_o, wout_o, arr_o, cot_o, nz_o,
        wc, wg, wo, smb, gb, nrm, halo, seg_in, bx, cx, cl, u_s, rates_s, hd, hdev, stot, h_all, pre_s, dwin, hin,
        st_v, acc, outb, cotb, nz,
        ld, zs, zr, ps, pr, c_s, c_r, t_s, t_r, h_s, h_r, d_s, d_r, q_s, q_r, k_s, k_r, n_s, n_r, x_s, x_r,
    ):
        s, me = lax.axis_index("seq"), lax.axis_index("exp")
        core = lax.rem(s, 2)
        sib = {"seq": s + 1 - 2 * core}
        seqs = [lax.rem(s + k, S) for k in range(1, S)]
        zz = [lax.rem(me + k, E) for k in range(1, E)]
        greet([{"seq": p} for p in seqs] + [{"exp": p} for p in zz])

        def remote(src, dst, send, recv, to):
            return pltpu.make_async_remote_copy(src, dst, send, recv, device_id=to, device_id_type=MESH)

        ahead = {"seq": lax.rem(s + 1, S)}
        edges = [remote(tail, halo, t_s.at[0], t_r.at[0], ahead), remote(seg_t, seg_in, t_s.at[1], t_r.at[1], ahead)]
        for c in edges:
            c.start()
        sems = lambda a: (zs.at[a], zr.at[a], ps.at[a], pr.at[a], c_s.at[a], c_r.at[a])
        if plane:
            parts = [
                Spread(E, sm_p, 0, smb, sm_p.shape[1], sm_p.shape[1], 0, sems(0)),
                Spread(E, g_p, 0, gb, g_p.shape[1], g_p.shape[1], 0, sems(1)),
                Spread(E, in_p, 0, wc, DI, DI - 4 * split, split, sems(2)),
                Spread(E, in_p, DI, wg, DI, DI - 4 * split, split, sems(3)),
                Spread(E, out_p, 0, wo, D, D - 4 * split_o, split_o, sems(4)),
            ]
            for p in parts[:4]:
                p.start()
            loads = [p.local(ld.at[a]) for a, p in enumerate(parts)]
        else:
            loads = [
                pltpu.make_async_copy(sm_p, smb, ld.at[0]),
                pltpu.make_async_copy(g_p, gb, ld.at[1]),
                pltpu.make_async_copy(in_p.at[:, 0:DI], wc, ld.at[2]),
                pltpu.make_async_copy(in_p.at[:, DI : 2 * DI], wg, ld.at[3]),
                pltpu.make_async_copy(out_p, wo, ld.at[4]),
            ]
        for c in loads:
            c.start()

        lane = lax.broadcasted_iota(jnp.int32, (T, LANES), 1)
        chosen = (lane == route[...]).astype(F32)
        choose[...] = chosen
        upto = lax.broadcasted_iota(jnp.int32, (T, T), 1) <= lax.broadcasted_iota(jnp.int32, (T, T), 0)
        counts = mm(upto.astype(F32).astype(BF16), chosen.astype(BF16))
        rank = jnp.sum(counts * chosen, axis=-1, keepdims=True).astype(jnp.int32) - 1
        slots = lax.broadcasted_iota(jnp.int32, (T, M), 1)
        table[...] = (slots == route[...] * CAP + rank).astype(F32).astype(BF16)
        cotb[...] = mm_tn(table[...], cot[...]).astype(BF16)

        if plane:
            for k in range(1, E):
                for p in parts[:4]:
                    p.hop(k)
                if k == 1:
                    parts[4].start()
                if k == 2:
                    parts[2].plane(1)
            for k in range(2, E):
                parts[2].plane(k)
        block_of = lambda ref, p: ref.at[pl.ds(pl.multiple_of(p * CAP, 16), CAP)]
        cot_moves = [remote(block_of(cotb, p), cot_o.at[core, me], k_s.at[k], k_r.at[k], {"exp": p}) for k, p in enumerate(zz)]
        if plane:
            for p in parts[:3]:
                p.landed()
        for c in loads:
            c.wait()
        for e in range(E):
            sm[:, e * DZ : (e + 1) * DZ] = smb[e * rs : (e + 1) * rs, :].astype(F32)[0 : z.SMALL]
        gp[...] = jnp.zeros_like(gp)
        rt[...] = jnp.zeros_like(rt)
        for e in range(E):
            cols = slice(e * NZ, (e + 1) * NZ)
            gp[:, cols] = gb[e * rg : e * rg + 16, :].astype(F32)[0:gr]
        rt[0:16, :] = jnp.concatenate([gp[2 : 2 + E, :], jnp.zeros((16 - E, D), F32)], axis=0).astype(BF16)

        for c in edges:
            c.wait()
        live = jnp.where(s > 0, 1.0, 0.0)
        masks[...] = msk_in[...]
        col8 = lax.broadcasted_iota(jnp.int32, (1, SUB), 1)
        for t in range(3):
            row = masks[SUB * t : SUB * t + 1, :]
            for o in range(3 - t):
                before = seg_in[t + o : t + o + 1, 0:SUB] * live
                same = (before == seg_h[t : t + 1, 0:SUB]).astype(F32)
                row = jnp.where(col8 == o, same, row)
            masks[SUB * t : SUB * t + 1, :] = row
        t32 = tok[...].astype(F32)
        nrm[0:T, :] = (t32 * rms_scale(t32) * gp[0:1, :]).astype(BF16)
        h32 = halo[...].astype(F32) * live
        nrm[T : T + H, :] = (h32 * rms_scale(h32) * gp[0:1, :]).astype(BF16)
        mixed[...] = jnp.zeros_like(mixed)

        def conv_block(i, carry):
            C = at_cols(i, cb)
            both = mm(nrm[...], wc[:, C])
            main, edge = both[:T], both[T:]
            conv_in[:, C] = main
            hconv[:, C] = edge
            xpad = padded_rows(main, edge, J, cb)
            out = jnp.broadcast_to(sm[CONV_B : CONV_B + 1, C], (T, cb))
            for o in range(4):
                m = jnp.broadcast_to(masks[:, o : o + 1], (T, cb))
                out = out + sm[CONV_W + o : CONV_W + o + 1, C] * xpad[o : o + J].reshape(T, cb) * m
            sv = (out * sigmoid(out)).astype(BF16)
            sig[:, C] = sv
            mixed[...] += mm_nt(sv, sm[z.X0 : z.X0 + z.XW, C].astype(BF16))
            return carry

        lax.fori_loop(0, DI // cb, conv_block, 0)
        for e in range(E):
            nz[e] = nrm[0:T, e * NZ : (e + 1) * NZ]
        nz_moves = [remote(nz.at[p], nz_o.at[me], n_s.at[k], n_r.at[k], {"exp": p}) for k, p in enumerate(zz)]
        nz_own = pltpu.make_async_copy(nz.at[me], nz_o.at[me], ld.at[5])
        nz_own.start()
        if plane:
            for k in range(1, E):
                parts[4].hop(k)
                parts[3].plane(k)
        for c in cot_moves + nz_moves:
            c.start()
        cot_own = pltpu.make_async_copy(block_of(cotb, me), cot_o.at[core, me], ld.at[6])
        cot_own.start()

        expand_columns(z, mixed, z.R, bx)
        expand_columns(z, mixed, z.R + N, cx)
        expand_closed(z, masks, cl)
        low = mixed[:, 0 : z.R].astype(BF16)

        def step_block(i, carry):
            C = at_cols(i, cs)
            pre = mm(low, sm[z.DT0 : z.DT0 + z.R, C].astype(BF16)) + sm[DT_B : DT_B + 1, C]
            step = softplus(pre)
            dt[:, C] = step
            u_s[:, C] = step * sig[:, C].astype(F32)
            rates_s[:, C] = -jnp.exp(sm[A_LOG : A_LOG + N, C]) * LOG2E
            return carry

        lax.fori_loop(0, DI // cs, step_block, 0)

        def chunk_block(p, carry):
            lanes = [lane_at(p, tg, k) for k in range(tg)]
            wins = []
            for k in range(tg):
                w1 = jnp.zeros((SUB, LANES), F32)
                for j in range(J):
                    w1 = w1 + (dt[j * SUB : j * SUB + SUB, lanes[k]] + cl[j * SUB : j * SUB + SUB, :])
                w2 = w1 + shift_down(w1, 1)
                w4 = w2 + shift_down(w2, 2)
                w8 = w4 + shift_down(w4, 4)
                wins.append((w1, w2, w4))
                dwin[:, lanes[k]] = shift_down(w8, 1)
                stot[:, lanes[k]] = w8[SUB - 1 : SUB, :]
            for g in range(0, N, ng):
                rr = [
                    [jnp.broadcast_to(rates_s[g + n : g + n + 1, lanes[k]], (SUB, LANES)) for k in range(tg)]
                    for n in range(ng)
                ]

                def step_j(j, hs):
                    dts = [dt[row8(j), lanes[k]] + cl[row8(j), :] for k in range(tg)]
                    us = [u_s[row8(j), lanes[k]] for k in range(tg)]
                    new = []
                    for n in range(ng):
                        b = bx[row8(j * N + g + n), :]
                        for k in range(tg):
                            new.append(jnp.exp2(dts[k] * rr[n][k]) * hs[n * tg + k] + us[k] * b)
                    return tuple(new)

                hs = lax.fori_loop(
                    0, J, step_j, tuple(jnp.zeros((SUB, LANES), F32) for _ in range(ng * tg)), unroll=2
                )
                for n in range(ng):
                    for k in range(tg):
                        h = hs[n * tg + k]
                        w1, w2, w4 = wins[k]
                        r = rr[n][k]
                        h = h + jnp.exp2(r * w1) * shift_down(h, 1)
                        h = h + jnp.exp2(r * w2) * shift_down(h, 2)
                        h = h + jnp.exp2(r * w4) * shift_down(h, 4)
                        pre_s[(g + n) * SUB : (g + n + 1) * SUB, lanes[k]] = shift_down(h, 1)
                        hd[g + n : g + n + 1, lanes[k]] = h[SUB - 1 : SUB, :]
            return carry

        lax.fori_loop(0, DI // wide, chunk_block, 0)
        hdev[...] = hd[...].astype(BF16)
        h_moves = [remote(hdev, h_all.at[s], h_s.at[0, k], h_r.at[0, k], {"seq": p}) for k, p in enumerate(seqs)]
        h_moves += [remote(stot, s_all.at[s], h_s.at[1, k], h_r.at[1, k], {"seq": p}) for k, p in enumerate(seqs)]
        for c in h_moves:
            c.start()
        h_all[s] = hdev[...]
        s_all[s] = stot[...]
        if plane:
            parts[3].landed()

        def gate_block(i, carry):
            C = at_cols(i, cb)
            gate[:, C] = mm(nrm[0:T, :], wg[:, C])
            return carry

        lax.fori_loop(0, DI // cb, gate_block, 0)
        if plane:
            for k in range(1, E):
                parts[4].plane(k)
            parts[4].landed()
        outs = [
            pltpu.make_async_copy(wc, win_o.at[:, 0:DI], ld.at[7]),
            pltpu.make_async_copy(wg, win_o.at[:, DI : 2 * DI], ld.at[8]),
            pltpu.make_async_copy(wo, wout_o, ld.at[9]),
        ]
        for c in outs:
            c.start()
        for c in h_moves:
            c.wait()
        acc[...] = jnp.zeros_like(acc)

        def save(i):
            return pltpu.make_async_copy(
                st_v.at[i % 2], st_o.at[:, i * cs : (i + 1) * cs], ld.at[10 + i % 2]
            )

        for i in range(steps):
            if i >= 2:
                save(i - 2).wait()
            C = slice(i * cs, (i + 1) * cs)
            hin[...] = chain_states(
                S - 1, lambda k: k < s, lambda k: k, lambda k: s_all[k, :, C], lambda k: h_all[k, :, C],
                rates_s[:, C],
            )

            def pair(p, carry):
                lanes = [lanes_of(i, cs, p, tg, k) for k in range(tg)]
                near = [lane_at(p, tg, k) for k in range(tg)]
                for g in range(0, N, ng):
                    rr = [
                        [jnp.broadcast_to(rates_s[g + n : g + n + 1, lanes[k]], (SUB, LANES)) for k in range(tg)]
                        for n in range(ng)
                    ]
                    init = []
                    for n in range(ng):
                        for k in range(tg):
                            at = (g + n) * SUB
                            init.append(
                                pre_s[at : at + SUB, lanes[k]]
                                + jnp.exp2(rr[n][k] * dwin[:, lanes[k]])
                                * jnp.broadcast_to(hin[g + n : g + n + 1, near[k]], (SUB, LANES))
                            )

                    def keep(j, hs):
                        for n in range(0, ng, 2):
                            for k in range(tg):
                                two = jnp.concatenate([hs[n * tg + k], hs[(n + 1) * tg + k]], axis=0)
                                at = pl.multiple_of(j * N * SUB + (g + n) * SUB, 2 * SUB)
                                st_v[i % 2, pl.ds(at, 2 * SUB), near[k]] = two.astype(BF16)

                    keep(0, init)

                    def step_j(j, hs):
                        dts = [dt[row8(j), lanes[k]] + cl[row8(j), :] for k in range(tg)]
                        us = [u_s[row8(j), lanes[k]] for k in range(tg)]
                        if g == 0:
                            ys = [jnp.zeros((SUB, LANES), F32) for k in range(tg)]
                        else:
                            ys = [y[row8(j), lanes[k]] for k in range(tg)]
                        new = []
                        for n in range(ng):
                            b = bx[row8(j * N + g + n), :]
                            c = cx[row8(j * N + g + n), :]
                            for k in range(tg):
                                h = jnp.exp2(dts[k] * rr[n][k]) * hs[n * tg + k] + us[k] * b
                                ys[k] = ys[k] + h * c
                                new.append(h)
                        for k in range(tg):
                            y[row8(j), lanes[k]] = ys[k]
                        keep(j + 1, new)
                        return tuple(new)

                    lax.fori_loop(0, J, step_j, tuple(init), unroll=2)
                return carry

            lax.fori_loop(0, cs // wide, pair, 0)
            save(i).start()
            yv = y[:, C] + sm[SKIP : SKIP + 1, C] * sig[:, C].astype(F32)
            y[:, C] = yv
            g_in = gate[:, C]
            gated = (yv * (g_in * sigmoid(g_in))).astype(BF16)
            acc[...] += mm(gated, wo[C, :])

        m32 = tok[...].astype(F32) + acc[...]
        mid[...] = m32
        moe[...] = (m32 * rms_scale(m32) * gp[1:2, :]).astype(BF16)
        ch_o[...] = router_softmax(mm_nt(moe[...], rt[...]), E)
        outb[...] = mm_tn(table[...], moe[...]).astype(BF16)
        out_moves = [remote(block_of(outb, p), arr_o.at[core, me], d_s.at[k], d_r.at[k], {"exp": p}) for k, p in enumerate(zz)]
        for c in out_moves:
            c.start()
        arr_own = pltpu.make_async_copy(block_of(outb, me), arr_o.at[core, me], ld.at[12])
        arr_own.start()
        passes = [
            remote(block_of(cotb, me), cot_o.at[core, me], x_s.at[0, 0], x_r.at[0, 0], sib),
            remote(block_of(outb, me), arr_o.at[core, me], x_s.at[1, 0], x_r.at[1, 0], sib),
        ]
        for c in passes:
            c.start()
        for w, ref, send, recv in ((0, cot_o, k_s, k_r), (1, arr_o, d_s, d_r)):
            for k in range(1, E):
                frm = lax.rem(me + E - k, E)
                at = ref.at[core, frm]
                remote(at, at, send.at[k - 1], recv.at[k - 1], {"exp": frm}).wait_recv()
                c = remote(at, at, x_s.at[w, k], x_r.at[w, k], sib)
                c.start()
                passes.append(c)
        if plane:
            for p in parts:
                p.finish()
        for c in outs + [nz_own, cot_own, arr_own]:
            c.wait()
        for i in range(max(0, steps - 2), steps):
            save(i).wait()
        for c in nz_moves:
            c.wait()
        for c in cot_moves + out_moves + passes:
            c.wait_send()
        for w, ref in ((0, cot_o), (1, arr_o)):
            for k in range(E):
                at = ref.at[1 - core, lax.rem(me + E - k, E)]
                remote(at, at, x_s.at[w, k], x_r.at[w, k], sib).wait_recv()

    v = pltpu.VMEM
    sem = lambda *dims: pltpu.SemaphoreType.DMA(dims)
    vm = pl.BlockSpec(memory_space=pltpu.VMEM)
    zslots = 2 * (E - 1)
    ins = (tok, tail, seg_tail, seg_head, cot, route, masks, in_proj, out_proj, small_own, g_own)
    vm_outs = [
        sds((z.SMALL, DI), F32), sds((gr, D), F32), sds((LANES, D), BF16), sds((T, M), BF16), sds((T, LANES), F32),
        sds((T, SUB), F32), sds((T, DI), F32), sds((H, DI), F32), sds((T, DI), F32), sds((T, DI), BF16),
        sds((T, z.XW), F32), sds((T, DI), F32), sds((T, DI), F32), sds((T, D), F32), sds((T, D), BF16),
        sds((T, LANES), F32), sds((S, 1, DI), F32),
    ]
    any_outs = [
        sds((ST, DI), BF16), sds((D, 2 * DI), BF16), sds((DI, D), BF16), sds((2, E, CAP, D), BF16),
        sds((2, E, CAP, D), BF16), sds((E, T, NZ), BF16),
    ]
    return pl.pallas_call(
        body,
        name="forward",
        in_specs=[vm] * 7 + [ANY] * 4,
        out_specs=[vm] * len(vm_outs) + [ANY] * len(any_outs),
        out_shape=vm_outs + any_outs,
        scratch_shapes=[
            v((D, DI), BF16), v((D, DI), BF16), v((DI, D), BF16), v((E * rs, DZ), BF16), v((E * rg, NZ), BF16),
            v((T + H, D), BF16), v((H, D), BF16), v((SUB, LANES), F32),
            v((J * N * SUB, LANES), F32), v((J * N * SUB, LANES), F32), v((T, LANES), F32), v((T, DI), F32),
            v((N, DI), F32), v((N, DI), F32), v((N, DI), BF16), v((1, DI), F32), v((S, N, DI), BF16),
            v((N * SUB, DI), F32), v((SUB, DI), F32), v((N, cs), F32),
            v((2, ST, cs), BF16), v((T, D), F32), v((M, D), BF16), v((M, D), BF16), v((E, T, NZ), BF16),
            sem(13), sem(5, 2, zslots), sem(5, 2, zslots), sem(5, 3, zslots), sem(5, 3, zslots),
            sem(5, 5, zslots), sem(5, 5, zslots), sem(2), sem(2), sem(2, S - 1), sem(2, S - 1),
            sem(E - 1), sem(E - 1), sem(1), sem(1), sem(E - 1), sem(E - 1), sem(E - 1), sem(E - 1),
            sem(2, E), sem(2, E),
        ],
        compiler_params=pltpu.CompilerParams(
            collective_id=cid, has_side_effects=True, vmem_limit_bytes=60 * 1024 * 1024
        ),
    )(*ins)


def backward(z, S, plane, dxp, outp, dwu, dwd, states, w_out, w_in, table, choose, chances, mid, moe, cot, gpack,
             router, gate, y, sig, small, mixed, dt, masks, conv_in, hconv, s_all, tok, cid):
    T, D, DI, N, J, E, CAP = z.T, z.D, z.DI, z.N, z.J, z.E, z.CAP
    M = E * CAP
    G = gpack.shape[0]
    H = hconv.shape[0]
    DZ = DI // E
    cb_m = pick(DI, (384, 256, 128))
    cb_s = pick(DI, (768, 384, 256, 128))
    steps_s = DI // cb_s
    tg_s = tile_groups(cb_s)
    ng_s = 4
    uq, uc = dwu.shape[0] // 4, dwu.shape[1]
    dq, dc = dwd.shape[0] // 4, dwd.shape[1]
    ST = (J + 1) * N * SUB
    rows_big = max(ST, 2 * D)
    chain_slots = 2 * (E - 1)

    def body(
        dxp, outp, dwu, dwd, states, w_out, w_in, table, choose, chances, mid, moe, cot, gp, router, gate, y, sig,
        small, mixed, dt, masks, conv_in, hconv, s_all, tok,
        tg_o, gs_o, gg_o, back_o, gate_o, pc_o, br_o, gz_o, up_o, down_o,
        big, wo_v, dx_a, dx_b, out_a, out_b, dx_z, yg, gi, gd, gz, br, mg, fdev, f_all, suf, ssg, dpl, cig, cg_edge,
        edge_in, pc, bx, cx, ia, oa, cl, u_s, rates_s, fin, dg_s, rs_s, rt_s, low_s, mxg, acc, fd,
        ua, ub, ub2, uf, da, db, db2,
        ld, sw_s, sw_r, dz_s, dz_r, oz_s, oz_r, f_s, f_r, e_s, e_r, g_s, g_r, p_s, p_r, b_s, b_r, a_s, a_r, x_s, x_r,
    ):
        s, me = lax.axis_index("seq"), lax.axis_index("exp")
        core = lax.rem(s, 2)
        other = 1 - core
        sib = {"seq": s + 1 - 2 * core}
        seqs = [lax.rem(s + k, S) for k in range(1, S)]
        zs = [lax.rem(me + k, E) for k in range(1, E)]
        greet([{"seq": p} for p in seqs] + [{"exp": p} for p in zs])

        def remote(src, dst, send, recv, to):
            return pltpu.make_async_remote_copy(src, dst, send, recv, device_id=to, device_id_type=MESH)

        swaps = [
            remote(dxp.at[other], dx_b, sw_s.at[0], sw_r.at[0], sib),
            remote(outp.at[other], out_b, sw_s.at[1], sw_r.at[1], sib),
        ]
        for c in swaps:
            c.start()
        loads = [
            pltpu.make_async_copy(dxp.at[core], dx_a, ld.at[0]),
            pltpu.make_async_copy(outp.at[core], out_a, ld.at[1]),
            pltpu.make_async_copy(w_out, wo_v, ld.at[2]),
        ]
        for c in loads:
            c.start()

        def state_load(i):
            half = pl.ds((i % 2) * cb_s, cb_s)
            return pltpu.make_async_copy(
                states.at[:, i * cb_s : (i + 1) * cb_s], big.at[0:ST, half], ld.at[3 + i % 2]
            )

        state_load(0).start()
        if plane:
            chip = s // 2
            xx, yy = lax.rem(chip, 2), chip // 2
            to_x = {"seq": s + 2 - 4 * xx}
            to_y = {"seq": s + 4 - 8 * yy}
            u4 = lambda ref, v, w: ref.at[pl.ds(pl.multiple_of((2 * v + w) * uq, 16), uq)]
            up1 = [
                remote(u4(dwu, v, 1 - xx), ub.at[v], a_s.at[v], a_r.at[v], to_x) for v in range(2)
            ]
            d_half = lambda v: pl.ds(pl.multiple_of(v * 2 * dq, 16), 2 * dq)
            down1 = remote(dwd.at[d_half(1 - yy)], db, a_s.at[2], a_r.at[2], to_y)
            for c in up1 + [down1]:
                c.start()
            mine = [pltpu.make_async_copy(u4(dwu, v, xx), ua.at[v], ld.at[5 + v]) for v in range(2)]
            mine.append(pltpu.make_async_copy(dwd.at[d_half(yy)], da, ld.at[7]))
            for c in mine:
                c.start()

        adds = lambda a, b: (a.astype(F32) + b.astype(F32)).astype(BF16)
        loads[0].wait()
        swaps[0].wait()
        dx_a[...] = adds(dx_a[...], dx_b[...])
        block_of = lambda ref, p: ref.at[pl.ds(pl.multiple_of(p * CAP, 16), CAP)]
        dx_moves = [
            remote(block_of(dx_a, p), block_of(dx_z, me), dz_s.at[k], dz_r.at[k], {"exp": p})
            for k, p in enumerate(zs)
        ]
        for c in dx_moves:
            c.start()
        here = pl.ds(pl.multiple_of(me * CAP, 16), CAP)
        dx_z[here, :] = dx_a[here, :]
        loads[1].wait()
        swaps[1].wait()
        out_a[...] = adds(out_a[...], out_b[...])
        out_moves = [
            remote(block_of(out_a, p), block_of(back_o, me), oz_s.at[k], oz_r.at[k], {"exp": p})
            for k, p in enumerate(zs)
        ]
        for c in out_moves:
            c.start()
        back_own = pltpu.make_async_copy(block_of(out_a, me), block_of(back_o, me), ld.at[8])
        back_own.start()
        expand_columns(z, mixed, z.R, bx)
        expand_columns(z, mixed, z.R + N, cx)
        expand_closed(z, masks, cl)
        for c in dx_moves:
            c.wait()

        back = mm(table[...], dx_z[...])
        grad = cot[...].astype(F32)
        ch = chances[...]
        pick_e = choose[...]
        gating = jnp.sum(ch * pick_e, axis=-1, keepdims=True)
        gate_grad = back[:, D : D + 1] + back[:, D + 1 : D + 2]
        lg = ch * (gate_grad * pick_e - gate_grad * gating)
        hi, lo = split_hi_lo(lg)
        rtv = router[...]
        mig = back[:, 0:D] + mm(hi, rtv) + mm(lo, rtv)
        mev = moe[...]
        rg = mm_tn(hi, mev) + mm_tn(lo, mev)
        d, gain_g = rms_back(mid[...], gp[1:2, :], mig)
        mg[...] = grad + d
        br[...] = mg[...].astype(BF16)
        gg_o[...] = jnp.zeros_like(gg_o)
        gg_o[1:2, :] = gain_g
        gg_o[2 : 2 + E, :] = rg[0:E, :]
        chain_b = Chain(E, br, br_o, b_s, b_r, ld.at[9])
        loads[2].wait()

        def middle_block(i, carry):
            C = at_cols(i, cb_m)
            gg = mm_nt(br[...], wo_v[C, :])
            g_in = gate[:, C]
            sg = sigmoid(g_in)
            act = g_in * sg
            yv = y[:, C]
            ygv = gg * act
            yg[:, C] = ygv
            gi[:, C] = (gg * yv * (sg * (1.0 + g_in * (1.0 - sg)))).astype(BF16)
            gd[:, C] = (yv * act).astype(BF16)
            gs_o[SKIP : SKIP + 1, C] = jnp.sum(ygv * sig[:, C].astype(F32), axis=0, keepdims=True)
            return carry

        lax.fori_loop(0, DI // cb_m, middle_block, 0)
        chain_g = Chain(E, gi, gate_o, g_s, g_r, ld.at[10])
        chain_g.start()
        chain_b.start()

        tg, ng = 2 if DI % 256 == 0 else 1, 8
        wide = tg * LANES

        def flow_block(i, carry):
            lanes = [pl.ds(pl.multiple_of(i * wide, LANES) + k * LANES, LANES) for k in range(tg)]
            both = pl.ds(pl.multiple_of(i * wide, LANES), wide)
            rates = -jnp.exp(small[A_LOG : A_LOG + N, both]) * LOG2E
            wins = []
            for k in range(tg):
                w1 = jnp.zeros((SUB, LANES), F32)
                for j in range(J):
                    w1 = w1 + (dt[j * SUB : j * SUB + SUB, lanes[k]] + cl[j * SUB : j * SUB + SUB, :])
                w2 = w1 + shift_up(w1, 1)
                w4 = w2 + shift_up(w2, 2)
                w8 = w4 + shift_up(w4, 4)
                wins.append((w1, w2, w4))
                suf[N * SUB : (N + 1) * SUB, lanes[k]] = shift_up(w8, 1)
            for g in range(0, N, ng):
                rr = [
                    [
                        jnp.broadcast_to(rates[g + n : g + n + 1, k * LANES : (k + 1) * LANES], (SUB, LANES))
                        for k in range(tg)
                    ]
                    for n in range(ng)
                ]

                def step_j(jj, fs):
                    j = J - 1 - jj
                    dts = [dt[row8(j), lanes[k]] + cl[row8(j), :] for k in range(tg)]
                    ygs = [yg[row8(j), lanes[k]] for k in range(tg)]
                    new = []
                    for n in range(ng):
                        c = cx[row8(j * N + g + n), :]
                        for k in range(tg):
                            new.append(jnp.exp2(dts[k] * rr[n][k]) * (fs[n * tg + k] + ygs[k] * c))
                    return tuple(new)

                fs = lax.fori_loop(
                    0, J, step_j, tuple(jnp.zeros((SUB, LANES), F32) for _ in range(ng * tg)), unroll=2
                )
                for n in range(ng):
                    for k in range(tg):
                        f = fs[n * tg + k]
                        w1, w2, w4 = wins[k]
                        r = rr[n][k]
                        f = f + jnp.exp2(r * w1) * shift_up(f, 1)
                        f = f + jnp.exp2(r * w2) * shift_up(f, 2)
                        f = f + jnp.exp2(r * w4) * shift_up(f, 4)
                        suf[(g + n) * SUB : (g + n + 1) * SUB, lanes[k]] = shift_up(f, 1)
                        fd[g + n : g + n + 1, lanes[k]] = f[0:1, :]
            return carry

        lax.fori_loop(0, DI // wide, flow_block, 0)
        fdev[...] = fd[...].astype(BF16)
        f_moves = [
            remote(fdev, f_all.at[s], f_s.at[k], f_r.at[k], {"seq": p}) for k, p in enumerate(seqs)
        ]
        for c in f_moves:
            c.start()
        f_all[s] = fdev[...]
        for e in range(E):
            gz[e] = gd[:, e * DZ : (e + 1) * DZ]
        gz_moves = [remote(gz.at[p], gz_o.at[me], x_s.at[k], x_r.at[k], {"exp": p}) for k, p in enumerate(zs)]
        for c in gz_moves:
            c.start()
        gz_own = pltpu.make_async_copy(gz.at[me], gz_o.at[me], ld.at[11])
        gz_own.start()
        chain_g.hop(1)
        chain_b.hop(1)
        if plane:
            for c in mine + up1 + [down1]:
                c.wait()
            ua[...] = adds(ua[...], ub[...])
            da[...] = adds(da[...], db[...])
            up2 = remote(ua.at[1 - yy], ub2, a_s.at[3], a_r.at[3], to_y)
            down2 = remote(
                da.at[pl.ds(pl.multiple_of((1 - xx) * dq, 16), dq)], db2, a_s.at[4], a_r.at[4], to_x
            )
            up2.start()
            down2.start()
        for c in f_moves:
            c.wait()

        ia[...] = jnp.zeros_like(ia)
        oa[...] = jnp.zeros_like(oa)
        low_s[...] = jnp.zeros_like(low_s)
        for i in range(steps_s):
            state_load(i).wait()
            if i + 1 < steps_s:
                state_load(i + 1).start()
            C = slice(i * cb_s, (i + 1) * cb_s)
            base = (i % 2) * cb_s
            rates2 = -jnp.exp(small[A_LOG : A_LOG + N, C]) * LOG2E
            rates_s[...] = rates2
            fin[...] = chain_states(
                S - 1, lambda k: k > s, lambda k: S - 1 - k, lambda k: s_all[k, :, C], lambda k: f_all[k, :, C],
                rates2,
            )
            sigf = sig[:, C].astype(F32)
            u_s[...] = dt[:, C] * sigf

            def pair(p, carry):
                lanes = [lanes_of(i, cb_s, p, tg_s, k) for k in range(tg_s)]
                near = [lane_at(p, tg_s, k) for k in range(tg_s)]
                held = [
                    pl.ds(base + pl.multiple_of(p * tg_s * LANES, LANES) + k * LANES, LANES) for k in range(tg_s)
                ]
                for g in range(0, N, ng_s):
                    rr = [
                        [
                            jnp.broadcast_to(rates_s[g + n : g + n + 1, near[k]], (SUB, LANES))
                            for k in range(tg_s)
                        ]
                        for n in range(ng_s)
                    ]
                    flow = []
                    for n in range(ng_s):
                        for k in range(tg_s):
                            at = (g + n) * SUB
                            flow.append(
                                suf[at : at + SUB, lanes[k]]
                                + jnp.exp2(rr[n][k] * suf[N * SUB : (N + 1) * SUB, lanes[k]])
                                * jnp.broadcast_to(fin[g + n : g + n + 1, near[k]], (SUB, LANES))
                            )

                    def load(j):
                        got = [[None] * tg_s for _ in range(ng_s)]
                        for n in range(0, ng_s, 2):
                            for k in range(tg_s):
                                at = pl.multiple_of(j * N * SUB + (g + n) * SUB, 2 * SUB)
                                two = big[pl.ds(at, 2 * SUB), held[k]].astype(F32)
                                got[n][k] = two[0:SUB]
                                got[n + 1][k] = two[SUB : 2 * SUB]
                        return [got[n][k] for n in range(ng_s) for k in range(tg_s)]

                    def step_j(jj, carry):
                        fs, hs, rts = carry
                        j = J - 1 - jj
                        dtp = [dt[row8(j), lanes[k]] for k in range(tg_s)]
                        dts = [dtp[k] + cl[row8(j), :] for k in range(tg_s)]
                        us = [u_s[row8(j), near[k]] for k in range(tg_s)]
                        ygs = [yg[row8(j), lanes[k]] for k in range(tg_s)]
                        before = load(j)
                        if g == 0:
                            dgs = [jnp.zeros((SUB, LANES), F32) for k in range(tg_s)]
                            rss = [jnp.zeros((SUB, LANES), F32) for k in range(tg_s)]
                        else:
                            dgs = [dg_s[row8(j), near[k]] for k in range(tg_s)]
                            rss = [rs_s[row8(j), near[k]] for k in range(tg_s)]
                        nf, nr = [], []
                        for n in range(ng_s):
                            at = row8(j * N + g + n)
                            b = bx[at, :]
                            c = cx[at, :]
                            ig = jnp.zeros((SUB, LANES), F32)
                            og = jnp.zeros((SUB, LANES), F32)
                            for k in range(tg_s):
                                q = n * tg_s + k
                                gr = ygs[k] * c + fs[q]
                                f = jnp.exp2(dts[k] * rr[n][k]) * gr
                                rt = f * before[q]
                                rss[k] = rss[k] + rt * rr[n][k]
                                dgs[k] = dgs[k] + gr * b
                                nr.append(rts[q] + rt * dtp[k])
                                ig = ig + gr * us[k]
                                og = og + hs[q] * ygs[k]
                                nf.append(f)
                            ia[at, :] += ig
                            oa[at, :] += og
                        for k in range(tg_s):
                            dg_s[row8(j), near[k]] = dgs[k]
                            rs_s[row8(j), near[k]] = rss[k]
                        return tuple(nf), tuple(before), tuple(nr)

                    zero = tuple(jnp.zeros((SUB, LANES), F32) for _ in range(ng_s * tg_s))
                    _, _, rts = lax.fori_loop(
                        0, J, step_j, (tuple(flow), tuple(load(J)), zero), unroll=2
                    )
                    for n in range(ng_s):
                        for k in range(tg_s):
                            rt_s[g + n : g + n + 1, near[k]] = jnp.sum(rts[n * tg_s + k], axis=0, keepdims=True)
                return carry

            lax.fori_loop(0, cb_s // (tg_s * LANES), pair, 0)
            dg = dg_s[...]
            ssg[:, C] = dg * dt[:, C] + yg[:, C] * small[SKIP : SKIP + 1, C]
            step_grad = rs_s[...] * LN2 + dg * sigf
            low = mixed[:, 0 : z.R].astype(BF16)
            dtw = small[z.DT0 : z.DT0 + z.R, C].astype(BF16)
            pre = mm(low, dtw) + small[DT_B : DT_B + 1, C]
            dpg = step_grad * sigmoid(pre)
            dpl = dpg.astype(BF16)
            gs_o[DT_B : DT_B + 1, C] = jnp.sum(dpg, axis=0, keepdims=True)
            gs_o[SKIP + 1 : SKIP + 2, C] = jnp.zeros((1, cb_s), F32)
            gs_o[A_LOG : A_LOG + N, C] = rt_s[...] * (rates2 * LN2)
            gs_o[z.DT0 : z.DT0 + z.R, C] = mm_tn(low, dpl)
            low_s[...] += mm_nt(dpl, dtw)
            if i + 2 <= E - 1:
                chain_g.hop(i + 2)
                chain_b.hop(i + 2)
        for k in range(steps_s + 2, E):
            chain_g.hop(k)
            chain_b.hop(k)

        mxg[:, 0 : z.R] = low_s[...].astype(BF16)
        lane = lax.broadcasted_iota(jnp.int32, (SUB, LANES), 1)

        def gather(j, carry):
            both = jnp.zeros((SUB, LANES), F32)
            for n in range(N):
                at = row8(j * N + n)
                both = jnp.where(lane == n, jnp.sum(ia[at, :], axis=1, keepdims=True), both)
                both = jnp.where(lane == N + n, jnp.sum(oa[at, :], axis=1, keepdims=True), both)
            cl[row8(j), :] = both
            return carry

        lax.fori_loop(0, J, gather, 0)
        mxg[:, z.R : z.R + 2 * N] = cl[:, 0 : 2 * N].astype(BF16)

        def weight_load(i):
            half = pl.ds((i % 2) * cb_s, cb_s)
            return [
                pltpu.make_async_copy(
                    w_in.at[:, h * DI + i * cb_s : h * DI + (i + 1) * cb_s], big.at[h * D : (h + 1) * D, half],
                    ld.at[12 + 2 * (i % 2) + h],
                )
                for h in range(2)
            ]

        for c in weight_load(0):
            c.start()

        def conv_block(i, carry):
            C = at_cols(i, cb_m)
            mgv = mxg[...]
            sgv = sig[:, C]
            xw = small[z.X0 : z.X0 + z.XW, C].astype(BF16)
            gs_o[z.X0 : z.X0 + z.XW, C] = mm_tn(mgv, sgv)
            sgrad = ssg[:, C] + mm(mgv, xw)
            xpad = padded_rows(conv_in[:, C], hconv[:, C], J, cb_m)
            valid = [jnp.broadcast_to(masks[:, o : o + 1], (T, cb_m)) for o in range(4)]
            out = jnp.broadcast_to(small[CONV_B : CONV_B + 1, C], (T, cb_m))
            for o in range(4):
                w = small[CONV_W + o : CONV_W + o + 1, C]
                out = out + w * xpad[o : o + J].reshape(T, cb_m) * valid[o]
            sv = sigmoid(out)
            cg = sgrad * (sv * (1.0 + out * (1.0 - sv)))
            gs_o[CONV_B : CONV_B + 1, C] = jnp.sum(cg, axis=0, keepdims=True)
            total = jnp.zeros((J, SUB, cb_m), F32)
            final = lax.broadcasted_iota(jnp.int32, (SUB, cb_m), 0) == SUB - 1
            edges = [jnp.zeros((1, cb_m), F32) for _ in range(3)]
            for o in range(4):
                masked = cg * valid[o]
                gs_o[CONV_W + o : CONV_W + o + 1, C] = jnp.sum(
                    masked * xpad[o : o + J].reshape(T, cb_m), axis=0, keepdims=True
                )
                c3 = (small[CONV_W + o : CONV_W + o + 1, C] * masked).reshape(J, SUB, cb_m)
                k = 3 - o
                if k == 0:
                    total = total + c3
                else:
                    wrap = jnp.stack(
                        [jnp.where(final, 0.0, pltpu.roll(c3[t], SUB - 1, 0)) for t in range(k)]
                    )
                    total = total + jnp.concatenate([c3[k:], wrap], axis=0)
                    for i2 in range(o, 3):
                        edges[i2] = edges[i2] + c3[i2 - o, 0:1, :]
            cig[:, C] = total.reshape(T, cb_m)
            cg_edge[:, C] = jnp.concatenate(edges + [jnp.zeros((SUB - 3, cb_m), F32)], axis=0)
            return carry

        lax.fori_loop(0, DI // cb_m, conv_block, 0)
        back_edge = remote(cg_edge, edge_in, e_s, e_r, {"seq": lax.rem(s + S - 1, S)})
        back_edge.start()
        if plane:
            up2.wait()
            down2.wait()
            uf[...] = adds(ua[yy], ub2[...])
            half_u = uq // 2
            rows_u = lambda c: pl.ds(pl.multiple_of(c * half_u, 16), half_u)
            up3 = remote(uf.at[rows_u(other)], up_o.at[core], a_s.at[5], a_r.at[5], sib)
            up3.start()
            up_own = pltpu.make_async_copy(uf.at[rows_u(core)], up_o.at[core], ld.at[16])
            up_own.start()
            down_o[...] = da[pl.ds(pl.multiple_of(xx * dq, 16), dq), :].astype(F32) + db2[...].astype(F32)
        else:
            down_o[...] = jnp.zeros_like(down_o)
        back_edge.wait()
        live = jnp.where(s < S - 1, 1.0, 0.0)

        def fix_block(i, carry):
            C = at_cols(i, cb_m)
            c3 = cig[:, C].reshape(J, SUB, cb_m)
            final = lax.broadcasted_iota(jnp.int32, (SUB, cb_m), 0) == SUB - 1
            fixed = jnp.stack(
                [
                    c3[J - 3 + k]
                    + jnp.where(final, jnp.broadcast_to(edge_in[k : k + 1, C] * live, (SUB, cb_m)), 0.0)
                    for k in range(3)
                ]
            )
            pc[:, C] = jnp.concatenate([c3[: J - 3], fixed], axis=0).reshape(T, cb_m).astype(BF16)
            return carry

        lax.fori_loop(0, DI // cb_m, fix_block, 0)
        chain_p = Chain(E, pc, pc_o, p_s, p_r, ld.at[17])
        chain_p.start()
        acc[...] = jnp.zeros_like(acc)
        for i in range(steps_s):
            for c in weight_load(i):
                c.wait()
            if i + 1 < steps_s:
                for c in weight_load(i + 1):
                    c.start()
            C = slice(i * cb_s, (i + 1) * cb_s)
            half = slice((i % 2) * cb_s, (i % 2 + 1) * cb_s)
            acc[...] += mm_nt(pc[:, C], big[0:D, half]) + mm_nt(gi[:, C], big[D : 2 * D, half])
        d, gain_g = rms_back(tok[...].astype(F32), gp[0:1, :], acc[...])
        tg_o[...] = mg[...] + d
        gg_o[0:1, :] = gain_g
        for k in range(1, E):
            chain_p.hop(k)
        for c in out_moves + gz_moves:
            c.wait()
        back_own.wait()
        gz_own.wait()
        if plane:
            up3.wait()
            up_own.wait()
        for ch_ in (chain_g, chain_b, chain_p):
            ch_.finish()

    v = pltpu.VMEM
    sem = lambda *dims: pltpu.SemaphoreType.DMA(dims)
    vm = pl.BlockSpec(memory_space=pltpu.VMEM)
    up_shape = (2, uq // 2, uc) if plane else (1, 16, LANES)
    down_shape = (dq, dc) if plane else (16, LANES)
    u_shape = (2, uq, uc) if plane else (2, 16, LANES)
    d_shape = (2 * dq, dc) if plane else (32, LANES)
    ins = (dxp, outp, dwu, dwd, states, w_out, w_in, table, choose, chances, mid, moe, cot, gpack, router, gate, y,
           sig, small, mixed, dt, masks, conv_in, hconv, s_all, tok)
    return pl.pallas_call(
        body,
        name="backward",
        in_specs=[ANY] * 7 + [vm] * (len(ins) - 7),
        out_specs=[vm] * 3 + [ANY] * 5 + [ANY, vm],
        out_shape=[
            sds((T, D), F32),
            sds((z.SMALL, DI), F32),
            sds((G, D), F32),
            sds((M, D), BF16),
            sds((E, T, DI), BF16),
            sds((E, T, DI), BF16),
            sds((E, T, D), BF16),
            sds((E, T, DZ), BF16),
            sds(up_shape, BF16),
            sds(down_shape, F32),
        ],
        scratch_shapes=[
            v((rows_big, 2 * cb_s), BF16),
            v((DI, D), BF16),
            v((M, D + LANES), BF16), v((M, D + LANES), BF16), v((M, D), BF16), v((M, D), BF16),
            v((M, D + LANES), BF16),
            v((T, DI), F32), v((T, DI), BF16), v((T, DI), BF16), v((E, T, DZ), BF16),
            v((T, D), BF16), v((T, D), F32),
            v((N, DI), BF16), v((S, N, DI), BF16), v(((N + 1) * SUB, DI), F32),
            v((T, DI), F32), v((SUB, LANES), F32), v((T, DI), F32), v((SUB, DI), F32), v((SUB, DI), F32),
            v((T, DI), BF16),
            v((J * N * SUB, LANES), F32), v((J * N * SUB, LANES), F32),
            v((J * N * SUB, LANES), F32), v((J * N * SUB, LANES), F32),
            v((T, LANES), F32), v((T, cb_s), F32), v((N, cb_s), F32), v((N, cb_s), F32),
            v((T, cb_s), F32), v((T, cb_s), F32), v((N, cb_s), F32), v((T, z.R), F32), v((T, z.XW), BF16),
            v((T, D), F32), v((N, DI), F32),
            v(u_shape, BF16), v(u_shape, BF16), v(u_shape[1:], BF16), v(u_shape[1:], BF16),
            v(d_shape, BF16), v(d_shape, BF16), v((d_shape[0] // 2, d_shape[1]), BF16),
            sem(18), sem(2), sem(2), sem(E - 1), sem(E - 1), sem(E - 1), sem(E - 1), sem(S - 1), sem(S - 1),
            pltpu.SemaphoreType.DMA, pltpu.SemaphoreType.DMA,
            sem(chain_slots), sem(chain_slots), sem(chain_slots), sem(chain_slots), sem(chain_slots), sem(chain_slots),
            sem(6), sem(6), sem(E - 1), sem(E - 1),
        ],
        compiler_params=pltpu.CompilerParams(
            collective_id=cid, has_side_effects=True, vmem_limit_bytes=60 * 1024 * 1024
        ),
    )(*ins)


def to_chunks(a, J):
    return a.reshape((SUB, J) + a.shape[1:]).swapaxes(0, 1).reshape(a.shape)


def from_chunks(a, J):
    return a.reshape((J, SUB) + a.shape[1:]).swapaxes(0, 1).reshape(a.shape)


def on_device(
    tokens, segment_ids, routes, cotangent, norm_gain, in_proj, conv_weight, conv_bias, x_proj,
    dt_proj, dt_bias, a_log, d_skip, out_proj, moe_gain, router, up_proj, down_proj,
):
    E = lax.axis_size("exp")
    S = lax.axis_size("seq")
    z = Sizes(tokens, in_proj, dt_proj, x_proj, a_log, up_proj, E)
    T, D, DI, N, J, CAP = z.T, z.D, z.DI, z.N, z.J, z.CAP
    me_s, me_e = lax.axis_index("seq"), lax.axis_index("exp")
    core = lax.rem(me_s, 2)
    where = jnp.stack([me_s, me_e, core]).astype(jnp.int32)
    seg = segment_ids[0]
    wide_rows = lambda v: jnp.pad(
        jnp.broadcast_to(v.astype(F32)[:, None], (3, LANES)), ((0, SUB - 3), (0, 0))
    )
    cw = dt_proj.shape[1]
    dw = norm_gain.shape[0]
    plane = S == 8 and dw % 32 == 0
    small_own = jnp.concatenate(
        [conv_weight, conv_bias[None], dt_bias[None], d_skip[None], jnp.zeros((1, cw), BF16), a_log, dt_proj,
         x_proj.T, jnp.zeros((-z.SMALL % 32, cw), BF16)], axis=0
    )
    g_own = jnp.concatenate(
        [norm_gain[None], moe_gain[None], router.T, jnp.zeros((32 - 2 - E, dw), BF16)], axis=0
    )
    owned = [in_proj, out_proj, small_own, g_own]
    if not plane:
        owned = [lax.all_gather(a, "exp", tiled=True) for a in owned]
    gr = 8 * -(-(2 + E) // 8)
    padded_seg = jnp.concatenate([jnp.zeros((3,), seg.dtype), seg])
    masks = jnp.stack([(padded_seg[o : o + T] == seg).astype(F32) for o in range(4)] + [seg * 0.0] * 4, axis=1)
    tok = to_chunks(tokens[0], J)
    cot = to_chunks(cotangent[0], J)
    route = to_chunks(routes[0], J)
    (
        small, gpack, router_t, table, choose_wide, masks, conv_in, hconv, gate, sig, mixed, dt, y, mid, moe, chances,
        s_all, states, w_in, w_out, arrived, cot_pair, normed_z,
    ) = forward(
        z, S, plane, tok, tokens[0, T - J :], wide_rows(seg[T - 3 :]), wide_rows(seg[:3]), cot, route,
        to_chunks(masks, J), *owned, gr, 1
    )
    normed_z = normed_z.reshape(E * T, -1)
    outp, dxp, dwu, dwd = expert(
        z, where, arrived.reshape(2 * E * CAP, D), cot_pair.reshape(2 * E * CAP, D), router_t, up_proj[0], down_proj[0]
    )
    token_grad, gsmall, ggrad, back_out, gate_all, conv_all, branch_all, gated_z, up_sum, down_part = backward(
        z, S, plane, dxp.reshape(2, E * CAP, -1), outp.reshape(2, E * CAP, D), dwu, dwd, states, w_out, w_in, table,
        choose_wide, chances, mid, moe, cot, gpack, router_t, gate, y, sig, small, mixed, dt, masks, conv_in, hconv,
        s_all, tok, 4
    )
    fb = z.FF // 8
    if plane:
        up_part = up_sum.reshape(2, D // 8, 4, fb).transpose(1, 2, 0, 3).reshape(D // 8, z.FF).astype(F32)
    else:
        up_full = jnp.zeros((D, 4, 2, fb), BF16)
        up_full = lax.dynamic_update_slice_in_dim(up_full, dwu.reshape(D, 4, 1, fb), core, axis=2)
        down_full = jnp.zeros((4, 2, fb, D), BF16)
        down_full = lax.dynamic_update_slice_in_dim(down_full, dwd.reshape(4, 1, fb, D), core, axis=1)
        up_part, down_part = [
            lax.psum_scatter(v, "seq", scatter_dimension=0, tiled=True).astype(F32)
            for v in (up_full.reshape(D, z.FF), down_full.reshape(z.FF, D))
        ]
    out_rows = contract(gated_z.reshape(E * T, -1), branch_all.reshape(E * T, D)).astype(BF16)
    gate_cols = contract(normed_z, gate_all.reshape(E * T, DI)).astype(BF16)
    conv_cols = contract(normed_z, conv_all.reshape(E * T, DI)).astype(BF16)
    gating = jnp.sum(chances * choose_wide, axis=-1, keepdims=True)
    output = (mid + gating * jnp.dot(table, back_out, preferred_element_type=F32)).astype(BF16)

    blocks = lambda a: a.reshape(a.shape[0], E, -1).swapaxes(0, 1)
    gpart = jnp.pad(blocks(ggrad), ((0, 0), (0, 0), (0, cw - dw)))
    rows = z.SMALL + gr
    pad = -rows % 128
    smalls = jnp.concatenate(
        [blocks(gsmall), gpart, jnp.zeros((E, pad, cw), F32)], axis=1
    ).astype(BF16)
    cols = jnp.concatenate([conv_cols, gate_cols], axis=1)
    if plane:
        each = cw // 8
        each_pad = 16 * -(-each // 16)
        padded = jnp.pad(out_rows.reshape(8, each, D), ((0, 0), (0, each_pad - each), (0, 0)))
        dw_in, dw_out, gsum = reduce_plane(E, cols, padded, smalls, 7)
        dw_out = dw_out[:, :each].reshape(cw, D)
    else:
        dw_in, dw_out = lax.psum(cols, "seq"), lax.psum(out_rows, "seq")
        gsum = lax.psum_scatter(lax.psum(smalls, "seq"), "exp", scatter_dimension=0, tiled=True)[0]
    gsum = gsum.astype(F32)
    return (
        from_chunks(output, J)[None],
        from_chunks(token_grad, J)[None],
        gsum[z.SMALL, :dw],
        dw_in.astype(F32),
        gsum[CONV_W : CONV_W + 4],
        gsum[CONV_B],
        gsum[z.X0 : z.SMALL].T,
        gsum[z.DT0 : z.X0],
        gsum[DT_B],
        gsum[A_LOG : A_LOG + N],
        gsum[SKIP],
        dw_out.astype(F32),
        gsum[z.SMALL + 1, :dw],
        gsum[z.SMALL + 2 : z.SMALL + 2 + E, :dw].T,
        up_part[None],
        down_part[None],
    )


def contract(a, b):
    return lax.dot_general(a, b, (((0,), (0,)), ((), ())), preferred_element_type=F32)


def solution(mesh):
    row = P("exp", "seq", None)
    in_specs = (
        row, P("exp", "seq"), row, row, P("exp"), P("exp", None), P(None, "exp"), P("exp"), P("exp", None),
        P(None, "exp"), P("exp"), P(None, "exp"), P("exp"), P("exp", None), P("exp"), P("exp", None),
        P("exp", None, None), P("exp", None, None),
    )
    out_specs = (
        row, row, P("exp"), P("exp", None), P(None, "exp"), P("exp"), P("exp", None), P(None, "exp"), P("exp"),
        P(None, "exp"), P("exp"), P("exp", None), P("exp"), P("exp", None), row, row,
    )
    return jax.shard_map(on_device, mesh=mesh, in_specs=in_specs, out_specs=out_specs, check_vma=False)
```

```python
import functools
import math

import jax
import jax.numpy as jnp
from jax import lax
from jax.experimental import pallas as pl
from jax.experimental.pallas import tpu as pltpu
from jax.sharding import PartitionSpec as P

EPSILON = 1e-05
LOG2E = math.log2(math.e)
LN2 = math.log(2.0)
CLOSED = 1e30
LANES = 128
SUB = 8
F32 = jnp.float32
BF16 = jnp.bfloat16
VMEM_LIMIT = 56 * 1024 * 1024


def mm(a, b):
    return lax.dot_general(a, b, (((1,), (0,)), ((), ())), preferred_element_type=F32)


def mm_nt(a, b):
    return lax.dot_general(a, b, (((1,), (1,)), ((), ())), preferred_element_type=F32)


def mm_tn(a, b):
    return lax.dot_general(a, b, (((0,), (0,)), ((), ())), preferred_element_type=F32)


def split_hi_lo(value):
    high = value.astype(BF16)
    return high, (value - high.astype(F32)).astype(BF16)


def sigmoid(v):
    return 1.0 / (1.0 + jnp.exp(-v))


def softplus(v):
    e = jnp.exp(-jnp.abs(v))
    small = e * (1.0 - e * (0.5 - e * (1.0 / 3.0 - e * 0.25)))
    return jnp.maximum(v, 0.0) + jnp.where(e < 0.01, small, jnp.log(1.0 + e))


def rms_scale(v):
    return lax.rsqrt(jnp.mean(v * v, axis=-1, keepdims=True) + EPSILON)


def rms_back(resid, gain, grad):
    s = rms_scale(resid)
    v = gain * grad
    out = s * v - resid * (s * s * s) * jnp.mean(resid * v, axis=-1, keepdims=True)
    return out, jnp.sum(grad * resid * s, axis=0, keepdims=True)


def block(shape, index):
    return pl.BlockSpec(shape, index)


def whole(shape):
    zeros = (0,) * len(shape)
    return pl.BlockSpec(shape, lambda *_: zeros)


def call(body, name, grid, ins, in_specs, outs, out_specs, scratch, cost=None):
    return pl.pallas_call(
        body,
        name=name,
        grid=grid,
        in_specs=in_specs,
        out_specs=out_specs,
        out_shape=outs,
        scratch_shapes=scratch,
        cost_estimate=cost,
        compiler_params=pltpu.CompilerParams(vmem_limit_bytes=VMEM_LIMIT),
    )(*ins)


def sds(shape, dtype):
    return jax.ShapeDtypeStruct(shape, dtype)


def pick(total, options):
    for o in options:
        if total % o == 0:
            return o
    return total


CONV_W, CONV_B, DT_B, SKIP, A_LOG = 0, 4, 5, 6, 8


class Sizes:
    def __init__(self, tokens, in_proj, dt_proj, x_proj, a_log, up_proj, exp_count):
        self.T = tokens.shape[1]
        self.D = tokens.shape[2]
        self.DI = in_proj.shape[1] // 2
        self.N = a_log.shape[0]
        self.R = dt_proj.shape[0]
        self.XW = x_proj.shape[1]
        self.FF = up_proj.shape[2]
        self.E = exp_count
        self.CAP = 2 * self.T // exp_count
        self.J = self.T // SUB
        self.DT0 = A_LOG + self.N
        self.X0 = self.DT0 + self.R
        self.SMALL = self.X0 + self.XW


MESH = pl.DeviceIdType.MESH
ANY = pl.BlockSpec(memory_space=pl.ANY)


def greet(peers):
    barrier = pltpu.get_barrier_semaphore()
    for peer in peers:
        pl.semaphore_signal(barrier, inc=1, device_id=peer, device_id_type=MESH)
    pl.semaphore_wait(barrier, len(peers))


def group_place(groups, g):
    main = groups // 8
    if g < 8 * main:
        return g // main, 16 * (g % main)
    return g - 8 * main, 16 * main


def chunk_rows(rows):
    groups = rows // 16
    return 16 * (groups // 8 + (1 if groups % 8 else 0))


class PlaneSum:
    def __init__(self, E, p, b, t, zb, out, add, sems):
        self.E, self.p, self.b, self.t, self.zb, self.out, self.add = E, p, b, t, zb, out, add
        self.cs, self.cr, self.qs, self.qr, self.zs, self.zr, self.gs, self.gr, self.fs, self.fr, self.own = sems
        s, self.me = lax.axis_index("seq"), lax.axis_index("exp")
        self.chip, self.core = s // 2, lax.rem(s, 2)
        self.sib = {"seq": s + 1 - 2 * self.core}
        self.chips = [self.chip + 1 - 2 * lax.rem(self.chip, 2), self.chip + 2 - 4 * (self.chip // 2), 3 - self.chip]
        self.far = [{"seq": q * 2 + self.core} for q in self.chips]
        self.zz = [lax.rem(self.me + k, E) for k in range(1, E)]

    def remote(self, src, dst, send, recv, to):
        return pltpu.make_async_remote_copy(src, dst, send, recv, device_id=to, device_id_type=MESH)

    def swap_start(self):
        self.swap = self.remote(self.p.at[:, :, 1 - self.core], self.b, self.cs, self.cr, self.sib)
        self.swap.start()

    def swap_finish(self):
        self.swap.wait()
        for l in range(self.p.shape[0]):
            self.p[l, :, self.core] = (self.p[l, :, self.core].astype(F32) + self.b[l].astype(F32)).astype(BF16)
        self.crossing = [
            self.remote(self.p.at[:, self.chips[k], self.core], self.t.at[k], self.qs.at[k], self.qr.at[k], self.far[k])
            for k in range(3)
        ]
        for c in self.crossing:
            c.start()

    def chips_finish(self):
        for c in self.crossing:
            c.wait()
        for l in range(self.p.shape[0]):
            v = self.p[l, self.chip, self.core].astype(F32)
            for k in range(3):
                v = v + self.t[k, l].astype(F32)
            self.p[l, self.chip, self.core] = v.astype(BF16)
        if self.zb is None:
            self.spread(self.p.at[:, self.chip, self.core])
            return
        self.along = [
            self.remote(self.p.at[d, self.chip, self.core], self.zb.at[self.me], self.zs.at[k], self.zr.at[k], {"exp": d})
            for k, d in enumerate(self.zz)
        ]
        for c in self.along:
            c.start()

    def z_finish(self):
        for c in self.along:
            c.wait()
        v = self.p[self.me, self.chip, self.core]
        if self.add:
            v = v.astype(F32)
            for d in self.zz:
                v = v + self.zb[d].astype(F32)
            self.zb[self.me] = v.astype(BF16)
            self.spread(self.zb.at[self.me])
        else:
            self.zb[self.me] = v
            self.spread(self.zb)

    def spread(self, ref):
        dst = self.out.at[self.chip, self.core]
        self.sends = [self.remote(ref, dst, self.gs.at[k], self.gr.at[k], self.far[k]) for k in range(3)]
        self.sends.append(self.remote(ref, dst, self.fs.at[3], self.fr.at[3], self.sib))
        for c in self.sends:
            c.start()
        self.local = pltpu.make_async_copy(ref, dst, self.own)
        self.local.start()

    def forward(self):
        for k in range(3):
            ref = self.out.at[self.chips[k], self.core]
            self.remote(ref, ref, self.gs.at[k], self.gr.at[k], self.far[k]).wait_recv()
            c = self.remote(ref, ref, self.fs.at[k], self.fr.at[k], self.sib)
            c.start()
            self.sends.append(c)

    def finish(self):
        for c in self.sends:
            c.wait_send()
        self.local.wait()
        for k in range(4):
            ref = self.out.at[self.chips[k] if k < 3 else self.chip, 1 - self.core]
            self.remote(ref, ref, self.fs.at[k], self.fr.at[k], self.sib).wait_recv()


def expand_columns(z, src, col0, dst):
    def one(j, carry):
        rows = src[pl.ds(pl.multiple_of(j * SUB, SUB), SUB), :]
        for n in range(z.N):
            at = pl.multiple_of((j * z.N + n) * SUB, SUB)
            dst[pl.ds(at, SUB), :] = jnp.broadcast_to(
                rows[:, col0 + n : col0 + n + 1], (SUB, LANES)
            )
        return carry

    lax.fori_loop(0, z.J, one, 0)


def expand_closed(z, masks, dst):
    dst[...] = jnp.broadcast_to((1.0 - masks[:, 2:3]) * CLOSED, (z.T, LANES))


def tile_groups(cb):
    return 2 if cb % (2 * LANES) == 0 else 1


def lane_at(p, tg, k):
    return pl.ds(pl.multiple_of(p * tg * LANES, LANES) + k * LANES, LANES)


def row8(j):
    return pl.ds(pl.multiple_of(j * SUB, SUB), SUB)


def shift_down(v, d):
    rows = lax.broadcasted_iota(jnp.int32, v.shape, 0)
    return jnp.where(rows >= d, pltpu.roll(v, d, 0), 0.0)


def shift_up(v, d):
    rows = lax.broadcasted_iota(jnp.int32, v.shape, 0)
    return jnp.where(rows < SUB - d, pltpu.roll(v, SUB - d, 0), 0.0)


def chain_states(count, mine, order, sums, heads, rates2):
    state = jnp.zeros_like(rates2)
    for k in range(count):
        at = order(k)
        new = jnp.exp2(rates2 * sums(at)) * state + heads(at).astype(F32)
        state = jnp.where(mine(at), new, state)
    return state


def router_softmax(logits, experts):
    lane = lax.broadcasted_iota(jnp.int32, logits.shape, 1)
    logits = jnp.where(lane < experts, logits, -1e30)
    top = jnp.max(logits, axis=-1, keepdims=True)
    e = jnp.where(lane < experts, jnp.exp(logits - top), 0.0)
    return e / jnp.sum(e, axis=-1, keepdims=True)


def expert(z, where, x, cot, router, up, down):
    D, FF, E = z.D, z.FF, z.E
    M = x.shape[0]
    fb = FF // 8
    steps = 4

    def body(wh, x_r, c_r, rt, up_r, dn_r, ret_o, rdx_o, dwu_o, dwd_o, g_s, out_s, dx_s):
        i = pl.program_id(0)

        @pl.when(i == 0)
        def _():
            ch = router_softmax(mm_nt(x_r[...], rt[...]), E)
            lane = lax.broadcasted_iota(jnp.int32, ch.shape, 1)
            gating = jnp.sum(jnp.where(lane == wh[1], ch, 0.0), axis=-1, keepdims=True)
            g_s[...] = (gating * c_r[...].astype(F32)).astype(BF16)
            out_s[...] = jnp.zeros_like(out_s)
            dx_s[...] = jnp.zeros_like(dx_s)

        xv, gv = x_r[...], g_s[...]
        upv, dnv = up_r[...], dn_r[...]
        pre = mm(xv, upv)
        cdf = 0.5 * (1.0 + lax.erf(pre * (2.0 ** -0.5)))
        hidden = (pre * cdf).astype(BF16)
        slope = cdf + pre * jnp.exp(-0.5 * pre * pre) * (1.0 / math.sqrt(2.0 * math.pi))
        out_s[...] += mm(hidden, dnv)
        pg = (mm_nt(gv, dnv) * slope).astype(BF16)
        dx_s[...] += mm_nt(pg, upv)
        dwd_o[...] = mm_tn(hidden, gv).astype(BF16)
        dwu_o[...] = mm_tn(xv, pg).astype(BF16)

        @pl.when(i == steps - 1)
        def _():
            out = out_s[...]
            ret_o[...] = out.astype(BF16)
            rdx_o[:, 0:D] = dx_s[...].astype(BF16)
            gg = jnp.sum(out * c_r[...].astype(F32), axis=-1, keepdims=True)
            hi, lo = split_hi_lo(gg)
            lane = lax.broadcasted_iota(jnp.int32, (M, LANES), 1)
            both = jnp.where(lane == 0, hi.astype(F32), jnp.where(lane == 1, lo.astype(F32), 0.0))
            rdx_o[:, D : D + LANES] = both.astype(BF16)

    whole_ = lambda shape: pl.BlockSpec(shape, lambda i, w: (0,) * len(shape))
    return pl.pallas_call(
        body,
        name="expert",
        grid_spec=pltpu.PrefetchScalarGridSpec(
            num_scalar_prefetch=1,
            grid=(steps,),
            in_specs=[
                whole_(x.shape),
                whole_(cot.shape),
                whole_(router.shape),
                pl.BlockSpec((D, fb), lambda i, w: (0, 2 * i + w[2])),
                pl.BlockSpec((fb, D), lambda i, w: (2 * i + w[2], 0)),
            ],
            out_specs=[
                whole_((M, D)),
                whole_((M, D + LANES)),
                pl.BlockSpec((D, fb), lambda i, w: (0, i)),
                pl.BlockSpec((fb, D), lambda i, w: (i, 0)),
            ],
            scratch_shapes=[pltpu.VMEM((M, D), BF16), pltpu.VMEM((M, D), F32), pltpu.VMEM((M, D), F32)],
        ),
        out_shape=[
            sds((M, D), BF16),
            sds((M, D + LANES), BF16),
            sds((D, steps * fb), BF16),
            sds((steps * fb, D), BF16),
        ],
        compiler_params=pltpu.CompilerParams(vmem_limit_bytes=VMEM_LIMIT),
    )(where, x, cot, router, up, down)


def padded_rows(main, edge, J, cb):
    H = edge.shape[0]
    m3 = main.reshape(J, SUB, cb)
    first = lax.broadcasted_iota(jnp.int32, (SUB, cb), 0) == 0
    tail = jnp.stack(
        [
            jnp.where(
                first,
                jnp.broadcast_to(edge[H - 3 + k : H - 2 + k, :], (SUB, cb)),
                pltpu.roll(m3[J - 3 + k], 1, 0),
            )
            for k in range(3)
        ]
    )
    return jnp.concatenate([tail, m3], axis=0)


def at_cols(i, cb):
    return pl.ds(pl.multiple_of(i * cb, LANES), cb)


def lanes_of(i, cb, p, tg, k):
    return pl.ds(pl.multiple_of(i * cb + p * tg * LANES, LANES) + k * LANES, LANES)


class Chain:
    def __init__(self, E, src, dst, send, recv, own):
        self.E, self.src, self.dst, self.send, self.recv, self.own = E, src, dst, send, recv, own
        self.me = lax.axis_index("exp")
        self.right, self.left = lax.rem(self.me + 1, E), lax.rem(self.me + E - 1, E)

    def slot(self, d):
        return 2 * (abs(d) - 1) + (1 if d > 0 else 0)

    def exists(self, d):
        return (self.me + d >= 0) & (self.me + d < self.E)

    def each(self, d, act):
        for to_right in (True, False):
            if (d <= 0) if to_right else (d >= 0):
                edge = self.me < self.E - 1 if to_right else self.me > 0
                there = self.slot(d - 1 if to_right else d + 1)

                @pl.when(self.exists(d) & edge)
                def _():
                    act(
                        pltpu.make_async_remote_copy(
                            self.src if d == 0 else self.dst.at[self.me + d],
                            self.dst.at[self.me + d],
                            self.send.at[there],
                            self.recv.at[there],
                            device_id={"exp": self.right if to_right else self.left},
                            device_id_type=MESH,
                        )
                    )

    def local(self):
        return pltpu.make_async_copy(self.src, self.dst.at[self.me], self.own)

    def start(self):
        self.each(0, lambda c: c.start())
        self.local().start()

    def hop(self, k):
        for d in (-k, k):
            ref = self.dst.at[self.me + d]

            @pl.when(self.exists(d))
            def _():
                pltpu.make_async_remote_copy(
                    ref, ref, self.send.at[self.slot(d)], self.recv.at[self.slot(d)],
                    device_id={"exp": self.right}, device_id_type=MESH,
                ).wait_recv()

            if k < self.E - 1:
                self.each(d, lambda c: c.start())

    def finish(self):
        for k in range(self.E - 1):
            for d in (-k, k) if k else (0,):
                self.each(d, lambda c: c.wait_send())
        self.local().wait()


class Spread:
    def __init__(self, E, src, col0, dst, cols, whole_cols, each, sems):
        self.E, self.src, self.col0, self.dst, self.cols = E, src, col0, dst, cols
        self.whole_cols, self.each_cols = whole_cols, each
        self.zs, self.zr, self.ps, self.pr, self.cs, self.cr = sems
        self.rows = src.shape[0]
        s, self.me = lax.axis_index("seq"), lax.axis_index("exp")
        self.chip, self.core = s // 2, lax.rem(s, 2)
        self.sib = {"seq": s + 1 - 2 * self.core}
        self.chips = [self.chip + 1 - 2 * lax.rem(self.chip, 2), self.chip + 2 - 4 * (self.chip // 2), 3 - self.chip]
        self.right, self.left = lax.rem(self.me + 1, E), lax.rem(self.me + E - 1, E)
        self.regions = [1, 0] if each else [0]
        self.offsets = [d for k in range(1, E) for d in (-k, k)]

    def slot(self, d):
        return 2 * (abs(d) - 1) + (1 if d > 0 else 0)

    def exists(self, d):
        return (self.me + d >= 0) & (self.me + d < self.E)

    def span(self, region, q):
        if region == 0:
            return 0, self.whole_cols
        return pl.multiple_of(self.whole_cols + q * self.each_cols, LANES), self.each_cols

    def there(self, d, region, q, core):
        half = self.rows // 2
        start, width = self.span(region, q)
        at = pl.ds(pl.multiple_of((self.me + d) * self.rows + core * half, 16), half)
        return self.dst.at[at] if width == self.cols else self.dst.at[at, pl.ds(start, width)]

    def own(self, region):
        half = self.rows // 2
        start, width = self.span(region, self.chip)
        at = pl.ds(pl.multiple_of(self.core * half, 16), half)
        if width == self.src.shape[1]:
            return self.src.at[at]
        return self.src.at[at, pl.ds(pl.multiple_of(self.col0 + start, LANES), width)]

    def local(self, sem):
        at = pl.ds(pl.multiple_of(self.me * self.rows, 16), self.rows)
        src = self.src if self.cols == self.src.shape[1] else self.src.at[:, self.col0 : self.col0 + self.cols]
        return pltpu.make_async_copy(src, self.dst.at[at], sem)

    def z_each(self, region, d, act):
        for to_right in (True, False):
            if (d <= 0) if to_right else (d >= 0):
                edge = self.me < self.E - 1 if to_right else self.me > 0
                slot = self.slot(d - 1 if to_right else d + 1)

                @pl.when(self.exists(d) & edge)
                def _():
                    act(
                        pltpu.make_async_remote_copy(
                            self.own(region) if d == 0 else self.there(d, region, self.chip, self.core),
                            self.there(d, region, self.chip, self.core),
                            self.zs.at[region, slot],
                            self.zr.at[region, slot],
                            device_id={"exp": self.right if to_right else self.left},
                            device_id_type=MESH,
                        )
                    )

    def start(self):
        for r in self.regions:
            self.z_each(r, 0, lambda c: c.start())

    def plane_copy(self, k, d):
        ref = self.there(d, 1, self.chip, self.core)
        return pltpu.make_async_remote_copy(
            ref, ref, self.ps.at[k, self.slot(d)], self.pr.at[k, self.slot(d)],
            device_id={"seq": self.chips[k] * 2 + self.core}, device_id_type=MESH,
        )

    def piece(self, which, d, core):
        if which == 0:
            return self.there(d, 0, self.chip, core)
        return self.there(d, 1, self.chip if which == 1 else self.chips[which - 2], core)

    def sib_copy(self, which, d, core):
        ref = self.piece(which, d, core)
        return pltpu.make_async_remote_copy(
            ref, ref, self.cs.at[which, self.slot(d)], self.cr.at[which, self.slot(d)],
            device_id=self.sib, device_id_type=MESH,
        )

    def hop(self, k):
        for r in self.regions:
            for d in (-k, k):
                @pl.when(self.exists(d))
                def _():
                    ref = self.there(d, r, self.chip, self.core)
                    pltpu.make_async_remote_copy(
                        ref, ref, self.zs.at[r, self.slot(d)], self.zr.at[r, self.slot(d)],
                        device_id={"exp": self.right}, device_id_type=MESH,
                    ).wait_recv()

                if k < self.E - 1:
                    self.z_each(r, d, lambda c: c.start())

                @pl.when(self.exists(d))
                def _():
                    if r == 1:
                        for j in range(3):
                            self.plane_copy(j, d).start()
                    self.sib_copy(r, d, self.core).start()

    def plane(self, k):
        if not self.each_cols:
            return
        for d in (-k, k):
            @pl.when(self.exists(d))
            def _():
                for j in range(3):
                    ref = self.there(d, 1, self.chips[j], self.core)
                    pltpu.make_async_remote_copy(
                        ref, ref, self.ps.at[j, self.slot(d)], self.pr.at[j, self.slot(d)],
                        device_id=self.sib, device_id_type=MESH,
                    ).wait_recv()
                    self.sib_copy(2 + j, d, self.core).start()

    def landed(self):
        for d in self.offsets:
            @pl.when(self.exists(d))
            def _():
                for w in range(5 if self.each_cols else 1):
                    self.sib_copy(w, d, 1 - self.core).wait_recv()

    def finish(self):
        for d in self.offsets:
            @pl.when(self.exists(d))
            def _():
                for w in range(5 if self.each_cols else 1):
                    self.sib_copy(w, d, self.core).wait_send()
                if self.each_cols:
                    for j in range(3):
                        self.plane_copy(j, d).wait_send()
        for r in self.regions:
            for k in range(self.E - 1):
                for d in (-k, k) if k else (0,):
                    self.z_each(r, d, lambda c: c.wait_send())


def small_rows(z):
    return z.SMALL + -z.SMALL % 32


def pack_small(z, par, own_sm, own_g):
    conv_w, conv_b, dt_b, skip, a_log, dt_w, x_w, gain_a, gain_b, router = par
    cw, dw = own_sm.shape[1], own_g.shape[1]
    eye = lambda r, c: (
        lax.broadcasted_iota(jnp.int32, (r, c), 0) == lax.broadcasted_iota(jnp.int32, (r, c), 1)
    ).astype(F32).astype(BF16)
    wide = lambda ref: ref[...].astype(F32)
    rows = [wide(conv_w), wide(conv_b), wide(dt_b), wide(skip), jnp.zeros((1, cw), F32), wide(a_log), wide(dt_w)]
    rows += [mm_nt(eye(z.XW, z.XW), x_w[...]), jnp.zeros((-z.SMALL % 32, cw), F32)]
    own_sm[...] = jnp.concatenate(rows, axis=0).astype(BF16)
    rows = [wide(gain_a), wide(gain_b), mm_nt(eye(16, z.E), router[...]), jnp.zeros((14, dw), F32)]
    own_g[...] = jnp.concatenate(rows, axis=0).astype(BF16)


def forward(z, S, plane, tokens, cotangent, seg, route, params, in_proj, out_proj, gr, cid):
    T, D, DI, N, J, E, CAP = z.T, z.D, z.DI, z.N, z.J, z.E, z.CAP
    H = J
    M = E * CAP
    DZ, NZ = DI // E, D // E
    rs, rg = small_rows(z), 32
    cb = pick(DI, (384, 256, 128))
    cs = pick(DI, (768, 384, 256, 128))
    tg = tile_groups(cs)
    wide = tg * LANES
    ng = 8
    steps = DI // cs
    ST = (J + 1) * N * SUB
    tiles, tiles_o = DI // LANES, D // LANES
    split = (tiles // 4 - (0 if tiles % 4 else 1)) * LANES
    split_o = max(1, tiles_o * 2 // 9) * LANES

    def body(*refs):
        tokn, cotn, seg_r, route_r = refs[:4]
        np_ = len(params)
        par = refs[4 : 4 + np_]
        (
            in_p, out_p,
            sm, gp, rt, table, choose, masks, conv_in, hconv, gate, sig, mixed, dt, y, mid, moe, ch_o, s_all, tok, cot,
            st_o, win_o, wout_o, arr_o, cot_o, nz_o,
            wc, wg, wo, smb, gb, nrm, halo, seg_in, bx, cx, cl, u_s, rates_s, hd, hdev, stot, h_all, pre_s, dwin, hin,
            st_v, acc, outb, cotb, own_sm, own_g, own_seg,
            ld, zs, zr, ps, pr, c_s, c_r, t_s, t_r, h_s, h_r, d_s, d_r, q_s, q_r, k_s, k_r, n_s, n_r, x_s, x_r,
        ) = refs[4 + np_ :]
        s, me = lax.axis_index("seq"), lax.axis_index("exp")
        core = lax.rem(s, 2)
        sib = {"seq": s + 1 - 2 * core}
        seqs = [lax.rem(s + k, S) for k in range(1, S)]
        zz = [lax.rem(me + k, E) for k in range(1, E)]
        barrier = pltpu.get_barrier_semaphore()
        peers = [{"seq": p} for p in seqs] + [{"exp": p} for p in zz]
        for peer in peers:
            pl.semaphore_signal(barrier, inc=1, device_id=peer, device_id_type=MESH)

        def remote(src, dst, send, recv, to):
            return pltpu.make_async_remote_copy(src, dst, send, recv, device_id=to, device_id_type=MESH)

        if plane:
            pack_small(z, par, own_sm, own_g)
        segrow = seg_r[...].astype(F32)
        own_seg[...] = jnp.broadcast_to(segrow, (SUB, T))
        pl.semaphore_wait(barrier, len(peers))
        sems = lambda a: (zs.at[a], zr.at[a], ps.at[a], pr.at[a], c_s.at[a], c_r.at[a])
        if plane:
            parts = [
                Spread(E, own_sm, 0, smb, DZ, DZ, 0, sems(0)),
                Spread(E, own_g, 0, gb, NZ, NZ, 0, sems(1)),
                Spread(E, in_p, 0, wc, DI, DI - 4 * split, split, sems(2)),
                Spread(E, in_p, DI, wg, DI, DI - 4 * split, split, sems(3)),
                Spread(E, out_p, 0, wo, D, D - 4 * split_o, split_o, sems(4)),
            ]
            for p in parts[:3]:
                p.start()
            loads = [p.local(ld.at[a]) for a, p in enumerate(parts)]
        else:
            loads = [
                pltpu.make_async_copy(par[0], smb, ld.at[0]),
                pltpu.make_async_copy(par[1], gb, ld.at[1]),
                pltpu.make_async_copy(in_p.at[:, 0:DI], wc, ld.at[2]),
                pltpu.make_async_copy(in_p.at[:, DI : 2 * DI], wg, ld.at[3]),
                pltpu.make_async_copy(out_p, wo, ld.at[4]),
            ]
        ahead = {"seq": lax.rem(s + 1, S)}
        edges = [
            remote(tokn.at[pl.ds(T - H, H)], halo, t_s.at[0], t_r.at[0], ahead),
            remote(own_seg, seg_in, t_s.at[1], t_r.at[1], ahead),
        ]
        for c in edges:
            c.start()
        for c in loads:
            c.start()
        queue = []
        if plane:
            wg_p, wo_p = parts[3], parts[4]
            queue = [wg_p.start] + [functools.partial(wg_p.hop, k) for k in range(1, E - 1)]
            queue += [wo_p.start, functools.partial(wg_p.hop, E - 1)]
            for k in range(1, E):
                queue += [functools.partial(wo_p.hop, k), functools.partial(wg_p.plane, k)]
            queue += [functools.partial(wo_p.plane, k) for k in range(1, E)]

        def progress(count):
            for _ in range(count):
                if queue:
                    queue.pop(0)()

        lane = lax.broadcasted_iota(jnp.int32, (T, T), 1)
        prow = lax.broadcasted_iota(jnp.int32, (T, T), 0)
        place = (prow % SUB) * J + prow // SUB
        order = (lane == place).astype(F32).astype(BF16)
        tok[...] = mm(order, tokn[...]).astype(BF16)
        cot[...] = mm(order, cotn[...]).astype(BF16)
        my_route = jnp.sum(
            jnp.where(lane == place, route_r[...].astype(F32), 0.0), axis=1, keepdims=True
        ).astype(jnp.int32)
        chosen = (lane == my_route).astype(F32)
        choose[...] = chosen
        counts = mm((lane <= prow).astype(F32).astype(BF16), chosen.astype(BF16))
        rank = jnp.sum(counts * chosen, axis=-1, keepdims=True).astype(jnp.int32) - 1
        slots = lax.broadcasted_iota(jnp.int32, (T, M), 1)
        table[...] = (slots == my_route * CAP + rank).astype(F32).astype(BF16)
        cotb[...] = mm_tn(table[...], cot[...]).astype(BF16)
        t32 = tok[...].astype(F32)
        scaled = t32 * rms_scale(t32)

        if plane:
            for k in range(1, E):
                for p in parts[:3]:
                    p.hop(k)
                if k == 1:
                    progress(1)
                elif k == 2:
                    progress(1)
                    parts[2].plane(1)
                else:
                    progress(1)
            for k in range(2, E):
                parts[2].plane(k)
            progress(1)
        block_of = lambda ref, p: ref.at[pl.ds(pl.multiple_of(p * CAP, 16), CAP)]
        cot_moves = [remote(block_of(cotb, p), cot_o.at[core, me], k_s.at[k], k_r.at[k], {"exp": p}) for k, p in enumerate(zz)]
        if plane:
            for p in parts[:3]:
                p.landed()
        for c in loads:
            c.wait()
        for e in range(E):
            sm[:, e * DZ : (e + 1) * DZ] = smb[e * rs : (e + 1) * rs, :].astype(F32)[0 : z.SMALL]
        gp[...] = jnp.zeros_like(gp)
        rt[...] = jnp.zeros_like(rt)
        for e in range(E):
            cols = slice(e * NZ, (e + 1) * NZ)
            gp[:, cols] = gb[e * rg : e * rg + 16, :].astype(F32)[0:gr]
        rt[0:16, :] = jnp.concatenate([gp[2 : 2 + E, :], jnp.zeros((16 - E, D), F32)], axis=0).astype(BF16)

        for c in edges:
            c.wait()
        live = jnp.where(s > 0, 1.0, 0.0)
        col8 = lax.broadcasted_iota(jnp.int32, (T, SUB), 1)
        prev = seg_in[0:1, :] * live

        def seg_at(k):
            own = jnp.where(lane == place - k, segrow, 0.0)
            return jnp.sum(own + jnp.where(lane == place - k + T, prev, 0.0), axis=1, keepdims=True)

        now = seg_at(0)
        same = jnp.zeros((T, SUB), F32)
        for o in range(4):
            same = jnp.where(col8 == o, (seg_at(3 - o) == now).astype(F32), same)
        masks[...] = same
        nrm[0:T, :] = (scaled * gp[0:1, :]).astype(BF16)
        h32 = halo[...].astype(F32) * live
        nrm[T : T + H, :] = (h32 * rms_scale(h32) * gp[0:1, :]).astype(BF16)
        mixed[...] = jnp.zeros_like(mixed)

        def conv_block(i, carry):
            C = at_cols(i, cb)
            both = mm(nrm[...], wc[:, C])
            main, edge = both[:T], both[T:]
            conv_in[:, C] = main
            hconv[:, C] = edge
            xpad = padded_rows(main, edge, J, cb)
            out = jnp.broadcast_to(sm[CONV_B : CONV_B + 1, C], (T, cb))
            for o in range(4):
                m = jnp.broadcast_to(masks[:, o : o + 1], (T, cb))
                out = out + sm[CONV_W + o : CONV_W + o + 1, C] * xpad[o : o + J].reshape(T, cb) * m
            sv = (out * sigmoid(out)).astype(BF16)
            sig[:, C] = sv
            mixed[...] += mm_nt(sv, sm[z.X0 : z.X0 + z.XW, C].astype(BF16))
            return carry

        lax.fori_loop(0, DI // cb, conv_block, 0)
        chain_n = Chain(E, nrm.at[0:T], nz_o, n_s, n_r, ld.at[5])
        progress(2)
        cot_own = pltpu.make_async_copy(block_of(cotb, me), cot_o.at[core, me], ld.at[6])
        cot_own.start()

        expand_columns(z, mixed, z.R, bx)
        expand_columns(z, mixed, z.R + N, cx)
        expand_closed(z, masks, cl)
        low = mixed[:, 0 : z.R].astype(BF16)

        def step_block(i, carry):
            C = at_cols(i, cs)
            pre = mm(low, sm[z.DT0 : z.DT0 + z.R, C].astype(BF16)) + sm[DT_B : DT_B + 1, C]
            step = softplus(pre)
            dt[:, C] = step
            u_s[:, C] = step * sig[:, C].astype(F32)
            rates_s[:, C] = -jnp.exp(sm[A_LOG : A_LOG + N, C]) * LOG2E
            return carry

        lax.fori_loop(0, DI // cs, step_block, 0)
        progress(2)

        def chunk_block(p, carry):
            lanes = [lane_at(p, tg, k) for k in range(tg)]
            wins = []
            for k in range(tg):
                w1 = jnp.zeros((SUB, LANES), F32)
                for j in range(J):
                    w1 = w1 + (dt[j * SUB : j * SUB + SUB, lanes[k]] + cl[j * SUB : j * SUB + SUB, :])
                w2 = w1 + shift_down(w1, 1)
                w4 = w2 + shift_down(w2, 2)
                w8 = w4 + shift_down(w4, 4)
                wins.append((w1, w2, w4))
                dwin[:, lanes[k]] = shift_down(w8, 1)
                stot[:, lanes[k]] = w8[SUB - 1 : SUB, :]
            for g in range(0, N, ng):
                rr = [
                    [jnp.broadcast_to(rates_s[g + n : g + n + 1, lanes[k]], (SUB, LANES)) for k in range(tg)]
                    for n in range(ng)
                ]

                def step_j(j, hs):
                    dts = [dt[row8(j), lanes[k]] + cl[row8(j), :] for k in range(tg)]
                    us = [u_s[row8(j), lanes[k]] for k in range(tg)]
                    new = []
                    for n in range(ng):
                        b = bx[row8(j * N + g + n), :]
                        for k in range(tg):
                            new.append(jnp.exp2(dts[k] * rr[n][k]) * hs[n * tg + k] + us[k] * b)
                    return tuple(new)

                hs = lax.fori_loop(
                    0, J, step_j, tuple(jnp.zeros((SUB, LANES), F32) for _ in range(ng * tg)), unroll=2
                )
                for n in range(ng):
                    for k in range(tg):
                        h = hs[n * tg + k]
                        w1, w2, w4 = wins[k]
                        r = rr[n][k]
                        h = h + jnp.exp2(r * w1) * shift_down(h, 1)
                        h = h + jnp.exp2(r * w2) * shift_down(h, 2)
                        h = h + jnp.exp2(r * w4) * shift_down(h, 4)
                        pre_s[(g + n) * SUB : (g + n + 1) * SUB, lanes[k]] = shift_down(h, 1)
                        hd[g + n : g + n + 1, lanes[k]] = h[SUB - 1 : SUB, :]
            return carry

        third = DI // wide // 3
        lax.fori_loop(0, third, chunk_block, 0)
        progress(2)
        lax.fori_loop(third, 2 * third, chunk_block, 0)
        progress(2)
        lax.fori_loop(2 * third, DI // wide, chunk_block, 0)
        hdev[...] = hd[...].astype(BF16)
        h_moves = [remote(hdev, h_all.at[s], h_s.at[0, k], h_r.at[0, k], {"seq": p}) for k, p in enumerate(seqs)]
        h_moves += [remote(stot, s_all.at[s], h_s.at[1, k], h_r.at[1, k], {"seq": p}) for k, p in enumerate(seqs)]
        for c in h_moves:
            c.start()
        h_all[s] = hdev[...]
        s_all[s] = stot[...]
        for c in cot_moves:
            c.start()
        chain_n.start()
        progress(len(queue))
        if plane:
            parts[3].landed()

        def gate_block(i, carry):
            C = at_cols(i, cb)
            gate[:, C] = mm(nrm[0:T, :], wg[:, C])
            return carry

        lax.fori_loop(0, DI // cb, gate_block, 0)
        if plane:
            parts[4].landed()
        outs = [
            pltpu.make_async_copy(wc, win_o.at[:, 0:DI], ld.at[7]),
            pltpu.make_async_copy(wg, win_o.at[:, DI : 2 * DI], ld.at[8]),
            pltpu.make_async_copy(wo, wout_o, ld.at[9]),
        ]
        for c in outs:
            c.start()
        for c in h_moves:
            c.wait()
        acc[...] = jnp.zeros_like(acc)

        def save(i):
            return pltpu.make_async_copy(
                st_v.at[i % 2], st_o.at[:, i * cs : (i + 1) * cs], ld.at[10 + i % 2]
            )

        for i in range(steps):
            if i >= 2:
                save(i - 2).wait()
            C = slice(i * cs, (i + 1) * cs)
            hin[...] = chain_states(
                S - 1, lambda k: k < s, lambda k: k, lambda k: s_all[k, :, C], lambda k: h_all[k, :, C],
                rates_s[:, C],
            )

            def pair(p, carry):
                lanes = [lanes_of(i, cs, p, tg, k) for k in range(tg)]
                near = [lane_at(p, tg, k) for k in range(tg)]
                for g in range(0, N, ng):
                    rr = [
                        [jnp.broadcast_to(rates_s[g + n : g + n + 1, lanes[k]], (SUB, LANES)) for k in range(tg)]
                        for n in range(ng)
                    ]
                    init = []
                    for n in range(ng):
                        for k in range(tg):
                            at = (g + n) * SUB
                            init.append(
                                pre_s[at : at + SUB, lanes[k]]
                                + jnp.exp2(rr[n][k] * dwin[:, lanes[k]])
                                * jnp.broadcast_to(hin[g + n : g + n + 1, near[k]], (SUB, LANES))
                            )

                    def keep(j, hs):
                        for n in range(0, ng, 2):
                            for k in range(tg):
                                two = jnp.concatenate([hs[n * tg + k], hs[(n + 1) * tg + k]], axis=0)
                                at = pl.multiple_of(j * N * SUB + (g + n) * SUB, 2 * SUB)
                                st_v[i % 2, pl.ds(at, 2 * SUB), near[k]] = two.astype(BF16)

                    keep(0, init)

                    def step_j(j, hs):
                        dts = [dt[row8(j), lanes[k]] + cl[row8(j), :] for k in range(tg)]
                        us = [u_s[row8(j), lanes[k]] for k in range(tg)]
                        if g == 0:
                            ys = [jnp.zeros((SUB, LANES), F32) for k in range(tg)]
                        else:
                            ys = [y[row8(j), lanes[k]] for k in range(tg)]
                        new = []
                        for n in range(ng):
                            b = bx[row8(j * N + g + n), :]
                            c = cx[row8(j * N + g + n), :]
                            for k in range(tg):
                                h = jnp.exp2(dts[k] * rr[n][k]) * hs[n * tg + k] + us[k] * b
                                ys[k] = ys[k] + h * c
                                new.append(h)
                        for k in range(tg):
                            y[row8(j), lanes[k]] = ys[k]
                        keep(j + 1, new)
                        return tuple(new)

                    lax.fori_loop(0, J, step_j, tuple(init), unroll=2)
                return carry

            lax.fori_loop(0, cs // wide, pair, 0)
            save(i).start()
            if i + 1 < E:
                chain_n.hop(i + 1)
            yv = y[:, C] + sm[SKIP : SKIP + 1, C] * sig[:, C].astype(F32)
            y[:, C] = yv
            g_in = gate[:, C]
            gated = (yv * (g_in * sigmoid(g_in))).astype(BF16)
            acc[...] += mm(gated, wo[C, :])

        for k in range(steps + 1, E):
            chain_n.hop(k)
        m32 = tok[...].astype(F32) + acc[...]
        mid[...] = m32
        moe[...] = (m32 * rms_scale(m32) * gp[1:2, :]).astype(BF16)
        ch_o[...] = router_softmax(mm_nt(moe[...], rt[...]), E)
        outb[...] = mm_tn(table[...], moe[...]).astype(BF16)
        out_moves = [remote(block_of(outb, p), arr_o.at[core, me], d_s.at[k], d_r.at[k], {"exp": p}) for k, p in enumerate(zz)]
        for c in out_moves:
            c.start()
        arr_own = pltpu.make_async_copy(block_of(outb, me), arr_o.at[core, me], ld.at[12])
        arr_own.start()
        passes = [
            remote(block_of(cotb, me), cot_o.at[core, me], x_s.at[0, 0], x_r.at[0, 0], sib),
            remote(block_of(outb, me), arr_o.at[core, me], x_s.at[1, 0], x_r.at[1, 0], sib),
        ]
        for c in passes:
            c.start()
        for w, ref, send, recv in ((0, cot_o, k_s, k_r), (1, arr_o, d_s, d_r)):
            for k in range(1, E):
                frm = lax.rem(me + E - k, E)
                at = ref.at[core, frm]
                remote(at, at, send.at[k - 1], recv.at[k - 1], {"exp": frm}).wait_recv()
                c = remote(at, at, x_s.at[w, k], x_r.at[w, k], sib)
                c.start()
                passes.append(c)
        if plane:
            for p in parts:
                p.finish()
        for c in outs + [cot_own, arr_own]:
            c.wait()
        chain_n.finish()
        for i in range(max(0, steps - 2), steps):
            save(i).wait()
        for c in cot_moves + out_moves + passes:
            c.wait_send()
        for w, ref in ((0, cot_o), (1, arr_o)):
            for k in range(E):
                at = ref.at[1 - core, lax.rem(me + E - k, E)]
                remote(at, at, x_s.at[w, k], x_r.at[w, k], sib).wait_recv()

    v = pltpu.VMEM
    sem = lambda *dims: pltpu.SemaphoreType.DMA(dims)
    vm = pl.BlockSpec(memory_space=pltpu.VMEM)
    zslots = 2 * (E - 1)
    ins = (tokens, cotangent, seg, route) + tuple(params) + (in_proj, out_proj)
    vm_outs = [
        sds((z.SMALL, DI), F32), sds((gr, D), F32), sds((LANES, D), BF16), sds((T, M), BF16), sds((T, LANES), F32),
        sds((T, SUB), F32), sds((T, DI), F32), sds((H, DI), F32), sds((T, DI), F32), sds((T, DI), BF16),
        sds((T, z.XW), F32), sds((T, DI), F32), sds((T, DI), F32), sds((T, D), F32), sds((T, D), BF16),
        sds((T, LANES), F32), sds((S, 1, DI), F32), sds((T, D), BF16), sds((T, D), BF16),
    ]
    any_outs = [
        sds((ST, DI), BF16), sds((D, 2 * DI), BF16), sds((DI, D), BF16), sds((2, E, CAP, D), BF16),
        sds((2, E, CAP, D), BF16), sds((E, T, D), BF16),
    ]
    return pl.pallas_call(
        body,
        name="forward",
        in_specs=[vm] * 4 + [vm if plane else ANY] * len(params) + [ANY] * 2,
        out_specs=[vm] * len(vm_outs) + [ANY] * len(any_outs),
        out_shape=vm_outs + any_outs,
        scratch_shapes=[
            v((D, DI), BF16), v((D, DI), BF16), v((DI, D), BF16), v((E * rs, DZ), BF16), v((E * rg, NZ), BF16),
            v((T + H, D), BF16), v((H, D), BF16), v((SUB, LANES), F32),
            v((J * N * SUB, LANES), F32), v((J * N * SUB, LANES), F32), v((T, LANES), F32), v((T, DI), F32),
            v((N, DI), F32), v((N, DI), F32), v((N, DI), BF16), v((1, DI), F32), v((S, N, DI), BF16),
            v((N * SUB, DI), F32), v((SUB, DI), F32), v((N, cs), F32),
            v((2, ST, cs), BF16), v((T, D), F32), v((M, D), BF16), v((M, D), BF16),
            v((rs, DZ), BF16), v((rg, NZ), BF16), v((SUB, T), F32),
            sem(13), sem(5, 2, zslots), sem(5, 2, zslots), sem(5, 3, zslots), sem(5, 3, zslots),
            sem(5, 5, zslots), sem(5, 5, zslots), sem(2), sem(2), sem(2, S - 1), sem(2, S - 1),
            sem(E - 1), sem(E - 1), sem(1), sem(1), sem(E - 1), sem(E - 1), sem(zslots), sem(zslots),
            sem(2, E), sem(2, E),
        ],
        compiler_params=pltpu.CompilerParams(
            collective_id=cid, has_side_effects=True, vmem_limit_bytes=60 * 1024 * 1024
        ),
    )(*ins)


def backward(z, S, plane, dxp, outp, dwu, dwd, states, w_out, w_in, table, choose, chances, mid, moe, cot, gpack,
             router, gate, y, sig, small, mixed, dt, masks, conv_in, hconv, s_all, tok, normed_all, cid):
    T, D, DI, N, J, E, CAP = z.T, z.D, z.DI, z.N, z.J, z.E, z.CAP
    M = E * CAP
    G = gpack.shape[0]
    H = hconv.shape[0]
    DZ, NZ = DI // E, D // E
    cb_m = pick(DI, (384, 256, 128))
    cb_s = pick(DI, (256, 128))
    steps_s = DI // cb_s
    tg_s = tile_groups(cb_s)
    ng_s = 4
    uq, uc = dwu.shape[0] // 4, dwu.shape[1]
    dq, dc = dwd.shape[0] // 4, dwd.shape[1]
    ST = (J + 1) * N * SUB
    rows_big = max(ST, 2 * D)
    chain_slots = 2 * (E - 1)

    def body(
        dxp, outp, dwu, dwd, states, w_out, w_in, table, choose, chances, mid, moe, cot, gp, router, gate, y, sig,
        small, mixed, dt, masks, conv_in, hconv, s_all, tok, nall,
        tg_o, gs_o, gg_o, back_o, pg_o, pc_o, pm_o, po_o, up_o, down_o,
        big, wo_v, n_v, dx_a, dx_b, out_a, out_b, dx_z, yg, gi, gz, br, mg, fdev, f_all, suf, cg_edge,
        edge_in, pc, bx, cx, ia, oa, cl, u_s, rates_s, fin, dg_s, rs_s, rt_s, low_s, mxg, fd,
        ua, ub, ub2, da, db, db2, gi_all, pc_all, br_all, gz_all, gi_b,
        p_g, p_c, p_m, p_o, bg, bc, bm, bo, tg_, tc_, tm_, to_, zg, zc, zm,
        pcs, pcr, pqs, pqr, pzs, pzr, pgs, pgr, pfs, pfr, pown,
        ld, sw_s, sw_r, dz_s, dz_r, oz_s, oz_r, f_s, f_r, e_s, e_r, g_s, g_r, p_s, p_r, b_s, b_r, a_s, a_r, x_s, x_r,
    ):
        psems = lambda a: (
            pcs.at[a], pcr.at[a], pqs.at[a], pqr.at[a], pzs.at[a], pzr.at[a], pgs.at[a], pgr.at[a], pfs.at[a],
            pfr.at[a], pown.at[a],
        )
        sum_g = PlaneSum(E, p_g, bg, tg_, zg, pg_o, False, psems(0))
        sum_c = PlaneSum(E, p_c, bc, tc_, zc, pc_o, False, psems(1))
        sum_m = PlaneSum(E, p_m, bm, tm_, zm, pm_o, True, psems(2))
        sum_o = PlaneSum(E, p_o, bo, to_, None, po_o, False, psems(3))
        stage = (lambda f: f()) if plane else (lambda f: None)
        s, me = lax.axis_index("seq"), lax.axis_index("exp")
        core = lax.rem(s, 2)
        other = 1 - core
        sib = {"seq": s + 1 - 2 * core}
        seqs = [lax.rem(s + k, S) for k in range(1, S)]
        zs = [lax.rem(me + k, E) for k in range(1, E)]
        greet([{"seq": p} for p in seqs] + [{"exp": p} for p in zs])

        def remote(src, dst, send, recv, to):
            return pltpu.make_async_remote_copy(src, dst, send, recv, device_id=to, device_id_type=MESH)

        swaps = [
            remote(dxp.at[other], dx_b, sw_s.at[0], sw_r.at[0], sib),
            remote(outp.at[other], out_b, sw_s.at[1], sw_r.at[1], sib),
        ]
        for c in swaps:
            c.start()
        loads = [
            pltpu.make_async_copy(dxp.at[core], dx_a, ld.at[0]),
            pltpu.make_async_copy(outp.at[core], out_a, ld.at[1]),
        ]
        for c in loads:
            c.start()

        def out_load(i):
            slot = lax.rem(i, 2)
            rows = pl.ds(pl.multiple_of(i * cb_m, LANES), cb_m)
            return pltpu.make_async_copy(w_out.at[rows], wo_v.at[slot], ld.at[2 + 15 * slot])

        out_load(0).start()
        normed_load = pltpu.make_async_copy(nall, n_v, ld.at[10])
        normed_load.start()

        def state_load(i):
            return pltpu.make_async_copy(
                states.at[:, at_cols(i, cb_s)], big.at[lax.rem(i, 2), 0:ST], ld.at[3 + lax.rem(i, 2)]
            )

        state_load(0).start()
        if plane:
            chip = s // 2
            xx, yy = lax.rem(chip, 2), chip // 2
            to_x = {"seq": s + 2 - 4 * xx}
            to_y = {"seq": s + 4 - 8 * yy}
            u4 = lambda ref, v, w: ref.at[pl.ds(pl.multiple_of((2 * v + w) * uq, 16), uq)]
            up1 = [
                remote(u4(dwu, v, 1 - xx), ub.at[v], a_s.at[v], a_r.at[v], to_x) for v in range(2)
            ]
            d_half = lambda v: pl.ds(pl.multiple_of(v * 2 * dq, 16), 2 * dq)
            down1 = remote(dwd.at[d_half(1 - yy)], db, a_s.at[2], a_r.at[2], to_y)
            for c in up1 + [down1]:
                c.start()
            mine = [pltpu.make_async_copy(u4(dwu, v, xx), ua.at[v], ld.at[5 + v]) for v in range(2)]
            mine.append(pltpu.make_async_copy(dwd.at[d_half(yy)], da, ld.at[7]))
            for c in mine:
                c.start()

        adds = lambda a, b: (a.astype(F32) + b.astype(F32)).astype(BF16)
        loads[0].wait()
        swaps[0].wait()
        dx_a[...] = adds(dx_a[...], dx_b[...])
        block_of = lambda ref, p: ref.at[pl.ds(pl.multiple_of(p * CAP, 16), CAP)]
        dx_moves = [
            remote(block_of(dx_a, p), block_of(dx_z, me), dz_s.at[k], dz_r.at[k], {"exp": p})
            for k, p in enumerate(zs)
        ]
        for c in dx_moves:
            c.start()
        here = pl.ds(pl.multiple_of(me * CAP, 16), CAP)
        dx_z[here, :] = dx_a[here, :]
        loads[1].wait()
        swaps[1].wait()
        out_a[...] = adds(out_a[...], out_b[...])
        out_moves = [
            remote(block_of(out_a, p), block_of(back_o, me), oz_s.at[k], oz_r.at[k], {"exp": p})
            for k, p in enumerate(zs)
        ]
        for c in out_moves:
            c.start()
        back_own = pltpu.make_async_copy(block_of(out_a, me), block_of(back_o, me), ld.at[8])
        back_own.start()
        expand_columns(z, mixed, z.R, bx)
        expand_columns(z, mixed, z.R + N, cx)
        expand_closed(z, masks, cl)
        for c in dx_moves:
            c.wait()

        back = mm(table[...], dx_z[...])
        grad = cot[...].astype(F32)
        ch = chances[...]
        pick_e = choose[...]
        gating = jnp.sum(ch * pick_e, axis=-1, keepdims=True)
        gate_grad = back[:, D : D + 1] + back[:, D + 1 : D + 2]
        lg = ch * (gate_grad * pick_e - gate_grad * gating)
        hi, lo = split_hi_lo(lg)
        rtv = router[...]
        mig = back[:, 0:D] + mm(hi, rtv) + mm(lo, rtv)
        mev = moe[...]
        rg = mm_tn(hi, mev) + mm_tn(lo, mev)
        d, gain_g = rms_back(mid[...], gp[1:2, :], mig)
        mg[...] = grad + d
        br[...] = mg[...].astype(BF16)
        gg_o[...] = jnp.zeros_like(gg_o)
        gg_o[1:2, :] = gain_g
        gg_o[2 : 2 + E, :] = rg[0:E, :]
        chain_b = Chain(E, br, br_all, b_s, b_r, ld.at[9])

        def middle_block(i, carry):
            C = at_cols(i, cb_m)
            out_load(i).wait()

            @pl.when(i + 1 < DI // cb_m)
            def _():
                out_load(i + 1).start()

            gg = mm_nt(br[...], wo_v[lax.rem(i, 2)])
            g_in = gate[:, C]
            sg = sigmoid(g_in)
            act = g_in * sg
            yv = y[:, C]
            ygv = gg * act
            yg[:, C] = ygv
            gi[:, C] = (gg * yv * (sg * (1.0 + g_in * (1.0 - sg)))).astype(BF16)
            pc[:, C] = (yv * act).astype(BF16)
            gs_o[SKIP : SKIP + 1, C] = jnp.sum(ygv * sig[:, C].astype(F32), axis=0, keepdims=True)
            return carry

        lax.fori_loop(0, DI // cb_m, middle_block, 0)
        for e in range(E):
            gi_b[e] = gi[:, e * DZ : (e + 1) * DZ]

        def trade(src, dst, send, recv):
            return [remote(src.at[p], dst.at[me], send.at[k], recv.at[k], {"exp": p}) for k, p in enumerate(zs)]

        gi_moves = trade(gi_b, gi_all, g_s, g_r)
        for c in gi_moves:
            c.start()
        gi_all[me] = gi_b[me]
        chain_b.start()

        tg, ng = 2 if DI % 256 == 0 else 1, 8
        wide = tg * LANES

        def flow_block(i, carry):
            lanes = [pl.ds(pl.multiple_of(i * wide, LANES) + k * LANES, LANES) for k in range(tg)]
            both = pl.ds(pl.multiple_of(i * wide, LANES), wide)
            rates = -jnp.exp(small[A_LOG : A_LOG + N, both]) * LOG2E
            wins = []
            for k in range(tg):
                w1 = jnp.zeros((SUB, LANES), F32)
                for j in range(J):
                    w1 = w1 + (dt[j * SUB : j * SUB + SUB, lanes[k]] + cl[j * SUB : j * SUB + SUB, :])
                w2 = w1 + shift_up(w1, 1)
                w4 = w2 + shift_up(w2, 2)
                w8 = w4 + shift_up(w4, 4)
                wins.append((w1, w2, w4))
                suf[N * SUB : (N + 1) * SUB, lanes[k]] = shift_up(w8, 1)
            for g in range(0, N, ng):
                rr = [
                    [
                        jnp.broadcast_to(rates[g + n : g + n + 1, k * LANES : (k + 1) * LANES], (SUB, LANES))
                        for k in range(tg)
                    ]
                    for n in range(ng)
                ]

                def step_j(jj, fs):
                    j = J - 1 - jj
                    dts = [dt[row8(j), lanes[k]] + cl[row8(j), :] for k in range(tg)]
                    ygs = [yg[row8(j), lanes[k]] for k in range(tg)]
                    new = []
                    for n in range(ng):
                        c = cx[row8(j * N + g + n), :]
                        for k in range(tg):
                            new.append(jnp.exp2(dts[k] * rr[n][k]) * (fs[n * tg + k] + ygs[k] * c))
                    return tuple(new)

                fs = lax.fori_loop(
                    0, J, step_j, tuple(jnp.zeros((SUB, LANES), F32) for _ in range(ng * tg)), unroll=2
                )
                for n in range(ng):
                    for k in range(tg):
                        f = fs[n * tg + k]
                        w1, w2, w4 = wins[k]
                        r = rr[n][k]
                        f = f + jnp.exp2(r * w1) * shift_up(f, 1)
                        f = f + jnp.exp2(r * w2) * shift_up(f, 2)
                        f = f + jnp.exp2(r * w4) * shift_up(f, 4)
                        suf[(g + n) * SUB : (g + n + 1) * SUB, lanes[k]] = shift_up(f, 1)
                        fd[g + n : g + n + 1, lanes[k]] = f[0:1, :]
            return carry

        lax.fori_loop(0, DI // wide, flow_block, 0)
        fdev[...] = fd[...].astype(BF16)
        f_moves = [
            remote(fdev, f_all.at[s], f_s.at[k], f_r.at[k], {"seq": p}) for k, p in enumerate(seqs)
        ]
        for c in f_moves:
            c.start()
        f_all[s] = fdev[...]
        for e in range(E):
            gz[e] = pc[:, e * DZ : (e + 1) * DZ]
        gz_moves = trade(gz, gz_all, x_s, x_r)
        for c in gz_moves:
            c.start()
        gz_all[me] = gz[me]
        p_g[...] = jnp.zeros_like(p_g)
        p_c[...] = jnp.zeros_like(p_c)
        p_o[...] = jnp.zeros_like(p_o)

        def place_in(dst, rhs):
            blk = pick(D, (384, 256, 128))
            for i in range(D // blk):
                val = mm_tn(n_v[:, i * blk : (i + 1) * blk], rhs)
                for g in range(blk // 16):
                    row = i * blk + 16 * g
                    chunk, off = group_place(D // E // 16, row % (D // E) // 16)
                    dst[row // (D // E), chunk // 2, chunk % 2, off : off + 16, :] = val[16 * g : 16 * g + 16].astype(
                        BF16
                    )

        flat = lambda ref: ref[...].reshape(E * T, ref.shape[-1])
        if plane:
            for c in mine + up1 + [down1]:
                c.wait()
            ua[...] = adds(ua[...], ub[...])
            da[...] = adds(da[...], db[...])
            up2 = remote(ua.at[1 - yy], ub2, a_s.at[3], a_r.at[3], to_y)
            down2 = remote(
                da.at[pl.ds(pl.multiple_of((1 - xx) * dq, 16), dq)], db2, a_s.at[4], a_r.at[4], to_x
            )
            up2.start()
            down2.start()
        for c in f_moves:
            c.wait()

        ia[...] = jnp.zeros_like(ia)
        oa[...] = jnp.zeros_like(oa)
        low_s[...] = jnp.zeros_like(low_s)
        low = mixed[:, 0 : z.R].astype(BF16)

        def scan_block(i, carry_):
            state_load(i).wait()

            @pl.when(i + 1 < steps_s)
            def _():
                state_load(i + 1).start()

            slot = lax.rem(i, 2)
            C = at_cols(i, cb_s)
            rates2 = -jnp.exp(small[A_LOG : A_LOG + N, C]) * LOG2E
            rates_s[...] = rates2
            fin[...] = chain_states(
                S - 1, lambda k: k > s, lambda k: S - 1 - k, lambda k: s_all[k, :, C], lambda k: f_all[k, :, C],
                rates2,
            )
            sigf = sig[:, C].astype(F32)
            u_s[...] = dt[:, C] * sigf

            def pair(p, carry):
                lanes = [lanes_of(i, cb_s, p, tg_s, k) for k in range(tg_s)]
                near = [slice(k * LANES, (k + 1) * LANES) for k in range(tg_s)]
                for g in range(0, N, ng_s):
                    rr = [
                        [
                            jnp.broadcast_to(rates_s[g + n : g + n + 1, near[k]], (SUB, LANES))
                            for k in range(tg_s)
                        ]
                        for n in range(ng_s)
                    ]
                    flow = []
                    for n in range(ng_s):
                        for k in range(tg_s):
                            at = (g + n) * SUB
                            flow.append(
                                suf[at : at + SUB, lanes[k]]
                                + jnp.exp2(rr[n][k] * suf[N * SUB : (N + 1) * SUB, lanes[k]])
                                * jnp.broadcast_to(fin[g + n : g + n + 1, near[k]], (SUB, LANES))
                            )

                    def load(j):
                        got = [[None] * tg_s for _ in range(ng_s)]
                        for n in range(0, ng_s, 2):
                            for k in range(tg_s):
                                at = pl.multiple_of(j * N * SUB + (g + n) * SUB, 2 * SUB)
                                two = big[slot, pl.ds(at, 2 * SUB), near[k]].astype(F32)
                                got[n][k] = two[0:SUB]
                                got[n + 1][k] = two[SUB : 2 * SUB]
                        return [got[n][k] for n in range(ng_s) for k in range(tg_s)]

                    def step_j(jj, carry):
                        fs, hs, rts = carry
                        j = J - 1 - jj
                        dtp = [dt[row8(j), lanes[k]] for k in range(tg_s)]
                        dts = [dtp[k] + cl[row8(j), :] for k in range(tg_s)]
                        us = [u_s[row8(j), near[k]] for k in range(tg_s)]
                        ygs = [yg[row8(j), lanes[k]] for k in range(tg_s)]
                        before = load(j)
                        if g == 0:
                            dgs = [jnp.zeros((SUB, LANES), F32) for k in range(tg_s)]
                            rss = [jnp.zeros((SUB, LANES), F32) for k in range(tg_s)]
                        else:
                            dgs = [dg_s[row8(j), near[k]] for k in range(tg_s)]
                            rss = [rs_s[row8(j), near[k]] for k in range(tg_s)]
                        nf, nr = [], []
                        for n in range(ng_s):
                            at = row8(j * N + g + n)
                            b = bx[at, :]
                            c = cx[at, :]
                            ig = jnp.zeros((SUB, LANES), F32)
                            og = jnp.zeros((SUB, LANES), F32)
                            for k in range(tg_s):
                                q = n * tg_s + k
                                gr = ygs[k] * c + fs[q]
                                f = jnp.exp2(dts[k] * rr[n][k]) * gr
                                rt = f * before[q]
                                rss[k] = rss[k] + rt * rr[n][k]
                                dgs[k] = dgs[k] + gr * b
                                nr.append(rts[q] + rt * dtp[k])
                                ig = ig + gr * us[k]
                                og = og + hs[q] * ygs[k]
                                nf.append(f)
                            ia[at, :] += ig
                            oa[at, :] += og
                        for k in range(tg_s):
                            dg_s[row8(j), near[k]] = dgs[k]
                            rs_s[row8(j), near[k]] = rss[k]
                        return tuple(nf), tuple(before), tuple(nr)

                    zero = tuple(jnp.zeros((SUB, LANES), F32) for _ in range(ng_s * tg_s))
                    _, _, rts = lax.fori_loop(
                        0, J, step_j, (tuple(flow), tuple(load(J)), zero), unroll=2
                    )
                    for n in range(ng_s):
                        for k in range(tg_s):
                            rt_s[g + n : g + n + 1, near[k]] = jnp.sum(rts[n * tg_s + k], axis=0, keepdims=True)
                return carry

            pair(0, 0)
            dg = dg_s[...]
            yg[:, C] = dg * dt[:, C] + yg[:, C] * small[SKIP : SKIP + 1, C]
            step_grad = rs_s[...] * LN2 + dg * sigf
            dtw = small[z.DT0 : z.DT0 + z.R, C].astype(BF16)
            pre = mm(low, dtw) + small[DT_B : DT_B + 1, C]
            dpg = step_grad * sigmoid(pre)
            dpl = dpg.astype(BF16)
            gs_o[DT_B : DT_B + 1, C] = jnp.sum(dpg, axis=0, keepdims=True)
            gs_o[SKIP + 1 : SKIP + 2, C] = jnp.zeros((1, cb_s), F32)
            gs_o[A_LOG : A_LOG + N, C] = rt_s[...] * (rates2 * LN2)
            gs_o[z.DT0 : z.DT0 + z.R, C] = mm_tn(low, dpl)
            low_s[...] += mm_nt(dpl, dtw)
            return carry_

        third = steps_s // 3
        lax.fori_loop(0, third, scan_block, 0)
        chain_b.hop(1)
        for c in gi_moves:
            c.wait()
        normed_load.wait()
        place_in(p_g, flat(gi_all))
        stage(sum_g.swap_start)
        lax.fori_loop(third, 2 * third, scan_block, 0)
        stage(sum_g.swap_finish)
        chain_b.hop(2)
        lax.fori_loop(2 * third, steps_s, scan_block, 0)
        for k in range(3, E):
            chain_b.hop(k)
        stage(sum_g.chips_finish)

        mxg[:, 0 : z.R] = low_s[...].astype(BF16)
        lane = lax.broadcasted_iota(jnp.int32, (SUB, LANES), 1)

        def gather(j, carry):
            both = jnp.zeros((SUB, LANES), F32)
            for n in range(N):
                at = row8(j * N + n)
                both = jnp.where(lane == n, jnp.sum(ia[at, :], axis=1, keepdims=True), both)
                both = jnp.where(lane == N + n, jnp.sum(oa[at, :], axis=1, keepdims=True), both)
            cl[row8(j), :] = both
            return carry

        lax.fori_loop(0, J, gather, 0)
        mxg[:, z.R : z.R + 2 * N] = cl[:, 0 : 2 * N].astype(BF16)

        def weight_load(i):
            return [
                pltpu.make_async_copy(
                    w_in.at[:, pl.ds(pl.multiple_of(h * DI + i * cb_s, LANES), cb_s)],
                    big.at[lax.rem(i, 2), h * D : (h + 1) * D],
                    ld.at[12 + 2 * lax.rem(i, 2) + h],
                )
                for h in range(2)
            ]

        for c in weight_load(0):
            c.start()

        def conv_block(i, carry):
            C = at_cols(i, cb_m)
            mgv = mxg[...]
            sgv = sig[:, C]
            xw = small[z.X0 : z.X0 + z.XW, C].astype(BF16)
            gs_o[z.X0 : z.X0 + z.XW, C] = mm_tn(mgv, sgv)
            sgrad = yg[:, C] + mm(mgv, xw)
            xpad = padded_rows(conv_in[:, C], hconv[:, C], J, cb_m)
            valid = [jnp.broadcast_to(masks[:, o : o + 1], (T, cb_m)) for o in range(4)]
            out = jnp.broadcast_to(small[CONV_B : CONV_B + 1, C], (T, cb_m))
            for o in range(4):
                w = small[CONV_W + o : CONV_W + o + 1, C]
                out = out + w * xpad[o : o + J].reshape(T, cb_m) * valid[o]
            sv = sigmoid(out)
            cg = sgrad * (sv * (1.0 + out * (1.0 - sv)))
            gs_o[CONV_B : CONV_B + 1, C] = jnp.sum(cg, axis=0, keepdims=True)
            total = jnp.zeros((J, SUB, cb_m), F32)
            final = lax.broadcasted_iota(jnp.int32, (SUB, cb_m), 0) == SUB - 1
            edges = [jnp.zeros((1, cb_m), F32) for _ in range(3)]
            for o in range(4):
                masked = cg * valid[o]
                gs_o[CONV_W + o : CONV_W + o + 1, C] = jnp.sum(
                    masked * xpad[o : o + J].reshape(T, cb_m), axis=0, keepdims=True
                )
                c3 = (small[CONV_W + o : CONV_W + o + 1, C] * masked).reshape(J, SUB, cb_m)
                k = 3 - o
                if k == 0:
                    total = total + c3
                else:
                    wrap = jnp.stack(
                        [jnp.where(final, 0.0, pltpu.roll(c3[t], SUB - 1, 0)) for t in range(k)]
                    )
                    total = total + jnp.concatenate([c3[k:], wrap], axis=0)
                    for i2 in range(o, 3):
                        edges[i2] = edges[i2] + c3[i2 - o, 0:1, :]
            yg[:, C] = total.reshape(T, cb_m)
            cg_edge[:, C] = jnp.concatenate(edges + [jnp.zeros((SUB - 3, cb_m), F32)], axis=0)
            return carry

        lax.fori_loop(0, DI // cb_m, conv_block, 0)
        back_edge = remote(cg_edge, edge_in, e_s, e_r, {"seq": lax.rem(s + S - 1, S)})
        back_edge.start()
        if plane:
            up2.wait()
            down2.wait()
            ub2[...] = adds(ua[yy], ub2[...])
            half_u = uq // 2
            rows_u = lambda c: pl.ds(pl.multiple_of(c * half_u, 16), half_u)
            up3 = remote(ub2.at[rows_u(other)], up_o.at[core], a_s.at[5], a_r.at[5], sib)
            up3.start()
            up_own = pltpu.make_async_copy(ub2.at[rows_u(core)], up_o.at[core], ld.at[16])
            up_own.start()
            db2[...] = adds(da[pl.ds(pl.multiple_of(xx * dq, 16), dq), :], db2[...])
            down_own = pltpu.make_async_copy(db2, down_o, ld.at[11])
            down_own.start()
        for c in gz_moves:
            c.wait()
        chain_b.local().wait()
        groups_o = DZ // 16
        bra = flat(br_all)
        for i in range(2):
            half_o = slice(i * (DZ // 2), (i + 1) * (DZ // 2))
            val = mm_tn(flat(gz_all)[:, half_o], bra)
            for g in range(DZ // 32):
                chunk, off = group_place(groups_o, i * (DZ // 32) + g)
                p_o[0, chunk // 2, chunk % 2, off : off + 16, :] = val[16 * g : 16 * g + 16].astype(BF16)
        stage(sum_o.swap_start)
        stage(sum_g.z_finish)
        back_edge.wait()
        live = jnp.where(s < S - 1, 1.0, 0.0)

        def fix_block(i, carry):
            C = at_cols(i, cb_m)
            c3 = yg[:, C].reshape(J, SUB, cb_m)
            final = lax.broadcasted_iota(jnp.int32, (SUB, cb_m), 0) == SUB - 1
            fixed = jnp.stack(
                [
                    c3[J - 3 + k]
                    + jnp.where(final, jnp.broadcast_to(edge_in[k : k + 1, C] * live, (SUB, cb_m)), 0.0)
                    for k in range(3)
                ]
            )
            pc[:, C] = jnp.concatenate([c3[: J - 3], fixed], axis=0).reshape(T, cb_m).astype(BF16)
            return carry

        lax.fori_loop(0, DI // cb_m, fix_block, 0)
        for e in range(E):
            gi_b[e] = pc[:, e * DZ : (e + 1) * DZ]
        pc_moves = trade(gi_b, pc_all, p_s, p_r)
        for c in pc_moves:
            c.start()
        pc_all[me] = gi_b[me]
        stage(sum_o.swap_finish)
        tg_o[...] = jnp.zeros_like(tg_o)

        def token_block(i, carry):
            for c in weight_load(i):
                c.wait()

            @pl.when(i + 1 < steps_s)
            def _():
                for c in weight_load(i + 1):
                    c.start()

            slot = lax.rem(i, 2)
            C = at_cols(i, cb_s)
            tg_o[...] += mm_nt(pc[:, C], big[slot, 0:D, :]) + mm_nt(gi[:, C], big[slot, D : 2 * D, :])
            return carry

        lax.fori_loop(0, steps_s, token_block, 0)
        d, gain_g = rms_back(tok[...].astype(F32), gp[0:1, :], tg_o[...])
        tg_o[...] = mg[...] + d
        gg_o[0:1, :] = gain_g
        cr = p_m.shape[3]
        for e in range(E):
            side = jnp.concatenate([gg_o[:, e * NZ : (e + 1) * NZ], jnp.zeros((G, DZ - NZ), F32)], axis=1)
            rows = [gs_o[:, e * DZ : (e + 1) * DZ], side, jnp.zeros((8 * cr - z.SMALL - G, DZ), F32)]
            p_m[e] = jnp.concatenate(rows, axis=0).astype(BF16).reshape(4, 2, cr, DZ)
        stage(sum_m.swap_start)
        for c in pc_moves:
            c.wait()
        place_in(p_c, flat(pc_all))
        stage(sum_c.swap_start)
        stage(sum_m.swap_finish)
        stage(sum_o.chips_finish)
        stage(sum_c.swap_finish)
        stage(sum_m.chips_finish)
        stage(sum_g.forward)
        stage(sum_c.chips_finish)
        stage(sum_m.z_finish)
        stage(sum_o.forward)
        stage(sum_c.z_finish)
        for c in out_moves:
            c.wait()
        back_own.wait()
        if plane:
            up3.wait()
            up_own.wait()
            down_own.wait()
            sum_m.forward()
            sum_c.forward()
            for sm_ in (sum_g, sum_o, sum_m, sum_c):
                sm_.finish()
        else:
            copies = [
                pltpu.make_async_copy(p, o, pown.at[a])
                for a, (p, o) in enumerate(((p_g, pg_o), (p_c, pc_o), (p_m, pm_o), (p_o, po_o)))
            ]
            for c in copies:
                c.start()
            for c in copies:
                c.wait()
        for k in range(E - 1):
            for d in (-k, k) if k else (0,):
                chain_b.each(d, lambda c: c.wait_send())

    v = pltpu.VMEM
    sem = lambda *dims: pltpu.SemaphoreType.DMA(dims)
    vm = pl.BlockSpec(memory_space=pltpu.VMEM)
    up_shape = (2, uq // 2, uc) if plane else (1, 16, LANES)
    down_shape = (dq, dc) if plane else (16, LANES)
    u_shape = (2, uq, uc) if plane else (2, 16, LANES)
    d_shape = (2 * dq, dc) if plane else (32, LANES)
    ins = (dxp, outp, dwu, dwd, states, w_out, w_in, table, choose, chances, mid, moe, cot, gpack, router, gate, y,
           sig, small, mixed, dt, masks, conv_in, hconv, s_all, tok, normed_all)
    rg, ro, rm = chunk_rows(NZ), chunk_rows(DZ), 16 * -(-(z.SMALL + G) // 128)
    p_shapes = [(E, 4, 2, rg, DZ), (E, 4, 2, rg, DZ), (E, 4, 2, rm, DZ), (1, 4, 2, ro, D)]
    o_shapes = [(4, 2, E, rg, DZ)] * 2 + [(4, 2, rm, DZ), (4, 2, 1, ro, D)] if plane else p_shapes
    return pl.pallas_call(
        body,
        name="backward",
        in_specs=[ANY] * 7 + [vm] * (len(ins) - 8) + [ANY],
        out_specs=[vm] * 3 + [ANY] * 7,
        out_shape=[
            sds((T, D), F32),
            sds((z.SMALL, DI), F32),
            sds((G, D), F32),
            sds((M, D), BF16),
        ]
        + [sds(o, BF16) for o in o_shapes]
        + [
            sds(up_shape, BF16),
            sds(down_shape, BF16),
        ],
        scratch_shapes=[
            v((2, rows_big, cb_s), BF16),
            v((2, cb_m, D), BF16), v((E * T, D), BF16),
            v((M, D + LANES), BF16), v((M, D + LANES), BF16), v((M, D), BF16), v((M, D), BF16),
            v((M, D + LANES), BF16),
            v((T, DI), F32), v((T, DI), BF16), v((E, T, DZ), BF16),
            v((T, D), BF16), v((T, D), F32),
            v((N, DI), BF16), v((S, N, DI), BF16), v(((N + 1) * SUB, DI), F32),
            v((SUB, DI), F32), v((SUB, DI), F32),
            v((T, DI), BF16),
            v((J * N * SUB, LANES), F32), v((J * N * SUB, LANES), F32),
            v((J * N * SUB, LANES), F32), v((J * N * SUB, LANES), F32),
            v((T, LANES), F32), v((T, cb_s), F32), v((N, cb_s), F32), v((N, cb_s), F32),
            v((T, cb_s), F32), v((T, cb_s), F32), v((N, cb_s), F32), v((T, z.R), F32), v((T, z.XW), BF16),
            v((N, DI), F32),
            v(u_shape, BF16), v(u_shape, BF16), v(u_shape[1:], BF16),
            v(d_shape, BF16), v(d_shape, BF16), v((d_shape[0] // 2, d_shape[1]), BF16),
            v((E, T, DZ), BF16), v((E, T, DZ), BF16), v((E, T, D), BF16), v((E, T, DZ), BF16),
            v((E, T, DZ), BF16),
        ]
        + [v(p, BF16) for p in p_shapes]
        + [v((p[0], 4) + p[3:], BF16) for p in p_shapes]
        + [v((3, p[0]) + p[3:], BF16) for p in p_shapes]
        + [v((E,) + p[3:], BF16) for p in p_shapes[:3]]
        + [
            sem(4), sem(4), sem(4, 3), sem(4, 3), sem(4, E - 1), sem(4, E - 1), sem(4, 3), sem(4, 3), sem(4, 4),
            sem(4, 4), sem(4),
            sem(18), sem(2), sem(2), sem(E - 1), sem(E - 1), sem(E - 1), sem(E - 1), sem(S - 1), sem(S - 1),
            pltpu.SemaphoreType.DMA, pltpu.SemaphoreType.DMA,
            sem(E - 1), sem(E - 1), sem(E - 1), sem(E - 1), sem(chain_slots), sem(chain_slots),
            sem(6), sem(6), sem(E - 1), sem(E - 1),
        ],
        compiler_params=pltpu.CompilerParams(
            collective_id=cid, has_side_effects=True, vmem_limit_bytes=60 * 1024 * 1024
        ),
    )(*ins)


def finish(z, gr, plane, pg, pc, pm, po, tg, mid, chances, choose, table, back, up, down):
    T, D, DI, N, J, E = z.T, z.D, z.DI, z.N, z.J, z.E
    DZ, NZ, FB = DI // E, D // E, z.FF // 8
    U = up.shape[1]

    def body(pg, pc, pm, po, tg, mid, ch, cho, tb, bk, up, dn, *outs):
        dwi, dwo, out, tgo, cw, cb, xw, dw, db, al, sk, na, nb, ro = outs[:14]
        for g in range(NZ // 16):
            chunk, off = group_place(NZ // 16, g)
            for h, src in enumerate((pc, pg)):
                for e in range(E):
                    dwi[16 * g : 16 * g + 16, h * DI + e * DZ : h * DI + (e + 1) * DZ] = src[
                        chunk, e, off : off + 16, :
                    ].astype(F32)
        for g in range(DZ // 16):
            chunk, off = group_place(DZ // 16, g)
            dwo[16 * g : 16 * g + 16, :] = po[chunk, off : off + 16, :].astype(F32)
        sm = pm[...].astype(F32)
        cw[...] = sm[CONV_W : CONV_W + 4]
        cb[...] = sm[CONV_B : CONV_B + 1]
        db[...] = sm[DT_B : DT_B + 1]
        sk[...] = sm[SKIP : SKIP + 1]
        al[...] = sm[A_LOG : A_LOG + N]
        dw[...] = sm[z.DT0 : z.X0]
        xw[...] = sm[z.X0 : z.SMALL]
        na[...] = sm[z.SMALL : z.SMALL + 1, 0:NZ]
        nb[...] = sm[z.SMALL + 1 : z.SMALL + 2, 0:NZ]
        ro[...] = sm[z.SMALL + 2 : z.SMALL + 2 + E, 0:NZ]
        lane = lax.broadcasted_iota(jnp.int32, (T, T), 1)
        prow = lax.broadcasted_iota(jnp.int32, (T, T), 0)
        order = (lane == (prow % SUB) * J + prow // SUB).astype(F32).astype(BF16)
        gating = jnp.sum(ch[...] * cho[...], axis=-1, keepdims=True)
        low = (mid[...] + gating * mm(tb[...], bk[...])).astype(BF16)
        out[...] = mm_tn(order, low).astype(BF16)
        v = tg[...]
        hi, rest = v.astype(BF16), v - v.astype(BF16).astype(F32)
        lo, end = split_hi_lo(rest)
        tgo[...] = mm_tn(order, hi) + (mm_tn(order, lo) + mm_tn(order, end))
        if plane:
            upo, dno = outs[14:]
            for c in range(2):
                for i in range(4):
                    at = (2 * i + c) * FB
                    upo[:, at : at + FB] = up[c, :, i * FB : (i + 1) * FB].astype(F32)
            dno[...] = dn[...].astype(F32)

    vm = pl.BlockSpec(memory_space=pltpu.VMEM)
    shapes = [
        sds((NZ, 2 * DI), F32), sds((DZ, D), F32), sds((T, D), BF16), sds((T, D), F32), sds((4, DZ), F32),
        sds((1, DZ), F32), sds((z.XW, DZ), F32), sds((z.R, DZ), F32), sds((1, DZ), F32), sds((N, DZ), F32),
        sds((1, DZ), F32), sds((1, NZ), F32), sds((1, NZ), F32), sds((E, NZ), F32),
    ]
    if plane:
        shapes += [sds((U, z.FF), F32), sds(down.shape, F32)]
    return pl.pallas_call(
        body,
        name="finish",
        in_specs=[vm] * 12,
        out_specs=[vm] * len(shapes),
        out_shape=shapes,
        compiler_params=pltpu.CompilerParams(vmem_limit_bytes=VMEM_LIMIT),
    )(pg, pc, pm, po, tg, mid, chances, choose, table, back, up, down)


def on_device(
    tokens, segment_ids, routes, cotangent, norm_gain, in_proj, conv_weight, conv_bias, x_proj,
    dt_proj, dt_bias, a_log, d_skip, out_proj, moe_gain, router, up_proj, down_proj,
):
    E = lax.axis_size("exp")
    S = lax.axis_size("seq")
    z = Sizes(tokens, in_proj, dt_proj, x_proj, a_log, up_proj, E)
    T, D, DI, N, J, CAP = z.T, z.D, z.DI, z.N, z.J, z.CAP
    me_s, me_e = lax.axis_index("seq"), lax.axis_index("exp")
    core = lax.rem(me_s, 2)
    where = jnp.stack([me_s, me_e, core]).astype(jnp.int32)
    cw = dt_proj.shape[1]
    dw = norm_gain.shape[0]
    plane = S == 8 and dw % 32 == 0
    line = lambda v: v.reshape(1, -1)
    if plane:
        params = [conv_weight, line(conv_bias), line(dt_bias), line(d_skip), a_log, dt_proj, x_proj,
                  line(norm_gain), line(moe_gain), router]
        w_in, w_out = in_proj, out_proj
    else:
        small_own = jnp.concatenate(
            [conv_weight, line(conv_bias), line(dt_bias), line(d_skip), jnp.zeros((1, cw), BF16), a_log, dt_proj,
             x_proj.T, jnp.zeros((-z.SMALL % 32, cw), BF16)], axis=0
        )
        g_own = jnp.concatenate(
            [line(norm_gain), line(moe_gain), router.T, jnp.zeros((32 - 2 - E, dw), BF16)], axis=0
        )
        gathered = [lax.all_gather(a, "exp", tiled=True) for a in (in_proj, out_proj, small_own, g_own)]
        w_in, w_out, params = gathered[0], gathered[1], gathered[2:]
    gr = 8 * -(-(2 + E) // 8)
    (
        small, gpack, router_t, table, choose_wide, masks, conv_in, hconv, gate, sig, mixed, dt, y, mid, moe, chances,
        s_all, tok, cot, states, w_in, w_out, arrived, cot_pair, normed_all,
    ) = forward(
        z, S, plane, tokens[0], cotangent[0], segment_ids, routes.reshape(1, T), params, w_in, w_out, gr, 1
    )
    outp, dxp, dwu, dwd = expert(
        z, where, arrived.reshape(2 * E * CAP, D), cot_pair.reshape(2 * E * CAP, D), router_t, up_proj[0], down_proj[0]
    )
    token_grad, _, _, back_out, pg, pc, pm, po, up_sum, down_sum = backward(
        z, S, plane, dxp.reshape(2, E * CAP, -1), outp.reshape(2, E * CAP, D), dwu, dwd, states, w_out, w_in, table,
        choose_wide, chances, mid, moe, cot, gpack, router_t, gate, y, sig, small, mixed, dt, masks, conv_in, hconv,
        s_all, tok, normed_all.reshape(E * T, D), 4
    )
    if not plane:
        pg, pc, pm, po = [lax.psum(a, "seq") for a in (pg, pc, pm, po)]
        pg, pc = [
            lax.all_to_all(a, "exp", split_axis=0, concat_axis=0, tiled=True).transpose(1, 2, 0, 3, 4)
            for a in (pg, pc)
        ]
        pm = lax.psum_scatter(pm, "exp", scatter_dimension=0, tiled=True)[0]
        po = po[0]
    eight = lambda a: a.reshape((8,) + a.shape[2:])
    dw_in, dw_out, output, token_grad, g_cw, g_cb, g_xw, g_dw, g_db, g_al, g_sk, g_na, g_nb, g_ro, *rest = finish(
        z, gr, plane, eight(pg), eight(pc), pm.reshape(-1, pm.shape[-1]), po.reshape(8, -1, D), token_grad, mid,
        chances, choose_wide, table, back_out, up_sum, down_sum
    )
    if plane:
        up_part, down_part = rest
    else:
        fb = z.FF // 8
        up_full = jnp.zeros((D, 4, 2, fb), BF16)
        up_full = lax.dynamic_update_slice_in_dim(up_full, dwu.reshape(D, 4, 1, fb), core, axis=2)
        down_full = jnp.zeros((4, 2, fb, D), BF16)
        down_full = lax.dynamic_update_slice_in_dim(down_full, dwd.reshape(4, 1, fb, D), core, axis=1)
        up_part, down_part = [
            lax.psum_scatter(v, "seq", scatter_dimension=0, tiled=True).astype(F32)
            for v in (up_full.reshape(D, z.FF), down_full.reshape(z.FF, D))
        ]
    return (
        output[None], token_grad[None], g_na[0], dw_in, g_cw, g_cb[0], g_xw.T, g_dw, g_db[0], g_al, g_sk[0], dw_out,
        g_nb[0], g_ro.T, up_part[None], down_part[None],
    )


def solution(mesh):
    row = P("exp", "seq", None)
    in_specs = (
        row, P("exp", "seq"), row, row, P("exp"), P("exp", None), P(None, "exp"), P("exp"), P("exp", None),
        P(None, "exp"), P("exp"), P(None, "exp"), P("exp"), P("exp", None), P("exp"), P("exp", None),
        P("exp", None, None), P("exp", None, None),
    )
    out_specs = (
        row, row, P("exp"), P("exp", None), P(None, "exp"), P("exp"), P("exp", None), P(None, "exp"), P("exp"),
        P(None, "exp"), P("exp"), P("exp", None), P("exp"), P("exp", None), row, row,
    )
    return jax.shard_map(on_device, mesh=mesh, in_specs=in_specs, out_specs=out_specs, check_vma=False)
```

```python
import functools
import math

import jax
import jax.numpy as jnp
from jax import lax
from jax.experimental import pallas as pl
from jax.experimental.pallas import tpu as pltpu
from jax.sharding import PartitionSpec as P

EPSILON = 1e-05
LOG2E = math.log2(math.e)
LN2 = math.log(2.0)
CLOSED = 1e30
LANES = 128
SUB = 8
F32 = jnp.float32
BF16 = jnp.bfloat16
VMEM_LIMIT = 56 * 1024 * 1024


def mm(a, b):
    return lax.dot_general(a, b, (((1,), (0,)), ((), ())), preferred_element_type=F32)


def mm_nt(a, b):
    return lax.dot_general(a, b, (((1,), (1,)), ((), ())), preferred_element_type=F32)


def mm_tn(a, b):
    return lax.dot_general(a, b, (((0,), (0,)), ((), ())), preferred_element_type=F32)


def split_hi_lo(value):
    high = value.astype(BF16)
    return high, (value - high.astype(F32)).astype(BF16)


def sigmoid(v):
    return 1.0 / (1.0 + jnp.exp(-v))


def softplus(v):
    e = jnp.exp(-jnp.abs(v))
    small = e * (1.0 - e * (0.5 - e * (1.0 / 3.0 - e * 0.25)))
    return jnp.maximum(v, 0.0) + jnp.where(e < 0.01, small, jnp.log(1.0 + e))


def rms_scale(v):
    return lax.rsqrt(jnp.mean(v * v, axis=-1, keepdims=True) + EPSILON)


def rms_back(resid, gain, grad):
    s = rms_scale(resid)
    v = gain * grad
    out = s * v - resid * (s * s * s) * jnp.mean(resid * v, axis=-1, keepdims=True)
    return out, jnp.sum(grad * resid * s, axis=0, keepdims=True)


def block(shape, index):
    return pl.BlockSpec(shape, index)


def whole(shape):
    zeros = (0,) * len(shape)
    return pl.BlockSpec(shape, lambda *_: zeros)


def call(body, name, grid, ins, in_specs, outs, out_specs, scratch, cost=None):
    return pl.pallas_call(
        body,
        name=name,
        grid=grid,
        in_specs=in_specs,
        out_specs=out_specs,
        out_shape=outs,
        scratch_shapes=scratch,
        cost_estimate=cost,
        compiler_params=pltpu.CompilerParams(vmem_limit_bytes=VMEM_LIMIT),
    )(*ins)


def sds(shape, dtype):
    return jax.ShapeDtypeStruct(shape, dtype)


def pick(total, options):
    for o in options:
        if total % o == 0:
            return o
    return total


CONV_W, CONV_B, DT_B, SKIP, A_LOG = 0, 4, 5, 6, 8


class Sizes:
    def __init__(self, tokens, in_proj, dt_proj, x_proj, a_log, up_proj, exp_count):
        self.T = tokens.shape[1]
        self.D = tokens.shape[2]
        self.DI = in_proj.shape[1] // 2
        self.N = a_log.shape[0]
        self.R = dt_proj.shape[0]
        self.XW = x_proj.shape[1]
        self.FF = up_proj.shape[2]
        self.E = exp_count
        self.CAP = 2 * self.T // exp_count
        self.J = self.T // SUB
        self.DT0 = A_LOG + self.N
        self.X0 = self.DT0 + self.R
        self.SMALL = self.X0 + self.XW


MESH = pl.DeviceIdType.MESH
ANY = pl.BlockSpec(memory_space=pl.ANY)


def greet(peers):
    barrier = pltpu.get_barrier_semaphore()
    for peer in peers:
        pl.semaphore_signal(barrier, inc=1, device_id=peer, device_id_type=MESH)
    pl.semaphore_wait(barrier, len(peers))


def group_place(groups, g):
    main = groups // 8
    if g < 8 * main:
        return g // main, 16 * (g % main)
    return g - 8 * main, 16 * main


def chunk_rows(rows):
    groups = rows // 16
    return 16 * (groups // 8 + (1 if groups % 8 else 0))


class PlaneSum:
    def __init__(self, E, p, b, t, zb, out, add, base, full, sems):
        self.E, self.p, self.b, self.t, self.zb, self.out, self.add = E, p, b, t, zb, out, add
        self.rows, self.full = p.shape[3], full
        self.base = base if full < 4 else self.rows
        self.cs, self.cr, self.qs, self.qr, self.zs, self.zr, self.gs, self.gr, self.fs, self.fr, self.own = sems
        s, self.me = lax.axis_index("seq"), lax.axis_index("exp")
        self.chip, self.core = s // 2, lax.rem(s, 2)
        self.sib = {"seq": s + 1 - 2 * self.core}
        self.chips = [self.chip + 1 - 2 * lax.rem(self.chip, 2), self.chip + 2 - 4 * (self.chip // 2), 3 - self.chip]
        self.far = [{"seq": q * 2 + self.core} for q in self.chips]
        self.zz = [lax.rem(self.me + k, E) for k in range(1, E)]

    def pair(self, src, dst, send, recv, to):
        cut = lambda ref, a, n: ref.at[(slice(None),) * (len(ref.shape) - 2) + (pl.ds(a, n),)]
        make = lambda a, n, i: pltpu.make_async_remote_copy(
            cut(src, a, n), cut(dst, a, n), send.at[i], recv.at[i], device_id=to, device_id_type=MESH
        )
        if self.base == self.rows:
            return [make(0, self.rows, 0)]
        return [make(0, self.base, 0), make(self.base, self.rows - self.base, 1)]

    def run(self, copies, chip, act):
        act(copies[0])
        if len(copies) > 1:
            @pl.when(chip < self.full)
            def _():
                act(copies[1])

    def swap_start(self):
        self.swap = self.pair(self.p.at[:, :, 1 - self.core], self.b, self.cs, self.cr, self.sib)
        if len(self.swap) > 1:
            src, dst = self.p.at[:, 0 : self.full, 1 - self.core], self.b.at[:, 0 : self.full]
            self.swap[1] = self.pair(src, dst, self.cs, self.cr, self.sib)[1]
        for c in self.swap:
            c.start()

    def swap_finish(self):
        for c in self.swap:
            c.wait()
        B = self.base
        for l in range(self.p.shape[0]):
            self.p[l, :, self.core, 0:B] = (
                self.p[l, :, self.core, 0:B].astype(F32) + self.b[l, :, 0:B].astype(F32)
            ).astype(BF16)
            if B < self.rows:
                F = self.full
                self.p[l, 0:F, self.core, B:] = (
                    self.p[l, 0:F, self.core, B:].astype(F32) + self.b[l, 0:F, B:].astype(F32)
                ).astype(BF16)
        self.crossing = [
            self.pair(self.p.at[:, self.chips[k], self.core], self.t.at[k], self.qs.at[k], self.qr.at[k], self.far[k])
            for k in range(3)
        ]
        for k in range(3):
            self.run(self.crossing[k], self.chips[k], lambda c: c.start())

    def chips_finish(self):
        for k in range(3):
            self.run(self.crossing[k], self.chips[k], lambda c: c.wait_send())
            self.run(self.crossing[k], self.chip, lambda c: c.wait_recv())

        def total(rows):
            for l in range(self.p.shape[0]):
                v = self.p[l, self.chip, self.core, rows].astype(F32)
                for k in range(3):
                    v = v + self.t[k, l, rows].astype(F32)
                self.p[l, self.chip, self.core, rows] = v.astype(BF16)

        total(slice(0, self.base))
        if self.base < self.rows:
            @pl.when(self.chip < self.full)
            def _():
                total(slice(self.base, self.rows))

        if self.zb is None:
            self.spread(self.p.at[:, self.chip, self.core])
            return
        self.along = [
            self.pair(self.p.at[d, self.chip, self.core], self.zb.at[self.me], self.zs.at[k], self.zr.at[k], {"exp": d})
            for k, d in enumerate(self.zz)
        ]
        for c in self.along:
            self.run(c, self.chip, lambda c: c.start())

    def z_finish(self):
        for c in self.along:
            self.run(c, self.chip, lambda c: c.wait())
        v = self.p[self.me, self.chip, self.core]
        if self.add:
            v = v.astype(F32)
            for d in self.zz:
                v = v + self.zb[d].astype(F32)
            self.zb[self.me] = v.astype(BF16)
            self.spread(self.zb.at[self.me])
        else:
            self.zb[self.me] = v
            self.spread(self.zb)

    def spread(self, ref):
        dst = self.out.at[self.chip, self.core]
        self.sends = [self.pair(ref, dst, self.gs.at[k], self.gr.at[k], self.far[k]) for k in range(3)]
        self.sends.append(self.pair(ref, dst, self.fs.at[3], self.fr.at[3], self.sib))
        for c in self.sends:
            self.run(c, self.chip, lambda c: c.start())
        self.local = pltpu.make_async_copy(ref, dst, self.own)
        self.local.start()

    def forward(self):
        self.passed = []
        for k in range(3):
            ref = self.out.at[self.chips[k], self.core]
            self.run(self.pair(ref, ref, self.gs.at[k], self.gr.at[k], self.far[k]), self.chips[k], lambda c: c.wait_recv())
            c = self.pair(ref, ref, self.fs.at[k], self.fr.at[k], self.sib)
            self.run(c, self.chips[k], lambda c: c.start())
            self.passed.append(c)

    def finish(self):
        for c in self.sends:
            self.run(c, self.chip, lambda c: c.wait_send())
        for k in range(3):
            self.run(self.passed[k], self.chips[k], lambda c: c.wait_send())
        self.local.wait()
        for k in range(4):
            q = self.chips[k] if k < 3 else self.chip
            ref = self.out.at[q, 1 - self.core]
            self.run(self.pair(ref, ref, self.fs.at[k], self.fr.at[k], self.sib), q, lambda c: c.wait_recv())


def expand_columns(z, src, col0, dst):
    def one(j, carry):
        rows = src[pl.ds(pl.multiple_of(j * SUB, SUB), SUB), :]
        for n in range(z.N):
            at = pl.multiple_of((j * z.N + n) * SUB, SUB)
            dst[pl.ds(at, SUB), :] = jnp.broadcast_to(
                rows[:, col0 + n : col0 + n + 1], (SUB, LANES)
            )
        return carry

    lax.fori_loop(0, z.J, one, 0)


def expand_closed(z, masks, dst):
    dst[...] = jnp.broadcast_to((1.0 - masks[:, 2:3]) * CLOSED, (z.T, LANES))


def tile_groups(cb):
    return 2 if cb % (2 * LANES) == 0 else 1


def lane_at(p, tg, k):
    return pl.ds(pl.multiple_of(p * tg * LANES, LANES) + k * LANES, LANES)


def row8(j):
    return pl.ds(pl.multiple_of(j * SUB, SUB), SUB)


def shift_down(v, d):
    rows = lax.broadcasted_iota(jnp.int32, v.shape, 0)
    return jnp.where(rows >= d, pltpu.roll(v, d, 0), 0.0)


def shift_up(v, d):
    rows = lax.broadcasted_iota(jnp.int32, v.shape, 0)
    return jnp.where(rows < SUB - d, pltpu.roll(v, SUB - d, 0), 0.0)


def chain_states(count, mine, order, sums, heads, rates2):
    state = jnp.zeros_like(rates2)
    for k in range(count):
        at = order(k)
        new = jnp.exp2(rates2 * sums(at)) * state + heads(at).astype(F32)
        state = jnp.where(mine(at), new, state)
    return state


def router_softmax(logits, experts):
    lane = lax.broadcasted_iota(jnp.int32, logits.shape, 1)
    logits = jnp.where(lane < experts, logits, -1e30)
    top = jnp.max(logits, axis=-1, keepdims=True)
    e = jnp.where(lane < experts, jnp.exp(logits - top), 0.0)
    return e / jnp.sum(e, axis=-1, keepdims=True)


def expert(z, x, cot, router, normed, up, down, cid):
    T, D, FF, E = z.T, z.D, z.FF, z.E
    M = x.shape[0] // 2
    CAP = z.CAP
    fb = FF // 8
    wb = 2 * fb

    def body(
        x_r, c_r, rt, nrm, up_r, dn_r, dxz, back_o, dwu_o, dwd_o, nz_o,
        up_v, dn_v, hid, pg_s, g_s, out_s, dx_s, dxb, outb, dx_r, out_r, dwu_v, dwd_v,
        ld, c_s, c_q, sw_s, sw_r, dz_s, dz_r,
    ):
        s, me = lax.axis_index("seq"), lax.axis_index("exp")
        core = lax.rem(s, 2)
        other = 1 - core
        sib = {"seq": s + 1 - 2 * core}
        zs = [lax.rem(me + k, E) for k in range(1, E)]
        loads = []
        for i in range(4):
            at = pl.multiple_of((2 * i + core) * fb, LANES)
            t, off = i // 2, i % 2 * fb
            loads.append(
                [
                    pltpu.make_async_copy(up_r.at[:, pl.ds(at, fb)], up_v.at[t, :, off : off + fb], ld.at[i]),
                    pltpu.make_async_copy(dn_r.at[pl.ds(at, fb)], dn_v.at[t, off : off + fb], ld.at[4 + i]),
                ]
            )
        for pair in loads:
            for c in pair:
                c.start()
        greet([sib] + [{"exp": p} for p in zs])

        def remote(src, dst, send, recv, to):
            return pltpu.make_async_remote_copy(src, dst, send, recv, device_id=to, device_id_type=MESH)

        chain = Chain(E, nrm, nz_o, c_s, c_q, ld.at[8])
        chain.start()
        ch = router_softmax(mm_nt(x_r[...], rt[...]), E)
        lane = lax.broadcasted_iota(jnp.int32, ch.shape, 1)
        gating = jnp.sum(jnp.where(lane == me, ch, 0.0), axis=-1, keepdims=True)
        g_s[...] = (gating * c_r[...].astype(F32)).astype(BF16)
        for t in range(2):
            W = slice(t * wb, (t + 1) * wb)
            for pair in loads[2 * t : 2 * t + 2]:
                for c in pair:
                    c.wait()
            pre = mm(x_r[...], up_v[t])
            cdf = 0.5 * (1.0 + lax.erf(pre * (2.0 ** -0.5)))
            hid[:, W] = (pre * cdf).astype(BF16)
            slope = cdf + pre * jnp.exp(-0.5 * pre * pre) * (1.0 / math.sqrt(2.0 * math.pi))
            pg_s[:, W] = (mm_nt(g_s[...], dn_v[t]) * slope).astype(BF16)
            if t == 0:
                dx_s[...] = mm_nt(pg_s[:, W], up_v[t])
                out_s[...] = mm(hid[:, W], dn_v[t])
                chain.hop(1)
            else:
                dxb[:, 0:D] = (dx_s[...] + mm_nt(pg_s[:, W], up_v[t])).astype(BF16)
                out = out_s[...] + mm(hid[:, W], dn_v[t])
                outb[...] = out.astype(BF16)
                gg = jnp.sum(out * c_r[...].astype(F32), axis=-1, keepdims=True)
                hi, lo = split_hi_lo(gg)
                lane = lax.broadcasted_iota(jnp.int32, (2 * M, LANES), 1)
                both = jnp.where(lane == 0, hi.astype(F32), jnp.where(lane == 1, lo.astype(F32), 0.0))
                dxb[:, D : D + LANES] = both.astype(BF16)
        half = lambda c: pl.ds(pl.multiple_of(c * M, 16), M)
        swaps = [
            remote(dxb.at[half(other)], dx_r, sw_s.at[0], sw_r.at[0], sib),
            remote(outb.at[half(other)], out_r, sw_s.at[1], sw_r.at[1], sib),
        ]
        for c in swaps:
            c.start()
        if E > 2:
            chain.hop(2)

        def grads(t):
            W = slice(t * wb, (t + 1) * wb)
            dwd_v[W, :] = mm_tn(hid[:, W], g_s[...]).astype(BF16)
            dwu_v[:, W] = mm_tn(x_r[...], pg_s[:, W]).astype(BF16)
            moves = [
                pltpu.make_async_copy(dwd_v.at[W], dwd_o.at[W], ld.at[9 + t]),
                pltpu.make_async_copy(dwu_v.at[:, W], dwu_o.at[:, W], ld.at[11 + t]),
            ]
            for c in moves:
                c.start()
            return moves

        block_of = lambda ref, p: ref.at[pl.ds(pl.multiple_of(p * CAP, 16), CAP)]
        here = pl.ds(pl.multiple_of(me * CAP, 16), CAP)
        swaps[0].wait()
        dx_r[...] = (dxb[half(core), :].astype(F32) + dx_r[...].astype(F32)).astype(BF16)
        moves = [
            remote(block_of(dx_r, p), block_of(dxz, me), dz_s.at[k], dz_r.at[k], {"exp": p}) for k, p in enumerate(zs)
        ]
        for c in moves:
            c.start()
        dxz[here, :] = dx_r[here, :]
        kept = grads(0)
        swaps[1].wait()
        out_r[...] = (outb[half(core), :].astype(F32) + out_r[...].astype(F32)).astype(BF16)
        kept.append(pltpu.make_async_copy(out_r, back_o, ld.at[13]))
        kept[-1].start()
        kept += grads(1)
        for k in range(3, E):
            chain.hop(k)
        for c in moves + kept:
            c.wait()
        chain.finish()

    v = pltpu.VMEM
    sem = lambda *dims: pltpu.SemaphoreType.DMA(dims)
    vm = pl.BlockSpec(memory_space=pltpu.VMEM)
    slots = 2 * (E - 1)
    return pl.pallas_call(
        body,
        name="expert",
        in_specs=[vm] * 4 + [ANY] * 2,
        out_specs=[vm] + [ANY] * 4,
        out_shape=[
            sds((M, D + LANES), BF16), sds((M, D), BF16), sds((D, 2 * wb), BF16), sds((2 * wb, D), BF16),
            sds((E, T, D), BF16),
        ],
        scratch_shapes=[
            v((2, D, wb), BF16), v((2, wb, D), BF16), v((2 * M, 2 * wb), BF16), v((2 * M, 2 * wb), BF16),
            v((2 * M, D), BF16), v((2 * M, D), F32), v((2 * M, D), F32), v((2 * M, D + LANES), BF16),
            v((2 * M, D), BF16), v((M, D + LANES), BF16), v((M, D), BF16), v((D, 2 * wb), BF16), v((2 * wb, D), BF16),
            sem(14), sem(slots), sem(slots), sem(2), sem(2), sem(E - 1), sem(E - 1),
        ],
        compiler_params=pltpu.CompilerParams(
            collective_id=cid, has_side_effects=True, vmem_limit_bytes=VMEM_LIMIT
        ),
    )(x, cot, router, normed, up, down)


def padded_rows(main, edge, J, cb):
    H = edge.shape[0]
    m3 = main.reshape(J, SUB, cb)
    first = lax.broadcasted_iota(jnp.int32, (SUB, cb), 0) == 0
    tail = jnp.stack(
        [
            jnp.where(
                first,
                jnp.broadcast_to(edge[H - 3 + k : H - 2 + k, :], (SUB, cb)),
                pltpu.roll(m3[J - 3 + k], 1, 0),
            )
            for k in range(3)
        ]
    )
    return jnp.concatenate([tail, m3], axis=0)


def at_cols(i, cb):
    return pl.ds(pl.multiple_of(i * cb, LANES), cb)


def lanes_of(i, cb, p, tg, k):
    return pl.ds(pl.multiple_of(i * cb + p * tg * LANES, LANES) + k * LANES, LANES)


class Chain:
    def __init__(self, E, src, dst, send, recv, own):
        self.E, self.src, self.dst, self.send, self.recv, self.own = E, src, dst, send, recv, own
        self.me = lax.axis_index("exp")
        self.right, self.left = lax.rem(self.me + 1, E), lax.rem(self.me + E - 1, E)

    def slot(self, d):
        return 2 * (abs(d) - 1) + (1 if d > 0 else 0)

    def exists(self, d):
        return (self.me + d >= 0) & (self.me + d < self.E)

    def each(self, d, act):
        for to_right in (True, False):
            if (d <= 0) if to_right else (d >= 0):
                edge = self.me < self.E - 1 if to_right else self.me > 0
                there = self.slot(d - 1 if to_right else d + 1)

                @pl.when(self.exists(d) & edge)
                def _():
                    act(
                        pltpu.make_async_remote_copy(
                            self.src if d == 0 else self.dst.at[self.me + d],
                            self.dst.at[self.me + d],
                            self.send.at[there],
                            self.recv.at[there],
                            device_id={"exp": self.right if to_right else self.left},
                            device_id_type=MESH,
                        )
                    )

    def local(self):
        return pltpu.make_async_copy(self.src, self.dst.at[self.me], self.own)

    def start(self):
        self.each(0, lambda c: c.start())
        self.local().start()

    def hop(self, k):
        for d in (-k, k):
            ref = self.dst.at[self.me + d]

            @pl.when(self.exists(d))
            def _():
                pltpu.make_async_remote_copy(
                    ref, ref, self.send.at[self.slot(d)], self.recv.at[self.slot(d)],
                    device_id={"exp": self.right}, device_id_type=MESH,
                ).wait_recv()

            if k < self.E - 1:
                self.each(d, lambda c: c.start())

    def finish(self):
        for k in range(self.E - 1):
            for d in (-k, k) if k else (0,):
                self.each(d, lambda c: c.wait_send())
        self.local().wait()


class Spread:
    def __init__(self, E, src, col0, dst, cols, each, by_rows, sems):
        self.E, self.src, self.col0, self.dst, self.cols, self.each_cols = E, src, col0, dst, cols, each
        self.by_rows = by_rows
        self.zs, self.zr, self.ps, self.pr, self.cs, self.cr = sems
        self.rows = src.shape[0]
        s, self.me = lax.axis_index("seq"), lax.axis_index("exp")
        self.chip, self.core = s // 2, lax.rem(s, 2)
        self.sib = {"seq": s + 1 - 2 * self.core}
        self.chips = [self.chip + 1 - 2 * lax.rem(self.chip, 2), self.chip + 2 - 4 * (self.chip // 2), 3 - self.chip]
        self.far = [{"seq": q * 2 + self.core} for q in self.chips]
        self.right, self.left = lax.rem(self.me + 1, E), lax.rem(self.me + E - 1, E)
        self.split = by_rows or each > 0
        self.rest = 0 if by_rows else cols - 4 * each
        self.regions = ([1] if self.split else []) + ([0] if self.rest else [])
        self.pieces = ([0] if self.rest else []) + ([1, 2, 3, 4] if self.split else [])
        self.offsets = [d for k in range(1, E) for d in (-k, k)]

    def slot(self, d):
        return 2 * (abs(d) - 1) + (1 if d > 0 else 0)

    def exists(self, d):
        return (self.me + d >= 0) & (self.me + d < self.E)

    def view(self, ref, row0, col0, region, q, core, half):
        rows = self.rows // 2
        row = row0 + core * rows
        if self.by_rows:
            rows = rows // 4
            row = row + q * rows
            if half is not None:
                rows = rows // 2
                row = row + half * rows
            return ref.at[pl.ds(pl.multiple_of(row, 16), rows)]
        at = pl.ds(pl.multiple_of(row, 16), rows)
        if region == 0:
            start, width = col0, self.rest
        else:
            start, width = col0 + self.rest + q * self.each_cols, self.each_cols
            if half is not None:
                width = width // 2
                start = start + half * width
        if width == ref.shape[1]:
            return ref.at[at]
        return ref.at[at, pl.ds(pl.multiple_of(start, LANES), width)]

    def there(self, d, region, q, core, half=None):
        return self.view(self.dst, (self.me + d) * self.rows, 0, region, q, core, half)

    def own(self, region):
        return self.view(self.src, 0, self.col0, region, self.chip, self.core, None)

    def local(self, sem):
        at = pl.ds(pl.multiple_of(self.me * self.rows, 16), self.rows)
        src = self.src if self.cols == self.src.shape[1] else self.src.at[:, self.col0 : self.col0 + self.cols]
        return pltpu.make_async_copy(src, self.dst.at[at], sem)

    def remote(self, src, dst, send, recv, to):
        return pltpu.make_async_remote_copy(src, dst, send, recv, device_id=to, device_id_type=MESH)

    def z_each(self, region, d, act):
        for to_right in (True, False):
            if (d <= 0) if to_right else (d >= 0):
                edge = self.me < self.E - 1 if to_right else self.me > 0
                slot = self.slot(d - 1 if to_right else d + 1)

                @pl.when(self.exists(d) & edge)
                def _():
                    act(
                        self.remote(
                            self.own(region) if d == 0 else self.there(d, region, self.chip, self.core),
                            self.there(d, region, self.chip, self.core),
                            self.zs.at[region, slot],
                            self.zr.at[region, slot],
                            {"exp": self.right if to_right else self.left},
                        )
                    )

    def start(self):
        for r in self.regions:
            self.z_each(r, 0, lambda c: c.start())

    def cross(self, j, d):
        if j < 2:
            ref = self.there(d, 1, self.chip, self.core)
        else:
            ref = self.there(d, 1, self.chips[j - 2], self.core, j - 2)
        to = self.far[(0, 1, 1, 0)[j]]
        return self.remote(ref, ref, self.ps.at[j, self.slot(d)], self.pr.at[j, self.slot(d)], to)

    def crossed(self, j, d):
        ref = self.there(d, 1, self.chips[j], self.core) if j < 2 else self.there(d, 1, self.chips[2], self.core, j - 2)
        self.remote(ref, ref, self.ps.at[j, self.slot(d)], self.pr.at[j, self.slot(d)], self.sib).wait_recv()

    def sib_copy(self, which, d, core):
        if which == 0:
            ref = self.there(d, 0, self.chip, core)
        else:
            ref = self.there(d, 1, self.chip if which == 1 else self.chips[which - 2], core)
        return self.remote(ref, ref, self.cs.at[which, self.slot(d)], self.cr.at[which, self.slot(d)], self.sib)

    def hop(self, k):
        for r in self.regions:
            for d in (-k, k):
                @pl.when(self.exists(d))
                def _():
                    ref = self.there(d, r, self.chip, self.core)
                    self.remote(
                        ref, ref, self.zs.at[r, self.slot(d)], self.zr.at[r, self.slot(d)], self.sib
                    ).wait_recv()

                if k < self.E - 1:
                    self.z_each(r, d, lambda c: c.start())

                @pl.when(self.exists(d))
                def _():
                    if r == 1:
                        for j in range(2):
                            self.cross(j, d).start()
                    self.sib_copy(r, d, self.core).start()

    def plane(self, k):
        for d in (-k, k) if self.split else ():
            @pl.when(self.exists(d))
            def _():
                for j in range(2):
                    self.crossed(j, d)
                    self.cross(2 + j, d).start()
                    self.sib_copy(2 + j, d, self.core).start()

    def fourth(self, k):
        for d in (-k, k) if self.split else ():
            @pl.when(self.exists(d))
            def _():
                self.crossed(2, d)
                self.crossed(3, d)
                self.sib_copy(4, d, self.core).start()

    def landed(self):
        for d in self.offsets:
            @pl.when(self.exists(d))
            def _():
                for w in self.pieces:
                    self.sib_copy(w, d, 1 - self.core).wait_recv()

    def finish(self):
        for d in self.offsets:
            @pl.when(self.exists(d))
            def _():
                for w in self.pieces:
                    self.sib_copy(w, d, self.core).wait_send()
                if self.split:
                    for j in range(4):
                        self.cross(j, d).wait_send()
        for r in self.regions:
            for k in range(self.E - 1):
                for d in (-k, k) if k else (0,):
                    self.z_each(r, d, lambda c: c.wait_send())


def small_rows(z):
    return 128 * -(-z.SMALL // 128)


def pack_small(z, par, own_sm, own_g):
    conv_w, conv_b, dt_b, skip, a_log, dt_w, x_w, gain_a, gain_b, router = par
    (rs, cw), (rg, dw) = own_sm.shape, own_g.shape
    wide = lambda ref: ref[...].astype(F32)
    line = lambda ref: ref[...].astype(F32).reshape(1, ref.shape[0])
    rows = [wide(conv_w), line(conv_b), line(dt_b), line(skip), jnp.zeros((1, cw), F32), wide(a_log), wide(dt_w)]
    rows += [wide(x_w), jnp.zeros((rs - z.SMALL, cw), F32)]
    own_sm[...] = jnp.concatenate(rows, axis=0).astype(BF16)
    rows = [line(gain_a), line(gain_b), wide(router), jnp.zeros((rg - 2 - z.E, dw), F32)]
    own_g[...] = jnp.concatenate(rows, axis=0).astype(BF16)


def forward(z, S, plane, tokens, cotangent, seg, route, params, in_proj, out_proj, gr, cid):
    T, D, DI, N, J, E, CAP = z.T, z.D, z.DI, z.N, z.J, z.E, z.CAP
    H = J
    M = E * CAP
    DZ, NZ = DI // E, D // E
    rs, rg = small_rows(z), 32
    cb = pick(DI, (384, 256, 128))
    cs = pick(DI, (768, 384, 256, 128))
    tg = tile_groups(cs)
    wide = tg * LANES
    ng = 8
    steps = DI // cs
    ST = (J + 1) * N * SUB
    tiles, tiles_o = DI // LANES, D // LANES
    split = (tiles // 4 - (0 if tiles % 4 else 1)) * LANES
    split_o = max(1, tiles_o * 2 // 9) * LANES

    def body(*refs):
        tokn, cotn, seg_r, route_r = refs[:4]
        np_ = len(params)
        par = refs[4 : 4 + np_]
        (
            in_p, out_p,
            sm, gp, rt, table, choose, masks, conv_in, hconv, gate, sig, mixed, dt, y, mid, moe, ch_o, s_all, tok, cot, normed_o,
            st_o, win_o, wout_o, arr_o, cot_o,
            wc, wg, wo, smb, gb, nrm, halo, seg_in, bx, cx, cl, u_s, rates_s, hd, hdev, stot, h_all, pre_s, dwin, hin,
            st_v, acc, outb, cotb, own_sm, own_g, own_seg,
            ld, zs, zr, ps, pr, c_s, c_r, t_s, t_r, h_s, h_r, d_s, d_r, q_s, q_r, k_s, k_r, x_s, x_r,
        ) = refs[4 + np_ :]
        s, me = lax.axis_index("seq"), lax.axis_index("exp")
        core = lax.rem(s, 2)
        sib = {"seq": s + 1 - 2 * core}
        seqs = [lax.rem(s + k, S) for k in range(1, S)]
        zz = [lax.rem(me + k, E) for k in range(1, E)]
        barrier = pltpu.get_barrier_semaphore()
        peers = [{"seq": p} for p in seqs] + [{"exp": p} for p in zz]
        for peer in peers:
            pl.semaphore_signal(barrier, inc=1, device_id=peer, device_id_type=MESH)

        def remote(src, dst, send, recv, to):
            return pltpu.make_async_remote_copy(src, dst, send, recv, device_id=to, device_id_type=MESH)

        if plane:
            pack_small(z, par, own_sm, own_g)
        segrow = seg_r[...].astype(F32)
        own_seg[...] = jnp.broadcast_to(segrow, (SUB, T))
        pl.semaphore_wait(barrier, len(peers))
        sems = lambda a: (zs.at[a], zr.at[a], ps.at[a], pr.at[a], c_s.at[a], c_r.at[a])
        if plane:
            parts = [
                Spread(E, own_sm, 0, smb, DZ, 0, True, sems(0)),
                Spread(E, own_g, 0, gb, NZ, 0, False, sems(1)),
                Spread(E, in_p, 0, wc, DI, split, False, sems(2)),
                Spread(E, in_p, DI, wg, DI, split, False, sems(3)),
                Spread(E, out_p, 0, wo, D, split_o, False, sems(4)),
            ]
            for p in parts[:3]:
                p.start()
            loads = [p.local(ld.at[a]) for a, p in enumerate(parts)]
        else:
            loads = [
                pltpu.make_async_copy(par[0], smb, ld.at[0]),
                pltpu.make_async_copy(par[1], gb, ld.at[1]),
                pltpu.make_async_copy(in_p.at[:, 0:DI], wc, ld.at[2]),
                pltpu.make_async_copy(in_p.at[:, DI : 2 * DI], wg, ld.at[3]),
                pltpu.make_async_copy(out_p, wo, ld.at[4]),
            ]
        ahead = {"seq": lax.rem(s + 1, S)}
        edges = [
            remote(tokn.at[pl.ds(T - H, H)], halo, t_s.at[0], t_r.at[0], ahead),
            remote(own_seg, seg_in, t_s.at[1], t_r.at[1], ahead),
        ]
        for c in edges:
            c.start()
        for c in loads:
            c.start()
        queue = []
        if plane:
            wg_p, wo_p = parts[3], parts[4]
            queue = [wg_p.start] + [functools.partial(wg_p.hop, k) for k in range(1, E - 1)]
            queue += [wo_p.start, functools.partial(wg_p.hop, E - 1)]
            for k in range(1, E):
                queue += [functools.partial(wg_p.plane, k), functools.partial(wo_p.hop, k)]
                queue += [functools.partial(wg_p.fourth, k)]
            for k in range(1, E):
                queue += [functools.partial(wo_p.plane, k)]
            for k in range(1, E):
                queue += [functools.partial(wo_p.fourth, k)]

        def progress(count):
            for _ in range(count):
                if queue:
                    queue.pop(0)()

        lane = lax.broadcasted_iota(jnp.int32, (T, T), 1)
        prow = lax.broadcasted_iota(jnp.int32, (T, T), 0)
        place = (prow % SUB) * J + prow // SUB
        order = (lane == place).astype(F32).astype(BF16)
        tok[...] = mm(order, tokn[...]).astype(BF16)
        cot[...] = mm(order, cotn[...]).astype(BF16)
        my_route = jnp.sum(
            jnp.where(lane == place, route_r[...].astype(F32), 0.0), axis=1, keepdims=True
        ).astype(jnp.int32)
        chosen = (lane == my_route).astype(F32)
        choose[...] = chosen
        counts = mm((lane <= prow).astype(F32).astype(BF16), chosen.astype(BF16))
        rank = jnp.sum(counts * chosen, axis=-1, keepdims=True).astype(jnp.int32) - 1
        slots = lax.broadcasted_iota(jnp.int32, (T, M), 1)
        table[...] = (slots == my_route * CAP + rank).astype(F32).astype(BF16)
        cotb[...] = mm_tn(table[...], cot[...]).astype(BF16)
        t32 = tok[...].astype(F32)
        scaled = t32 * rms_scale(t32)

        if plane:
            for k in range(1, E + 2):
                if k < E:
                    for p in parts[:3]:
                        p.hop(k)
                    progress(1)
                if 1 <= k - 1 < E:
                    parts[0].plane(k - 1)
                    parts[2].plane(k - 1)
                    progress(1)
                if 1 <= k - 2 < E:
                    parts[0].fourth(k - 2)
                    parts[2].fourth(k - 2)
        block_of = lambda ref, p: ref.at[pl.ds(pl.multiple_of(p * CAP, 16), CAP)]
        cot_moves = [remote(block_of(cotb, p), cot_o.at[core, me], k_s.at[k], k_r.at[k], {"exp": p}) for k, p in enumerate(zz)]
        if plane:
            for p in parts[:3]:
                p.landed()
        for c in loads:
            c.wait()
        for e in range(E):
            sm[:, e * DZ : (e + 1) * DZ] = smb[e * rs : (e + 1) * rs, :].astype(F32)[0 : z.SMALL]
        gp[...] = jnp.zeros_like(gp)
        rt[...] = jnp.zeros_like(rt)
        for e in range(E):
            cols = slice(e * NZ, (e + 1) * NZ)
            gp[:, cols] = gb[e * rg : e * rg + 16, :].astype(F32)[0:gr]
        rt[0:16, :] = jnp.concatenate([gp[2 : 2 + E, :], jnp.zeros((16 - E, D), F32)], axis=0).astype(BF16)

        for c in edges:
            c.wait()
        live = jnp.where(s > 0, 1.0, 0.0)
        col8 = lax.broadcasted_iota(jnp.int32, (T, SUB), 1)
        prev = seg_in[0:1, :] * live

        def seg_at(k):
            own = jnp.where(lane == place - k, segrow, 0.0)
            return jnp.sum(own + jnp.where(lane == place - k + T, prev, 0.0), axis=1, keepdims=True)

        now = seg_at(0)
        same = jnp.zeros((T, SUB), F32)
        for o in range(4):
            same = jnp.where(col8 == o, (seg_at(3 - o) == now).astype(F32), same)
        masks[...] = same
        nrm[0:T, :] = (scaled * gp[0:1, :]).astype(BF16)
        h32 = halo[...].astype(F32) * live
        nrm[T : T + H, :] = (h32 * rms_scale(h32) * gp[0:1, :]).astype(BF16)
        mixed[...] = jnp.zeros_like(mixed)

        def conv_block(i, carry):
            C = at_cols(i, cb)
            both = mm(nrm[...], wc[:, C])
            main, edge = both[:T], both[T:]
            conv_in[:, C] = main
            hconv[:, C] = edge
            xpad = padded_rows(main, edge, J, cb)
            out = jnp.broadcast_to(sm[CONV_B : CONV_B + 1, C], (T, cb))
            for o in range(4):
                m = jnp.broadcast_to(masks[:, o : o + 1], (T, cb))
                out = out + sm[CONV_W + o : CONV_W + o + 1, C] * xpad[o : o + J].reshape(T, cb) * m
            sv = (out * sigmoid(out)).astype(BF16)
            sig[:, C] = sv
            mixed[...] += mm_nt(sv, sm[z.X0 : z.X0 + z.XW, C].astype(BF16))
            return carry

        lax.fori_loop(0, DI // cb, conv_block, 0)
        normed_o[...] = nrm[0:T, :]
        progress(3)
        cot_own = pltpu.make_async_copy(block_of(cotb, me), cot_o.at[core, me], ld.at[6])
        cot_own.start()

        expand_columns(z, mixed, z.R, bx)
        expand_columns(z, mixed, z.R + N, cx)
        expand_closed(z, masks, cl)
        low = mixed[:, 0 : z.R].astype(BF16)

        def step_block(i, carry):
            C = at_cols(i, cs)
            pre = mm(low, sm[z.DT0 : z.DT0 + z.R, C].astype(BF16)) + sm[DT_B : DT_B + 1, C]
            step = softplus(pre)
            dt[:, C] = step
            u_s[:, C] = step * sig[:, C].astype(F32)
            rates_s[:, C] = -jnp.exp(sm[A_LOG : A_LOG + N, C]) * LOG2E
            return carry

        lax.fori_loop(0, DI // cs, step_block, 0)
        progress(3)

        def chunk_block(p, carry):
            lanes = [lane_at(p, tg, k) for k in range(tg)]
            wins = []
            for k in range(tg):
                w1 = jnp.zeros((SUB, LANES), F32)
                for j in range(J):
                    w1 = w1 + (dt[j * SUB : j * SUB + SUB, lanes[k]] + cl[j * SUB : j * SUB + SUB, :])
                w2 = w1 + shift_down(w1, 1)
                w4 = w2 + shift_down(w2, 2)
                w8 = w4 + shift_down(w4, 4)
                wins.append((w1, w2, w4))
                dwin[:, lanes[k]] = shift_down(w8, 1)
                stot[:, lanes[k]] = w8[SUB - 1 : SUB, :]
            for g in range(0, N, ng):
                rr = [
                    [jnp.broadcast_to(rates_s[g + n : g + n + 1, lanes[k]], (SUB, LANES)) for k in range(tg)]
                    for n in range(ng)
                ]

                def step_j(j, hs):
                    dts = [dt[row8(j), lanes[k]] + cl[row8(j), :] for k in range(tg)]
                    us = [u_s[row8(j), lanes[k]] for k in range(tg)]
                    new = []
                    for n in range(ng):
                        b = bx[row8(j * N + g + n), :]
                        for k in range(tg):
                            new.append(jnp.exp2(dts[k] * rr[n][k]) * hs[n * tg + k] + us[k] * b)
                    return tuple(new)

                hs = lax.fori_loop(
                    0, J, step_j, tuple(jnp.zeros((SUB, LANES), F32) for _ in range(ng * tg)), unroll=2
                )
                for n in range(ng):
                    for k in range(tg):
                        h = hs[n * tg + k]
                        w1, w2, w4 = wins[k]
                        r = rr[n][k]
                        h = h + jnp.exp2(r * w1) * shift_down(h, 1)
                        h = h + jnp.exp2(r * w2) * shift_down(h, 2)
                        h = h + jnp.exp2(r * w4) * shift_down(h, 4)
                        pre_s[(g + n) * SUB : (g + n + 1) * SUB, lanes[k]] = shift_down(h, 1)
                        hd[g + n : g + n + 1, lanes[k]] = h[SUB - 1 : SUB, :]
            return carry

        third = DI // wide // 3
        lax.fori_loop(0, third, chunk_block, 0)
        progress(3)
        lax.fori_loop(third, 2 * third, chunk_block, 0)
        progress(3)
        lax.fori_loop(2 * third, DI // wide, chunk_block, 0)
        hdev[...] = hd[...].astype(BF16)
        h_moves = [remote(hdev, h_all.at[s], h_s.at[0, k], h_r.at[0, k], {"seq": p}) for k, p in enumerate(seqs)]
        h_moves += [remote(stot, s_all.at[s], h_s.at[1, k], h_r.at[1, k], {"seq": p}) for k, p in enumerate(seqs)]
        for c in h_moves:
            c.start()
        h_all[s] = hdev[...]
        s_all[s] = stot[...]
        for c in cot_moves:
            c.start()
        progress(len(queue))
        if plane:
            parts[3].landed()

        def gate_block(i, carry):
            C = at_cols(i, cb)
            gate[:, C] = mm(nrm[0:T, :], wg[:, C])
            return carry

        lax.fori_loop(0, DI // cb, gate_block, 0)
        if plane:
            parts[4].landed()
        outs = [
            pltpu.make_async_copy(wc, win_o.at[:, 0:DI], ld.at[7]),
            pltpu.make_async_copy(wg, win_o.at[:, DI : 2 * DI], ld.at[8]),
            pltpu.make_async_copy(wo, wout_o, ld.at[9]),
        ]
        for c in outs:
            c.start()
        for c in h_moves:
            c.wait()
        acc[...] = jnp.zeros_like(acc)

        def save(i):
            return pltpu.make_async_copy(
                st_v.at[i % 2], st_o.at[:, i * cs : (i + 1) * cs], ld.at[10 + i % 2]
            )

        for i in range(steps):
            if i >= 2:
                save(i - 2).wait()
            C = slice(i * cs, (i + 1) * cs)
            hin[...] = chain_states(
                S - 1, lambda k: k < s, lambda k: k, lambda k: s_all[k, :, C], lambda k: h_all[k, :, C],
                rates_s[:, C],
            )

            def pair(p, carry):
                lanes = [lanes_of(i, cs, p, tg, k) for k in range(tg)]
                near = [lane_at(p, tg, k) for k in range(tg)]
                for g in range(0, N, ng):
                    rr = [
                        [jnp.broadcast_to(rates_s[g + n : g + n + 1, lanes[k]], (SUB, LANES)) for k in range(tg)]
                        for n in range(ng)
                    ]
                    init = []
                    for n in range(ng):
                        for k in range(tg):
                            at = (g + n) * SUB
                            init.append(
                                pre_s[at : at + SUB, lanes[k]]
                                + jnp.exp2(rr[n][k] * dwin[:, lanes[k]])
                                * jnp.broadcast_to(hin[g + n : g + n + 1, near[k]], (SUB, LANES))
                            )

                    def keep(j, hs):
                        for n in range(0, ng, 2):
                            for k in range(tg):
                                two = jnp.concatenate([hs[n * tg + k], hs[(n + 1) * tg + k]], axis=0)
                                at = pl.multiple_of(j * N * SUB + (g + n) * SUB, 2 * SUB)
                                st_v[i % 2, pl.ds(at, 2 * SUB), near[k]] = two.astype(BF16)

                    keep(0, init)

                    def step_j(j, hs):
                        dts = [dt[row8(j), lanes[k]] + cl[row8(j), :] for k in range(tg)]
                        us = [u_s[row8(j), lanes[k]] for k in range(tg)]
                        if g == 0:
                            ys = [jnp.zeros((SUB, LANES), F32) for k in range(tg)]
                        else:
                            ys = [y[row8(j), lanes[k]] for k in range(tg)]
                        new = []
                        for n in range(ng):
                            b = bx[row8(j * N + g + n), :]
                            c = cx[row8(j * N + g + n), :]
                            for k in range(tg):
                                h = jnp.exp2(dts[k] * rr[n][k]) * hs[n * tg + k] + us[k] * b
                                ys[k] = ys[k] + h * c
                                new.append(h)
                        for k in range(tg):
                            y[row8(j), lanes[k]] = ys[k]
                        keep(j + 1, new)
                        return tuple(new)

                    lax.fori_loop(0, J, step_j, tuple(init), unroll=2)
                return carry

            lax.fori_loop(0, cs // wide, pair, 0)
            save(i).start()
            yv = y[:, C] + sm[SKIP : SKIP + 1, C] * sig[:, C].astype(F32)
            y[:, C] = yv
            g_in = gate[:, C]
            gated = (yv * (g_in * sigmoid(g_in))).astype(BF16)
            acc[...] += mm(gated, wo[C, :])

        m32 = tok[...].astype(F32) + acc[...]
        mid[...] = m32
        moe[...] = (m32 * rms_scale(m32) * gp[1:2, :]).astype(BF16)
        ch_o[...] = router_softmax(mm_nt(moe[...], rt[...]), E)
        outb[...] = mm_tn(table[...], moe[...]).astype(BF16)
        out_moves = [remote(block_of(outb, p), arr_o.at[core, me], d_s.at[k], d_r.at[k], {"exp": p}) for k, p in enumerate(zz)]
        for c in out_moves:
            c.start()
        arr_own = pltpu.make_async_copy(block_of(outb, me), arr_o.at[core, me], ld.at[12])
        arr_own.start()
        passes = [
            remote(block_of(cotb, me), cot_o.at[core, me], x_s.at[0, 0], x_r.at[0, 0], sib),
            remote(block_of(outb, me), arr_o.at[core, me], x_s.at[1, 0], x_r.at[1, 0], sib),
        ]
        for c in passes:
            c.start()
        for w, ref, send, recv in ((0, cot_o, k_s, k_r), (1, arr_o, d_s, d_r)):
            for k in range(1, E):
                frm = lax.rem(me + E - k, E)
                at = ref.at[core, frm]
                remote(at, at, send.at[k - 1], recv.at[k - 1], {"exp": frm}).wait_recv()
                c = remote(at, at, x_s.at[w, k], x_r.at[w, k], sib)
                c.start()
                passes.append(c)
        if plane:
            for p in parts:
                p.finish()
        for c in outs + [cot_own, arr_own]:
            c.wait()
        for i in range(max(0, steps - 2), steps):
            save(i).wait()
        for c in cot_moves + out_moves + passes:
            c.wait_send()
        for w, ref in ((0, cot_o), (1, arr_o)):
            for k in range(E):
                at = ref.at[1 - core, lax.rem(me + E - k, E)]
                remote(at, at, x_s.at[w, k], x_r.at[w, k], sib).wait_recv()

    v = pltpu.VMEM
    sem = lambda *dims: pltpu.SemaphoreType.DMA(dims)
    vm = pl.BlockSpec(memory_space=pltpu.VMEM)
    zslots = 2 * (E - 1)
    ins = (tokens, cotangent, seg, route) + tuple(params) + (in_proj, out_proj)
    vm_outs = [
        sds((z.SMALL, DI), F32), sds((gr, D), F32), sds((LANES, D), BF16), sds((T, M), BF16), sds((T, LANES), F32),
        sds((T, SUB), F32), sds((T, DI), F32), sds((H, DI), F32), sds((T, DI), F32), sds((T, DI), BF16),
        sds((T, z.XW), F32), sds((T, DI), F32), sds((T, DI), F32), sds((T, D), F32), sds((T, D), BF16),
        sds((T, LANES), F32), sds((S, 1, DI), F32), sds((T, D), BF16), sds((T, D), BF16), sds((T, D), BF16),
    ]
    any_outs = [
        sds((ST, DI), BF16), sds((D, 2 * DI), BF16), sds((DI, D), BF16), sds((2, E, CAP, D), BF16),
        sds((2, E, CAP, D), BF16),
    ]
    return pl.pallas_call(
        body,
        name="forward",
        in_specs=[vm] * 4 + [vm if plane else ANY] * len(params) + [ANY] * 2,
        out_specs=[vm] * len(vm_outs) + [ANY] * len(any_outs),
        out_shape=vm_outs + any_outs,
        scratch_shapes=[
            v((D, DI), BF16), v((D, DI), BF16), v((DI, D), BF16), v((E * rs, DZ), BF16), v((E * rg, NZ), BF16),
            v((T + H, D), BF16), v((H, D), BF16), v((SUB, LANES), F32),
            v((J * N * SUB, LANES), F32), v((J * N * SUB, LANES), F32), v((T, LANES), F32), v((T, DI), F32),
            v((N, DI), F32), v((N, DI), F32), v((N, DI), BF16), v((1, DI), F32), v((S, N, DI), BF16),
            v((N * SUB, DI), F32), v((SUB, DI), F32), v((N, cs), F32),
            v((2, ST, cs), BF16), v((T, D), F32), v((M, D), BF16), v((M, D), BF16),
            v((rs, DZ), BF16), v((rg, NZ), BF16), v((SUB, T), F32),
            sem(13), sem(5, 2, zslots), sem(5, 2, zslots), sem(5, 4, zslots), sem(5, 4, zslots),
            sem(5, 5, zslots), sem(5, 5, zslots), sem(2), sem(2), sem(2, S - 1), sem(2, S - 1),
            sem(E - 1), sem(E - 1), sem(1), sem(1), sem(E - 1), sem(E - 1),
            sem(2, E), sem(2, E),
        ],
        compiler_params=pltpu.CompilerParams(
            collective_id=cid, has_side_effects=True, vmem_limit_bytes=60 * 1024 * 1024
        ),
    )(*ins)


def backward(z, S, plane, expert_out, dx_z, dwu, dwd, states, w_out, w_in, table, choose, chances, mid, moe, cot, gpack,
             router, gate, y, sig, small, mixed, dt, masks, conv_in, hconv, s_all, tok, normed_all, cid):
    T, D, DI, N, J, E, CAP = z.T, z.D, z.DI, z.N, z.J, z.E, z.CAP
    M = E * CAP
    G = gpack.shape[0]
    H = hconv.shape[0]
    DZ, NZ = DI // E, D // E
    cb_m = pick(DI, (384, 256, 128))
    cb_s = pick(DI, (256, 128))
    steps_s = DI // cb_s
    tg_s = tile_groups(cb_s)
    ng_s = 4
    uq, uc = dwu.shape[0] // 4, dwu.shape[1]
    dq, dc = dwd.shape[0] // 4, dwd.shape[1]
    ST = (J + 1) * N * SUB
    rows_big = max(ST, 2 * D)
    chain_slots = 2 * (E - 1)

    def body(
        eo, dwu, dwd, states, w_out, w_in, dx_z, table, choose, chances, mid, moe, cot, gp, router, gate, y, sig,
        small, mixed, dt, masks, conv_in, hconv, s_all, tok, nall,
        tg_o, gs_o, gg_o, back_o, pg_o, pc_o, pm_o, po_o, up_o, down_o,
        own_v, big, wo_v, n_v, yg, gi, gz, br, mg, fdev, f_all, suf, cg_edge,
        edge_in, pc, bx, cx, ia, oa, cl, u_s, rates_s, fin, dg_s, rs_s, rt_s, low_s, mxg, fd,
        ua, ub, ub2, da, db, db2, gi_all, pc_all, br_all, gz_all, gi_b,
        p_g, p_c, p_m, p_o, bg, bc, bm, bo, tg_, tc_, tm_, to_, zg, zc, zm,
        pcs, pcr, pqs, pqr, pzs, pzr, pgs, pgr, pfs, pfr, pown,
        ld, oz_s, oz_r, f_s, f_r, e_s, e_r, g_s, g_r, p_s, p_r, b_s, b_r, a_s, a_r, x_s, x_r,
    ):
        psems = lambda a: (
            pcs.at[a], pcr.at[a], pqs.at[a], pqr.at[a], pzs.at[a], pzr.at[a], pgs.at[a], pgr.at[a], pfs.at[a],
            pfr.at[a], pown.at[a],
        )
        extra = lambda rows: (16 * (rows // 128), -(-(rows // 16 % 8) // 2) if rows // 16 % 8 else 4)
        sum_g = PlaneSum(E, p_g, bg, tg_, zg, pg_o, False, *extra(NZ), psems(0))
        sum_c = PlaneSum(E, p_c, bc, tc_, zc, pc_o, False, *extra(NZ), psems(1))
        sum_m = PlaneSum(E, p_m, bm, tm_, zm, pm_o, True, 0, 4, psems(2))
        sum_o = PlaneSum(E, p_o, bo, to_, None, po_o, False, *extra(DZ), psems(3))
        stage = (lambda f: f()) if plane else (lambda f: None)
        s, me = lax.axis_index("seq"), lax.axis_index("exp")
        core = lax.rem(s, 2)
        other = 1 - core
        sib = {"seq": s + 1 - 2 * core}
        seqs = [lax.rem(s + k, S) for k in range(1, S)]
        zs = [lax.rem(me + k, E) for k in range(1, E)]
        greet([{"seq": p} for p in seqs] + [{"exp": p} for p in zs])

        def remote(src, dst, send, recv, to):
            return pltpu.make_async_remote_copy(src, dst, send, recv, device_id=to, device_id_type=MESH)

        def out_load(i):
            slot = lax.rem(i, 2)
            rows = pl.ds(pl.multiple_of(i * cb_m, LANES), cb_m)
            return pltpu.make_async_copy(w_out.at[rows], wo_v.at[slot], ld.at[2 + 15 * slot])

        out_load(0).start()
        normed_load = pltpu.make_async_copy(nall, n_v, ld.at[10])
        normed_load.start()

        def state_load(i):
            return pltpu.make_async_copy(
                states.at[:, at_cols(i, cb_s)], big.at[lax.rem(i, 2), 0:ST], ld.at[3 + lax.rem(i, 2)]
            )

        state_load(0).start()
        if plane:
            chip = s // 2
            xx, yy = lax.rem(chip, 2), chip // 2
            to_x = {"seq": s + 2 - 4 * xx}
            to_y = {"seq": s + 4 - 8 * yy}
            u4 = lambda ref, v, w: ref.at[pl.ds(pl.multiple_of((2 * v + w) * uq, 16), uq)]
            up1 = [
                remote(u4(dwu, v, 1 - xx), ub.at[v], a_s.at[v], a_r.at[v], to_x) for v in range(2)
            ]
            d_half = lambda v: pl.ds(pl.multiple_of(v * 2 * dq, 16), 2 * dq)
            down1 = remote(dwd.at[d_half(1 - yy)], db, a_s.at[2], a_r.at[2], to_y)
            for c in up1 + [down1]:
                c.start()
            mine = [pltpu.make_async_copy(u4(dwu, v, xx), ua.at[v], ld.at[5 + v]) for v in range(2)]
            mine.append(pltpu.make_async_copy(dwd.at[d_half(yy)], da, ld.at[7]))
            for c in mine:
                c.start()

        adds = lambda a, b: (a.astype(F32) + b.astype(F32)).astype(BF16)
        block_of = lambda ref, p: ref.at[pl.ds(pl.multiple_of(p * CAP, 16), CAP)]
        out_moves = [
            remote(block_of(eo, p), block_of(back_o, me), oz_s.at[k], oz_r.at[k], {"exp": p}) for k, p in enumerate(zs)
        ]
        for c in out_moves:
            c.start()
        back_load = pltpu.make_async_copy(block_of(eo, me), own_v, ld.at[8])
        back_own = pltpu.make_async_copy(own_v, block_of(back_o, me), ld.at[8])
        back_load.start()
        expand_columns(z, mixed, z.R, bx)
        expand_columns(z, mixed, z.R + N, cx)
        expand_closed(z, masks, cl)

        back = mm(table[...], dx_z[...])
        grad = cot[...].astype(F32)
        ch = chances[...]
        pick_e = choose[...]
        gating = jnp.sum(ch * pick_e, axis=-1, keepdims=True)
        gate_grad = back[:, D : D + 1] + back[:, D + 1 : D + 2]
        lg = ch * (gate_grad * pick_e - gate_grad * gating)
        hi, lo = split_hi_lo(lg)
        rtv = router[...]
        mig = back[:, 0:D] + mm(hi, rtv) + mm(lo, rtv)
        mev = moe[...]
        rg = mm_tn(hi, mev) + mm_tn(lo, mev)
        d, gain_g = rms_back(mid[...], gp[1:2, :], mig)
        mg[...] = grad + d
        br[...] = mg[...].astype(BF16)
        gg_o[...] = jnp.zeros_like(gg_o)
        gg_o[1:2, :] = gain_g
        gg_o[2 : 2 + E, :] = rg[0:E, :]
        chain_b = Chain(E, br, br_all, b_s, b_r, ld.at[9])

        def middle_block(i, carry):
            C = at_cols(i, cb_m)
            out_load(i).wait()

            @pl.when(i + 1 < DI // cb_m)
            def _():
                out_load(i + 1).start()

            gg = mm_nt(br[...], wo_v[lax.rem(i, 2)])
            g_in = gate[:, C]
            sg = sigmoid(g_in)
            act = g_in * sg
            yv = y[:, C]
            ygv = gg * act
            yg[:, C] = ygv
            gi[:, C] = (gg * yv * (sg * (1.0 + g_in * (1.0 - sg)))).astype(BF16)
            pc[:, C] = (yv * act).astype(BF16)
            gs_o[SKIP : SKIP + 1, C] = jnp.sum(ygv * sig[:, C].astype(F32), axis=0, keepdims=True)
            return carry

        lax.fori_loop(0, DI // cb_m, middle_block, 0)
        for e in range(E):
            gi_b[e] = gi[:, e * DZ : (e + 1) * DZ]

        def trade(src, dst, send, recv):
            return [remote(src.at[p], dst.at[me], send.at[k], recv.at[k], {"exp": p}) for k, p in enumerate(zs)]

        gi_moves = trade(gi_b, gi_all, g_s, g_r)
        for c in gi_moves:
            c.start()
        gi_all[me] = gi_b[me]
        chain_b.start()
        back_load.wait()
        back_own.start()

        tg, ng = 2 if DI % 256 == 0 else 1, 8
        wide = tg * LANES

        def flow_block(i, carry):
            lanes = [pl.ds(pl.multiple_of(i * wide, LANES) + k * LANES, LANES) for k in range(tg)]
            both = pl.ds(pl.multiple_of(i * wide, LANES), wide)
            rates = -jnp.exp(small[A_LOG : A_LOG + N, both]) * LOG2E
            wins = []
            for k in range(tg):
                w1 = jnp.zeros((SUB, LANES), F32)
                for j in range(J):
                    w1 = w1 + (dt[j * SUB : j * SUB + SUB, lanes[k]] + cl[j * SUB : j * SUB + SUB, :])
                w2 = w1 + shift_up(w1, 1)
                w4 = w2 + shift_up(w2, 2)
                w8 = w4 + shift_up(w4, 4)
                wins.append((w1, w2, w4))
                suf[N * SUB : (N + 1) * SUB, lanes[k]] = shift_up(w8, 1)
            for g in range(0, N, ng):
                rr = [
                    [
                        jnp.broadcast_to(rates[g + n : g + n + 1, k * LANES : (k + 1) * LANES], (SUB, LANES))
                        for k in range(tg)
                    ]
                    for n in range(ng)
                ]

                def step_j(jj, fs):
                    j = J - 1 - jj
                    dts = [dt[row8(j), lanes[k]] + cl[row8(j), :] for k in range(tg)]
                    ygs = [yg[row8(j), lanes[k]] for k in range(tg)]
                    new = []
                    for n in range(ng):
                        c = cx[row8(j * N + g + n), :]
                        for k in range(tg):
                            new.append(jnp.exp2(dts[k] * rr[n][k]) * (fs[n * tg + k] + ygs[k] * c))
                    return tuple(new)

                fs = lax.fori_loop(
                    0, J, step_j, tuple(jnp.zeros((SUB, LANES), F32) for _ in range(ng * tg)), unroll=2
                )
                for n in range(ng):
                    for k in range(tg):
                        f = fs[n * tg + k]
                        w1, w2, w4 = wins[k]
                        r = rr[n][k]
                        f = f + jnp.exp2(r * w1) * shift_up(f, 1)
                        f = f + jnp.exp2(r * w2) * shift_up(f, 2)
                        f = f + jnp.exp2(r * w4) * shift_up(f, 4)
                        suf[(g + n) * SUB : (g + n + 1) * SUB, lanes[k]] = shift_up(f, 1)
                        fd[g + n : g + n + 1, lanes[k]] = f[0:1, :]
            return carry

        lax.fori_loop(0, DI // wide, flow_block, 0)
        fdev[...] = fd[...].astype(BF16)
        f_moves = [
            remote(fdev, f_all.at[s], f_s.at[k], f_r.at[k], {"seq": p}) for k, p in enumerate(seqs)
        ]
        for c in f_moves:
            c.start()
        f_all[s] = fdev[...]
        for e in range(E):
            gz[e] = pc[:, e * DZ : (e + 1) * DZ]
        gz_moves = trade(gz, gz_all, x_s, x_r)
        for c in gz_moves:
            c.start()
        gz_all[me] = gz[me]
        p_g[...] = jnp.zeros_like(p_g)
        p_c[...] = jnp.zeros_like(p_c)
        p_o[...] = jnp.zeros_like(p_o)

        def place_in(dst, rhs):
            blk = pick(D, (384, 256, 128))
            for i in range(D // blk):
                val = mm_tn(n_v[:, i * blk : (i + 1) * blk], rhs)
                for g in range(blk // 16):
                    row = i * blk + 16 * g
                    chunk, off = group_place(D // E // 16, row % (D // E) // 16)
                    dst[row // (D // E), chunk // 2, chunk % 2, off : off + 16, :] = val[16 * g : 16 * g + 16].astype(
                        BF16
                    )

        flat = lambda ref: ref[...].reshape(E * T, ref.shape[-1])
        if plane:
            for c in mine + up1 + [down1]:
                c.wait()
            ua[...] = adds(ua[...], ub[...])
            da[...] = adds(da[...], db[...])
            up2 = remote(ua.at[1 - yy], ub2, a_s.at[3], a_r.at[3], to_y)
            down2 = remote(
                da.at[pl.ds(pl.multiple_of((1 - xx) * dq, 16), dq)], db2, a_s.at[4], a_r.at[4], to_x
            )
            up2.start()
            down2.start()
        for c in f_moves:
            c.wait()

        ia[...] = jnp.zeros_like(ia)
        oa[...] = jnp.zeros_like(oa)
        low_s[...] = jnp.zeros_like(low_s)
        low = mixed[:, 0 : z.R].astype(BF16)

        def scan_block(i, carry_):
            state_load(i).wait()

            @pl.when(i + 1 < steps_s)
            def _():
                state_load(i + 1).start()

            slot = lax.rem(i, 2)
            C = at_cols(i, cb_s)
            rates2 = -jnp.exp(small[A_LOG : A_LOG + N, C]) * LOG2E
            rates_s[...] = rates2
            fin[...] = chain_states(
                S - 1, lambda k: k > s, lambda k: S - 1 - k, lambda k: s_all[k, :, C], lambda k: f_all[k, :, C],
                rates2,
            )
            sigf = sig[:, C].astype(F32)
            u_s[...] = dt[:, C] * sigf

            def pair(p, carry):
                lanes = [lanes_of(i, cb_s, p, tg_s, k) for k in range(tg_s)]
                near = [slice(k * LANES, (k + 1) * LANES) for k in range(tg_s)]
                for g in range(0, N, ng_s):
                    rr = [
                        [
                            jnp.broadcast_to(rates_s[g + n : g + n + 1, near[k]], (SUB, LANES))
                            for k in range(tg_s)
                        ]
                        for n in range(ng_s)
                    ]
                    flow = []
                    for n in range(ng_s):
                        for k in range(tg_s):
                            at = (g + n) * SUB
                            flow.append(
                                suf[at : at + SUB, lanes[k]]
                                + jnp.exp2(rr[n][k] * suf[N * SUB : (N + 1) * SUB, lanes[k]])
                                * jnp.broadcast_to(fin[g + n : g + n + 1, near[k]], (SUB, LANES))
                            )

                    def load(j):
                        got = [[None] * tg_s for _ in range(ng_s)]
                        for n in range(0, ng_s, 2):
                            for k in range(tg_s):
                                at = pl.multiple_of(j * N * SUB + (g + n) * SUB, 2 * SUB)
                                two = big[slot, pl.ds(at, 2 * SUB), near[k]].astype(F32)
                                got[n][k] = two[0:SUB]
                                got[n + 1][k] = two[SUB : 2 * SUB]
                        return [got[n][k] for n in range(ng_s) for k in range(tg_s)]

                    def step_j(jj, carry):
                        fs, hs, rts = carry
                        j = J - 1 - jj
                        dtp = [dt[row8(j), lanes[k]] for k in range(tg_s)]
                        dts = [dtp[k] + cl[row8(j), :] for k in range(tg_s)]
                        us = [u_s[row8(j), near[k]] for k in range(tg_s)]
                        ygs = [yg[row8(j), lanes[k]] for k in range(tg_s)]
                        before = load(j)
                        if g == 0:
                            dgs = [jnp.zeros((SUB, LANES), F32) for k in range(tg_s)]
                            rss = [jnp.zeros((SUB, LANES), F32) for k in range(tg_s)]
                        else:
                            dgs = [dg_s[row8(j), near[k]] for k in range(tg_s)]
                            rss = [rs_s[row8(j), near[k]] for k in range(tg_s)]
                        nf, nr = [], []
                        for n in range(ng_s):
                            at = row8(j * N + g + n)
                            b = bx[at, :]
                            c = cx[at, :]
                            ig = jnp.zeros((SUB, LANES), F32)
                            og = jnp.zeros((SUB, LANES), F32)
                            for k in range(tg_s):
                                q = n * tg_s + k
                                gr = ygs[k] * c + fs[q]
                                f = jnp.exp2(dts[k] * rr[n][k]) * gr
                                rt = f * before[q]
                                rss[k] = rss[k] + rt * rr[n][k]
                                dgs[k] = dgs[k] + gr * b
                                nr.append(rts[q] + rt * dtp[k])
                                ig = ig + gr * us[k]
                                og = og + hs[q] * ygs[k]
                                nf.append(f)
                            ia[at, :] += ig
                            oa[at, :] += og
                        for k in range(tg_s):
                            dg_s[row8(j), near[k]] = dgs[k]
                            rs_s[row8(j), near[k]] = rss[k]
                        return tuple(nf), tuple(before), tuple(nr)

                    zero = tuple(jnp.zeros((SUB, LANES), F32) for _ in range(ng_s * tg_s))
                    _, _, rts = lax.fori_loop(
                        0, J, step_j, (tuple(flow), tuple(load(J)), zero), unroll=2
                    )
                    for n in range(ng_s):
                        for k in range(tg_s):
                            rt_s[g + n : g + n + 1, near[k]] = jnp.sum(rts[n * tg_s + k], axis=0, keepdims=True)
                return carry

            pair(0, 0)
            dg = dg_s[...]
            yg[:, C] = dg * dt[:, C] + yg[:, C] * small[SKIP : SKIP + 1, C]
            step_grad = rs_s[...] * LN2 + dg * sigf
            dtw = small[z.DT0 : z.DT0 + z.R, C].astype(BF16)
            pre = mm(low, dtw) + small[DT_B : DT_B + 1, C]
            dpg = step_grad * sigmoid(pre)
            dpl = dpg.astype(BF16)
            gs_o[DT_B : DT_B + 1, C] = jnp.sum(dpg, axis=0, keepdims=True)
            gs_o[SKIP + 1 : SKIP + 2, C] = jnp.zeros((1, cb_s), F32)
            gs_o[A_LOG : A_LOG + N, C] = rt_s[...] * (rates2 * LN2)
            gs_o[z.DT0 : z.DT0 + z.R, C] = mm_tn(low, dpl)
            low_s[...] += mm_nt(dpl, dtw)
            return carry_

        third = steps_s // 3
        lax.fori_loop(0, third, scan_block, 0)
        chain_b.hop(1)
        for c in gi_moves:
            c.wait()
        normed_load.wait()
        place_in(p_g, flat(gi_all))
        stage(sum_g.swap_start)
        lax.fori_loop(third, 2 * third, scan_block, 0)
        stage(sum_g.swap_finish)
        chain_b.hop(2)
        lax.fori_loop(2 * third, steps_s, scan_block, 0)
        for k in range(3, E):
            chain_b.hop(k)
        stage(sum_g.chips_finish)

        mxg[:, 0 : z.R] = low_s[...].astype(BF16)
        lane = lax.broadcasted_iota(jnp.int32, (SUB, LANES), 1)

        def gather(j, carry):
            both = jnp.zeros((SUB, LANES), F32)
            for n in range(N):
                at = row8(j * N + n)
                both = jnp.where(lane == n, jnp.sum(ia[at, :], axis=1, keepdims=True), both)
                both = jnp.where(lane == N + n, jnp.sum(oa[at, :], axis=1, keepdims=True), both)
            cl[row8(j), :] = both
            return carry

        lax.fori_loop(0, J, gather, 0)
        mxg[:, z.R : z.R + 2 * N] = cl[:, 0 : 2 * N].astype(BF16)

        def weight_load(i):
            return [
                pltpu.make_async_copy(
                    w_in.at[:, pl.ds(pl.multiple_of(h * DI + i * cb_s, LANES), cb_s)],
                    big.at[lax.rem(i, 2), h * D : (h + 1) * D],
                    ld.at[12 + 2 * lax.rem(i, 2) + h],
                )
                for h in range(2)
            ]

        for c in weight_load(0):
            c.start()

        def conv_block(i, carry):
            C = at_cols(i, cb_m)
            mgv = mxg[...]
            sgv = sig[:, C]
            xw = small[z.X0 : z.X0 + z.XW, C].astype(BF16)
            gs_o[z.X0 : z.X0 + z.XW, C] = mm_tn(mgv, sgv)
            sgrad = yg[:, C] + mm(mgv, xw)
            xpad = padded_rows(conv_in[:, C], hconv[:, C], J, cb_m)
            valid = [jnp.broadcast_to(masks[:, o : o + 1], (T, cb_m)) for o in range(4)]
            out = jnp.broadcast_to(small[CONV_B : CONV_B + 1, C], (T, cb_m))
            for o in range(4):
                w = small[CONV_W + o : CONV_W + o + 1, C]
                out = out + w * xpad[o : o + J].reshape(T, cb_m) * valid[o]
            sv = sigmoid(out)
            cg = sgrad * (sv * (1.0 + out * (1.0 - sv)))
            gs_o[CONV_B : CONV_B + 1, C] = jnp.sum(cg, axis=0, keepdims=True)
            total = jnp.zeros((J, SUB, cb_m), F32)
            final = lax.broadcasted_iota(jnp.int32, (SUB, cb_m), 0) == SUB - 1
            edges = [jnp.zeros((1, cb_m), F32) for _ in range(3)]
            for o in range(4):
                masked = cg * valid[o]
                gs_o[CONV_W + o : CONV_W + o + 1, C] = jnp.sum(
                    masked * xpad[o : o + J].reshape(T, cb_m), axis=0, keepdims=True
                )
                c3 = (small[CONV_W + o : CONV_W + o + 1, C] * masked).reshape(J, SUB, cb_m)
                k = 3 - o
                if k == 0:
                    total = total + c3
                else:
                    wrap = jnp.stack(
                        [jnp.where(final, 0.0, pltpu.roll(c3[t], SUB - 1, 0)) for t in range(k)]
                    )
                    total = total + jnp.concatenate([c3[k:], wrap], axis=0)
                    for i2 in range(o, 3):
                        edges[i2] = edges[i2] + c3[i2 - o, 0:1, :]
            yg[:, C] = total.reshape(T, cb_m)
            cg_edge[:, C] = jnp.concatenate(edges + [jnp.zeros((SUB - 3, cb_m), F32)], axis=0)
            return carry

        lax.fori_loop(0, DI // cb_m, conv_block, 0)
        back_edge = remote(cg_edge, edge_in, e_s, e_r, {"seq": lax.rem(s + S - 1, S)})
        back_edge.start()
        if plane:
            up2.wait()
            down2.wait()
            ub2[...] = adds(ua[yy], ub2[...])
            half_u = uq // 2
            rows_u = lambda c: pl.ds(pl.multiple_of(c * half_u, 16), half_u)
            up3 = remote(ub2.at[rows_u(other)], up_o.at[core], a_s.at[5], a_r.at[5], sib)
            up3.start()
            up_own = pltpu.make_async_copy(ub2.at[rows_u(core)], up_o.at[core], ld.at[16])
            up_own.start()
            db2[...] = adds(da[pl.ds(pl.multiple_of(xx * dq, 16), dq), :], db2[...])
            down_own = pltpu.make_async_copy(db2, down_o, ld.at[11])
            down_own.start()
        for c in gz_moves:
            c.wait()
        chain_b.local().wait()
        groups_o = DZ // 16
        bra = flat(br_all)
        for i in range(2):
            half_o = slice(i * (DZ // 2), (i + 1) * (DZ // 2))
            val = mm_tn(flat(gz_all)[:, half_o], bra)
            for g in range(DZ // 32):
                chunk, off = group_place(groups_o, i * (DZ // 32) + g)
                p_o[0, chunk // 2, chunk % 2, off : off + 16, :] = val[16 * g : 16 * g + 16].astype(BF16)
        stage(sum_o.swap_start)
        stage(sum_g.z_finish)
        back_edge.wait()
        live = jnp.where(s < S - 1, 1.0, 0.0)

        def fix_block(i, carry):
            C = at_cols(i, cb_m)
            c3 = yg[:, C].reshape(J, SUB, cb_m)
            final = lax.broadcasted_iota(jnp.int32, (SUB, cb_m), 0) == SUB - 1
            fixed = jnp.stack(
                [
                    c3[J - 3 + k]
                    + jnp.where(final, jnp.broadcast_to(edge_in[k : k + 1, C] * live, (SUB, cb_m)), 0.0)
                    for k in range(3)
                ]
            )
            pc[:, C] = jnp.concatenate([c3[: J - 3], fixed], axis=0).reshape(T, cb_m).astype(BF16)
            return carry

        lax.fori_loop(0, DI // cb_m, fix_block, 0)
        for e in range(E):
            gi_b[e] = pc[:, e * DZ : (e + 1) * DZ]
        pc_moves = trade(gi_b, pc_all, p_s, p_r)
        for c in pc_moves:
            c.start()
        pc_all[me] = gi_b[me]
        stage(sum_o.swap_finish)
        tg_o[...] = jnp.zeros_like(tg_o)

        def token_block(i, carry):
            for c in weight_load(i):
                c.wait()

            @pl.when(i + 1 < steps_s)
            def _():
                for c in weight_load(i + 1):
                    c.start()

            slot = lax.rem(i, 2)
            C = at_cols(i, cb_s)
            tg_o[...] += mm_nt(pc[:, C], big[slot, 0:D, :]) + mm_nt(gi[:, C], big[slot, D : 2 * D, :])
            return carry

        lax.fori_loop(0, steps_s, token_block, 0)
        d, gain_g = rms_back(tok[...].astype(F32), gp[0:1, :], tg_o[...])
        tg_o[...] = mg[...] + d
        gg_o[0:1, :] = gain_g
        cr = p_m.shape[3]
        for e in range(E):
            side = jnp.concatenate([gg_o[:, e * NZ : (e + 1) * NZ], jnp.zeros((G, DZ - NZ), F32)], axis=1)
            rows = [gs_o[:, e * DZ : (e + 1) * DZ], side, jnp.zeros((8 * cr - z.SMALL - G, DZ), F32)]
            p_m[e] = jnp.concatenate(rows, axis=0).astype(BF16).reshape(4, 2, cr, DZ)
        stage(sum_m.swap_start)
        for c in pc_moves:
            c.wait()
        place_in(p_c, flat(pc_all))
        stage(sum_c.swap_start)
        stage(sum_m.swap_finish)
        stage(sum_o.chips_finish)
        stage(sum_c.swap_finish)
        stage(sum_m.chips_finish)
        stage(sum_g.forward)
        stage(sum_c.chips_finish)
        stage(sum_m.z_finish)
        stage(sum_o.forward)
        stage(sum_c.z_finish)
        for c in out_moves:
            c.wait()
        back_own.wait()
        if plane:
            up3.wait()
            up_own.wait()
            down_own.wait()
            sum_m.forward()
            sum_c.forward()
            for sm_ in (sum_g, sum_o, sum_m, sum_c):
                sm_.finish()
        else:
            copies = [
                pltpu.make_async_copy(p, o, pown.at[a])
                for a, (p, o) in enumerate(((p_g, pg_o), (p_c, pc_o), (p_m, pm_o), (p_o, po_o)))
            ]
            for c in copies:
                c.start()
            for c in copies:
                c.wait()
        for k in range(E - 1):
            for d in (-k, k) if k else (0,):
                chain_b.each(d, lambda c: c.wait_send())

    v = pltpu.VMEM
    sem = lambda *dims: pltpu.SemaphoreType.DMA(dims)
    vm = pl.BlockSpec(memory_space=pltpu.VMEM)
    up_shape = (2, uq // 2, uc) if plane else (1, 16, LANES)
    down_shape = (dq, dc) if plane else (16, LANES)
    u_shape = (2, uq, uc) if plane else (2, 16, LANES)
    d_shape = (2 * dq, dc) if plane else (32, LANES)
    ins = (expert_out, dwu, dwd, states, w_out, w_in, dx_z, table, choose, chances, mid, moe, cot, gpack, router, gate, y,
           sig, small, mixed, dt, masks, conv_in, hconv, s_all, tok, normed_all)
    rg, ro, rm = chunk_rows(NZ), chunk_rows(DZ), 16 * -(-(z.SMALL + G) // 128)
    p_shapes = [(E, 4, 2, rg, DZ), (E, 4, 2, rg, DZ), (E, 4, 2, rm, DZ), (1, 4, 2, ro, D)]
    o_shapes = [(4, 2, E, rg, DZ)] * 2 + [(4, 2, rm, DZ), (4, 2, 1, ro, D)] if plane else p_shapes
    return pl.pallas_call(
        body,
        name="backward",
        in_specs=[ANY] * 6 + [vm] * (len(ins) - 7) + [ANY],
        out_specs=[vm] * 3 + [ANY] * 7,
        out_shape=[
            sds((T, D), F32),
            sds((z.SMALL, DI), F32),
            sds((G, D), F32),
            sds((M, D), BF16),
        ]
        + [sds(o, BF16) for o in o_shapes]
        + [
            sds(up_shape, BF16),
            sds(down_shape, BF16),
        ],
        scratch_shapes=[
            v((CAP, D), BF16),
            v((2, rows_big, cb_s), BF16),
            v((2, cb_m, D), BF16), v((E * T, D), BF16),
            v((T, DI), F32), v((T, DI), BF16), v((E, T, DZ), BF16),
            v((T, D), BF16), v((T, D), F32),
            v((N, DI), BF16), v((S, N, DI), BF16), v(((N + 1) * SUB, DI), F32),
            v((SUB, DI), F32), v((SUB, DI), F32),
            v((T, DI), BF16),
            v((J * N * SUB, LANES), F32), v((J * N * SUB, LANES), F32),
            v((J * N * SUB, LANES), F32), v((J * N * SUB, LANES), F32),
            v((T, LANES), F32), v((T, cb_s), F32), v((N, cb_s), F32), v((N, cb_s), F32),
            v((T, cb_s), F32), v((T, cb_s), F32), v((N, cb_s), F32), v((T, z.R), F32), v((T, z.XW), BF16),
            v((N, DI), F32),
            v(u_shape, BF16), v(u_shape, BF16), v(u_shape[1:], BF16),
            v(d_shape, BF16), v(d_shape, BF16), v((d_shape[0] // 2, d_shape[1]), BF16),
            v((E, T, DZ), BF16), v((E, T, DZ), BF16), v((E, T, D), BF16), v((E, T, DZ), BF16),
            v((E, T, DZ), BF16),
        ]
        + [v(p, BF16) for p in p_shapes]
        + [v((p[0], 4) + p[3:], BF16) for p in p_shapes]
        + [v((3, p[0]) + p[3:], BF16) for p in p_shapes]
        + [v((E,) + p[3:], BF16) for p in p_shapes[:3]]
        + [
            sem(4, 2), sem(4, 2), sem(4, 3, 2), sem(4, 3, 2), sem(4, E - 1, 2), sem(4, E - 1, 2), sem(4, 3, 2),
            sem(4, 3, 2), sem(4, 4, 2), sem(4, 4, 2), sem(4),
            sem(18), sem(E - 1), sem(E - 1), sem(S - 1), sem(S - 1),
            pltpu.SemaphoreType.DMA, pltpu.SemaphoreType.DMA,
            sem(E - 1), sem(E - 1), sem(E - 1), sem(E - 1), sem(chain_slots), sem(chain_slots),
            sem(6), sem(6), sem(E - 1), sem(E - 1),
        ],
        compiler_params=pltpu.CompilerParams(
            collective_id=cid, has_side_effects=True, vmem_limit_bytes=60 * 1024 * 1024
        ),
    )(*ins)


def finish(z, gr, plane, pg, pc, pm, po, tg, mid, chances, choose, table, back, up, down):
    T, D, DI, N, J, E = z.T, z.D, z.DI, z.N, z.J, z.E
    DZ, NZ, FB = DI // E, D // E, z.FF // 8
    U = up.shape[1]

    def body(pg, pc, pm, po, tg, mid, ch, cho, tb, bk, up, dn, *outs):
        dwi, dwo, out, tgo, cw, cb, xw, dw, db, al, sk, na, nb, ro = outs[:14]
        for g in range(NZ // 16):
            chunk, off = group_place(NZ // 16, g)
            for h, src in enumerate((pc, pg)):
                for e in range(E):
                    dwi[16 * g : 16 * g + 16, h * DI + e * DZ : h * DI + (e + 1) * DZ] = src[
                        chunk, e, off : off + 16, :
                    ].astype(F32)
        for g in range(DZ // 16):
            chunk, off = group_place(DZ // 16, g)
            dwo[16 * g : 16 * g + 16, :] = po[chunk, off : off + 16, :].astype(F32)
        sm = pm[...].astype(F32)
        cw[...] = sm[CONV_W : CONV_W + 4]
        for ref, row in ((cb, CONV_B), (db, DT_B), (sk, SKIP)):
            ref[...] = sm[row : row + 1].reshape(DZ)
        al[...] = sm[A_LOG : A_LOG + N]
        dw[...] = sm[z.DT0 : z.X0]
        xw[...] = sm[z.X0 : z.SMALL]
        na[...] = sm[z.SMALL : z.SMALL + 1, 0:NZ].reshape(NZ)
        nb[...] = sm[z.SMALL + 1 : z.SMALL + 2, 0:NZ].reshape(NZ)
        ro[...] = sm[z.SMALL + 2 : z.SMALL + 2 + E, 0:NZ]
        lane = lax.broadcasted_iota(jnp.int32, (T, T), 1)
        prow = lax.broadcasted_iota(jnp.int32, (T, T), 0)
        order = (lane == (prow % SUB) * J + prow // SUB).astype(F32).astype(BF16)
        gating = jnp.sum(ch[...] * cho[...], axis=-1, keepdims=True)
        low = (mid[...] + gating * mm(tb[...], bk[...])).astype(BF16)
        out[...] = mm_tn(order, low).astype(BF16)
        v = tg[...]
        hi, rest = v.astype(BF16), v - v.astype(BF16).astype(F32)
        lo, end = split_hi_lo(rest)
        tgo[...] = mm_tn(order, hi) + (mm_tn(order, lo) + mm_tn(order, end))
        if plane:
            upo, dno = outs[14:]
            for c in range(2):
                for i in range(4):
                    at = (2 * i + c) * FB
                    upo[:, at : at + FB] = up[c, :, i * FB : (i + 1) * FB].astype(F32)
            dno[...] = dn[...].astype(F32)

    vm = pl.BlockSpec(memory_space=pltpu.VMEM)
    shapes = [
        sds((NZ, 2 * DI), F32), sds((DZ, D), F32), sds((T, D), BF16), sds((T, D), F32), sds((4, DZ), F32),
        sds((DZ,), F32), sds((z.XW, DZ), F32), sds((z.R, DZ), F32), sds((DZ,), F32), sds((N, DZ), F32),
        sds((DZ,), F32), sds((NZ,), F32), sds((NZ,), F32), sds((E, NZ), F32),
    ]
    if plane:
        shapes += [sds((U, z.FF), F32), sds(down.shape, F32)]
    return pl.pallas_call(
        body,
        name="finish",
        in_specs=[vm] * 12,
        out_specs=[vm] * len(shapes),
        out_shape=shapes,
        compiler_params=pltpu.CompilerParams(vmem_limit_bytes=VMEM_LIMIT),
    )(pg, pc, pm, po, tg, mid, chances, choose, table, back, up, down)


def on_device(
    tokens, segment_ids, routes, cotangent, norm_gain, in_proj, conv_weight, conv_bias, x_proj,
    dt_proj, dt_bias, a_log, d_skip, out_proj, moe_gain, router, up_proj, down_proj,
):
    E = lax.axis_size("exp")
    S = lax.axis_size("seq")
    z = Sizes(tokens, in_proj, dt_proj, x_proj, a_log, up_proj, E)
    T, D, DI, N, J, CAP = z.T, z.D, z.DI, z.N, z.J, z.CAP
    me_s, me_e = lax.axis_index("seq"), lax.axis_index("exp")
    core = lax.rem(me_s, 2)
    cw = dt_proj.shape[1]
    dw = norm_gain.shape[0]
    plane = S == 8 and dw % 32 == 0
    line = lambda v: v.reshape(1, -1)
    if plane:
        params = [conv_weight, conv_bias, dt_bias, d_skip, a_log, dt_proj, x_proj.T, norm_gain, moe_gain, router.T]
        w_in, w_out = in_proj, out_proj
    else:
        small_own = jnp.concatenate(
            [conv_weight, line(conv_bias), line(dt_bias), line(d_skip), jnp.zeros((1, cw), BF16), a_log, dt_proj,
             x_proj.T, jnp.zeros((small_rows(z) - z.SMALL, cw), BF16)], axis=0
        )
        g_own = jnp.concatenate(
            [line(norm_gain), line(moe_gain), router.T, jnp.zeros((32 - 2 - E, dw), BF16)], axis=0
        )
        gathered = [lax.all_gather(a, "exp", tiled=True) for a in (in_proj, out_proj, small_own, g_own)]
        w_in, w_out, params = gathered[0], gathered[1], gathered[2:]
    gr = 8 * -(-(2 + E) // 8)
    (
        small, gpack, router_t, table, choose_wide, masks, conv_in, hconv, gate, sig, mixed, dt, y, mid, moe, chances,
        s_all, tok, cot, normed, states, w_in, w_out, arrived, cot_pair,
    ) = forward(
        z, S, plane, tokens[0], cotangent[0], segment_ids, routes.reshape(1, T), params, w_in, w_out, gr, 1
    )
    dx_z, expert_out, dwu, dwd, normed_all = expert(
        z, arrived.reshape(2 * E * CAP, D), cot_pair.reshape(2 * E * CAP, D), router_t, normed, up_proj[0],
        down_proj[0], 3
    )
    token_grad, _, _, back_out, pg, pc, pm, po, up_sum, down_sum = backward(
        z, S, plane, expert_out, dx_z, dwu, dwd, states, w_out, w_in, table, choose_wide, chances, mid, moe, cot, gpack, router_t,
        gate, y, sig, small, mixed, dt, masks, conv_in, hconv, s_all, tok, normed_all.reshape(E * T, D), 4
    )
    if not plane:
        pg, pc, pm, po = [lax.psum(a, "seq") for a in (pg, pc, pm, po)]
        pg, pc = [
            lax.all_to_all(a, "exp", split_axis=0, concat_axis=0, tiled=True).transpose(1, 2, 0, 3, 4)
            for a in (pg, pc)
        ]
        pm = lax.psum_scatter(pm, "exp", scatter_dimension=0, tiled=True)[0]
        po = po[0]
    eight = lambda a: a.reshape((8,) + a.shape[2:])
    dw_in, dw_out, output, token_grad, g_cw, g_cb, g_xw, g_dw, g_db, g_al, g_sk, g_na, g_nb, g_ro, *rest = finish(
        z, gr, plane, eight(pg), eight(pc), pm.reshape(-1, pm.shape[-1]), po.reshape(8, -1, D), token_grad, mid,
        chances, choose_wide, table, back_out, up_sum, down_sum
    )
    if plane:
        up_part, down_part = rest
    else:
        fb = z.FF // 8
        up_full = jnp.zeros((D, 4, 2, fb), BF16)
        up_full = lax.dynamic_update_slice_in_dim(up_full, dwu.reshape(D, 4, 1, fb), core, axis=2)
        down_full = jnp.zeros((4, 2, fb, D), BF16)
        down_full = lax.dynamic_update_slice_in_dim(down_full, dwd.reshape(4, 1, fb, D), core, axis=1)
        up_part, down_part = [
            lax.psum_scatter(v, "seq", scatter_dimension=0, tiled=True).astype(F32)
            for v in (up_full.reshape(D, z.FF), down_full.reshape(z.FF, D))
        ]
    return (
        output[None], token_grad[None], g_na, dw_in, g_cw, g_cb, g_xw.T, g_dw, g_db, g_al, g_sk, dw_out,
        g_nb, g_ro.T, up_part[None], down_part[None],
    )


def solution(mesh):
    row = P("exp", "seq", None)
    in_specs = (
        row, P("exp", "seq"), row, row, P("exp"), P("exp", None), P(None, "exp"), P("exp"), P("exp", None),
        P(None, "exp"), P("exp"), P(None, "exp"), P("exp"), P("exp", None), P("exp"), P("exp", None),
        P("exp", None, None), P("exp", None, None),
    )
    out_specs = (
        row, row, P("exp"), P("exp", None), P(None, "exp"), P("exp"), P("exp", None), P(None, "exp"), P("exp"),
        P(None, "exp"), P("exp"), P("exp", None), P("exp"), P("exp", None), row, row,
    )
    return jax.shard_map(on_device, mesh=mesh, in_specs=in_specs, out_specs=out_specs, check_vma=False)
```

```python
import functools
import math

import jax
import jax.numpy as jnp
from jax import lax
from jax.experimental import pallas as pl
from jax.experimental.pallas import tpu as pltpu
from jax.sharding import PartitionSpec as P

EPSILON = 1e-05
LOG2E = math.log2(math.e)
LN2 = math.log(2.0)
CLOSED = 1e30
LANES = 128
SUB = 8
F32 = jnp.float32
BF16 = jnp.bfloat16
VMEM_LIMIT = 56 * 1024 * 1024


def mm(a, b):
    return lax.dot_general(a, b, (((1,), (0,)), ((), ())), preferred_element_type=F32)


def mm_nt(a, b):
    return lax.dot_general(a, b, (((1,), (1,)), ((), ())), preferred_element_type=F32)


def mm_tn(a, b):
    return lax.dot_general(a, b, (((0,), (0,)), ((), ())), preferred_element_type=F32)


def split_hi_lo(value):
    high = value.astype(BF16)
    return high, (value - high.astype(F32)).astype(BF16)


def sigmoid(v):
    return 1.0 / (1.0 + jnp.exp(-v))


def softplus(v):
    e = jnp.exp(-jnp.abs(v))
    small = e * (1.0 - e * (0.5 - e * (1.0 / 3.0 - e * 0.25)))
    return jnp.maximum(v, 0.0) + jnp.where(e < 0.01, small, jnp.log(1.0 + e))


def rms_scale(v):
    return lax.rsqrt(jnp.mean(v * v, axis=-1, keepdims=True) + EPSILON)


def rms_back(resid, gain, grad):
    s = rms_scale(resid)
    v = gain * grad
    out = s * v - resid * (s * s * s) * jnp.mean(resid * v, axis=-1, keepdims=True)
    return out, jnp.sum(grad * resid * s, axis=0, keepdims=True)


def block(shape, index):
    return pl.BlockSpec(shape, index)


def whole(shape):
    zeros = (0,) * len(shape)
    return pl.BlockSpec(shape, lambda *_: zeros)


def call(body, name, grid, ins, in_specs, outs, out_specs, scratch, cost=None):
    return pl.pallas_call(
        body,
        name=name,
        grid=grid,
        in_specs=in_specs,
        out_specs=out_specs,
        out_shape=outs,
        scratch_shapes=scratch,
        cost_estimate=cost,
        compiler_params=pltpu.CompilerParams(vmem_limit_bytes=VMEM_LIMIT),
    )(*ins)


def sds(shape, dtype):
    return jax.ShapeDtypeStruct(shape, dtype)


def pick(total, options):
    for o in options:
        if total % o == 0:
            return o
    return total


CONV_W, CONV_B, DT_B, SKIP, A_LOG = 0, 4, 5, 6, 8


class Sizes:
    def __init__(self, tokens, in_proj, dt_proj, x_proj, a_log, up_proj, exp_count):
        self.T = tokens.shape[1]
        self.D = tokens.shape[2]
        self.DI = in_proj.shape[1] // 2
        self.N = a_log.shape[0]
        self.R = dt_proj.shape[0]
        self.XW = x_proj.shape[1]
        self.FF = up_proj.shape[2]
        self.E = exp_count
        self.CAP = 2 * self.T // exp_count
        self.J = self.T // SUB
        self.DT0 = A_LOG + self.N
        self.X0 = self.DT0 + self.R
        self.SMALL = self.X0 + self.XW


MESH = pl.DeviceIdType.MESH
ANY = pl.BlockSpec(memory_space=pl.ANY)


def greet(peers):
    barrier = pltpu.get_barrier_semaphore()
    for peer in peers:
        pl.semaphore_signal(barrier, inc=1, device_id=peer, device_id_type=MESH)
    pl.semaphore_wait(barrier, len(peers))


def group_place(groups, g):
    main = groups // 8
    if g < 8 * main:
        return g // main, 16 * (g % main)
    return g - 8 * main, 16 * main


def chunk_rows(rows):
    groups = rows // 16
    return 16 * (groups // 8 + (1 if groups % 8 else 0))


class PlaneSum:
    def __init__(self, E, p, b, t, zb, out, add, base, full, sems):
        self.E, self.p, self.b, self.t, self.zb, self.out, self.add = E, p, b, t, zb, out, add
        self.rows, self.full = p.shape[3], full
        self.base = base if full < 4 else self.rows
        self.cs, self.cr, self.qs, self.qr, self.zs, self.zr, self.gs, self.gr, self.fs, self.fr, self.own = sems
        s, self.me = lax.axis_index("seq"), lax.axis_index("exp")
        self.chip, self.core = s // 2, lax.rem(s, 2)
        self.sib = {"seq": s + 1 - 2 * self.core}
        self.chips = [self.chip + 1 - 2 * lax.rem(self.chip, 2), self.chip + 2 - 4 * (self.chip // 2), 3 - self.chip]
        self.far = [{"seq": q * 2 + self.core} for q in self.chips]
        self.zz = [lax.rem(self.me + k, E) for k in range(1, E)]

    def pair(self, src, dst, send, recv, to):
        cut = lambda ref, a, n: ref.at[(slice(None),) * (len(ref.shape) - 2) + (pl.ds(a, n),)]
        make = lambda a, n, i: pltpu.make_async_remote_copy(
            cut(src, a, n), cut(dst, a, n), send.at[i], recv.at[i], device_id=to, device_id_type=MESH
        )
        if self.base == self.rows:
            return [make(0, self.rows, 0)]
        return [make(0, self.base, 0), make(self.base, self.rows - self.base, 1)]

    def run(self, copies, chip, act):
        act(copies[0])
        if len(copies) > 1:
            @pl.when(chip < self.full)
            def _():
                act(copies[1])

    def swap_start(self):
        self.swap = self.pair(self.p.at[:, :, 1 - self.core], self.b, self.cs, self.cr, self.sib)
        if len(self.swap) > 1:
            src, dst = self.p.at[:, 0 : self.full, 1 - self.core], self.b.at[:, 0 : self.full]
            self.swap[1] = self.pair(src, dst, self.cs, self.cr, self.sib)[1]
        for c in self.swap:
            c.start()

    def swap_finish(self):
        for c in self.swap:
            c.wait()
        B = self.base
        for l in range(self.p.shape[0]):
            self.p[l, :, self.core, 0:B] = (
                self.p[l, :, self.core, 0:B].astype(F32) + self.b[l, :, 0:B].astype(F32)
            ).astype(BF16)
            if B < self.rows:
                F = self.full
                self.p[l, 0:F, self.core, B:] = (
                    self.p[l, 0:F, self.core, B:].astype(F32) + self.b[l, 0:F, B:].astype(F32)
                ).astype(BF16)
        self.crossing = [
            self.pair(self.p.at[:, self.chips[k], self.core], self.t.at[k], self.qs.at[k], self.qr.at[k], self.far[k])
            for k in range(3)
        ]
        for k in range(3):
            self.run(self.crossing[k], self.chips[k], lambda c: c.start())

    def chips_finish(self):
        for k in range(3):
            self.run(self.crossing[k], self.chips[k], lambda c: c.wait_send())
            self.run(self.crossing[k], self.chip, lambda c: c.wait_recv())

        def total(rows):
            for l in range(self.p.shape[0]):
                v = self.p[l, self.chip, self.core, rows].astype(F32)
                for k in range(3):
                    v = v + self.t[k, l, rows].astype(F32)
                self.p[l, self.chip, self.core, rows] = v.astype(BF16)

        total(slice(0, self.base))
        if self.base < self.rows:
            @pl.when(self.chip < self.full)
            def _():
                total(slice(self.base, self.rows))

        if self.zb is None:
            self.spread(self.p.at[:, self.chip, self.core])
            return
        self.along = [
            self.pair(self.p.at[d, self.chip, self.core], self.zb.at[self.me], self.zs.at[k], self.zr.at[k], {"exp": d})
            for k, d in enumerate(self.zz)
        ]
        for c in self.along:
            self.run(c, self.chip, lambda c: c.start())

    def z_finish(self):
        for c in self.along:
            self.run(c, self.chip, lambda c: c.wait())
        v = self.p[self.me, self.chip, self.core]
        if self.add:
            v = v.astype(F32)
            for d in self.zz:
                v = v + self.zb[d].astype(F32)
            self.zb[self.me] = v.astype(BF16)
            self.spread(self.zb.at[self.me])
        else:
            self.zb[self.me] = v
            self.spread(self.zb)

    def spread(self, ref):
        dst = self.out.at[self.chip, self.core]
        self.sends = [self.pair(ref, dst, self.gs.at[k], self.gr.at[k], self.far[k]) for k in range(3)]
        self.sends.append(self.pair(ref, dst, self.fs.at[3], self.fr.at[3], self.sib))
        for c in self.sends:
            self.run(c, self.chip, lambda c: c.start())
        self.local = pltpu.make_async_copy(ref, dst, self.own)
        self.local.start()

    def forward(self):
        self.passed = []
        for k in range(3):
            ref = self.out.at[self.chips[k], self.core]
            self.run(self.pair(ref, ref, self.gs.at[k], self.gr.at[k], self.far[k]), self.chips[k], lambda c: c.wait_recv())
            c = self.pair(ref, ref, self.fs.at[k], self.fr.at[k], self.sib)
            self.run(c, self.chips[k], lambda c: c.start())
            self.passed.append(c)

    def finish(self):
        for c in self.sends:
            self.run(c, self.chip, lambda c: c.wait_send())
        for k in range(3):
            self.run(self.passed[k], self.chips[k], lambda c: c.wait_send())
        self.local.wait()
        for k in range(4):
            q = self.chips[k] if k < 3 else self.chip
            ref = self.out.at[q, 1 - self.core]
            self.run(self.pair(ref, ref, self.fs.at[k], self.fr.at[k], self.sib), q, lambda c: c.wait_recv())


def expand_columns(z, src, col0, dst):
    def one(j, carry):
        rows = src[pl.ds(pl.multiple_of(j * SUB, SUB), SUB), :]
        for n in range(z.N):
            at = pl.multiple_of((j * z.N + n) * SUB, SUB)
            dst[pl.ds(at, SUB), :] = jnp.broadcast_to(
                rows[:, col0 + n : col0 + n + 1], (SUB, LANES)
            )
        return carry

    lax.fori_loop(0, z.J, one, 0)


def expand_closed(z, masks, dst):
    dst[...] = jnp.broadcast_to((1.0 - masks[:, 2:3]) * CLOSED, (z.T, LANES))


def tile_groups(cb):
    return 2 if cb % (2 * LANES) == 0 else 1


def lane_at(p, tg, k):
    return pl.ds(pl.multiple_of(p * tg * LANES, LANES) + k * LANES, LANES)


def row8(j):
    return pl.ds(pl.multiple_of(j * SUB, SUB), SUB)


def shift_down(v, d):
    rows = lax.broadcasted_iota(jnp.int32, v.shape, 0)
    return jnp.where(rows >= d, pltpu.roll(v, d, 0), 0.0)


def shift_up(v, d):
    rows = lax.broadcasted_iota(jnp.int32, v.shape, 0)
    return jnp.where(rows < SUB - d, pltpu.roll(v, SUB - d, 0), 0.0)


def chain_states(count, mine, order, sums, heads, rates2):
    state = jnp.zeros_like(rates2)
    for k in range(count):
        at = order(k)
        new = jnp.exp2(rates2 * sums(at)) * state + heads(at).astype(F32)
        state = jnp.where(mine(at), new, state)
    return state


def router_softmax(logits, experts):
    lane = lax.broadcasted_iota(jnp.int32, logits.shape, 1)
    logits = jnp.where(lane < experts, logits, -1e30)
    top = jnp.max(logits, axis=-1, keepdims=True)
    e = jnp.where(lane < experts, jnp.exp(logits - top), 0.0)
    return e / jnp.sum(e, axis=-1, keepdims=True)


def expert(z, x, cot, router, normed, up, down, cid):
    T, D, FF, E = z.T, z.D, z.FF, z.E
    M = x.shape[0] // 2
    CAP = z.CAP
    fb = FF // 8
    wb = 2 * fb

    def body(
        x_r, c_r, rt, nrm, up_r, dn_r, dxz, back_o, dwu_o, dwd_o, nz_o,
        up_v, dn_v, hid, pg_s, g_s, out_s, dx_s, dxb, outb, dx_r, out_r, dwu_v, dwd_v,
        ld, c_s, c_q, sw_s, sw_r, dz_s, dz_r,
    ):
        s, me = lax.axis_index("seq"), lax.axis_index("exp")
        core = lax.rem(s, 2)
        other = 1 - core
        sib = {"seq": s + 1 - 2 * core}
        zs = [lax.rem(me + k, E) for k in range(1, E)]
        loads = []
        for i in range(4):
            at = pl.multiple_of((2 * i + core) * fb, LANES)
            t, off = i // 2, i % 2 * fb
            loads.append(
                [
                    pltpu.make_async_copy(up_r.at[:, pl.ds(at, fb)], up_v.at[t, :, off : off + fb], ld.at[i]),
                    pltpu.make_async_copy(dn_r.at[pl.ds(at, fb)], dn_v.at[t, off : off + fb], ld.at[4 + i]),
                ]
            )
        for pair in loads:
            for c in pair:
                c.start()
        greet([sib] + [{"exp": p} for p in zs])

        def remote(src, dst, send, recv, to):
            return pltpu.make_async_remote_copy(src, dst, send, recv, device_id=to, device_id_type=MESH)

        chain = Chain(E, nrm, nz_o, c_s, c_q, ld.at[8])
        chain.start()
        ch = router_softmax(mm_nt(x_r[...], rt[...]), E)
        lane = lax.broadcasted_iota(jnp.int32, ch.shape, 1)
        gating = jnp.sum(jnp.where(lane == me, ch, 0.0), axis=-1, keepdims=True)
        g_s[...] = (gating * c_r[...].astype(F32)).astype(BF16)
        for t in range(2):
            W = slice(t * wb, (t + 1) * wb)
            for pair in loads[2 * t : 2 * t + 2]:
                for c in pair:
                    c.wait()
            pre = mm(x_r[...], up_v[t])
            cdf = 0.5 * (1.0 + lax.erf(pre * (2.0 ** -0.5)))
            hid[:, W] = (pre * cdf).astype(BF16)
            slope = cdf + pre * jnp.exp(-0.5 * pre * pre) * (1.0 / math.sqrt(2.0 * math.pi))
            pg_s[:, W] = (mm_nt(g_s[...], dn_v[t]) * slope).astype(BF16)
            if t == 0:
                dx_s[...] = mm_nt(pg_s[:, W], up_v[t])
                out_s[...] = mm(hid[:, W], dn_v[t])
                chain.hop(1)
            else:
                dxb[:, 0:D] = (dx_s[...] + mm_nt(pg_s[:, W], up_v[t])).astype(BF16)
                out = out_s[...] + mm(hid[:, W], dn_v[t])
                outb[...] = out.astype(BF16)
                gg = jnp.sum(out * c_r[...].astype(F32), axis=-1, keepdims=True)
                hi, lo = split_hi_lo(gg)
                lane = lax.broadcasted_iota(jnp.int32, (2 * M, LANES), 1)
                both = jnp.where(lane == 0, hi.astype(F32), jnp.where(lane == 1, lo.astype(F32), 0.0))
                dxb[:, D : D + LANES] = both.astype(BF16)
        half = lambda c: pl.ds(pl.multiple_of(c * M, 16), M)
        swaps = [
            remote(dxb.at[half(other)], dx_r, sw_s.at[0], sw_r.at[0], sib),
            remote(outb.at[half(other)], out_r, sw_s.at[1], sw_r.at[1], sib),
        ]
        for c in swaps:
            c.start()
        if E > 2:
            chain.hop(2)

        def grads(t):
            W = slice(t * wb, (t + 1) * wb)
            dwd_v[W, :] = mm_tn(hid[:, W], g_s[...]).astype(BF16)
            dwu_v[:, W] = mm_tn(x_r[...], pg_s[:, W]).astype(BF16)
            moves = [
                pltpu.make_async_copy(dwd_v.at[W], dwd_o.at[W], ld.at[9 + t]),
                pltpu.make_async_copy(dwu_v.at[:, W], dwu_o.at[:, W], ld.at[11 + t]),
            ]
            for c in moves:
                c.start()
            return moves

        block_of = lambda ref, p: ref.at[pl.ds(pl.multiple_of(p * CAP, 16), CAP)]
        here = pl.ds(pl.multiple_of(me * CAP, 16), CAP)
        swaps[0].wait()
        dx_r[...] = (dxb[half(core), :].astype(F32) + dx_r[...].astype(F32)).astype(BF16)
        moves = [
            remote(block_of(dx_r, p), block_of(dxz, me), dz_s.at[k], dz_r.at[k], {"exp": p}) for k, p in enumerate(zs)
        ]
        for c in moves:
            c.start()
        dxz[here, :] = dx_r[here, :]
        kept = grads(0)
        swaps[1].wait()
        out_r[...] = (outb[half(core), :].astype(F32) + out_r[...].astype(F32)).astype(BF16)
        kept.append(pltpu.make_async_copy(out_r, back_o, ld.at[13]))
        kept[-1].start()
        kept += grads(1)
        for k in range(3, E):
            chain.hop(k)
        for c in moves + kept:
            c.wait()
        chain.finish()

    v = pltpu.VMEM
    sem = lambda *dims: pltpu.SemaphoreType.DMA(dims)
    vm = pl.BlockSpec(memory_space=pltpu.VMEM)
    slots = 2 * (E - 1)
    return pl.pallas_call(
        body,
        name="expert",
        in_specs=[vm] * 4 + [ANY] * 2,
        out_specs=[vm] + [ANY] * 4,
        out_shape=[
            sds((M, D + LANES), BF16), sds((M, D), BF16), sds((D, 2 * wb), BF16), sds((2 * wb, D), BF16),
            sds((E, T, D), BF16),
        ],
        scratch_shapes=[
            v((2, D, wb), BF16), v((2, wb, D), BF16), v((2 * M, 2 * wb), BF16), v((2 * M, 2 * wb), BF16),
            v((2 * M, D), BF16), v((2 * M, D), F32), v((2 * M, D), F32), v((2 * M, D + LANES), BF16),
            v((2 * M, D), BF16), v((M, D + LANES), BF16), v((M, D), BF16), v((D, 2 * wb), BF16), v((2 * wb, D), BF16),
            sem(14), sem(slots), sem(slots), sem(2), sem(2), sem(E - 1), sem(E - 1),
        ],
        compiler_params=pltpu.CompilerParams(
            collective_id=cid, has_side_effects=True, vmem_limit_bytes=VMEM_LIMIT
        ),
    )(x, cot, router, normed, up, down)


def padded_rows(main, edge, J, cb):
    H = edge.shape[0]
    m3 = main.reshape(J, SUB, cb)
    first = lax.broadcasted_iota(jnp.int32, (SUB, cb), 0) == 0
    tail = jnp.stack(
        [
            jnp.where(
                first,
                jnp.broadcast_to(edge[H - 3 + k : H - 2 + k, :], (SUB, cb)),
                pltpu.roll(m3[J - 3 + k], 1, 0),
            )
            for k in range(3)
        ]
    )
    return jnp.concatenate([tail, m3], axis=0)


def at_cols(i, cb):
    return pl.ds(pl.multiple_of(i * cb, LANES), cb)


def lanes_of(i, cb, p, tg, k):
    return pl.ds(pl.multiple_of(i * cb + p * tg * LANES, LANES) + k * LANES, LANES)


class Chain:
    def __init__(self, E, src, dst, send, recv, own):
        self.E, self.src, self.dst, self.send, self.recv, self.own = E, src, dst, send, recv, own
        self.me = lax.axis_index("exp")
        self.right, self.left = lax.rem(self.me + 1, E), lax.rem(self.me + E - 1, E)

    def slot(self, d):
        return 2 * (abs(d) - 1) + (1 if d > 0 else 0)

    def exists(self, d):
        return (self.me + d >= 0) & (self.me + d < self.E)

    def each(self, d, act):
        for to_right in (True, False):
            if (d <= 0) if to_right else (d >= 0):
                edge = self.me < self.E - 1 if to_right else self.me > 0
                there = self.slot(d - 1 if to_right else d + 1)

                @pl.when(self.exists(d) & edge)
                def _():
                    act(
                        pltpu.make_async_remote_copy(
                            self.src if d == 0 else self.dst.at[self.me + d],
                            self.dst.at[self.me + d],
                            self.send.at[there],
                            self.recv.at[there],
                            device_id={"exp": self.right if to_right else self.left},
                            device_id_type=MESH,
                        )
                    )

    def local(self):
        return pltpu.make_async_copy(self.src, self.dst.at[self.me], self.own)

    def start(self):
        self.each(0, lambda c: c.start())
        self.local().start()

    def hop(self, k):
        for d in (-k, k):
            ref = self.dst.at[self.me + d]

            @pl.when(self.exists(d))
            def _():
                pltpu.make_async_remote_copy(
                    ref, ref, self.send.at[self.slot(d)], self.recv.at[self.slot(d)],
                    device_id={"exp": self.right}, device_id_type=MESH,
                ).wait_recv()

            if k < self.E - 1:
                self.each(d, lambda c: c.start())

    def finish(self):
        for k in range(self.E - 1):
            for d in (-k, k) if k else (0,):
                self.each(d, lambda c: c.wait_send())
        self.local().wait()


class Spread:
    def __init__(self, E, src, col0, dst, cols, each, by_rows, sems):
        self.E, self.src, self.col0, self.dst, self.cols, self.each_cols = E, src, col0, dst, cols, each
        self.by_rows = by_rows
        self.zs, self.zr, self.ps, self.pr, self.cs, self.cr = sems
        self.rows = src.shape[0]
        s, self.me = lax.axis_index("seq"), lax.axis_index("exp")
        self.chip, self.core = s // 2, lax.rem(s, 2)
        self.sib = {"seq": s + 1 - 2 * self.core}
        self.chips = [self.chip + 1 - 2 * lax.rem(self.chip, 2), self.chip + 2 - 4 * (self.chip // 2), 3 - self.chip]
        self.far = [{"seq": q * 2 + self.core} for q in self.chips]
        self.right, self.left = lax.rem(self.me + 1, E), lax.rem(self.me + E - 1, E)
        self.split = by_rows or each > 0
        self.rest = 0 if by_rows else cols - 4 * each
        self.regions = ([1] if self.split else []) + ([0] if self.rest else [])
        self.pieces = ([0] if self.rest else []) + ([1, 2, 3, 4] if self.split else [])
        self.offsets = [d for k in range(1, E) for d in (-k, k)]

    def slot(self, d):
        return 2 * (abs(d) - 1) + (1 if d > 0 else 0)

    def exists(self, d):
        return (self.me + d >= 0) & (self.me + d < self.E)

    def view(self, ref, row0, col0, region, q, core, half):
        rows = self.rows // 2
        row = row0 + core * rows
        if self.by_rows:
            rows = rows // 4
            row = row + q * rows
            if half is not None:
                rows = rows // 2
                row = row + half * rows
            return ref.at[pl.ds(pl.multiple_of(row, 16), rows)]
        at = pl.ds(pl.multiple_of(row, 16), rows)
        if region == 0:
            start, width = col0, self.rest
        else:
            start, width = col0 + self.rest + q * self.each_cols, self.each_cols
            if half is not None:
                width = width // 2
                start = start + half * width
        if width == ref.shape[1]:
            return ref.at[at]
        return ref.at[at, pl.ds(pl.multiple_of(start, LANES), width)]

    def there(self, d, region, q, core, half=None):
        return self.view(self.dst, (self.me + d) * self.rows, 0, region, q, core, half)

    def own(self, region):
        return self.view(self.src, 0, self.col0, region, self.chip, self.core, None)

    def local(self, sem):
        at = pl.ds(pl.multiple_of(self.me * self.rows, 16), self.rows)
        src = self.src if self.cols == self.src.shape[1] else self.src.at[:, self.col0 : self.col0 + self.cols]
        return pltpu.make_async_copy(src, self.dst.at[at], sem)

    def remote(self, src, dst, send, recv, to):
        return pltpu.make_async_remote_copy(src, dst, send, recv, device_id=to, device_id_type=MESH)

    def z_each(self, region, d, act):
        for to_right in (True, False):
            if (d <= 0) if to_right else (d >= 0):
                edge = self.me < self.E - 1 if to_right else self.me > 0
                slot = self.slot(d - 1 if to_right else d + 1)

                @pl.when(self.exists(d) & edge)
                def _():
                    act(
                        self.remote(
                            self.own(region) if d == 0 else self.there(d, region, self.chip, self.core),
                            self.there(d, region, self.chip, self.core),
                            self.zs.at[region, slot],
                            self.zr.at[region, slot],
                            {"exp": self.right if to_right else self.left},
                        )
                    )

    def start(self):
        for r in self.regions:
            self.z_each(r, 0, lambda c: c.start())

    def cross(self, j, d):
        if j < 2:
            ref = self.there(d, 1, self.chip, self.core)
        else:
            ref = self.there(d, 1, self.chips[j - 2], self.core, j - 2)
        to = self.far[(0, 1, 1, 0)[j]]
        return self.remote(ref, ref, self.ps.at[j, self.slot(d)], self.pr.at[j, self.slot(d)], to)

    def crossed(self, j, d):
        ref = self.there(d, 1, self.chips[j], self.core) if j < 2 else self.there(d, 1, self.chips[2], self.core, j - 2)
        self.remote(ref, ref, self.ps.at[j, self.slot(d)], self.pr.at[j, self.slot(d)], self.sib).wait_recv()

    def sib_copy(self, which, d, core):
        if which == 0:
            ref = self.there(d, 0, self.chip, core)
        else:
            ref = self.there(d, 1, self.chip if which == 1 else self.chips[which - 2], core)
        return self.remote(ref, ref, self.cs.at[which, self.slot(d)], self.cr.at[which, self.slot(d)], self.sib)

    def hop(self, k):
        for r in self.regions:
            for d in (-k, k):
                @pl.when(self.exists(d))
                def _():
                    ref = self.there(d, r, self.chip, self.core)
                    self.remote(
                        ref, ref, self.zs.at[r, self.slot(d)], self.zr.at[r, self.slot(d)], self.sib
                    ).wait_recv()

                if k < self.E - 1:
                    self.z_each(r, d, lambda c: c.start())

                @pl.when(self.exists(d))
                def _():
                    if r == 1:
                        for j in range(2):
                            self.cross(j, d).start()
                    self.sib_copy(r, d, self.core).start()

    def plane(self, k):
        for d in (-k, k) if self.split else ():
            @pl.when(self.exists(d))
            def _():
                for j in range(2):
                    self.crossed(j, d)
                    self.cross(2 + j, d).start()
                    self.sib_copy(2 + j, d, self.core).start()

    def fourth(self, k):
        for d in (-k, k) if self.split else ():
            @pl.when(self.exists(d))
            def _():
                self.crossed(2, d)
                self.crossed(3, d)
                self.sib_copy(4, d, self.core).start()

    def landed(self):
        for d in self.offsets:
            @pl.when(self.exists(d))
            def _():
                for w in self.pieces:
                    self.sib_copy(w, d, 1 - self.core).wait_recv()

    def finish(self):
        for d in self.offsets:
            @pl.when(self.exists(d))
            def _():
                for w in self.pieces:
                    self.sib_copy(w, d, self.core).wait_send()
                if self.split:
                    for j in range(4):
                        self.cross(j, d).wait_send()
        for r in self.regions:
            for k in range(self.E - 1):
                for d in (-k, k) if k else (0,):
                    self.z_each(r, d, lambda c: c.wait_send())


def small_rows(z):
    return 128 * -(-z.SMALL // 128)


def pack_small(z, par, own_sm, own_g):
    conv_w, conv_b, dt_b, skip, a_log, dt_w, x_w, gain_a, gain_b, router = par
    (rs, cw), (rg, dw) = own_sm.shape, own_g.shape
    wide = lambda ref: ref[...].astype(F32)
    line = lambda ref: ref[...].astype(F32).reshape(1, ref.shape[0])
    rows = [wide(conv_w), line(conv_b), line(dt_b), line(skip), jnp.zeros((1, cw), F32), wide(a_log), wide(dt_w)]
    rows += [wide(x_w), jnp.zeros((rs - z.SMALL, cw), F32)]
    own_sm[...] = jnp.concatenate(rows, axis=0).astype(BF16)
    rows = [line(gain_a), line(gain_b), wide(router), jnp.zeros((rg - 2 - z.E, dw), F32)]
    own_g[...] = jnp.concatenate(rows, axis=0).astype(BF16)


def forward(z, S, plane, tokens, cotangent, seg, route, params, in_proj, out_proj, gr, cid):
    T, D, DI, N, J, E, CAP = z.T, z.D, z.DI, z.N, z.J, z.E, z.CAP
    H = J
    M = E * CAP
    DZ, NZ = DI // E, D // E
    rs, rg = small_rows(z), 32
    cb = pick(DI, (384, 256, 128))
    cs = pick(DI, (768, 384, 256, 128))
    tg = tile_groups(cs)
    wide = tg * LANES
    ng = 8
    steps = DI // cs
    ST = (J + 1) * N * SUB
    tiles, tiles_o = DI // LANES, D // LANES
    split = (tiles // 4 - (0 if tiles % 4 else 1)) * LANES
    split_o = max(1, tiles_o * 2 // 9) * LANES

    def body(*refs):
        tokn, cotn, seg_r, route_r = refs[:4]
        np_ = len(params)
        par = refs[4 : 4 + np_]
        (
            in_p, out_p,
            sm, gp, rt, table, choose, masks, hconv, mixed, mid, moe, ch_o, s_all, tok, cot, normed_o,
            st_o, win_o, wout_o, arr_o, cot_o, conv_o, gate_o, sig_o, dt_o, y_o,
            conv_in, gate, sig, dt, y,
            wc, wg, wo, smb, gb, nrm, halo, seg_in, bx, cx, cl, u_s, rates_s, hd, hdev, stot, h_all, pre_s, dwin, hin,
            st_v, acc, outb, cotb, own_sm, own_g, own_seg,
            ld, zs, zr, ps, pr, c_s, c_r, t_s, t_r, h_s, h_r, d_s, d_r, q_s, q_r, k_s, k_r, x_s, x_r,
        ) = refs[4 + np_ :]
        s, me = lax.axis_index("seq"), lax.axis_index("exp")
        core = lax.rem(s, 2)
        sib = {"seq": s + 1 - 2 * core}
        seqs = [lax.rem(s + k, S) for k in range(1, S)]
        zz = [lax.rem(me + k, E) for k in range(1, E)]
        barrier = pltpu.get_barrier_semaphore()
        peers = [{"seq": p} for p in seqs] + [{"exp": p} for p in zz]
        for peer in peers:
            pl.semaphore_signal(barrier, inc=1, device_id=peer, device_id_type=MESH)

        def remote(src, dst, send, recv, to):
            return pltpu.make_async_remote_copy(src, dst, send, recv, device_id=to, device_id_type=MESH)

        if plane:
            pack_small(z, par, own_sm, own_g)
        segrow = seg_r[...].astype(F32)
        own_seg[...] = jnp.broadcast_to(segrow, (SUB, T))
        pl.semaphore_wait(barrier, len(peers))
        sems = lambda a: (zs.at[a], zr.at[a], ps.at[a], pr.at[a], c_s.at[a], c_r.at[a])
        if plane:
            parts = [
                Spread(E, own_sm, 0, smb, DZ, 0, True, sems(0)),
                Spread(E, own_g, 0, gb, NZ, 0, False, sems(1)),
                Spread(E, in_p, 0, wc, DI, split, False, sems(2)),
                Spread(E, in_p, DI, wg, DI, split, False, sems(3)),
                Spread(E, out_p, 0, wo, D, split_o, False, sems(4)),
            ]
            for p in parts[:3]:
                p.start()
            loads = [p.local(ld.at[a]) for a, p in enumerate(parts)]
        else:
            loads = [
                pltpu.make_async_copy(par[0], smb, ld.at[0]),
                pltpu.make_async_copy(par[1], gb, ld.at[1]),
                pltpu.make_async_copy(in_p.at[:, 0:DI], wc, ld.at[2]),
                pltpu.make_async_copy(in_p.at[:, DI : 2 * DI], wg, ld.at[3]),
                pltpu.make_async_copy(out_p, wo, ld.at[4]),
            ]
        ahead = {"seq": lax.rem(s + 1, S)}
        edges = [
            remote(tokn.at[pl.ds(T - H, H)], halo, t_s.at[0], t_r.at[0], ahead),
            remote(own_seg, seg_in, t_s.at[1], t_r.at[1], ahead),
        ]
        for c in edges:
            c.start()
        for c in loads:
            c.start()
        queue = []
        if plane:
            wg_p, wo_p = parts[3], parts[4]
            queue = [wg_p.start] + [functools.partial(wg_p.hop, k) for k in range(1, E - 1)]
            queue += [wo_p.start, functools.partial(wg_p.hop, E - 1)]
            for k in range(1, E):
                queue += [functools.partial(wg_p.plane, k), functools.partial(wo_p.hop, k)]
                queue += [functools.partial(wg_p.fourth, k)]
            for k in range(1, E):
                queue += [functools.partial(wo_p.plane, k)]
            for k in range(1, E):
                queue += [functools.partial(wo_p.fourth, k)]

        def progress(count):
            for _ in range(count):
                if queue:
                    queue.pop(0)()

        lane = lax.broadcasted_iota(jnp.int32, (T, T), 1)
        prow = lax.broadcasted_iota(jnp.int32, (T, T), 0)
        place = (prow % SUB) * J + prow // SUB
        order = (lane == place).astype(F32).astype(BF16)
        tok[...] = mm(order, tokn[...]).astype(BF16)
        cot[...] = mm(order, cotn[...]).astype(BF16)
        my_route = jnp.sum(
            jnp.where(lane == place, route_r[...].astype(F32), 0.0), axis=1, keepdims=True
        ).astype(jnp.int32)
        chosen = (lane == my_route).astype(F32)
        choose[...] = chosen
        counts = mm((lane <= prow).astype(F32).astype(BF16), chosen.astype(BF16))
        rank = jnp.sum(counts * chosen, axis=-1, keepdims=True).astype(jnp.int32) - 1
        slots = lax.broadcasted_iota(jnp.int32, (T, M), 1)
        table[...] = (slots == my_route * CAP + rank).astype(F32).astype(BF16)
        cotb[...] = mm_tn(table[...], cot[...]).astype(BF16)
        t32 = tok[...].astype(F32)
        scaled = t32 * rms_scale(t32)

        if plane:
            for k in range(1, E + 2):
                if k < E:
                    for p in parts[:3]:
                        p.hop(k)
                    progress(1)
                if 1 <= k - 1 < E:
                    parts[0].plane(k - 1)
                    parts[2].plane(k - 1)
                    progress(1)
                if 1 <= k - 2 < E:
                    parts[0].fourth(k - 2)
                    parts[2].fourth(k - 2)
        block_of = lambda ref, p: ref.at[pl.ds(pl.multiple_of(p * CAP, 16), CAP)]
        cot_moves = [remote(block_of(cotb, p), cot_o.at[core, me], k_s.at[k], k_r.at[k], {"exp": p}) for k, p in enumerate(zz)]
        if plane:
            for p in parts[:3]:
                p.landed()
        for c in loads:
            c.wait()
        for e in range(E):
            sm[:, e * DZ : (e + 1) * DZ] = smb[e * rs : (e + 1) * rs, :].astype(F32)[0 : z.SMALL]
        gp[...] = jnp.zeros_like(gp)
        rt[...] = jnp.zeros_like(rt)
        for e in range(E):
            cols = slice(e * NZ, (e + 1) * NZ)
            gp[:, cols] = gb[e * rg : e * rg + 16, :].astype(F32)[0:gr]
        rt[0:16, :] = jnp.concatenate([gp[2 : 2 + E, :], jnp.zeros((16 - E, D), F32)], axis=0).astype(BF16)

        for c in edges:
            c.wait()
        live = jnp.where(s > 0, 1.0, 0.0)
        col8 = lax.broadcasted_iota(jnp.int32, (T, SUB), 1)
        prev = seg_in[0:1, :] * live

        def seg_at(k):
            own = jnp.where(lane == place - k, segrow, 0.0)
            return jnp.sum(own + jnp.where(lane == place - k + T, prev, 0.0), axis=1, keepdims=True)

        now = seg_at(0)
        same = jnp.zeros((T, SUB), F32)
        for o in range(4):
            same = jnp.where(col8 == o, (seg_at(3 - o) == now).astype(F32), same)
        masks[...] = same
        nrm[0:T, :] = (scaled * gp[0:1, :]).astype(BF16)
        h32 = halo[...].astype(F32) * live
        nrm[T : T + H, :] = (h32 * rms_scale(h32) * gp[0:1, :]).astype(BF16)
        mixed[...] = jnp.zeros_like(mixed)

        def conv_block(i, carry):
            C = at_cols(i, cb)
            both = mm(nrm[...], wc[:, C])
            main, edge = both[:T], both[T:]
            conv_in[:, C] = main
            hconv[:, C] = edge
            xpad = padded_rows(main, edge, J, cb)
            out = jnp.broadcast_to(sm[CONV_B : CONV_B + 1, C], (T, cb))
            for o in range(4):
                m = jnp.broadcast_to(masks[:, o : o + 1], (T, cb))
                out = out + sm[CONV_W + o : CONV_W + o + 1, C] * xpad[o : o + J].reshape(T, cb) * m
            sv = (out * sigmoid(out)).astype(BF16)
            sig[:, C] = sv
            mixed[...] += mm_nt(sv, sm[z.X0 : z.X0 + z.XW, C].astype(BF16))
            return carry

        lax.fori_loop(0, DI // cb, conv_block, 0)
        normed_o[...] = nrm[0:T, :]
        keeps = [
            pltpu.make_async_copy(a, b, ld.at[13 + n])
            for n, (a, b) in enumerate(((conv_in, conv_o), (sig, sig_o), (dt, dt_o), (gate, gate_o), (y, y_o)))
        ]
        keeps[0].start()
        keeps[1].start()
        progress(3)
        cot_own = pltpu.make_async_copy(block_of(cotb, me), cot_o.at[core, me], ld.at[6])
        cot_own.start()

        expand_columns(z, mixed, z.R, bx)
        expand_columns(z, mixed, z.R + N, cx)
        expand_closed(z, masks, cl)
        low = mixed[:, 0 : z.R].astype(BF16)

        def step_block(i, carry):
            C = at_cols(i, cs)
            pre = mm(low, sm[z.DT0 : z.DT0 + z.R, C].astype(BF16)) + sm[DT_B : DT_B + 1, C]
            step = softplus(pre)
            dt[:, C] = step
            u_s[:, C] = step * sig[:, C].astype(F32)
            rates_s[:, C] = -jnp.exp(sm[A_LOG : A_LOG + N, C]) * LOG2E
            return carry

        lax.fori_loop(0, DI // cs, step_block, 0)
        progress(3)

        def chunk_block(p, carry):
            lanes = [lane_at(p, tg, k) for k in range(tg)]
            wins = []
            for k in range(tg):
                w1 = jnp.zeros((SUB, LANES), F32)
                for j in range(J):
                    w1 = w1 + (dt[j * SUB : j * SUB + SUB, lanes[k]] + cl[j * SUB : j * SUB + SUB, :])
                w2 = w1 + shift_down(w1, 1)
                w4 = w2 + shift_down(w2, 2)
                w8 = w4 + shift_down(w4, 4)
                wins.append((w1, w2, w4))
                dwin[:, lanes[k]] = shift_down(w8, 1)
                stot[:, lanes[k]] = w8[SUB - 1 : SUB, :]
            for g in range(0, N, ng):
                rr = [
                    [jnp.broadcast_to(rates_s[g + n : g + n + 1, lanes[k]], (SUB, LANES)) for k in range(tg)]
                    for n in range(ng)
                ]

                def step_j(j, hs):
                    dts = [dt[row8(j), lanes[k]] + cl[row8(j), :] for k in range(tg)]
                    us = [u_s[row8(j), lanes[k]] for k in range(tg)]
                    new = []
                    for n in range(ng):
                        b = bx[row8(j * N + g + n), :]
                        for k in range(tg):
                            new.append(jnp.exp2(dts[k] * rr[n][k]) * hs[n * tg + k] + us[k] * b)
                    return tuple(new)

                hs = lax.fori_loop(
                    0, J, step_j, tuple(jnp.zeros((SUB, LANES), F32) for _ in range(ng * tg)), unroll=2
                )
                for n in range(ng):
                    for k in range(tg):
                        h = hs[n * tg + k]
                        w1, w2, w4 = wins[k]
                        r = rr[n][k]
                        h = h + jnp.exp2(r * w1) * shift_down(h, 1)
                        h = h + jnp.exp2(r * w2) * shift_down(h, 2)
                        h = h + jnp.exp2(r * w4) * shift_down(h, 4)
                        pre_s[(g + n) * SUB : (g + n + 1) * SUB, lanes[k]] = shift_down(h, 1)
                        hd[g + n : g + n + 1, lanes[k]] = h[SUB - 1 : SUB, :]
            return carry

        keeps[2].start()
        third = DI // wide // 3
        lax.fori_loop(0, third, chunk_block, 0)
        progress(3)
        lax.fori_loop(third, 2 * third, chunk_block, 0)
        progress(3)
        lax.fori_loop(2 * third, DI // wide, chunk_block, 0)
        hdev[...] = hd[...].astype(BF16)
        h_moves = [remote(hdev, h_all.at[s], h_s.at[0, k], h_r.at[0, k], {"seq": p}) for k, p in enumerate(seqs)]
        h_moves += [remote(stot, s_all.at[s], h_s.at[1, k], h_r.at[1, k], {"seq": p}) for k, p in enumerate(seqs)]
        for c in h_moves:
            c.start()
        h_all[s] = hdev[...]
        s_all[s] = stot[...]
        for c in cot_moves:
            c.start()
        progress(len(queue))
        if plane:
            parts[3].landed()

        def gate_block(i, carry):
            C = at_cols(i, cb)
            gate[:, C] = mm(nrm[0:T, :], wg[:, C])
            return carry

        lax.fori_loop(0, DI // cb, gate_block, 0)
        keeps[3].start()
        if plane:
            parts[4].landed()
        outs = [
            pltpu.make_async_copy(wc, win_o.at[:, 0:DI], ld.at[7]),
            pltpu.make_async_copy(wg, win_o.at[:, DI : 2 * DI], ld.at[8]),
            pltpu.make_async_copy(wo, wout_o, ld.at[9]),
        ]
        for c in outs:
            c.start()
        for c in h_moves:
            c.wait()
        acc[...] = jnp.zeros_like(acc)

        def save(i):
            return pltpu.make_async_copy(
                st_v.at[i % 2], st_o.at[:, i * cs : (i + 1) * cs], ld.at[10 + i % 2]
            )

        for i in range(steps):
            if i >= 2:
                save(i - 2).wait()
            C = slice(i * cs, (i + 1) * cs)
            hin[...] = chain_states(
                S - 1, lambda k: k < s, lambda k: k, lambda k: s_all[k, :, C], lambda k: h_all[k, :, C],
                rates_s[:, C],
            )

            def pair(p, carry):
                lanes = [lanes_of(i, cs, p, tg, k) for k in range(tg)]
                near = [lane_at(p, tg, k) for k in range(tg)]
                for g in range(0, N, ng):
                    rr = [
                        [jnp.broadcast_to(rates_s[g + n : g + n + 1, lanes[k]], (SUB, LANES)) for k in range(tg)]
                        for n in range(ng)
                    ]
                    init = []
                    for n in range(ng):
                        for k in range(tg):
                            at = (g + n) * SUB
                            init.append(
                                pre_s[at : at + SUB, lanes[k]]
                                + jnp.exp2(rr[n][k] * dwin[:, lanes[k]])
                                * jnp.broadcast_to(hin[g + n : g + n + 1, near[k]], (SUB, LANES))
                            )

                    def keep(j, hs):
                        for n in range(0, ng, 2):
                            for k in range(tg):
                                two = jnp.concatenate([hs[n * tg + k], hs[(n + 1) * tg + k]], axis=0)
                                at = pl.multiple_of(j * N * SUB + (g + n) * SUB, 2 * SUB)
                                st_v[i % 2, pl.ds(at, 2 * SUB), near[k]] = two.astype(BF16)

                    keep(0, init)

                    def step_j(j, hs):
                        dts = [dt[row8(j), lanes[k]] + cl[row8(j), :] for k in range(tg)]
                        us = [u_s[row8(j), lanes[k]] for k in range(tg)]
                        if g == 0:
                            ys = [jnp.zeros((SUB, LANES), F32) for k in range(tg)]
                        else:
                            ys = [y[row8(j), lanes[k]] for k in range(tg)]
                        new = []
                        for n in range(ng):
                            b = bx[row8(j * N + g + n), :]
                            c = cx[row8(j * N + g + n), :]
                            for k in range(tg):
                                h = jnp.exp2(dts[k] * rr[n][k]) * hs[n * tg + k] + us[k] * b
                                ys[k] = ys[k] + h * c
                                new.append(h)
                        for k in range(tg):
                            y[row8(j), lanes[k]] = ys[k]
                        keep(j + 1, new)
                        return tuple(new)

                    lax.fori_loop(0, J, step_j, tuple(init), unroll=2)
                return carry

            lax.fori_loop(0, cs // wide, pair, 0)
            save(i).start()
            yv = y[:, C] + sm[SKIP : SKIP + 1, C] * sig[:, C].astype(F32)
            y[:, C] = yv
            g_in = gate[:, C]
            gated = (yv * (g_in * sigmoid(g_in))).astype(BF16)
            acc[...] += mm(gated, wo[C, :])

        keeps[4].start()
        m32 = tok[...].astype(F32) + acc[...]
        mid[...] = m32
        moe[...] = (m32 * rms_scale(m32) * gp[1:2, :]).astype(BF16)
        ch_o[...] = router_softmax(mm_nt(moe[...], rt[...]), E)
        outb[...] = mm_tn(table[...], moe[...]).astype(BF16)
        out_moves = [remote(block_of(outb, p), arr_o.at[core, me], d_s.at[k], d_r.at[k], {"exp": p}) for k, p in enumerate(zz)]
        for c in out_moves:
            c.start()
        arr_own = pltpu.make_async_copy(block_of(outb, me), arr_o.at[core, me], ld.at[12])
        arr_own.start()
        passes = [
            remote(block_of(cotb, me), cot_o.at[core, me], x_s.at[0, 0], x_r.at[0, 0], sib),
            remote(block_of(outb, me), arr_o.at[core, me], x_s.at[1, 0], x_r.at[1, 0], sib),
        ]
        for c in passes:
            c.start()
        for w, ref, send, recv in ((0, cot_o, k_s, k_r), (1, arr_o, d_s, d_r)):
            for k in range(1, E):
                frm = lax.rem(me + E - k, E)
                at = ref.at[core, frm]
                remote(at, at, send.at[k - 1], recv.at[k - 1], {"exp": frm}).wait_recv()
                c = remote(at, at, x_s.at[w, k], x_r.at[w, k], sib)
                c.start()
                passes.append(c)
        if plane:
            for p in parts:
                p.finish()
        for c in outs + keeps + [cot_own, arr_own]:
            c.wait()
        for i in range(max(0, steps - 2), steps):
            save(i).wait()
        for c in cot_moves + out_moves + passes:
            c.wait_send()
        for w, ref in ((0, cot_o), (1, arr_o)):
            for k in range(E):
                at = ref.at[1 - core, lax.rem(me + E - k, E)]
                remote(at, at, x_s.at[w, k], x_r.at[w, k], sib).wait_recv()

    v = pltpu.VMEM
    sem = lambda *dims: pltpu.SemaphoreType.DMA(dims)
    vm = pl.BlockSpec(memory_space=pltpu.VMEM)
    zslots = 2 * (E - 1)
    ins = (tokens, cotangent, seg, route) + tuple(params) + (in_proj, out_proj)
    vm_outs = [
        sds((z.SMALL, DI), F32), sds((gr, D), F32), sds((LANES, D), BF16), sds((T, M), BF16), sds((T, LANES), F32),
        sds((T, SUB), F32), sds((H, DI), F32), sds((T, z.XW), F32), sds((T, D), F32), sds((T, D), BF16),
        sds((T, LANES), F32), sds((S, 1, DI), F32), sds((T, D), BF16), sds((T, D), BF16), sds((T, D), BF16),
    ]
    any_outs = [
        sds((ST, DI), BF16), sds((D, 2 * DI), BF16), sds((DI, D), BF16), sds((2, E, CAP, D), BF16),
        sds((2, E, CAP, D), BF16), sds((T, DI), F32), sds((T, DI), F32), sds((T, DI), BF16), sds((T, DI), F32),
        sds((T, DI), F32),
    ]
    return pl.pallas_call(
        body,
        name="forward",
        in_specs=[vm] * 4 + [vm if plane else ANY] * len(params) + [ANY] * 2,
        out_specs=[vm] * len(vm_outs) + [ANY] * len(any_outs),
        out_shape=vm_outs + any_outs,
        scratch_shapes=[
            v((T, DI), F32), v((T, DI), F32), v((T, DI), BF16), v((T, DI), F32), v((T, DI), F32),
            v((D, DI), BF16), v((D, DI), BF16), v((DI, D), BF16), v((E * rs, DZ), BF16), v((E * rg, NZ), BF16),
            v((T + H, D), BF16), v((H, D), BF16), v((SUB, LANES), F32),
            v((J * N * SUB, LANES), F32), v((J * N * SUB, LANES), F32), v((T, LANES), F32), v((T, DI), F32),
            v((N, DI), F32), v((N, DI), F32), v((N, DI), BF16), v((1, DI), F32), v((S, N, DI), BF16),
            v((N * SUB, DI), F32), v((SUB, DI), F32), v((N, cs), F32),
            v((2, ST, cs), BF16), v((T, D), F32), v((M, D), BF16), v((M, D), BF16),
            v((rs, DZ), BF16), v((rg, NZ), BF16), v((SUB, T), F32),
            sem(18), sem(5, 2, zslots), sem(5, 2, zslots), sem(5, 4, zslots), sem(5, 4, zslots),
            sem(5, 5, zslots), sem(5, 5, zslots), sem(2), sem(2), sem(2, S - 1), sem(2, S - 1),
            sem(E - 1), sem(E - 1), sem(1), sem(1), sem(E - 1), sem(E - 1),
            sem(2, E), sem(2, E),
        ],
        compiler_params=pltpu.CompilerParams(
            collective_id=cid, has_side_effects=True, vmem_limit_bytes=60 * 1024 * 1024
        ),
    )(*ins)


def backward(z, S, plane, expert_out, dx_z, dwu, dwd, states, w_out, w_in, table, choose, chances, mid, moe, cot, gpack,
             router, gate, y, sig, small, mixed, dt, masks, conv_in, hconv, s_all, tok, normed_all, cid):
    T, D, DI, N, J, E, CAP = z.T, z.D, z.DI, z.N, z.J, z.E, z.CAP
    M = E * CAP
    G = gpack.shape[0]
    H = hconv.shape[0]
    DZ, NZ = DI // E, D // E
    cb_m = pick(DI, (384, 256, 128))
    cb_s = pick(DI, (256, 128))
    steps_s = DI // cb_s
    tg_s = tile_groups(cb_s)
    ng_s = 4
    uq, uc = dwu.shape[0] // 4, dwu.shape[1]
    dq, dc = dwd.shape[0] // 4, dwd.shape[1]
    ST = (J + 1) * N * SUB
    rows_big = max(ST, 2 * D)
    chain_slots = 2 * (E - 1)

    def body(
        eo, dwu, dwd, states, w_out, w_in, dx_z, table, choose, chances, mid, moe, cot, gp, router, gate_h, y_h, sig_h,
        small_h, mixed, dt_h, masks, conv_h, hconv, s_all, tok, nall,
        tg_o, gs_o, gg_o, back_o, pg_o, pc_o, pm_o, po_o, up_o, down_o,
        gate, y, sig, small, dt, conv_in, own_v, big, wo_v, n_v, yg, gi, gz, br, mg, fdev, f_all, suf, cg_edge,
        edge_in, pc, bx, cx, ia, oa, cl, u_s, rates_s, fin, dg_s, rs_s, rt_s, low_s, mxg, fd,
        ua, ub, ub2, da, db, db2, gi_all, pc_all, br_all, gz_all, gi_b,
        p_g, p_c, p_m, p_o, bg, bc, bm, bo, tg_, tc_, tm_, to_, zg, zc, zm,
        pcs, pcr, pqs, pqr, pzs, pzr, pgs, pgr, pfs, pfr, pown,
        ld, oz_s, oz_r, f_s, f_r, e_s, e_r, g_s, g_r, p_s, p_r, b_s, b_r, a_s, a_r, x_s, x_r,
    ):
        wide_loads = [
            pltpu.make_async_copy(a, b, ld.at[18 + n])
            for n, (a, b) in enumerate(
                ((gate_h, gate), (y_h, y), (sig_h, sig), (small_h, small), (dt_h, dt), (conv_h, conv_in))
            )
        ]
        for c in wide_loads:
            c.start()
        psems = lambda a: (
            pcs.at[a], pcr.at[a], pqs.at[a], pqr.at[a], pzs.at[a], pzr.at[a], pgs.at[a], pgr.at[a], pfs.at[a],
            pfr.at[a], pown.at[a],
        )
        extra = lambda rows: (16 * (rows // 128), -(-(rows // 16 % 8) // 2) if rows // 16 % 8 else 4)
        sum_g = PlaneSum(E, p_g, bg, tg_, zg, pg_o, False, *extra(NZ), psems(0))
        sum_c = PlaneSum(E, p_c, bc, tc_, zc, pc_o, False, *extra(NZ), psems(1))
        sum_m = PlaneSum(E, p_m, bm, tm_, zm, pm_o, True, 0, 4, psems(2))
        sum_o = PlaneSum(E, p_o, bo, to_, None, po_o, False, *extra(DZ), psems(3))
        stage = (lambda f: f()) if plane else (lambda f: None)
        s, me = lax.axis_index("seq"), lax.axis_index("exp")
        core = lax.rem(s, 2)
        other = 1 - core
        sib = {"seq": s + 1 - 2 * core}
        seqs = [lax.rem(s + k, S) for k in range(1, S)]
        zs = [lax.rem(me + k, E) for k in range(1, E)]
        greet([{"seq": p} for p in seqs] + [{"exp": p} for p in zs])

        def remote(src, dst, send, recv, to):
            return pltpu.make_async_remote_copy(src, dst, send, recv, device_id=to, device_id_type=MESH)

        def out_load(i):
            slot = lax.rem(i, 2)
            rows = pl.ds(pl.multiple_of(i * cb_m, LANES), cb_m)
            return pltpu.make_async_copy(w_out.at[rows], wo_v.at[slot], ld.at[2 + 15 * slot])

        out_load(0).start()
        normed_load = pltpu.make_async_copy(nall, n_v, ld.at[10])
        normed_load.start()

        def state_load(i):
            return pltpu.make_async_copy(
                states.at[:, at_cols(i, cb_s)], big.at[lax.rem(i, 2), 0:ST], ld.at[3 + lax.rem(i, 2)]
            )

        state_load(0).start()
        if plane:
            chip = s // 2
            xx, yy = lax.rem(chip, 2), chip // 2
            to_x = {"seq": s + 2 - 4 * xx}
            to_y = {"seq": s + 4 - 8 * yy}
            u4 = lambda ref, v, w: ref.at[pl.ds(pl.multiple_of((2 * v + w) * uq, 16), uq)]
            up1 = [
                remote(u4(dwu, v, 1 - xx), ub.at[v], a_s.at[v], a_r.at[v], to_x) for v in range(2)
            ]
            d_half = lambda v: pl.ds(pl.multiple_of(v * 2 * dq, 16), 2 * dq)
            down1 = remote(dwd.at[d_half(1 - yy)], db, a_s.at[2], a_r.at[2], to_y)
            for c in up1 + [down1]:
                c.start()
            mine = [pltpu.make_async_copy(u4(dwu, v, xx), ua.at[v], ld.at[5 + v]) for v in range(2)]
            mine.append(pltpu.make_async_copy(dwd.at[d_half(yy)], da, ld.at[7]))
            for c in mine:
                c.start()

        adds = lambda a, b: (a.astype(F32) + b.astype(F32)).astype(BF16)
        block_of = lambda ref, p: ref.at[pl.ds(pl.multiple_of(p * CAP, 16), CAP)]
        out_moves = [
            remote(block_of(eo, p), block_of(back_o, me), oz_s.at[k], oz_r.at[k], {"exp": p}) for k, p in enumerate(zs)
        ]
        for c in out_moves:
            c.start()
        back_load = pltpu.make_async_copy(block_of(eo, me), own_v, ld.at[8])
        back_own = pltpu.make_async_copy(own_v, block_of(back_o, me), ld.at[8])
        back_load.start()
        expand_columns(z, mixed, z.R, bx)
        expand_columns(z, mixed, z.R + N, cx)
        expand_closed(z, masks, cl)

        back = mm(table[...], dx_z[...])
        grad = cot[...].astype(F32)
        ch = chances[...]
        pick_e = choose[...]
        gating = jnp.sum(ch * pick_e, axis=-1, keepdims=True)
        gate_grad = back[:, D : D + 1] + back[:, D + 1 : D + 2]
        lg = ch * (gate_grad * pick_e - gate_grad * gating)
        hi, lo = split_hi_lo(lg)
        rtv = router[...]
        mig = back[:, 0:D] + mm(hi, rtv) + mm(lo, rtv)
        mev = moe[...]
        rg = mm_tn(hi, mev) + mm_tn(lo, mev)
        d, gain_g = rms_back(mid[...], gp[1:2, :], mig)
        mg[...] = grad + d
        br[...] = mg[...].astype(BF16)
        gg_o[...] = jnp.zeros_like(gg_o)
        gg_o[1:2, :] = gain_g
        gg_o[2 : 2 + E, :] = rg[0:E, :]
        chain_b = Chain(E, br, br_all, b_s, b_r, ld.at[9])
        for c in wide_loads:
            c.wait()

        def middle_block(i, carry):
            C = at_cols(i, cb_m)
            out_load(i).wait()

            @pl.when(i + 1 < DI // cb_m)
            def _():
                out_load(i + 1).start()

            gg = mm_nt(br[...], wo_v[lax.rem(i, 2)])
            g_in = gate[:, C]
            sg = sigmoid(g_in)
            act = g_in * sg
            yv = y[:, C]
            ygv = gg * act
            yg[:, C] = ygv
            gi[:, C] = (gg * yv * (sg * (1.0 + g_in * (1.0 - sg)))).astype(BF16)
            pc[:, C] = (yv * act).astype(BF16)
            gs_o[SKIP : SKIP + 1, C] = jnp.sum(ygv * sig[:, C].astype(F32), axis=0, keepdims=True)
            return carry

        lax.fori_loop(0, DI // cb_m, middle_block, 0)
        for e in range(E):
            gi_b[e] = gi[:, e * DZ : (e + 1) * DZ]

        def trade(src, dst, send, recv):
            return [remote(src.at[p], dst.at[me], send.at[k], recv.at[k], {"exp": p}) for k, p in enumerate(zs)]

        gi_moves = trade(gi_b, gi_all, g_s, g_r)
        for c in gi_moves:
            c.start()
        gi_all[me] = gi_b[me]
        chain_b.start()
        back_load.wait()
        back_own.start()

        tg, ng = 2 if DI % 256 == 0 else 1, 8
        wide = tg * LANES

        def flow_block(i, carry):
            lanes = [pl.ds(pl.multiple_of(i * wide, LANES) + k * LANES, LANES) for k in range(tg)]
            both = pl.ds(pl.multiple_of(i * wide, LANES), wide)
            rates = -jnp.exp(small[A_LOG : A_LOG + N, both]) * LOG2E
            wins = []
            for k in range(tg):
                w1 = jnp.zeros((SUB, LANES), F32)
                for j in range(J):
                    w1 = w1 + (dt[j * SUB : j * SUB + SUB, lanes[k]] + cl[j * SUB : j * SUB + SUB, :])
                w2 = w1 + shift_up(w1, 1)
                w4 = w2 + shift_up(w2, 2)
                w8 = w4 + shift_up(w4, 4)
                wins.append((w1, w2, w4))
                suf[N * SUB : (N + 1) * SUB, lanes[k]] = shift_up(w8, 1)
            for g in range(0, N, ng):
                rr = [
                    [
                        jnp.broadcast_to(rates[g + n : g + n + 1, k * LANES : (k + 1) * LANES], (SUB, LANES))
                        for k in range(tg)
                    ]
                    for n in range(ng)
                ]

                def step_j(jj, fs):
                    j = J - 1 - jj
                    dts = [dt[row8(j), lanes[k]] + cl[row8(j), :] for k in range(tg)]
                    ygs = [yg[row8(j), lanes[k]] for k in range(tg)]
                    new = []
                    for n in range(ng):
                        c = cx[row8(j * N + g + n), :]
                        for k in range(tg):
                            new.append(jnp.exp2(dts[k] * rr[n][k]) * (fs[n * tg + k] + ygs[k] * c))
                    return tuple(new)

                fs = lax.fori_loop(
                    0, J, step_j, tuple(jnp.zeros((SUB, LANES), F32) for _ in range(ng * tg)), unroll=2
                )
                for n in range(ng):
                    for k in range(tg):
                        f = fs[n * tg + k]
                        w1, w2, w4 = wins[k]
                        r = rr[n][k]
                        f = f + jnp.exp2(r * w1) * shift_up(f, 1)
                        f = f + jnp.exp2(r * w2) * shift_up(f, 2)
                        f = f + jnp.exp2(r * w4) * shift_up(f, 4)
                        suf[(g + n) * SUB : (g + n + 1) * SUB, lanes[k]] = shift_up(f, 1)
                        fd[g + n : g + n + 1, lanes[k]] = f[0:1, :]
            return carry

        lax.fori_loop(0, DI // wide, flow_block, 0)
        fdev[...] = fd[...].astype(BF16)
        f_moves = [
            remote(fdev, f_all.at[s], f_s.at[k], f_r.at[k], {"seq": p}) for k, p in enumerate(seqs)
        ]
        for c in f_moves:
            c.start()
        f_all[s] = fdev[...]
        for e in range(E):
            gz[e] = pc[:, e * DZ : (e + 1) * DZ]
        gz_moves = trade(gz, gz_all, x_s, x_r)
        for c in gz_moves:
            c.start()
        gz_all[me] = gz[me]
        p_g[...] = jnp.zeros_like(p_g)
        p_c[...] = jnp.zeros_like(p_c)
        p_o[...] = jnp.zeros_like(p_o)

        def place_in(dst, rhs):
            blk = pick(D, (384, 256, 128))
            for i in range(D // blk):
                val = mm_tn(n_v[:, i * blk : (i + 1) * blk], rhs)
                for g in range(blk // 16):
                    row = i * blk + 16 * g
                    chunk, off = group_place(D // E // 16, row % (D // E) // 16)
                    dst[row // (D // E), chunk // 2, chunk % 2, off : off + 16, :] = val[16 * g : 16 * g + 16].astype(
                        BF16
                    )

        flat = lambda ref: ref[...].reshape(E * T, ref.shape[-1])
        if plane:
            for c in mine + up1 + [down1]:
                c.wait()
            ua[...] = adds(ua[...], ub[...])
            da[...] = adds(da[...], db[...])
            up2 = remote(ua.at[1 - yy], ub2, a_s.at[3], a_r.at[3], to_y)
            down2 = remote(
                da.at[pl.ds(pl.multiple_of((1 - xx) * dq, 16), dq)], db2, a_s.at[4], a_r.at[4], to_x
            )
            up2.start()
            down2.start()
        for c in f_moves:
            c.wait()

        ia[...] = jnp.zeros_like(ia)
        oa[...] = jnp.zeros_like(oa)
        low_s[...] = jnp.zeros_like(low_s)
        low = mixed[:, 0 : z.R].astype(BF16)

        def scan_block(i, carry_):
            state_load(i).wait()

            @pl.when(i + 1 < steps_s)
            def _():
                state_load(i + 1).start()

            slot = lax.rem(i, 2)
            C = at_cols(i, cb_s)
            rates2 = -jnp.exp(small[A_LOG : A_LOG + N, C]) * LOG2E
            rates_s[...] = rates2
            fin[...] = chain_states(
                S - 1, lambda k: k > s, lambda k: S - 1 - k, lambda k: s_all[k, :, C], lambda k: f_all[k, :, C],
                rates2,
            )
            sigf = sig[:, C].astype(F32)
            u_s[...] = dt[:, C] * sigf

            def pair(p, carry):
                lanes = [lanes_of(i, cb_s, p, tg_s, k) for k in range(tg_s)]
                near = [slice(k * LANES, (k + 1) * LANES) for k in range(tg_s)]
                for g in range(0, N, ng_s):
                    rr = [
                        [
                            jnp.broadcast_to(rates_s[g + n : g + n + 1, near[k]], (SUB, LANES))
                            for k in range(tg_s)
                        ]
                        for n in range(ng_s)
                    ]
                    flow = []
                    for n in range(ng_s):
                        for k in range(tg_s):
                            at = (g + n) * SUB
                            flow.append(
                                suf[at : at + SUB, lanes[k]]
                                + jnp.exp2(rr[n][k] * suf[N * SUB : (N + 1) * SUB, lanes[k]])
                                * jnp.broadcast_to(fin[g + n : g + n + 1, near[k]], (SUB, LANES))
                            )

                    def load(j):
                        got = [[None] * tg_s for _ in range(ng_s)]
                        for n in range(0, ng_s, 2):
                            for k in range(tg_s):
                                at = pl.multiple_of(j * N * SUB + (g + n) * SUB, 2 * SUB)
                                two = big[slot, pl.ds(at, 2 * SUB), near[k]].astype(F32)
                                got[n][k] = two[0:SUB]
                                got[n + 1][k] = two[SUB : 2 * SUB]
                        return [got[n][k] for n in range(ng_s) for k in range(tg_s)]

                    def step_j(jj, carry):
                        fs, hs, rts = carry
                        j = J - 1 - jj
                        dtp = [dt[row8(j), lanes[k]] for k in range(tg_s)]
                        dts = [dtp[k] + cl[row8(j), :] for k in range(tg_s)]
                        us = [u_s[row8(j), near[k]] for k in range(tg_s)]
                        ygs = [yg[row8(j), lanes[k]] for k in range(tg_s)]
                        before = load(j)
                        if g == 0:
                            dgs = [jnp.zeros((SUB, LANES), F32) for k in range(tg_s)]
                            rss = [jnp.zeros((SUB, LANES), F32) for k in range(tg_s)]
                        else:
                            dgs = [dg_s[row8(j), near[k]] for k in range(tg_s)]
                            rss = [rs_s[row8(j), near[k]] for k in range(tg_s)]
                        nf, nr = [], []
                        for n in range(ng_s):
                            at = row8(j * N + g + n)
                            b = bx[at, :]
                            c = cx[at, :]
                            ig = jnp.zeros((SUB, LANES), F32)
                            og = jnp.zeros((SUB, LANES), F32)
                            for k in range(tg_s):
                                q = n * tg_s + k
                                gr = ygs[k] * c + fs[q]
                                f = jnp.exp2(dts[k] * rr[n][k]) * gr
                                rt = f * before[q]
                                rss[k] = rss[k] + rt * rr[n][k]
                                dgs[k] = dgs[k] + gr * b
                                nr.append(rts[q] + rt * dtp[k])
                                ig = ig + gr * us[k]
                                og = og + hs[q] * ygs[k]
                                nf.append(f)
                            ia[at, :] += ig
                            oa[at, :] += og
                        for k in range(tg_s):
                            dg_s[row8(j), near[k]] = dgs[k]
                            rs_s[row8(j), near[k]] = rss[k]
                        return tuple(nf), tuple(before), tuple(nr)

                    zero = tuple(jnp.zeros((SUB, LANES), F32) for _ in range(ng_s * tg_s))
                    _, _, rts = lax.fori_loop(
                        0, J, step_j, (tuple(flow), tuple(load(J)), zero), unroll=2
                    )
                    for n in range(ng_s):
                        for k in range(tg_s):
                            rt_s[g + n : g + n + 1, near[k]] = jnp.sum(rts[n * tg_s + k], axis=0, keepdims=True)
                return carry

            pair(0, 0)
            dg = dg_s[...]
            yg[:, C] = dg * dt[:, C] + yg[:, C] * small[SKIP : SKIP + 1, C]
            step_grad = rs_s[...] * LN2 + dg * sigf
            dtw = small[z.DT0 : z.DT0 + z.R, C].astype(BF16)
            pre = mm(low, dtw) + small[DT_B : DT_B + 1, C]
            dpg = step_grad * sigmoid(pre)
            dpl = dpg.astype(BF16)
            gs_o[DT_B : DT_B + 1, C] = jnp.sum(dpg, axis=0, keepdims=True)
            gs_o[SKIP + 1 : SKIP + 2, C] = jnp.zeros((1, cb_s), F32)
            gs_o[A_LOG : A_LOG + N, C] = rt_s[...] * (rates2 * LN2)
            gs_o[z.DT0 : z.DT0 + z.R, C] = mm_tn(low, dpl)
            low_s[...] += mm_nt(dpl, dtw)
            return carry_

        third = steps_s // 3
        lax.fori_loop(0, third, scan_block, 0)
        chain_b.hop(1)
        for c in gi_moves:
            c.wait()
        normed_load.wait()
        place_in(p_g, flat(gi_all))
        stage(sum_g.swap_start)
        lax.fori_loop(third, 2 * third, scan_block, 0)
        stage(sum_g.swap_finish)
        chain_b.hop(2)
        lax.fori_loop(2 * third, steps_s, scan_block, 0)
        for k in range(3, E):
            chain_b.hop(k)
        stage(sum_g.chips_finish)

        mxg[:, 0 : z.R] = low_s[...].astype(BF16)
        lane = lax.broadcasted_iota(jnp.int32, (SUB, LANES), 1)

        def gather(j, carry):
            both = jnp.zeros((SUB, LANES), F32)
            for n in range(N):
                at = row8(j * N + n)
                both = jnp.where(lane == n, jnp.sum(ia[at, :], axis=1, keepdims=True), both)
                both = jnp.where(lane == N + n, jnp.sum(oa[at, :], axis=1, keepdims=True), both)
            cl[row8(j), :] = both
            return carry

        lax.fori_loop(0, J, gather, 0)
        mxg[:, z.R : z.R + 2 * N] = cl[:, 0 : 2 * N].astype(BF16)

        def weight_load(i):
            return [
                pltpu.make_async_copy(
                    w_in.at[:, pl.ds(pl.multiple_of(h * DI + i * cb_s, LANES), cb_s)],
                    big.at[lax.rem(i, 2), h * D : (h + 1) * D],
                    ld.at[12 + 2 * lax.rem(i, 2) + h],
                )
                for h in range(2)
            ]

        for c in weight_load(0):
            c.start()

        def conv_block(i, carry):
            C = at_cols(i, cb_m)
            mgv = mxg[...]
            sgv = sig[:, C]
            xw = small[z.X0 : z.X0 + z.XW, C].astype(BF16)
            gs_o[z.X0 : z.X0 + z.XW, C] = mm_tn(mgv, sgv)
            sgrad = yg[:, C] + mm(mgv, xw)
            xpad = padded_rows(conv_in[:, C], hconv[:, C], J, cb_m)
            valid = [jnp.broadcast_to(masks[:, o : o + 1], (T, cb_m)) for o in range(4)]
            out = jnp.broadcast_to(small[CONV_B : CONV_B + 1, C], (T, cb_m))
            for o in range(4):
                w = small[CONV_W + o : CONV_W + o + 1, C]
                out = out + w * xpad[o : o + J].reshape(T, cb_m) * valid[o]
            sv = sigmoid(out)
            cg = sgrad * (sv * (1.0 + out * (1.0 - sv)))
            gs_o[CONV_B : CONV_B + 1, C] = jnp.sum(cg, axis=0, keepdims=True)
            total = jnp.zeros((J, SUB, cb_m), F32)
            final = lax.broadcasted_iota(jnp.int32, (SUB, cb_m), 0) == SUB - 1
            edges = [jnp.zeros((1, cb_m), F32) for _ in range(3)]
            for o in range(4):
                masked = cg * valid[o]
                gs_o[CONV_W + o : CONV_W + o + 1, C] = jnp.sum(
                    masked * xpad[o : o + J].reshape(T, cb_m), axis=0, keepdims=True
                )
                c3 = (small[CONV_W + o : CONV_W + o + 1, C] * masked).reshape(J, SUB, cb_m)
                k = 3 - o
                if k == 0:
                    total = total + c3
                else:
                    wrap = jnp.stack(
                        [jnp.where(final, 0.0, pltpu.roll(c3[t], SUB - 1, 0)) for t in range(k)]
                    )
                    total = total + jnp.concatenate([c3[k:], wrap], axis=0)
                    for i2 in range(o, 3):
                        edges[i2] = edges[i2] + c3[i2 - o, 0:1, :]
            yg[:, C] = total.reshape(T, cb_m)
            cg_edge[:, C] = jnp.concatenate(edges + [jnp.zeros((SUB - 3, cb_m), F32)], axis=0)
            return carry

        lax.fori_loop(0, DI // cb_m, conv_block, 0)
        back_edge = remote(cg_edge, edge_in, e_s, e_r, {"seq": lax.rem(s + S - 1, S)})
        back_edge.start()
        if plane:
            up2.wait()
            down2.wait()
            ub2[...] = adds(ua[yy], ub2[...])
            half_u = uq // 2
            rows_u = lambda c: pl.ds(pl.multiple_of(c * half_u, 16), half_u)
            up3 = remote(ub2.at[rows_u(other)], up_o.at[core], a_s.at[5], a_r.at[5], sib)
            up3.start()
            up_own = pltpu.make_async_copy(ub2.at[rows_u(core)], up_o.at[core], ld.at[16])
            up_own.start()
            db2[...] = adds(da[pl.ds(pl.multiple_of(xx * dq, 16), dq), :], db2[...])
            down_own = pltpu.make_async_copy(db2, down_o, ld.at[11])
            down_own.start()
        for c in gz_moves:
            c.wait()
        chain_b.local().wait()
        groups_o = DZ // 16
        bra = flat(br_all)
        for i in range(2):
            half_o = slice(i * (DZ // 2), (i + 1) * (DZ // 2))
            val = mm_tn(flat(gz_all)[:, half_o], bra)
            for g in range(DZ // 32):
                chunk, off = group_place(groups_o, i * (DZ // 32) + g)
                p_o[0, chunk // 2, chunk % 2, off : off + 16, :] = val[16 * g : 16 * g + 16].astype(BF16)
        stage(sum_o.swap_start)
        stage(sum_g.z_finish)
        back_edge.wait()
        live = jnp.where(s < S - 1, 1.0, 0.0)

        def fix_block(i, carry):
            C = at_cols(i, cb_m)
            c3 = yg[:, C].reshape(J, SUB, cb_m)
            final = lax.broadcasted_iota(jnp.int32, (SUB, cb_m), 0) == SUB - 1
            fixed = jnp.stack(
                [
                    c3[J - 3 + k]
                    + jnp.where(final, jnp.broadcast_to(edge_in[k : k + 1, C] * live, (SUB, cb_m)), 0.0)
                    for k in range(3)
                ]
            )
            pc[:, C] = jnp.concatenate([c3[: J - 3], fixed], axis=0).reshape(T, cb_m).astype(BF16)
            return carry

        lax.fori_loop(0, DI // cb_m, fix_block, 0)
        for e in range(E):
            gi_b[e] = pc[:, e * DZ : (e + 1) * DZ]
        pc_moves = trade(gi_b, pc_all, p_s, p_r)
        for c in pc_moves:
            c.start()
        pc_all[me] = gi_b[me]
        stage(sum_o.swap_finish)
        tg_o[...] = jnp.zeros_like(tg_o)

        def token_block(i, carry):
            for c in weight_load(i):
                c.wait()

            @pl.when(i + 1 < steps_s)
            def _():
                for c in weight_load(i + 1):
                    c.start()

            slot = lax.rem(i, 2)
            C = at_cols(i, cb_s)
            tg_o[...] += mm_nt(pc[:, C], big[slot, 0:D, :]) + mm_nt(gi[:, C], big[slot, D : 2 * D, :])
            return carry

        lax.fori_loop(0, steps_s, token_block, 0)
        d, gain_g = rms_back(tok[...].astype(F32), gp[0:1, :], tg_o[...])
        tg_o[...] = mg[...] + d
        gg_o[0:1, :] = gain_g
        cr = p_m.shape[3]
        for e in range(E):
            side = jnp.concatenate([gg_o[:, e * NZ : (e + 1) * NZ], jnp.zeros((G, DZ - NZ), F32)], axis=1)
            rows = [gs_o[:, e * DZ : (e + 1) * DZ], side, jnp.zeros((8 * cr - z.SMALL - G, DZ), F32)]
            p_m[e] = jnp.concatenate(rows, axis=0).astype(BF16).reshape(4, 2, cr, DZ)
        stage(sum_m.swap_start)
        for c in pc_moves:
            c.wait()
        place_in(p_c, flat(pc_all))
        stage(sum_c.swap_start)
        stage(sum_m.swap_finish)
        stage(sum_o.chips_finish)
        stage(sum_c.swap_finish)
        stage(sum_m.chips_finish)
        stage(sum_g.forward)
        stage(sum_c.chips_finish)
        stage(sum_m.z_finish)
        stage(sum_o.forward)
        stage(sum_c.z_finish)
        for c in out_moves:
            c.wait()
        back_own.wait()
        if plane:
            up3.wait()
            up_own.wait()
            down_own.wait()
            sum_m.forward()
            sum_c.forward()
            for sm_ in (sum_g, sum_o, sum_m, sum_c):
                sm_.finish()
        else:
            copies = [
                pltpu.make_async_copy(p, o, pown.at[a])
                for a, (p, o) in enumerate(((p_g, pg_o), (p_c, pc_o), (p_m, pm_o), (p_o, po_o)))
            ]
            for c in copies:
                c.start()
            for c in copies:
                c.wait()
        for k in range(E - 1):
            for d in (-k, k) if k else (0,):
                chain_b.each(d, lambda c: c.wait_send())

    v = pltpu.VMEM
    sem = lambda *dims: pltpu.SemaphoreType.DMA(dims)
    vm = pl.BlockSpec(memory_space=pltpu.VMEM)
    up_shape = (2, uq // 2, uc) if plane else (1, 16, LANES)
    down_shape = (dq, dc) if plane else (16, LANES)
    u_shape = (2, uq, uc) if plane else (2, 16, LANES)
    d_shape = (2 * dq, dc) if plane else (32, LANES)
    ins = (expert_out, dwu, dwd, states, w_out, w_in, dx_z, table, choose, chances, mid, moe, cot, gpack, router, gate, y,
           sig, small, mixed, dt, masks, conv_in, hconv, s_all, tok, normed_all)
    rg, ro, rm = chunk_rows(NZ), chunk_rows(DZ), 16 * -(-(z.SMALL + G) // 128)
    p_shapes = [(E, 4, 2, rg, DZ), (E, 4, 2, rg, DZ), (E, 4, 2, rm, DZ), (1, 4, 2, ro, D)]
    o_shapes = [(4, 2, E, rg, DZ)] * 2 + [(4, 2, rm, DZ), (4, 2, 1, ro, D)] if plane else p_shapes
    return pl.pallas_call(
        body,
        name="backward",
        in_specs=[ANY if a in (0, 1, 2, 3, 4, 5, 15, 16, 17, 18, 20, 22, 26) else vm for a in range(len(ins))],
        out_specs=[vm] * 3 + [ANY] * 7,
        out_shape=[
            sds((T, D), F32),
            sds((z.SMALL, DI), F32),
            sds((G, D), F32),
            sds((M, D), BF16),
        ]
        + [sds(o, BF16) for o in o_shapes]
        + [
            sds(up_shape, BF16),
            sds(down_shape, BF16),
        ],
        scratch_shapes=[
            v((T, DI), F32), v((T, DI), F32), v((T, DI), BF16), v((z.SMALL, DI), F32), v((T, DI), F32), v((T, DI), F32),
            v((CAP, D), BF16),
            v((2, rows_big, cb_s), BF16),
            v((2, cb_m, D), BF16), v((E * T, D), BF16),
            v((T, DI), F32), v((T, DI), BF16), v((E, T, DZ), BF16),
            v((T, D), BF16), v((T, D), F32),
            v((N, DI), BF16), v((S, N, DI), BF16), v(((N + 1) * SUB, DI), F32),
            v((SUB, DI), F32), v((SUB, DI), F32),
            v((T, DI), BF16),
            v((J * N * SUB, LANES), F32), v((J * N * SUB, LANES), F32),
            v((J * N * SUB, LANES), F32), v((J * N * SUB, LANES), F32),
            v((T, LANES), F32), v((T, cb_s), F32), v((N, cb_s), F32), v((N, cb_s), F32),
            v((T, cb_s), F32), v((T, cb_s), F32), v((N, cb_s), F32), v((T, z.R), F32), v((T, z.XW), BF16),
            v((N, DI), F32),
            v(u_shape, BF16), v(u_shape, BF16), v(u_shape[1:], BF16),
            v(d_shape, BF16), v(d_shape, BF16), v((d_shape[0] // 2, d_shape[1]), BF16),
            v((E, T, DZ), BF16), v((E, T, DZ), BF16), v((E, T, D), BF16), v((E, T, DZ), BF16),
            v((E, T, DZ), BF16),
        ]
        + [v(p, BF16) for p in p_shapes]
        + [v((p[0], 4) + p[3:], BF16) for p in p_shapes]
        + [v((3, p[0]) + p[3:], BF16) for p in p_shapes]
        + [v((E,) + p[3:], BF16) for p in p_shapes[:3]]
        + [
            sem(4, 2), sem(4, 2), sem(4, 3, 2), sem(4, 3, 2), sem(4, E - 1, 2), sem(4, E - 1, 2), sem(4, 3, 2),
            sem(4, 3, 2), sem(4, 4, 2), sem(4, 4, 2), sem(4),
            sem(24), sem(E - 1), sem(E - 1), sem(S - 1), sem(S - 1),
            pltpu.SemaphoreType.DMA, pltpu.SemaphoreType.DMA,
            sem(E - 1), sem(E - 1), sem(E - 1), sem(E - 1), sem(chain_slots), sem(chain_slots),
            sem(6), sem(6), sem(E - 1), sem(E - 1),
        ],
        compiler_params=pltpu.CompilerParams(
            collective_id=cid, has_side_effects=True, vmem_limit_bytes=60 * 1024 * 1024
        ),
    )(*ins)


def finish(z, gr, plane, pg, pc, pm, po, tg, mid, chances, choose, table, back, up, down):
    T, D, DI, N, J, E = z.T, z.D, z.DI, z.N, z.J, z.E
    DZ, NZ, FB = DI // E, D // E, z.FF // 8
    U = up.shape[1]

    def body(pg, pc, pm, po, tg, mid, ch, cho, tb, bk, up, dn, *outs):
        dwi, dwo, out, tgo, cw, cb, xw, dw, db, al, sk, na, nb, ro = outs[:14]
        for g in range(NZ // 16):
            chunk, off = group_place(NZ // 16, g)
            for h, src in enumerate((pc, pg)):
                for e in range(E):
                    dwi[16 * g : 16 * g + 16, h * DI + e * DZ : h * DI + (e + 1) * DZ] = src[
                        chunk, e, off : off + 16, :
                    ].astype(F32)
        for g in range(DZ // 16):
            chunk, off = group_place(DZ // 16, g)
            dwo[16 * g : 16 * g + 16, :] = po[chunk, off : off + 16, :].astype(F32)
        sm = pm[...].astype(F32)
        cw[...] = sm[CONV_W : CONV_W + 4]
        for ref, row in ((cb, CONV_B), (db, DT_B), (sk, SKIP)):
            ref[...] = sm[row : row + 1].reshape(DZ)
        al[...] = sm[A_LOG : A_LOG + N]
        dw[...] = sm[z.DT0 : z.X0]
        xw[...] = sm[z.X0 : z.SMALL]
        na[...] = sm[z.SMALL : z.SMALL + 1, 0:NZ].reshape(NZ)
        nb[...] = sm[z.SMALL + 1 : z.SMALL + 2, 0:NZ].reshape(NZ)
        ro[...] = sm[z.SMALL + 2 : z.SMALL + 2 + E, 0:NZ]
        lane = lax.broadcasted_iota(jnp.int32, (T, T), 1)
        prow = lax.broadcasted_iota(jnp.int32, (T, T), 0)
        order = (lane == (prow % SUB) * J + prow // SUB).astype(F32).astype(BF16)
        gating = jnp.sum(ch[...] * cho[...], axis=-1, keepdims=True)
        low = (mid[...] + gating * mm(tb[...], bk[...])).astype(BF16)
        out[...] = mm_tn(order, low).astype(BF16)
        v = tg[...]
        hi, rest = v.astype(BF16), v - v.astype(BF16).astype(F32)
        lo, end = split_hi_lo(rest)
        tgo[...] = mm_tn(order, hi) + (mm_tn(order, lo) + mm_tn(order, end))
        if plane:
            upo, dno = outs[14:]
            for c in range(2):
                for i in range(4):
                    at = (2 * i + c) * FB
                    upo[:, at : at + FB] = up[c, :, i * FB : (i + 1) * FB].astype(F32)
            dno[...] = dn[...].astype(F32)

    vm = pl.BlockSpec(memory_space=pltpu.VMEM)
    shapes = [
        sds((NZ, 2 * DI), F32), sds((DZ, D), F32), sds((T, D), BF16), sds((T, D), F32), sds((4, DZ), F32),
        sds((DZ,), F32), sds((z.XW, DZ), F32), sds((z.R, DZ), F32), sds((DZ,), F32), sds((N, DZ), F32),
        sds((DZ,), F32), sds((NZ,), F32), sds((NZ,), F32), sds((E, NZ), F32),
    ]
    if plane:
        shapes += [sds((U, z.FF), F32), sds(down.shape, F32)]
    return pl.pallas_call(
        body,
        name="finish",
        in_specs=[vm] * 12,
        out_specs=[vm] * len(shapes),
        out_shape=shapes,
        compiler_params=pltpu.CompilerParams(vmem_limit_bytes=VMEM_LIMIT),
    )(pg, pc, pm, po, tg, mid, chances, choose, table, back, up, down)


def on_device(
    tokens, segment_ids, routes, cotangent, norm_gain, in_proj, conv_weight, conv_bias, x_proj,
    dt_proj, dt_bias, a_log, d_skip, out_proj, moe_gain, router, up_proj, down_proj,
):
    E = lax.axis_size("exp")
    S = lax.axis_size("seq")
    z = Sizes(tokens, in_proj, dt_proj, x_proj, a_log, up_proj, E)
    T, D, DI, N, J, CAP = z.T, z.D, z.DI, z.N, z.J, z.CAP
    me_s, me_e = lax.axis_index("seq"), lax.axis_index("exp")
    core = lax.rem(me_s, 2)
    cw = dt_proj.shape[1]
    dw = norm_gain.shape[0]
    plane = S == 8 and dw % 32 == 0
    line = lambda v: v.reshape(1, -1)
    if plane:
        params = [conv_weight, conv_bias, dt_bias, d_skip, a_log, dt_proj, x_proj.T, norm_gain, moe_gain, router.T]
        w_in, w_out = in_proj, out_proj
    else:
        small_own = jnp.concatenate(
            [conv_weight, line(conv_bias), line(dt_bias), line(d_skip), jnp.zeros((1, cw), BF16), a_log, dt_proj,
             x_proj.T, jnp.zeros((small_rows(z) - z.SMALL, cw), BF16)], axis=0
        )
        g_own = jnp.concatenate(
            [line(norm_gain), line(moe_gain), router.T, jnp.zeros((32 - 2 - E, dw), BF16)], axis=0
        )
        gathered = [lax.all_gather(a, "exp", tiled=True) for a in (in_proj, out_proj, small_own, g_own)]
        w_in, w_out, params = gathered[0], gathered[1], gathered[2:]
    gr = 8 * -(-(2 + E) // 8)
    (
        small, gpack, router_t, table, choose_wide, masks, hconv, mixed, mid, moe, chances, s_all, tok, cot, normed,
        states, w_in, w_out, arrived, cot_pair, conv_in, gate, sig, dt, y,
    ) = forward(
        z, S, plane, tokens[0], cotangent[0], segment_ids, routes.reshape(1, T), params, w_in, w_out, gr, 1
    )
    dx_z, expert_out, dwu, dwd, normed_all = expert(
        z, arrived.reshape(2 * E * CAP, D), cot_pair.reshape(2 * E * CAP, D), router_t, normed, up_proj[0],
        down_proj[0], 3
    )
    token_grad, _, _, back_out, pg, pc, pm, po, up_sum, down_sum = backward(
        z, S, plane, expert_out, dx_z, dwu, dwd, states, w_out, w_in, table, choose_wide, chances, mid, moe, cot, gpack, router_t,
        gate, y, sig, small, mixed, dt, masks, conv_in, hconv, s_all, tok, normed_all.reshape(E * T, D), 4
    )
    if not plane:
        pg, pc, pm, po = [lax.psum(a, "seq") for a in (pg, pc, pm, po)]
        pg, pc = [
            lax.all_to_all(a, "exp", split_axis=0, concat_axis=0, tiled=True).transpose(1, 2, 0, 3, 4)
            for a in (pg, pc)
        ]
        pm = lax.psum_scatter(pm, "exp", scatter_dimension=0, tiled=True)[0]
        po = po[0]
    eight = lambda a: a.reshape((8,) + a.shape[2:])
    dw_in, dw_out, output, token_grad, g_cw, g_cb, g_xw, g_dw, g_db, g_al, g_sk, g_na, g_nb, g_ro, *rest = finish(
        z, gr, plane, eight(pg), eight(pc), pm.reshape(-1, pm.shape[-1]), po.reshape(8, -1, D), token_grad, mid,
        chances, choose_wide, table, back_out, up_sum, down_sum
    )
    if plane:
        up_part, down_part = rest
    else:
        fb = z.FF // 8
        up_full = jnp.zeros((D, 4, 2, fb), BF16)
        up_full = lax.dynamic_update_slice_in_dim(up_full, dwu.reshape(D, 4, 1, fb), core, axis=2)
        down_full = jnp.zeros((4, 2, fb, D), BF16)
        down_full = lax.dynamic_update_slice_in_dim(down_full, dwd.reshape(4, 1, fb, D), core, axis=1)
        up_part, down_part = [
            lax.psum_scatter(v, "seq", scatter_dimension=0, tiled=True).astype(F32)
            for v in (up_full.reshape(D, z.FF), down_full.reshape(z.FF, D))
        ]
    return (
        output[None], token_grad[None], g_na, dw_in, g_cw, g_cb, g_xw.T, g_dw, g_db, g_al, g_sk, dw_out,
        g_nb, g_ro.T, up_part[None], down_part[None],
    )


def solution(mesh):
    row = P("exp", "seq", None)
    in_specs = (
        row, P("exp", "seq"), row, row, P("exp"), P("exp", None), P(None, "exp"), P("exp"), P("exp", None),
        P(None, "exp"), P("exp"), P(None, "exp"), P("exp"), P("exp", None), P("exp"), P("exp", None),
        P("exp", None, None), P("exp", None, None),
    )
    out_specs = (
        row, row, P("exp"), P("exp", None), P(None, "exp"), P("exp"), P("exp", None), P(None, "exp"), P("exp"),
        P(None, "exp"), P("exp"), P("exp", None), P("exp"), P("exp", None), row, row,
    )
    return jax.shard_map(on_device, mesh=mesh, in_specs=in_specs, out_specs=out_specs, check_vma=False)
```

```python
import functools
import math

import jax
import jax.numpy as jnp
from jax import lax
from jax.experimental import pallas as pl
from jax.experimental.pallas import tpu as pltpu
from jax.sharding import PartitionSpec as P

EPSILON = 1e-05
LOG2E = math.log2(math.e)
LN2 = math.log(2.0)
CLOSED = 1e30
LANES = 128
SUB = 8
F32 = jnp.float32
BF16 = jnp.bfloat16
VMEM_LIMIT = 56 * 1024 * 1024


def mm(a, b):
    return lax.dot_general(a, b, (((1,), (0,)), ((), ())), preferred_element_type=F32)


def mm_nt(a, b):
    return lax.dot_general(a, b, (((1,), (1,)), ((), ())), preferred_element_type=F32)


def mm_tn(a, b):
    return lax.dot_general(a, b, (((0,), (0,)), ((), ())), preferred_element_type=F32)


def split_hi_lo(value):
    high = value.astype(BF16)
    return high, (value - high.astype(F32)).astype(BF16)


def sigmoid(v):
    return 1.0 / (1.0 + jnp.exp(-v))


def softplus(v):
    e = jnp.exp(-jnp.abs(v))
    small = e * (1.0 - e * (0.5 - e * (1.0 / 3.0 - e * 0.25)))
    return jnp.maximum(v, 0.0) + jnp.where(e < 0.01, small, jnp.log(1.0 + e))


def rms_scale(v):
    return lax.rsqrt(jnp.mean(v * v, axis=-1, keepdims=True) + EPSILON)


def rms_back(resid, gain, grad):
    s = rms_scale(resid)
    v = gain * grad
    out = s * v - resid * (s * s * s) * jnp.mean(resid * v, axis=-1, keepdims=True)
    return out, jnp.sum(grad * resid * s, axis=0, keepdims=True)


def block(shape, index):
    return pl.BlockSpec(shape, index)


def whole(shape):
    zeros = (0,) * len(shape)
    return pl.BlockSpec(shape, lambda *_: zeros)


def call(body, name, grid, ins, in_specs, outs, out_specs, scratch, cost=None):
    return pl.pallas_call(
        body,
        name=name,
        grid=grid,
        in_specs=in_specs,
        out_specs=out_specs,
        out_shape=outs,
        scratch_shapes=scratch,
        cost_estimate=cost,
        compiler_params=pltpu.CompilerParams(vmem_limit_bytes=VMEM_LIMIT),
    )(*ins)


def sds(shape, dtype):
    return jax.ShapeDtypeStruct(shape, dtype)


def pick(total, options):
    for o in options:
        if total % o == 0:
            return o
    return total


CONV_W, CONV_B, DT_B, SKIP, A_LOG = 0, 4, 5, 6, 8


class Sizes:
    def __init__(self, tokens, in_proj, dt_proj, x_proj, a_log, up_proj, exp_count):
        self.T = tokens.shape[1]
        self.D = tokens.shape[2]
        self.DI = in_proj.shape[1] // 2
        self.N = a_log.shape[0]
        self.R = dt_proj.shape[0]
        self.XW = x_proj.shape[1]
        self.FF = up_proj.shape[2]
        self.E = exp_count
        self.CAP = 2 * self.T // exp_count
        self.J = self.T // SUB
        self.DT0 = A_LOG + self.N
        self.X0 = self.DT0 + self.R
        self.SMALL = self.X0 + self.XW


MESH = pl.DeviceIdType.MESH
ANY = pl.BlockSpec(memory_space=pl.ANY)


def greet(peers):
    barrier = pltpu.get_barrier_semaphore()
    for peer in peers:
        pl.semaphore_signal(barrier, inc=1, device_id=peer, device_id_type=MESH)
    pl.semaphore_wait(barrier, len(peers))


def group_place(groups, g):
    main = groups // 8
    if g < 8 * main:
        return g // main, 16 * (g % main)
    return g - 8 * main, 16 * main


def chunk_rows(rows):
    groups = rows // 16
    return 16 * (groups // 8 + (1 if groups % 8 else 0))


class PlaneSum:
    def __init__(self, E, p, b, t, zb, out, add, base, full, sems):
        self.E, self.p, self.b, self.t, self.zb, self.out, self.add = E, p, b, t, zb, out, add
        self.rows, self.full = p.shape[3], full
        self.base = base if full < 4 else self.rows
        self.cs, self.cr, self.qs, self.qr, self.zs, self.zr, self.gs, self.gr, self.fs, self.fr, self.own = sems
        s, self.me = lax.axis_index("seq"), lax.axis_index("exp")
        self.chip, self.core = s // 2, lax.rem(s, 2)
        self.sib = {"seq": s + 1 - 2 * self.core}
        self.chips = [self.chip + 1 - 2 * lax.rem(self.chip, 2), self.chip + 2 - 4 * (self.chip // 2), 3 - self.chip]
        self.far = [{"seq": q * 2 + self.core} for q in self.chips]
        self.zz = [lax.rem(self.me + k, E) for k in range(1, E)]

    def pair(self, src, dst, send, recv, to):
        cut = lambda ref, a, n: ref.at[(slice(None),) * (len(ref.shape) - 2) + (pl.ds(a, n),)]
        make = lambda a, n, i: pltpu.make_async_remote_copy(
            cut(src, a, n), cut(dst, a, n), send.at[i], recv.at[i], device_id=to, device_id_type=MESH
        )
        if self.base == self.rows:
            return [make(0, self.rows, 0)]
        return [make(0, self.base, 0), make(self.base, self.rows - self.base, 1)]

    def run(self, copies, chip, act):
        act(copies[0])
        if len(copies) > 1:
            @pl.when(chip < self.full)
            def _():
                act(copies[1])

    def swap_start(self):
        self.swap = self.pair(self.p.at[:, :, 1 - self.core], self.b, self.cs, self.cr, self.sib)
        if len(self.swap) > 1:
            src, dst = self.p.at[:, 0 : self.full, 1 - self.core], self.b.at[:, 0 : self.full]
            self.swap[1] = self.pair(src, dst, self.cs, self.cr, self.sib)[1]
        for c in self.swap:
            c.start()

    def swap_finish(self):
        for c in self.swap:
            c.wait()
        B = self.base
        for l in range(self.p.shape[0]):
            self.p[l, :, self.core, 0:B] = (
                self.p[l, :, self.core, 0:B].astype(F32) + self.b[l, :, 0:B].astype(F32)
            ).astype(BF16)
            if B < self.rows:
                F = self.full
                self.p[l, 0:F, self.core, B:] = (
                    self.p[l, 0:F, self.core, B:].astype(F32) + self.b[l, 0:F, B:].astype(F32)
                ).astype(BF16)
        self.crossing = [
            self.pair(self.p.at[:, self.chips[k], self.core], self.t.at[k], self.qs.at[k], self.qr.at[k], self.far[k])
            for k in range(3)
        ]
        for k in range(3):
            self.run(self.crossing[k], self.chips[k], lambda c: c.start())

    def chips_finish(self):
        for k in range(3):
            self.run(self.crossing[k], self.chips[k], lambda c: c.wait_send())
            self.run(self.crossing[k], self.chip, lambda c: c.wait_recv())

        def total(rows):
            for l in range(self.p.shape[0]):
                v = self.p[l, self.chip, self.core, rows].astype(F32)
                for k in range(3):
                    v = v + self.t[k, l, rows].astype(F32)
                self.p[l, self.chip, self.core, rows] = v.astype(BF16)

        total(slice(0, self.base))
        if self.base < self.rows:
            @pl.when(self.chip < self.full)
            def _():
                total(slice(self.base, self.rows))

        if self.zb is None:
            self.spread(self.p.at[:, self.chip, self.core])
            return
        self.along = [
            self.pair(self.p.at[d, self.chip, self.core], self.zb.at[self.me], self.zs.at[k], self.zr.at[k], {"exp": d})
            for k, d in enumerate(self.zz)
        ]
        for c in self.along:
            self.run(c, self.chip, lambda c: c.start())

    def z_finish(self):
        for c in self.along:
            self.run(c, self.chip, lambda c: c.wait())
        v = self.p[self.me, self.chip, self.core]
        if self.add:
            v = v.astype(F32)
            for d in self.zz:
                v = v + self.zb[d].astype(F32)
            self.zb[self.me] = v.astype(BF16)
            self.spread(self.zb.at[self.me])
        else:
            self.zb[self.me] = v
            self.spread(self.zb)

    def spread(self, ref):
        dst = self.out.at[self.chip, self.core]
        self.sends = [self.pair(ref, dst, self.gs.at[k], self.gr.at[k], self.far[k]) for k in range(3)]
        self.sends.append(self.pair(ref, dst, self.fs.at[3], self.fr.at[3], self.sib))
        for c in self.sends:
            self.run(c, self.chip, lambda c: c.start())
        self.local = pltpu.make_async_copy(ref, dst, self.own)
        self.local.start()

    def forward(self):
        self.passed = []
        for k in range(3):
            ref = self.out.at[self.chips[k], self.core]
            self.run(self.pair(ref, ref, self.gs.at[k], self.gr.at[k], self.far[k]), self.chips[k], lambda c: c.wait_recv())
            c = self.pair(ref, ref, self.fs.at[k], self.fr.at[k], self.sib)
            self.run(c, self.chips[k], lambda c: c.start())
            self.passed.append(c)

    def finish(self):
        for c in self.sends:
            self.run(c, self.chip, lambda c: c.wait_send())
        for k in range(3):
            self.run(self.passed[k], self.chips[k], lambda c: c.wait_send())
        self.local.wait()
        for k in range(4):
            q = self.chips[k] if k < 3 else self.chip
            ref = self.out.at[q, 1 - self.core]
            self.run(self.pair(ref, ref, self.fs.at[k], self.fr.at[k], self.sib), q, lambda c: c.wait_recv())


def expand_columns(z, src, col0, dst):
    def one(j, carry):
        rows = src[pl.ds(pl.multiple_of(j * SUB, SUB), SUB), :]
        for n in range(z.N):
            at = pl.multiple_of((j * z.N + n) * SUB, SUB)
            dst[pl.ds(at, SUB), :] = jnp.broadcast_to(
                rows[:, col0 + n : col0 + n + 1], (SUB, LANES)
            )
        return carry

    lax.fori_loop(0, z.J, one, 0)


def expand_closed(z, masks, dst):
    dst[...] = jnp.broadcast_to((1.0 - masks[:, 2:3]) * CLOSED, (z.T, LANES))


def tile_groups(cb):
    return 2 if cb % (2 * LANES) == 0 else 1


def lane_at(p, tg, k):
    return pl.ds(pl.multiple_of(p * tg * LANES, LANES) + k * LANES, LANES)


def row8(j):
    return pl.ds(pl.multiple_of(j * SUB, SUB), SUB)


def shift_down(v, d):
    rows = lax.broadcasted_iota(jnp.int32, v.shape, 0)
    return jnp.where(rows >= d, pltpu.roll(v, d, 0), 0.0)


def shift_up(v, d):
    rows = lax.broadcasted_iota(jnp.int32, v.shape, 0)
    return jnp.where(rows < SUB - d, pltpu.roll(v, SUB - d, 0), 0.0)


def chain_states(count, mine, order, sums, heads, rates2):
    state = jnp.zeros_like(rates2)
    for k in range(count):
        at = order(k)
        new = jnp.exp2(rates2 * sums(at)) * state + heads(at).astype(F32)
        state = jnp.where(mine(at), new, state)
    return state


def router_softmax(logits, experts):
    lane = lax.broadcasted_iota(jnp.int32, logits.shape, 1)
    logits = jnp.where(lane < experts, logits, -1e30)
    top = jnp.max(logits, axis=-1, keepdims=True)
    e = jnp.where(lane < experts, jnp.exp(logits - top), 0.0)
    return e / jnp.sum(e, axis=-1, keepdims=True)


def expert(z, x, cot, router, normed, up, down, cid):
    T, D, FF, E = z.T, z.D, z.FF, z.E
    M = x.shape[0] // 2
    CAP = z.CAP
    fb = FF // 8
    wb = 2 * fb

    def body(
        x_r, c_r, rt, nrm, up_r, dn_r, dxz, back_o, dwu_o, dwd_o, nz_o,
        up_v, dn_v, hid, pg_s, g_s, out_s, dx_s, dxb, outb, dx_r, out_r, dwu_v, dwd_v,
        ld, c_s, c_q, sw_s, sw_r, dz_s, dz_r,
    ):
        s, me = lax.axis_index("seq"), lax.axis_index("exp")
        core = lax.rem(s, 2)
        other = 1 - core
        sib = {"seq": s + 1 - 2 * core}
        zs = [lax.rem(me + k, E) for k in range(1, E)]
        loads = []
        for i in range(4):
            at = pl.multiple_of((2 * i + core) * fb, LANES)
            t, off = i // 2, i % 2 * fb
            loads.append(
                [
                    pltpu.make_async_copy(up_r.at[:, pl.ds(at, fb)], up_v.at[t, :, off : off + fb], ld.at[i]),
                    pltpu.make_async_copy(dn_r.at[pl.ds(at, fb)], dn_v.at[t, off : off + fb], ld.at[4 + i]),
                ]
            )
        for pair in loads:
            for c in pair:
                c.start()
        greet([sib] + [{"exp": p} for p in zs])

        def remote(src, dst, send, recv, to):
            return pltpu.make_async_remote_copy(src, dst, send, recv, device_id=to, device_id_type=MESH)

        chain = Chain(E, nrm, nz_o, c_s, c_q, ld.at[8])
        chain.start()
        ch = router_softmax(mm_nt(x_r[...], rt[...]), E)
        lane = lax.broadcasted_iota(jnp.int32, ch.shape, 1)
        gating = jnp.sum(jnp.where(lane == me, ch, 0.0), axis=-1, keepdims=True)
        g_s[...] = (gating * c_r[...].astype(F32)).astype(BF16)
        for t in range(2):
            W = slice(t * wb, (t + 1) * wb)
            for pair in loads[2 * t : 2 * t + 2]:
                for c in pair:
                    c.wait()
            pre = mm(x_r[...], up_v[t])
            cdf = 0.5 * (1.0 + lax.erf(pre * (2.0 ** -0.5)))
            hid[:, W] = (pre * cdf).astype(BF16)
            slope = cdf + pre * jnp.exp(-0.5 * pre * pre) * (1.0 / math.sqrt(2.0 * math.pi))
            pg_s[:, W] = (mm_nt(g_s[...], dn_v[t]) * slope).astype(BF16)
            if t == 0:
                dx_s[...] = mm_nt(pg_s[:, W], up_v[t])
                out_s[...] = mm(hid[:, W], dn_v[t])
                chain.hop(1)
            else:
                dxb[:, 0:D] = (dx_s[...] + mm_nt(pg_s[:, W], up_v[t])).astype(BF16)
                out = out_s[...] + mm(hid[:, W], dn_v[t])
                outb[...] = out.astype(BF16)
                gg = jnp.sum(out * c_r[...].astype(F32), axis=-1, keepdims=True)
                hi, lo = split_hi_lo(gg)
                lane = lax.broadcasted_iota(jnp.int32, (2 * M, LANES), 1)
                both = jnp.where(lane == 0, hi.astype(F32), jnp.where(lane == 1, lo.astype(F32), 0.0))
                dxb[:, D : D + LANES] = both.astype(BF16)
        half = lambda c: pl.ds(pl.multiple_of(c * M, 16), M)
        swaps = [
            remote(dxb.at[half(other)], dx_r, sw_s.at[0], sw_r.at[0], sib),
            remote(outb.at[half(other)], out_r, sw_s.at[1], sw_r.at[1], sib),
        ]
        for c in swaps:
            c.start()
        if E > 2:
            chain.hop(2)

        def grads(t):
            W = slice(t * wb, (t + 1) * wb)
            dwd_v[W, :] = mm_tn(hid[:, W], g_s[...]).astype(BF16)
            dwu_v[:, W] = mm_tn(x_r[...], pg_s[:, W]).astype(BF16)
            moves = [
                pltpu.make_async_copy(dwd_v.at[W], dwd_o.at[W], ld.at[9 + t]),
                pltpu.make_async_copy(dwu_v.at[:, W], dwu_o.at[:, W], ld.at[11 + t]),
            ]
            for c in moves:
                c.start()
            return moves

        block_of = lambda ref, p: ref.at[pl.ds(pl.multiple_of(p * CAP, 16), CAP)]
        here = pl.ds(pl.multiple_of(me * CAP, 16), CAP)
        swaps[0].wait()
        dx_r[...] = (dxb[half(core), :].astype(F32) + dx_r[...].astype(F32)).astype(BF16)
        moves = [
            remote(block_of(dx_r, p), block_of(dxz, me), dz_s.at[k], dz_r.at[k], {"exp": p}) for k, p in enumerate(zs)
        ]
        for c in moves:
            c.start()
        dxz[here, :] = dx_r[here, :]
        kept = grads(0)
        swaps[1].wait()
        out_r[...] = (outb[half(core), :].astype(F32) + out_r[...].astype(F32)).astype(BF16)
        kept.append(pltpu.make_async_copy(out_r, back_o, ld.at[13]))
        kept[-1].start()
        kept += grads(1)
        for k in range(3, E):
            chain.hop(k)
        for c in moves + kept:
            c.wait()
        chain.finish()

    v = pltpu.VMEM
    sem = lambda *dims: pltpu.SemaphoreType.DMA(dims)
    vm = pl.BlockSpec(memory_space=pltpu.VMEM)
    slots = 2 * (E - 1)
    return pl.pallas_call(
        body,
        name="expert",
        in_specs=[vm] * 4 + [ANY] * 2,
        out_specs=[vm] + [ANY] * 4,
        out_shape=[
            sds((M, D + LANES), BF16), sds((M, D), BF16), sds((D, 2 * wb), BF16), sds((2 * wb, D), BF16),
            sds((E, T, D), BF16),
        ],
        scratch_shapes=[
            v((2, D, wb), BF16), v((2, wb, D), BF16), v((2 * M, 2 * wb), BF16), v((2 * M, 2 * wb), BF16),
            v((2 * M, D), BF16), v((2 * M, D), F32), v((2 * M, D), F32), v((2 * M, D + LANES), BF16),
            v((2 * M, D), BF16), v((M, D + LANES), BF16), v((M, D), BF16), v((D, 2 * wb), BF16), v((2 * wb, D), BF16),
            sem(14), sem(slots), sem(slots), sem(2), sem(2), sem(E - 1), sem(E - 1),
        ],
        compiler_params=pltpu.CompilerParams(
            collective_id=cid, has_side_effects=True, vmem_limit_bytes=VMEM_LIMIT
        ),
    )(x, cot, router, normed, up, down)


def padded_rows(main, edge, J, cb):
    H = edge.shape[0]
    m3 = main.reshape(J, SUB, cb)
    first = lax.broadcasted_iota(jnp.int32, (SUB, cb), 0) == 0
    tail = jnp.stack(
        [
            jnp.where(
                first,
                jnp.broadcast_to(edge[H - 3 + k : H - 2 + k, :], (SUB, cb)),
                pltpu.roll(m3[J - 3 + k], 1, 0),
            )
            for k in range(3)
        ]
    )
    return jnp.concatenate([tail, m3], axis=0)


def at_cols(i, cb):
    return pl.ds(pl.multiple_of(i * cb, LANES), cb)


def lanes_of(i, cb, p, tg, k):
    return pl.ds(pl.multiple_of(i * cb + p * tg * LANES, LANES) + k * LANES, LANES)


class Chain:
    def __init__(self, E, src, dst, send, recv, own):
        self.E, self.src, self.dst, self.send, self.recv, self.own = E, src, dst, send, recv, own
        self.me = lax.axis_index("exp")
        self.right, self.left = lax.rem(self.me + 1, E), lax.rem(self.me + E - 1, E)

    def slot(self, d):
        return 2 * (abs(d) - 1) + (1 if d > 0 else 0)

    def exists(self, d):
        return (self.me + d >= 0) & (self.me + d < self.E)

    def each(self, d, act):
        for to_right in (True, False):
            if (d <= 0) if to_right else (d >= 0):
                edge = self.me < self.E - 1 if to_right else self.me > 0
                there = self.slot(d - 1 if to_right else d + 1)

                @pl.when(self.exists(d) & edge)
                def _():
                    act(
                        pltpu.make_async_remote_copy(
                            self.src if d == 0 else self.dst.at[self.me + d],
                            self.dst.at[self.me + d],
                            self.send.at[there],
                            self.recv.at[there],
                            device_id={"exp": self.right if to_right else self.left},
                            device_id_type=MESH,
                        )
                    )

    def local(self):
        return pltpu.make_async_copy(self.src, self.dst.at[self.me], self.own)

    def start(self):
        self.each(0, lambda c: c.start())
        self.local().start()

    def hop(self, k):
        for d in (-k, k):
            ref = self.dst.at[self.me + d]

            @pl.when(self.exists(d))
            def _():
                pltpu.make_async_remote_copy(
                    ref, ref, self.send.at[self.slot(d)], self.recv.at[self.slot(d)],
                    device_id={"exp": self.right}, device_id_type=MESH,
                ).wait_recv()

            if k < self.E - 1:
                self.each(d, lambda c: c.start())

    def finish(self):
        for k in range(self.E - 1):
            for d in (-k, k) if k else (0,):
                self.each(d, lambda c: c.wait_send())
        self.local().wait()


class Spread:
    def __init__(self, E, src, col0, dst, cols, each, by_rows, sems):
        self.E, self.src, self.col0, self.dst, self.cols, self.each_cols = E, src, col0, dst, cols, each
        self.by_rows = by_rows
        self.zs, self.zr, self.ps, self.pr, self.cs, self.cr = sems
        self.rows = src.shape[0]
        s, self.me = lax.axis_index("seq"), lax.axis_index("exp")
        self.chip, self.core = s // 2, lax.rem(s, 2)
        self.sib = {"seq": s + 1 - 2 * self.core}
        self.chips = [self.chip + 1 - 2 * lax.rem(self.chip, 2), self.chip + 2 - 4 * (self.chip // 2), 3 - self.chip]
        self.far = [{"seq": q * 2 + self.core} for q in self.chips]
        self.right, self.left = lax.rem(self.me + 1, E), lax.rem(self.me + E - 1, E)
        self.split = by_rows or each > 0
        self.rest = 0 if by_rows else cols - 4 * each
        self.regions = ([1] if self.split else []) + ([0] if self.rest else [])
        self.pieces = ([0] if self.rest else []) + ([1, 2, 3, 4] if self.split else [])
        self.offsets = [d for k in range(1, E) for d in (-k, k)]

    def slot(self, d):
        return 2 * (abs(d) - 1) + (1 if d > 0 else 0)

    def exists(self, d):
        return (self.me + d >= 0) & (self.me + d < self.E)

    def view(self, ref, row0, col0, region, q, core, half):
        rows = self.rows // 2
        row = row0 + core * rows
        if self.by_rows:
            rows = rows // 4
            row = row + q * rows
            if half is not None:
                rows = rows // 2
                row = row + half * rows
            return ref.at[pl.ds(pl.multiple_of(row, 16), rows)]
        at = pl.ds(pl.multiple_of(row, 16), rows)
        if region == 0:
            start, width = col0, self.rest
        else:
            start, width = col0 + self.rest + q * self.each_cols, self.each_cols
            if half is not None:
                width = width // 2
                start = start + half * width
        if width == ref.shape[1]:
            return ref.at[at]
        return ref.at[at, pl.ds(pl.multiple_of(start, LANES), width)]

    def there(self, d, region, q, core, half=None):
        return self.view(self.dst, (self.me + d) * self.rows, 0, region, q, core, half)

    def own(self, region):
        return self.view(self.src, 0, self.col0, region, self.chip, self.core, None)

    def local(self, sem):
        at = pl.ds(pl.multiple_of(self.me * self.rows, 16), self.rows)
        src = self.src if self.cols == self.src.shape[1] else self.src.at[:, self.col0 : self.col0 + self.cols]
        return pltpu.make_async_copy(src, self.dst.at[at], sem)

    def remote(self, src, dst, send, recv, to):
        return pltpu.make_async_remote_copy(src, dst, send, recv, device_id=to, device_id_type=MESH)

    def z_each(self, region, d, act):
        for to_right in (True, False):
            if (d <= 0) if to_right else (d >= 0):
                edge = self.me < self.E - 1 if to_right else self.me > 0
                slot = self.slot(d - 1 if to_right else d + 1)

                @pl.when(self.exists(d) & edge)
                def _():
                    act(
                        self.remote(
                            self.own(region) if d == 0 else self.there(d, region, self.chip, self.core),
                            self.there(d, region, self.chip, self.core),
                            self.zs.at[region, slot],
                            self.zr.at[region, slot],
                            {"exp": self.right if to_right else self.left},
                        )
                    )

    def start(self):
        for r in self.regions:
            self.z_each(r, 0, lambda c: c.start())

    def cross(self, j, d):
        if j < 2:
            ref = self.there(d, 1, self.chip, self.core)
        else:
            ref = self.there(d, 1, self.chips[j - 2], self.core, j - 2)
        to = self.far[(0, 1, 1, 0)[j]]
        return self.remote(ref, ref, self.ps.at[j, self.slot(d)], self.pr.at[j, self.slot(d)], to)

    def crossed(self, j, d):
        ref = self.there(d, 1, self.chips[j], self.core) if j < 2 else self.there(d, 1, self.chips[2], self.core, j - 2)
        self.remote(ref, ref, self.ps.at[j, self.slot(d)], self.pr.at[j, self.slot(d)], self.sib).wait_recv()

    def sib_copy(self, which, d, core):
        if which == 0:
            ref = self.there(d, 0, self.chip, core)
        else:
            ref = self.there(d, 1, self.chip if which == 1 else self.chips[which - 2], core)
        return self.remote(ref, ref, self.cs.at[which, self.slot(d)], self.cr.at[which, self.slot(d)], self.sib)

    def hop(self, k):
        for r in self.regions:
            for d in (-k, k):
                @pl.when(self.exists(d))
                def _():
                    ref = self.there(d, r, self.chip, self.core)
                    self.remote(
                        ref, ref, self.zs.at[r, self.slot(d)], self.zr.at[r, self.slot(d)], self.sib
                    ).wait_recv()

                if k < self.E - 1:
                    self.z_each(r, d, lambda c: c.start())

                @pl.when(self.exists(d))
                def _():
                    if r == 1:
                        for j in range(2):
                            self.cross(j, d).start()
                    self.sib_copy(r, d, self.core).start()

    def plane(self, k):
        for d in (-k, k) if self.split else ():
            @pl.when(self.exists(d))
            def _():
                for j in range(2):
                    self.crossed(j, d)
                    self.cross(2 + j, d).start()
                    self.sib_copy(2 + j, d, self.core).start()

    def fourth(self, k):
        for d in (-k, k) if self.split else ():
            @pl.when(self.exists(d))
            def _():
                self.crossed(2, d)
                self.crossed(3, d)
                self.sib_copy(4, d, self.core).start()

    def landed(self):
        for d in self.offsets:
            @pl.when(self.exists(d))
            def _():
                for w in self.pieces:
                    self.sib_copy(w, d, 1 - self.core).wait_recv()

    def finish(self):
        for d in self.offsets:
            @pl.when(self.exists(d))
            def _():
                for w in self.pieces:
                    self.sib_copy(w, d, self.core).wait_send()
                if self.split:
                    for j in range(4):
                        self.cross(j, d).wait_send()
        for r in self.regions:
            for k in range(self.E - 1):
                for d in (-k, k) if k else (0,):
                    self.z_each(r, d, lambda c: c.wait_send())


def small_rows(z):
    return 128 * -(-z.SMALL // 128)


def pack_small(z, par, own_sm, own_g):
    conv_w, conv_b, dt_b, skip, a_log, dt_w, x_w, gain_a, gain_b, router = par
    (rs, cw), (rg, dw) = own_sm.shape, own_g.shape
    wide = lambda ref: ref[...].astype(F32)
    line = lambda ref: ref[...].astype(F32).reshape(1, ref.shape[0])
    rows = [wide(conv_w), line(conv_b), line(dt_b), line(skip), jnp.zeros((1, cw), F32), wide(a_log), wide(dt_w)]
    rows += [wide(x_w), jnp.zeros((rs - z.SMALL, cw), F32)]
    own_sm[...] = jnp.concatenate(rows, axis=0).astype(BF16)
    rows = [line(gain_a), line(gain_b), wide(router), jnp.zeros((rg - 2 - z.E, dw), F32)]
    own_g[...] = jnp.concatenate(rows, axis=0).astype(BF16)


def forward(z, S, plane, tokens, cotangent, seg, route, params, in_proj, out_proj, gr, cid):
    T, D, DI, N, J, E, CAP = z.T, z.D, z.DI, z.N, z.J, z.E, z.CAP
    H = J
    M = E * CAP
    DZ, NZ = DI // E, D // E
    rs, rg = small_rows(z), 32
    cb = pick(DI, (384, 256, 128))
    cs = pick(DI, (768, 384, 256, 128))
    tg = tile_groups(cs)
    wide = tg * LANES
    ng = 8
    steps = DI // cs
    ST = (J + 1) * N * SUB
    tiles, tiles_o = DI // LANES, D // LANES
    split = (tiles // 4 - (0 if tiles % 4 else 1)) * LANES
    split_o = max(1, tiles_o * 2 // 9) * LANES

    def body(*refs):
        tokn, cotn, seg_r, route_r = refs[:4]
        np_ = len(params)
        par = refs[4 : 4 + np_]
        (
            in_p, out_p,
            sm, gp, rt, table, choose, masks, hconv, mixed, mid, moe, ch_o, s_all, tok, cot, normed_o,
            st_o, win_o, wout_o, arr_o, cot_o, conv_o, gate_o, sig_o, dt_o, y_o,
            conv_in, gate, sig, dt, y,
            wc, wg, wo, smb, gb, nrm, halo, seg_in, bx, cx, cl, u_s, rates_s, hd, hdev, stot, h_all, pre_s, dwin, hin,
            st_v, acc, outb, cotb, own_sm, own_g, own_seg,
            ld, zs, zr, ps, pr, c_s, c_r, t_s, t_r, h_s, h_r, d_s, d_r, q_s, q_r, k_s, k_r, x_s, x_r,
        ) = refs[4 + np_ :]
        s, me = lax.axis_index("seq"), lax.axis_index("exp")
        core = lax.rem(s, 2)
        sib = {"seq": s + 1 - 2 * core}
        seqs = [lax.rem(s + k, S) for k in range(1, S)]
        zz = [lax.rem(me + k, E) for k in range(1, E)]
        barrier = pltpu.get_barrier_semaphore()
        peers = [{"seq": p} for p in seqs] + [{"exp": p} for p in zz]
        for peer in peers:
            pl.semaphore_signal(barrier, inc=1, device_id=peer, device_id_type=MESH)

        def remote(src, dst, send, recv, to):
            return pltpu.make_async_remote_copy(src, dst, send, recv, device_id=to, device_id_type=MESH)

        if plane:
            pack_small(z, par, own_sm, own_g)
        segrow = seg_r[...].astype(F32)
        own_seg[...] = jnp.broadcast_to(segrow, (SUB, T))
        pl.semaphore_wait(barrier, len(peers))
        sems = lambda a: (zs.at[a], zr.at[a], ps.at[a], pr.at[a], c_s.at[a], c_r.at[a])
        if plane:
            parts = [
                Spread(E, own_sm, 0, smb, DZ, 0, True, sems(0)),
                Spread(E, own_g, 0, gb, NZ, 0, False, sems(1)),
                Spread(E, in_p, 0, wc, DI, split, False, sems(2)),
                Spread(E, in_p, DI, wg, DI, split, False, sems(3)),
                Spread(E, out_p, 0, wo, D, split_o, False, sems(4)),
            ]
            for p in parts[:3]:
                p.start()
            loads = [p.local(ld.at[a]) for a, p in enumerate(parts)]
        else:
            loads = [
                pltpu.make_async_copy(par[0], smb, ld.at[0]),
                pltpu.make_async_copy(par[1], gb, ld.at[1]),
                pltpu.make_async_copy(in_p.at[:, 0:DI], wc, ld.at[2]),
                pltpu.make_async_copy(in_p.at[:, DI : 2 * DI], wg, ld.at[3]),
                pltpu.make_async_copy(out_p, wo, ld.at[4]),
            ]
        ahead = {"seq": lax.rem(s + 1, S)}
        edges = [
            remote(tokn.at[pl.ds(T - H, H)], halo, t_s.at[0], t_r.at[0], ahead),
            remote(own_seg, seg_in, t_s.at[1], t_r.at[1], ahead),
        ]
        for c in edges:
            c.start()
        for c in loads:
            c.start()
        queue = []
        if plane:
            wg_p, wo_p = parts[3], parts[4]
            queue = [wg_p.start] + [functools.partial(wg_p.hop, k) for k in range(1, E - 1)]
            queue += [wo_p.start, functools.partial(wg_p.hop, E - 1)]
            for k in range(1, E):
                queue += [functools.partial(wg_p.plane, k), functools.partial(wo_p.hop, k)]
                queue += [functools.partial(wg_p.fourth, k)]
            for k in range(1, E):
                queue += [functools.partial(wo_p.plane, k)]
            for k in range(1, E):
                queue += [functools.partial(wo_p.fourth, k)]

        def progress(count):
            for _ in range(count):
                if queue:
                    queue.pop(0)()

        lane = lax.broadcasted_iota(jnp.int32, (T, T), 1)
        prow = lax.broadcasted_iota(jnp.int32, (T, T), 0)
        place = (prow % SUB) * J + prow // SUB
        order = (lane == place).astype(F32).astype(BF16)
        tok[...] = mm(order, tokn[...]).astype(BF16)
        cot[...] = mm(order, cotn[...]).astype(BF16)
        my_route = jnp.sum(
            jnp.where(lane == place, route_r[...].astype(F32), 0.0), axis=1, keepdims=True
        ).astype(jnp.int32)
        chosen = (lane == my_route).astype(F32)
        choose[...] = chosen
        counts = mm((lane <= prow).astype(F32).astype(BF16), chosen.astype(BF16))
        rank = jnp.sum(counts * chosen, axis=-1, keepdims=True).astype(jnp.int32) - 1
        slots = lax.broadcasted_iota(jnp.int32, (T, M), 1)
        table[...] = (slots == my_route * CAP + rank).astype(F32).astype(BF16)
        cotb[...] = mm_tn(table[...], cot[...]).astype(BF16)
        t32 = tok[...].astype(F32)
        scaled = t32 * rms_scale(t32)

        if plane:
            for k in range(1, E + 2):
                if k < E:
                    for p in parts[:3]:
                        p.hop(k)
                    progress(1)
                if 1 <= k - 1 < E:
                    parts[0].plane(k - 1)
                    parts[2].plane(k - 1)
                    progress(1)
                if 1 <= k - 2 < E:
                    parts[0].fourth(k - 2)
                    parts[2].fourth(k - 2)
        block_of = lambda ref, p: ref.at[pl.ds(pl.multiple_of(p * CAP, 16), CAP)]
        cot_moves = [remote(block_of(cotb, p), cot_o.at[core, me], k_s.at[k], k_r.at[k], {"exp": p}) for k, p in enumerate(zz)]
        if plane:
            for p in parts[:3]:
                p.landed()
        for c in loads:
            c.wait()
        for e in range(E):
            sm[:, e * DZ : (e + 1) * DZ] = smb[e * rs : (e + 1) * rs, :].astype(F32)[0 : z.SMALL]
        gp[...] = jnp.zeros_like(gp)
        rt[...] = jnp.zeros_like(rt)
        for e in range(E):
            cols = slice(e * NZ, (e + 1) * NZ)
            gp[:, cols] = gb[e * rg : e * rg + 16, :].astype(F32)[0:gr]
        rt[0:16, :] = jnp.concatenate([gp[2 : 2 + E, :], jnp.zeros((16 - E, D), F32)], axis=0).astype(BF16)

        for c in edges:
            c.wait()
        live = jnp.where(s > 0, 1.0, 0.0)
        col8 = lax.broadcasted_iota(jnp.int32, (T, SUB), 1)
        prev = seg_in[0:1, :] * live

        def seg_at(k):
            own = jnp.where(lane == place - k, segrow, 0.0)
            return jnp.sum(own + jnp.where(lane == place - k + T, prev, 0.0), axis=1, keepdims=True)

        now = seg_at(0)
        same = jnp.zeros((T, SUB), F32)
        for o in range(4):
            same = jnp.where(col8 == o, (seg_at(3 - o) == now).astype(F32), same)
        masks[...] = same
        nrm[0:T, :] = (scaled * gp[0:1, :]).astype(BF16)
        h32 = halo[...].astype(F32) * live
        nrm[T : T + H, :] = (h32 * rms_scale(h32) * gp[0:1, :]).astype(BF16)
        mixed[...] = jnp.zeros_like(mixed)

        def conv_block(i, carry):
            C = at_cols(i, cb)
            both = mm(nrm[...], wc[:, C])
            main, edge = both[:T], both[T:]
            conv_in[:, C] = main
            hconv[:, C] = edge
            xpad = padded_rows(main, edge, J, cb)
            out = jnp.broadcast_to(sm[CONV_B : CONV_B + 1, C], (T, cb))
            for o in range(4):
                m = jnp.broadcast_to(masks[:, o : o + 1], (T, cb))
                out = out + sm[CONV_W + o : CONV_W + o + 1, C] * xpad[o : o + J].reshape(T, cb) * m
            sv = (out * sigmoid(out)).astype(BF16)
            sig[:, C] = sv
            mixed[...] += mm_nt(sv, sm[z.X0 : z.X0 + z.XW, C].astype(BF16))
            return carry

        lax.fori_loop(0, DI // cb, conv_block, 0)
        normed_o[...] = nrm[0:T, :]
        keeps = [
            pltpu.make_async_copy(a, b, ld.at[13 + n])
            for n, (a, b) in enumerate(((conv_in, conv_o), (sig, sig_o), (dt, dt_o), (gate, gate_o), (y, y_o)))
        ]
        keeps[0].start()
        keeps[1].start()
        progress(3)
        cot_own = pltpu.make_async_copy(block_of(cotb, me), cot_o.at[core, me], ld.at[6])
        cot_own.start()

        expand_columns(z, mixed, z.R, bx)
        expand_columns(z, mixed, z.R + N, cx)
        expand_closed(z, masks, cl)
        low = mixed[:, 0 : z.R].astype(BF16)

        def step_block(i, carry):
            C = at_cols(i, cs)
            pre = mm(low, sm[z.DT0 : z.DT0 + z.R, C].astype(BF16)) + sm[DT_B : DT_B + 1, C]
            step = softplus(pre)
            dt[:, C] = step
            u_s[:, C] = step * sig[:, C].astype(F32)
            rates_s[:, C] = -jnp.exp(sm[A_LOG : A_LOG + N, C]) * LOG2E
            return carry

        lax.fori_loop(0, DI // cs, step_block, 0)
        progress(3)

        def chunk_block(p, carry):
            lanes = [lane_at(p, tg, k) for k in range(tg)]
            wins = []
            for k in range(tg):
                w1 = jnp.zeros((SUB, LANES), F32)
                for j in range(J):
                    w1 = w1 + (dt[j * SUB : j * SUB + SUB, lanes[k]] + cl[j * SUB : j * SUB + SUB, :])
                w2 = w1 + shift_down(w1, 1)
                w4 = w2 + shift_down(w2, 2)
                w8 = w4 + shift_down(w4, 4)
                wins.append((w1, w2, w4))
                dwin[:, lanes[k]] = shift_down(w8, 1)
                stot[:, lanes[k]] = w8[SUB - 1 : SUB, :]
            for g in range(0, N, ng):
                rr = [
                    [jnp.broadcast_to(rates_s[g + n : g + n + 1, lanes[k]], (SUB, LANES)) for k in range(tg)]
                    for n in range(ng)
                ]

                def step_j(j, hs):
                    dts = [dt[row8(j), lanes[k]] + cl[row8(j), :] for k in range(tg)]
                    us = [u_s[row8(j), lanes[k]] for k in range(tg)]
                    new = []
                    for n in range(ng):
                        b = bx[row8(j * N + g + n), :]
                        for k in range(tg):
                            new.append(jnp.exp2(dts[k] * rr[n][k]) * hs[n * tg + k] + us[k] * b)
                    return tuple(new)

                hs = lax.fori_loop(
                    0, J, step_j, tuple(jnp.zeros((SUB, LANES), F32) for _ in range(ng * tg)), unroll=2
                )
                for n in range(ng):
                    for k in range(tg):
                        h = hs[n * tg + k]
                        w1, w2, w4 = wins[k]
                        r = rr[n][k]
                        h = h + jnp.exp2(r * w1) * shift_down(h, 1)
                        h = h + jnp.exp2(r * w2) * shift_down(h, 2)
                        h = h + jnp.exp2(r * w4) * shift_down(h, 4)
                        pre_s[(g + n) * SUB : (g + n + 1) * SUB, lanes[k]] = shift_down(h, 1)
                        hd[g + n : g + n + 1, lanes[k]] = h[SUB - 1 : SUB, :]
            return carry

        keeps[2].start()
        third = DI // wide // 3
        lax.fori_loop(0, third, chunk_block, 0)
        progress(3)
        lax.fori_loop(third, 2 * third, chunk_block, 0)
        progress(3)
        lax.fori_loop(2 * third, DI // wide, chunk_block, 0)
        hdev[...] = hd[...].astype(BF16)
        h_moves = [remote(hdev, h_all.at[s], h_s.at[0, k], h_r.at[0, k], {"seq": p}) for k, p in enumerate(seqs)]
        h_moves += [remote(stot, s_all.at[s], h_s.at[1, k], h_r.at[1, k], {"seq": p}) for k, p in enumerate(seqs)]
        for c in h_moves:
            c.start()
        h_all[s] = hdev[...]
        s_all[s] = stot[...]
        for c in cot_moves:
            c.start()
        progress(len(queue))
        if plane:
            parts[3].landed()

        def gate_block(i, carry):
            C = at_cols(i, cb)
            gate[:, C] = mm(nrm[0:T, :], wg[:, C])
            return carry

        lax.fori_loop(0, DI // cb, gate_block, 0)
        keeps[3].start()
        if plane:
            parts[4].landed()
        outs = [
            pltpu.make_async_copy(wc, win_o.at[:, 0:DI], ld.at[7]),
            pltpu.make_async_copy(wg, win_o.at[:, DI : 2 * DI], ld.at[8]),
            pltpu.make_async_copy(wo, wout_o, ld.at[9]),
        ]
        for c in outs:
            c.start()
        for c in h_moves:
            c.wait()
        acc[...] = jnp.zeros_like(acc)

        def save(i):
            return pltpu.make_async_copy(
                st_v.at[i % 2], st_o.at[:, i * cs : (i + 1) * cs], ld.at[10 + i % 2]
            )

        for i in range(steps):
            if i >= 2:
                save(i - 2).wait()
            C = slice(i * cs, (i + 1) * cs)
            hin[...] = chain_states(
                S - 1, lambda k: k < s, lambda k: k, lambda k: s_all[k, :, C], lambda k: h_all[k, :, C],
                rates_s[:, C],
            )

            def pair(p, carry):
                lanes = [lanes_of(i, cs, p, tg, k) for k in range(tg)]
                near = [lane_at(p, tg, k) for k in range(tg)]
                for g in range(0, N, ng):
                    rr = [
                        [jnp.broadcast_to(rates_s[g + n : g + n + 1, lanes[k]], (SUB, LANES)) for k in range(tg)]
                        for n in range(ng)
                    ]
                    init = []
                    for n in range(ng):
                        for k in range(tg):
                            at = (g + n) * SUB
                            init.append(
                                pre_s[at : at + SUB, lanes[k]]
                                + jnp.exp2(rr[n][k] * dwin[:, lanes[k]])
                                * jnp.broadcast_to(hin[g + n : g + n + 1, near[k]], (SUB, LANES))
                            )

                    def keep(j, hs):
                        for n in range(0, ng, 2):
                            for k in range(tg):
                                two = jnp.concatenate([hs[n * tg + k], hs[(n + 1) * tg + k]], axis=0)
                                at = pl.multiple_of(j * N * SUB + (g + n) * SUB, 2 * SUB)
                                st_v[i % 2, pl.ds(at, 2 * SUB), near[k]] = two.astype(BF16)

                    keep(0, init)

                    def step_j(j, hs):
                        dts = [dt[row8(j), lanes[k]] + cl[row8(j), :] for k in range(tg)]
                        us = [u_s[row8(j), lanes[k]] for k in range(tg)]
                        if g == 0:
                            ys = [jnp.zeros((SUB, LANES), F32) for k in range(tg)]
                        else:
                            ys = [y[row8(j), lanes[k]] for k in range(tg)]
                        new = []
                        for n in range(ng):
                            b = bx[row8(j * N + g + n), :]
                            c = cx[row8(j * N + g + n), :]
                            for k in range(tg):
                                h = jnp.exp2(dts[k] * rr[n][k]) * hs[n * tg + k] + us[k] * b
                                ys[k] = ys[k] + h * c
                                new.append(h)
                        for k in range(tg):
                            y[row8(j), lanes[k]] = ys[k]
                        keep(j + 1, new)
                        return tuple(new)

                    lax.fori_loop(0, J, step_j, tuple(init), unroll=2)
                return carry

            lax.fori_loop(0, cs // wide, pair, 0)
            save(i).start()
            yv = y[:, C] + sm[SKIP : SKIP + 1, C] * sig[:, C].astype(F32)
            y[:, C] = yv
            g_in = gate[:, C]
            gated = (yv * (g_in * sigmoid(g_in))).astype(BF16)
            acc[...] += mm(gated, wo[C, :])

        keeps[4].start()
        m32 = tok[...].astype(F32) + acc[...]
        mid[...] = m32
        moe[...] = (m32 * rms_scale(m32) * gp[1:2, :]).astype(BF16)
        ch_o[...] = router_softmax(mm_nt(moe[...], rt[...]), E)
        outb[...] = mm_tn(table[...], moe[...]).astype(BF16)
        out_moves = [remote(block_of(outb, p), arr_o.at[core, me], d_s.at[k], d_r.at[k], {"exp": p}) for k, p in enumerate(zz)]
        for c in out_moves:
            c.start()
        arr_own = pltpu.make_async_copy(block_of(outb, me), arr_o.at[core, me], ld.at[12])
        arr_own.start()
        passes = [
            remote(block_of(cotb, me), cot_o.at[core, me], x_s.at[0, 0], x_r.at[0, 0], sib),
            remote(block_of(outb, me), arr_o.at[core, me], x_s.at[1, 0], x_r.at[1, 0], sib),
        ]
        for c in passes:
            c.start()
        for w, ref, send, recv in ((0, cot_o, k_s, k_r), (1, arr_o, d_s, d_r)):
            for k in range(1, E):
                frm = lax.rem(me + E - k, E)
                at = ref.at[core, frm]
                remote(at, at, send.at[k - 1], recv.at[k - 1], {"exp": frm}).wait_recv()
                c = remote(at, at, x_s.at[w, k], x_r.at[w, k], sib)
                c.start()
                passes.append(c)
        if plane:
            for p in parts:
                p.finish()
        for c in outs + keeps + [cot_own, arr_own]:
            c.wait()
        for i in range(max(0, steps - 2), steps):
            save(i).wait()
        for c in cot_moves + out_moves + passes:
            c.wait_send()
        for w, ref in ((0, cot_o), (1, arr_o)):
            for k in range(E):
                at = ref.at[1 - core, lax.rem(me + E - k, E)]
                remote(at, at, x_s.at[w, k], x_r.at[w, k], sib).wait_recv()

    v = pltpu.VMEM
    sem = lambda *dims: pltpu.SemaphoreType.DMA(dims)
    vm = pl.BlockSpec(memory_space=pltpu.VMEM)
    zslots = 2 * (E - 1)
    ins = (tokens, cotangent, seg, route) + tuple(params) + (in_proj, out_proj)
    vm_outs = [
        sds((z.SMALL, DI), F32), sds((gr, D), F32), sds((LANES, D), BF16), sds((T, M), BF16), sds((T, LANES), F32),
        sds((T, SUB), F32), sds((H, DI), F32), sds((T, z.XW), F32), sds((T, D), F32), sds((T, D), BF16),
        sds((T, LANES), F32), sds((S, 1, DI), F32), sds((T, D), BF16), sds((T, D), BF16), sds((T, D), BF16),
    ]
    any_outs = [
        sds((ST, DI), BF16), sds((D, 2 * DI), BF16), sds((DI, D), BF16), sds((2, E, CAP, D), BF16),
        sds((2, E, CAP, D), BF16), sds((T, DI), F32), sds((T, DI), F32), sds((T, DI), BF16), sds((T, DI), F32),
        sds((T, DI), F32),
    ]
    return pl.pallas_call(
        body,
        name="forward",
        in_specs=[vm] * 4 + [vm if plane else ANY] * len(params) + [ANY] * 2,
        out_specs=[vm] * len(vm_outs) + [ANY] * len(any_outs),
        out_shape=vm_outs + any_outs,
        scratch_shapes=[
            v((T, DI), F32), v((T, DI), F32), v((T, DI), BF16), v((T, DI), F32), v((T, DI), F32),
            v((D, DI), BF16), v((D, DI), BF16), v((DI, D), BF16), v((E * rs, DZ), BF16), v((E * rg, NZ), BF16),
            v((T + H, D), BF16), v((H, D), BF16), v((SUB, LANES), F32),
            v((J * N * SUB, LANES), F32), v((J * N * SUB, LANES), F32), v((T, LANES), F32), v((T, DI), F32),
            v((N, DI), F32), v((N, DI), F32), v((N, DI), BF16), v((1, DI), F32), v((S, N, DI), BF16),
            v((N * SUB, DI), F32), v((SUB, DI), F32), v((N, cs), F32),
            v((2, ST, cs), BF16), v((T, D), F32), v((M, D), BF16), v((M, D), BF16),
            v((rs, DZ), BF16), v((rg, NZ), BF16), v((SUB, T), F32),
            sem(18), sem(5, 2, zslots), sem(5, 2, zslots), sem(5, 4, zslots), sem(5, 4, zslots),
            sem(5, 5, zslots), sem(5, 5, zslots), sem(2), sem(2), sem(2, S - 1), sem(2, S - 1),
            sem(E - 1), sem(E - 1), sem(1), sem(1), sem(E - 1), sem(E - 1),
            sem(2, E), sem(2, E),
        ],
        compiler_params=pltpu.CompilerParams(
            collective_id=cid, has_side_effects=True, vmem_limit_bytes=60 * 1024 * 1024
        ),
    )(*ins)


def backward(z, S, plane, expert_out, dx_z, dwu, dwd, states, w_out, w_in, table, choose, chances, mid, moe, cot, gpack,
             router, gate, y, sig, small, mixed, dt, masks, conv_in, hconv, s_all, tok, normed_all, cid):
    T, D, DI, N, J, E, CAP = z.T, z.D, z.DI, z.N, z.J, z.E, z.CAP
    M = E * CAP
    G = gpack.shape[0]
    H = hconv.shape[0]
    DZ, NZ = DI // E, D // E
    cb_m = pick(DI, (384, 256, 128))
    cb_s = pick(DI, (256, 128))
    steps_s = DI // cb_s
    tg_s = tile_groups(cb_s)
    ng_s = 4
    uq, uc = dwu.shape[0] // 4, dwu.shape[1]
    dq, dc = dwd.shape[0] // 4, dwd.shape[1]
    ST = (J + 1) * N * SUB
    rows_big = max(ST, 2 * D)
    chain_slots = 2 * (E - 1)

    def body(
        eo, dwu, dwd, states, w_out, w_in, dx_z, table, choose, chances, mid, moe, cot, gp, router, gate_h, y_h, sig_h,
        small_h, mixed, dt_h, masks, conv_h, hconv, s_all, tok, nall,
        tg_o, gs_o, gg_o, back_o, pg_o, pc_o, pm_o, po_o, up_o, down_o,
        gate, y, sig, small, dt, conv_in, own_v, big, wo_v, n_v, yg, gi, gz, br, mg, fdev, f_all, suf, cg_edge,
        edge_in, pc, bx, cx, ia, oa, cl, u_s, rates_s, fin, dg_s, rs_s, rt_s, low_s, mxg, fd,
        ua, ub, ub2, da, db, db2, gi_all, pc_all, br_all, gz_all, gi_b,
        p_g, p_c, p_m, p_o, bg, bc, bm, bo, tg_, tc_, tm_, to_, zg, zc, zm,
        pcs, pcr, pqs, pqr, pzs, pzr, pgs, pgr, pfs, pfr, pown,
        ld, oz_s, oz_r, f_s, f_r, e_s, e_r, g_s, g_r, p_s, p_r, b_s, b_r, a_s, a_r, x_s, x_r,
    ):
        wide_loads = [
            pltpu.make_async_copy(a, b, ld.at[18 + n])
            for n, (a, b) in enumerate(
                ((gate_h, gate), (y_h, y), (sig_h, sig), (small_h, small), (dt_h, dt), (conv_h, conv_in))
            )
        ]
        for c in wide_loads:
            c.start()
        psems = lambda a: (
            pcs.at[a], pcr.at[a], pqs.at[a], pqr.at[a], pzs.at[a], pzr.at[a], pgs.at[a], pgr.at[a], pfs.at[a],
            pfr.at[a], pown.at[a],
        )
        extra = lambda rows: (16 * (rows // 128), -(-(rows // 16 % 8) // 2) if rows // 16 % 8 else 4)
        sum_g = PlaneSum(E, p_g, bg, tg_, zg, pg_o, False, *extra(NZ), psems(0))
        sum_c = PlaneSum(E, p_c, bc, tc_, zc, pc_o, False, *extra(NZ), psems(1))
        sum_m = PlaneSum(E, p_m, bm, tm_, zm, pm_o, True, 0, 4, psems(2))
        sum_o = PlaneSum(E, p_o, bo, to_, None, po_o, False, *extra(DZ), psems(3))
        stage = (lambda f: f()) if plane else (lambda f: None)
        s, me = lax.axis_index("seq"), lax.axis_index("exp")
        core = lax.rem(s, 2)
        other = 1 - core
        sib = {"seq": s + 1 - 2 * core}
        seqs = [lax.rem(s + k, S) for k in range(1, S)]
        zs = [lax.rem(me + k, E) for k in range(1, E)]
        greet([{"seq": p} for p in seqs] + [{"exp": p} for p in zs])

        def remote(src, dst, send, recv, to):
            return pltpu.make_async_remote_copy(src, dst, send, recv, device_id=to, device_id_type=MESH)

        def out_load(i):
            slot = lax.rem(i, 2)
            rows = pl.ds(pl.multiple_of(i * cb_m, LANES), cb_m)
            return pltpu.make_async_copy(w_out.at[rows], wo_v.at[slot], ld.at[2 + 15 * slot])

        out_load(0).start()
        normed_load = pltpu.make_async_copy(nall, n_v, ld.at[10])
        normed_load.start()

        def state_load(i):
            return pltpu.make_async_copy(
                states.at[:, at_cols(i, cb_s)], big.at[lax.rem(i, 2), 0:ST], ld.at[3 + lax.rem(i, 2)]
            )

        state_load(0).start()
        if plane:
            chip = s // 2
            xx, yy = lax.rem(chip, 2), chip // 2
            to_x = {"seq": s + 2 - 4 * xx}
            to_y = {"seq": s + 4 - 8 * yy}
            u4 = lambda ref, v, w: ref.at[pl.ds(pl.multiple_of((2 * v + w) * uq, 16), uq)]
            up1 = [
                remote(u4(dwu, v, 1 - xx), ub.at[v], a_s.at[v], a_r.at[v], to_x) for v in range(2)
            ]
            d_half = lambda v: pl.ds(pl.multiple_of(v * 2 * dq, 16), 2 * dq)
            down1 = remote(dwd.at[d_half(1 - yy)], db, a_s.at[2], a_r.at[2], to_y)
            for c in up1 + [down1]:
                c.start()
            mine = [pltpu.make_async_copy(u4(dwu, v, xx), ua.at[v], ld.at[5 + v]) for v in range(2)]
            mine.append(pltpu.make_async_copy(dwd.at[d_half(yy)], da, ld.at[7]))
            for c in mine:
                c.start()

        adds = lambda a, b: (a.astype(F32) + b.astype(F32)).astype(BF16)
        block_of = lambda ref, p: ref.at[pl.ds(pl.multiple_of(p * CAP, 16), CAP)]
        out_moves = [
            remote(block_of(eo, p), block_of(back_o, me), oz_s.at[k], oz_r.at[k], {"exp": p}) for k, p in enumerate(zs)
        ]
        back_load = pltpu.make_async_copy(block_of(eo, me), own_v, ld.at[8])
        back_own = pltpu.make_async_copy(own_v, block_of(back_o, me), ld.at[8])
        back_load.start()
        expand_columns(z, mixed, z.R, bx)
        expand_columns(z, mixed, z.R + N, cx)
        expand_closed(z, masks, cl)

        back = mm(table[...], dx_z[...])
        grad = cot[...].astype(F32)
        ch = chances[...]
        pick_e = choose[...]
        gating = jnp.sum(ch * pick_e, axis=-1, keepdims=True)
        gate_grad = back[:, D : D + 1] + back[:, D + 1 : D + 2]
        lg = ch * (gate_grad * pick_e - gate_grad * gating)
        hi, lo = split_hi_lo(lg)
        rtv = router[...]
        mig = back[:, 0:D] + mm(hi, rtv) + mm(lo, rtv)
        mev = moe[...]
        rg = mm_tn(hi, mev) + mm_tn(lo, mev)
        d, gain_g = rms_back(mid[...], gp[1:2, :], mig)
        mg[...] = grad + d
        br[...] = mg[...].astype(BF16)
        gg_o[...] = jnp.zeros_like(gg_o)
        gg_o[1:2, :] = gain_g
        gg_o[2 : 2 + E, :] = rg[0:E, :]
        chain_b = Chain(E, br, br_all, b_s, b_r, ld.at[9])
        for c in wide_loads:
            c.wait()

        def middle_block(i, carry):
            C = at_cols(i, cb_m)
            out_load(i).wait()

            @pl.when(i + 1 < DI // cb_m)
            def _():
                out_load(i + 1).start()

            gg = mm_nt(br[...], wo_v[lax.rem(i, 2)])
            g_in = gate[:, C]
            sg = sigmoid(g_in)
            act = g_in * sg
            yv = y[:, C]
            ygv = gg * act
            yg[:, C] = ygv
            gi[:, C] = (gg * yv * (sg * (1.0 + g_in * (1.0 - sg)))).astype(BF16)
            pc[:, C] = (yv * act).astype(BF16)
            gs_o[SKIP : SKIP + 1, C] = jnp.sum(ygv * sig[:, C].astype(F32), axis=0, keepdims=True)
            return carry

        lax.fori_loop(0, DI // cb_m, middle_block, 0)
        for e in range(E):
            gi_b[e] = gi[:, e * DZ : (e + 1) * DZ]

        def trade(src, dst, send, recv):
            return [remote(src.at[p], dst.at[me], send.at[k], recv.at[k], {"exp": p}) for k, p in enumerate(zs)]

        gi_moves = trade(gi_b, gi_all, g_s, g_r)
        for c in gi_moves:
            c.start()
        gi_all[me] = gi_b[me]
        chain_b.start()
        back_load.wait()
        back_own.start()

        tg, ng = 2 if DI % 256 == 0 else 1, 8
        wide = tg * LANES

        def flow_block(i, carry):
            lanes = [pl.ds(pl.multiple_of(i * wide, LANES) + k * LANES, LANES) for k in range(tg)]
            both = pl.ds(pl.multiple_of(i * wide, LANES), wide)
            rates = -jnp.exp(small[A_LOG : A_LOG + N, both]) * LOG2E
            wins = []
            for k in range(tg):
                w1 = jnp.zeros((SUB, LANES), F32)
                for j in range(J):
                    w1 = w1 + (dt[j * SUB : j * SUB + SUB, lanes[k]] + cl[j * SUB : j * SUB + SUB, :])
                w2 = w1 + shift_up(w1, 1)
                w4 = w2 + shift_up(w2, 2)
                w8 = w4 + shift_up(w4, 4)
                wins.append((w1, w2, w4))
                suf[N * SUB : (N + 1) * SUB, lanes[k]] = shift_up(w8, 1)
            for g in range(0, N, ng):
                rr = [
                    [
                        jnp.broadcast_to(rates[g + n : g + n + 1, k * LANES : (k + 1) * LANES], (SUB, LANES))
                        for k in range(tg)
                    ]
                    for n in range(ng)
                ]

                def step_j(jj, fs):
                    j = J - 1 - jj
                    dts = [dt[row8(j), lanes[k]] + cl[row8(j), :] for k in range(tg)]
                    ygs = [yg[row8(j), lanes[k]] for k in range(tg)]
                    new = []
                    for n in range(ng):
                        c = cx[row8(j * N + g + n), :]
                        for k in range(tg):
                            new.append(jnp.exp2(dts[k] * rr[n][k]) * (fs[n * tg + k] + ygs[k] * c))
                    return tuple(new)

                fs = lax.fori_loop(
                    0, J, step_j, tuple(jnp.zeros((SUB, LANES), F32) for _ in range(ng * tg)), unroll=2
                )
                for n in range(ng):
                    for k in range(tg):
                        f = fs[n * tg + k]
                        w1, w2, w4 = wins[k]
                        r = rr[n][k]
                        f = f + jnp.exp2(r * w1) * shift_up(f, 1)
                        f = f + jnp.exp2(r * w2) * shift_up(f, 2)
                        f = f + jnp.exp2(r * w4) * shift_up(f, 4)
                        suf[(g + n) * SUB : (g + n + 1) * SUB, lanes[k]] = shift_up(f, 1)
                        fd[g + n : g + n + 1, lanes[k]] = f[0:1, :]
            return carry

        lax.fori_loop(0, DI // wide, flow_block, 0)
        fdev[...] = fd[...].astype(BF16)
        f_moves = [
            remote(fdev, f_all.at[s], f_s.at[k], f_r.at[k], {"seq": p}) for k, p in enumerate(seqs)
        ]
        for c in f_moves:
            c.start()
        f_all[s] = fdev[...]
        for e in range(E):
            gz[e] = pc[:, e * DZ : (e + 1) * DZ]
        gz_moves = trade(gz, gz_all, x_s, x_r)
        for c in gz_moves:
            c.start()
        gz_all[me] = gz[me]
        p_g[...] = jnp.zeros_like(p_g)
        p_c[...] = jnp.zeros_like(p_c)
        p_o[...] = jnp.zeros_like(p_o)

        def place_in(dst, rhs):
            blk = pick(D, (384, 256, 128))
            for i in range(D // blk):
                val = mm_tn(n_v[:, i * blk : (i + 1) * blk], rhs)
                for g in range(blk // 16):
                    row = i * blk + 16 * g
                    chunk, off = group_place(D // E // 16, row % (D // E) // 16)
                    dst[row // (D // E), chunk // 2, chunk % 2, off : off + 16, :] = val[16 * g : 16 * g + 16].astype(
                        BF16
                    )

        flat = lambda ref: ref[...].reshape(E * T, ref.shape[-1])
        if plane:
            for c in mine + up1 + [down1]:
                c.wait()
            ua[...] = adds(ua[...], ub[...])
            da[...] = adds(da[...], db[...])
            up2 = remote(ua.at[1 - yy], ub2, a_s.at[3], a_r.at[3], to_y)
            down2 = remote(
                da.at[pl.ds(pl.multiple_of((1 - xx) * dq, 16), dq)], db2, a_s.at[4], a_r.at[4], to_x
            )
            up2.start()
            down2.start()
        for c in f_moves:
            c.wait()

        ia[...] = jnp.zeros_like(ia)
        oa[...] = jnp.zeros_like(oa)
        low_s[...] = jnp.zeros_like(low_s)
        low = mixed[:, 0 : z.R].astype(BF16)

        def scan_block(i, carry_):
            state_load(i).wait()

            @pl.when(i + 1 < steps_s)
            def _():
                state_load(i + 1).start()

            slot = lax.rem(i, 2)
            C = at_cols(i, cb_s)
            rates2 = -jnp.exp(small[A_LOG : A_LOG + N, C]) * LOG2E
            rates_s[...] = rates2
            fin[...] = chain_states(
                S - 1, lambda k: k > s, lambda k: S - 1 - k, lambda k: s_all[k, :, C], lambda k: f_all[k, :, C],
                rates2,
            )
            sigf = sig[:, C].astype(F32)
            u_s[...] = dt[:, C] * sigf

            def pair(p, carry):
                lanes = [lanes_of(i, cb_s, p, tg_s, k) for k in range(tg_s)]
                near = [slice(k * LANES, (k + 1) * LANES) for k in range(tg_s)]
                for g in range(0, N, ng_s):
                    rr = [
                        [
                            jnp.broadcast_to(rates_s[g + n : g + n + 1, near[k]], (SUB, LANES))
                            for k in range(tg_s)
                        ]
                        for n in range(ng_s)
                    ]
                    flow = []
                    for n in range(ng_s):
                        for k in range(tg_s):
                            at = (g + n) * SUB
                            flow.append(
                                suf[at : at + SUB, lanes[k]]
                                + jnp.exp2(rr[n][k] * suf[N * SUB : (N + 1) * SUB, lanes[k]])
                                * jnp.broadcast_to(fin[g + n : g + n + 1, near[k]], (SUB, LANES))
                            )

                    def load(j):
                        got = [[None] * tg_s for _ in range(ng_s)]
                        for n in range(0, ng_s, 2):
                            for k in range(tg_s):
                                at = pl.multiple_of(j * N * SUB + (g + n) * SUB, 2 * SUB)
                                two = big[slot, pl.ds(at, 2 * SUB), near[k]].astype(F32)
                                got[n][k] = two[0:SUB]
                                got[n + 1][k] = two[SUB : 2 * SUB]
                        return [got[n][k] for n in range(ng_s) for k in range(tg_s)]

                    def step_j(jj, carry):
                        fs, hs, rts = carry
                        j = J - 1 - jj
                        dtp = [dt[row8(j), lanes[k]] for k in range(tg_s)]
                        dts = [dtp[k] + cl[row8(j), :] for k in range(tg_s)]
                        us = [u_s[row8(j), near[k]] for k in range(tg_s)]
                        ygs = [yg[row8(j), lanes[k]] for k in range(tg_s)]
                        before = load(j)
                        if g == 0:
                            dgs = [jnp.zeros((SUB, LANES), F32) for k in range(tg_s)]
                            rss = [jnp.zeros((SUB, LANES), F32) for k in range(tg_s)]
                        else:
                            dgs = [dg_s[row8(j), near[k]] for k in range(tg_s)]
                            rss = [rs_s[row8(j), near[k]] for k in range(tg_s)]
                        nf, nr = [], []
                        for n in range(ng_s):
                            at = row8(j * N + g + n)
                            b = bx[at, :]
                            c = cx[at, :]
                            ig = jnp.zeros((SUB, LANES), F32)
                            og = jnp.zeros((SUB, LANES), F32)
                            for k in range(tg_s):
                                q = n * tg_s + k
                                gr = ygs[k] * c + fs[q]
                                f = jnp.exp2(dts[k] * rr[n][k]) * gr
                                rt = f * before[q]
                                rss[k] = rss[k] + rt * rr[n][k]
                                dgs[k] = dgs[k] + gr * b
                                nr.append(rts[q] + rt * dtp[k])
                                ig = ig + gr * us[k]
                                og = og + hs[q] * ygs[k]
                                nf.append(f)
                            ia[at, :] += ig
                            oa[at, :] += og
                        for k in range(tg_s):
                            dg_s[row8(j), near[k]] = dgs[k]
                            rs_s[row8(j), near[k]] = rss[k]
                        return tuple(nf), tuple(before), tuple(nr)

                    zero = tuple(jnp.zeros((SUB, LANES), F32) for _ in range(ng_s * tg_s))
                    _, _, rts = lax.fori_loop(
                        0, J, step_j, (tuple(flow), tuple(load(J)), zero), unroll=2
                    )
                    for n in range(ng_s):
                        for k in range(tg_s):
                            rt_s[g + n : g + n + 1, near[k]] = jnp.sum(rts[n * tg_s + k], axis=0, keepdims=True)
                return carry

            pair(0, 0)
            dg = dg_s[...]
            yg[:, C] = dg * dt[:, C] + yg[:, C] * small[SKIP : SKIP + 1, C]
            step_grad = rs_s[...] * LN2 + dg * sigf
            dtw = small[z.DT0 : z.DT0 + z.R, C].astype(BF16)
            pre = mm(low, dtw) + small[DT_B : DT_B + 1, C]
            dpg = step_grad * sigmoid(pre)
            dpl = dpg.astype(BF16)
            gs_o[DT_B : DT_B + 1, C] = jnp.sum(dpg, axis=0, keepdims=True)
            gs_o[SKIP + 1 : SKIP + 2, C] = jnp.zeros((1, cb_s), F32)
            gs_o[A_LOG : A_LOG + N, C] = rt_s[...] * (rates2 * LN2)
            gs_o[z.DT0 : z.DT0 + z.R, C] = mm_tn(low, dpl)
            low_s[...] += mm_nt(dpl, dtw)
            return carry_

        third = steps_s // 3
        lax.fori_loop(0, third, scan_block, 0)
        chain_b.hop(1)
        for c in gi_moves:
            c.wait()
        normed_load.wait()
        place_in(p_g, flat(gi_all))
        stage(sum_g.swap_start)
        lax.fori_loop(third, 2 * third, scan_block, 0)
        stage(sum_g.swap_finish)
        chain_b.hop(2)
        lax.fori_loop(2 * third, steps_s, scan_block, 0)
        for k in range(3, E):
            chain_b.hop(k)
        stage(sum_g.chips_finish)

        mxg[:, 0 : z.R] = low_s[...].astype(BF16)
        lane = lax.broadcasted_iota(jnp.int32, (SUB, LANES), 1)

        def gather(j, carry):
            both = jnp.zeros((SUB, LANES), F32)
            for n in range(N):
                at = row8(j * N + n)
                both = jnp.where(lane == n, jnp.sum(ia[at, :], axis=1, keepdims=True), both)
                both = jnp.where(lane == N + n, jnp.sum(oa[at, :], axis=1, keepdims=True), both)
            cl[row8(j), :] = both
            return carry

        lax.fori_loop(0, J, gather, 0)
        mxg[:, z.R : z.R + 2 * N] = cl[:, 0 : 2 * N].astype(BF16)

        def weight_load(i):
            return [
                pltpu.make_async_copy(
                    w_in.at[:, pl.ds(pl.multiple_of(h * DI + i * cb_s, LANES), cb_s)],
                    big.at[lax.rem(i, 2), h * D : (h + 1) * D],
                    ld.at[12 + 2 * lax.rem(i, 2) + h],
                )
                for h in range(2)
            ]

        for c in weight_load(0):
            c.start()

        def conv_block(i, carry):
            C = at_cols(i, cb_m)
            mgv = mxg[...]
            sgv = sig[:, C]
            xw = small[z.X0 : z.X0 + z.XW, C].astype(BF16)
            gs_o[z.X0 : z.X0 + z.XW, C] = mm_tn(mgv, sgv)
            sgrad = yg[:, C] + mm(mgv, xw)
            xpad = padded_rows(conv_in[:, C], hconv[:, C], J, cb_m)
            valid = [jnp.broadcast_to(masks[:, o : o + 1], (T, cb_m)) for o in range(4)]
            out = jnp.broadcast_to(small[CONV_B : CONV_B + 1, C], (T, cb_m))
            for o in range(4):
                w = small[CONV_W + o : CONV_W + o + 1, C]
                out = out + w * xpad[o : o + J].reshape(T, cb_m) * valid[o]
            sv = sigmoid(out)
            cg = sgrad * (sv * (1.0 + out * (1.0 - sv)))
            gs_o[CONV_B : CONV_B + 1, C] = jnp.sum(cg, axis=0, keepdims=True)
            total = jnp.zeros((J, SUB, cb_m), F32)
            final = lax.broadcasted_iota(jnp.int32, (SUB, cb_m), 0) == SUB - 1
            edges = [jnp.zeros((1, cb_m), F32) for _ in range(3)]
            for o in range(4):
                masked = cg * valid[o]
                gs_o[CONV_W + o : CONV_W + o + 1, C] = jnp.sum(
                    masked * xpad[o : o + J].reshape(T, cb_m), axis=0, keepdims=True
                )
                c3 = (small[CONV_W + o : CONV_W + o + 1, C] * masked).reshape(J, SUB, cb_m)
                k = 3 - o
                if k == 0:
                    total = total + c3
                else:
                    wrap = jnp.stack(
                        [jnp.where(final, 0.0, pltpu.roll(c3[t], SUB - 1, 0)) for t in range(k)]
                    )
                    total = total + jnp.concatenate([c3[k:], wrap], axis=0)
                    for i2 in range(o, 3):
                        edges[i2] = edges[i2] + c3[i2 - o, 0:1, :]
            yg[:, C] = total.reshape(T, cb_m)
            cg_edge[:, C] = jnp.concatenate(edges + [jnp.zeros((SUB - 3, cb_m), F32)], axis=0)
            return carry

        lax.fori_loop(0, DI // cb_m, conv_block, 0)
        back_edge = remote(cg_edge, edge_in, e_s, e_r, {"seq": lax.rem(s + S - 1, S)})
        back_edge.start()
        if plane:
            up2.wait()
            down2.wait()
            ub2[...] = adds(ua[yy], ub2[...])
            half_u = uq // 2
            rows_u = lambda c: pl.ds(pl.multiple_of(c * half_u, 16), half_u)
            up3 = remote(ub2.at[rows_u(other)], up_o.at[core], a_s.at[5], a_r.at[5], sib)
            up3.start()
            up_own = pltpu.make_async_copy(ub2.at[rows_u(core)], up_o.at[core], ld.at[16])
            up_own.start()
            db2[...] = adds(da[pl.ds(pl.multiple_of(xx * dq, 16), dq), :], db2[...])
            down_own = pltpu.make_async_copy(db2, down_o, ld.at[11])
            down_own.start()
        for c in gz_moves:
            c.wait()
        chain_b.local().wait()
        groups_o = DZ // 16
        bra = flat(br_all)
        for i in range(2):
            half_o = slice(i * (DZ // 2), (i + 1) * (DZ // 2))
            val = mm_tn(flat(gz_all)[:, half_o], bra)
            for g in range(DZ // 32):
                chunk, off = group_place(groups_o, i * (DZ // 32) + g)
                p_o[0, chunk // 2, chunk % 2, off : off + 16, :] = val[16 * g : 16 * g + 16].astype(BF16)
        stage(sum_o.swap_start)
        stage(sum_g.z_finish)
        back_edge.wait()
        live = jnp.where(s < S - 1, 1.0, 0.0)

        def fix_block(i, carry):
            C = at_cols(i, cb_m)
            c3 = yg[:, C].reshape(J, SUB, cb_m)
            final = lax.broadcasted_iota(jnp.int32, (SUB, cb_m), 0) == SUB - 1
            fixed = jnp.stack(
                [
                    c3[J - 3 + k]
                    + jnp.where(final, jnp.broadcast_to(edge_in[k : k + 1, C] * live, (SUB, cb_m)), 0.0)
                    for k in range(3)
                ]
            )
            pc[:, C] = jnp.concatenate([c3[: J - 3], fixed], axis=0).reshape(T, cb_m).astype(BF16)
            return carry

        lax.fori_loop(0, DI // cb_m, fix_block, 0)
        for e in range(E):
            gi_b[e] = pc[:, e * DZ : (e + 1) * DZ]
        pc_moves = trade(gi_b, pc_all, p_s, p_r)
        for c in pc_moves:
            c.start()
        pc_all[me] = gi_b[me]
        stage(sum_o.swap_finish)
        tg_o[...] = jnp.zeros_like(tg_o)

        def token_block(i, carry):
            for c in weight_load(i):
                c.wait()

            @pl.when(i + 1 < steps_s)
            def _():
                for c in weight_load(i + 1):
                    c.start()

            slot = lax.rem(i, 2)
            C = at_cols(i, cb_s)
            tg_o[...] += mm_nt(pc[:, C], big[slot, 0:D, :]) + mm_nt(gi[:, C], big[slot, D : 2 * D, :])
            return carry

        lax.fori_loop(0, steps_s, token_block, 0)
        d, gain_g = rms_back(tok[...].astype(F32), gp[0:1, :], tg_o[...])
        tg_o[...] = mg[...] + d
        gg_o[0:1, :] = gain_g
        cr = p_m.shape[3]
        for e in range(E):
            side = jnp.concatenate([gg_o[:, e * NZ : (e + 1) * NZ], jnp.zeros((G, DZ - NZ), F32)], axis=1)
            rows = [gs_o[:, e * DZ : (e + 1) * DZ], side, jnp.zeros((8 * cr - z.SMALL - G, DZ), F32)]
            p_m[e] = jnp.concatenate(rows, axis=0).astype(BF16).reshape(4, 2, cr, DZ)
        stage(sum_m.swap_start)
        for c in pc_moves:
            c.wait()
        for c in out_moves:
            c.start()
        place_in(p_c, flat(pc_all))
        stage(sum_c.swap_start)
        stage(sum_m.swap_finish)
        stage(sum_o.chips_finish)
        stage(sum_c.swap_finish)
        stage(sum_m.chips_finish)
        stage(sum_g.forward)
        stage(sum_c.chips_finish)
        stage(sum_m.z_finish)
        stage(sum_o.forward)
        stage(sum_c.z_finish)
        for c in out_moves:
            c.wait()
        back_own.wait()
        if plane:
            up3.wait()
            up_own.wait()
            down_own.wait()
            sum_m.forward()
            sum_c.forward()
            for sm_ in (sum_g, sum_o, sum_m, sum_c):
                sm_.finish()
        else:
            copies = [
                pltpu.make_async_copy(p, o, pown.at[a])
                for a, (p, o) in enumerate(((p_g, pg_o), (p_c, pc_o), (p_m, pm_o), (p_o, po_o)))
            ]
            for c in copies:
                c.start()
            for c in copies:
                c.wait()
        for k in range(E - 1):
            for d in (-k, k) if k else (0,):
                chain_b.each(d, lambda c: c.wait_send())

    v = pltpu.VMEM
    sem = lambda *dims: pltpu.SemaphoreType.DMA(dims)
    vm = pl.BlockSpec(memory_space=pltpu.VMEM)
    up_shape = (2, uq // 2, uc) if plane else (1, 16, LANES)
    down_shape = (dq, dc) if plane else (16, LANES)
    u_shape = (2, uq, uc) if plane else (2, 16, LANES)
    d_shape = (2 * dq, dc) if plane else (32, LANES)
    ins = (expert_out, dwu, dwd, states, w_out, w_in, dx_z, table, choose, chances, mid, moe, cot, gpack, router, gate, y,
           sig, small, mixed, dt, masks, conv_in, hconv, s_all, tok, normed_all)
    rg, ro, rm = chunk_rows(NZ), chunk_rows(DZ), 16 * -(-(z.SMALL + G) // 128)
    p_shapes = [(E, 4, 2, rg, DZ), (E, 4, 2, rg, DZ), (E, 4, 2, rm, DZ), (1, 4, 2, ro, D)]
    o_shapes = [(4, 2, E, rg, DZ)] * 2 + [(4, 2, rm, DZ), (4, 2, 1, ro, D)] if plane else p_shapes
    return pl.pallas_call(
        body,
        name="backward",
        in_specs=[ANY if a in (0, 1, 2, 3, 4, 5, 15, 16, 17, 18, 20, 22, 26) else vm for a in range(len(ins))],
        out_specs=[vm] * 3 + [ANY] * 7,
        out_shape=[
            sds((T, D), F32),
            sds((z.SMALL, DI), F32),
            sds((G, D), F32),
            sds((M, D), BF16),
        ]
        + [sds(o, BF16) for o in o_shapes]
        + [
            sds(up_shape, BF16),
            sds(down_shape, BF16),
        ],
        scratch_shapes=[
            v((T, DI), F32), v((T, DI), F32), v((T, DI), BF16), v((z.SMALL, DI), F32), v((T, DI), F32), v((T, DI), F32),
            v((CAP, D), BF16),
            v((2, rows_big, cb_s), BF16),
            v((2, cb_m, D), BF16), v((E * T, D), BF16),
            v((T, DI), F32), v((T, DI), BF16), v((E, T, DZ), BF16),
            v((T, D), BF16), v((T, D), F32),
            v((N, DI), BF16), v((S, N, DI), BF16), v(((N + 1) * SUB, DI), F32),
            v((SUB, DI), F32), v((SUB, DI), F32),
            v((T, DI), BF16),
            v((J * N * SUB, LANES), F32), v((J * N * SUB, LANES), F32),
            v((J * N * SUB, LANES), F32), v((J * N * SUB, LANES), F32),
            v((T, LANES), F32), v((T, cb_s), F32), v((N, cb_s), F32), v((N, cb_s), F32),
            v((T, cb_s), F32), v((T, cb_s), F32), v((N, cb_s), F32), v((T, z.R), F32), v((T, z.XW), BF16),
            v((N, DI), F32),
            v(u_shape, BF16), v(u_shape, BF16), v(u_shape[1:], BF16),
            v(d_shape, BF16), v(d_shape, BF16), v((d_shape[0] // 2, d_shape[1]), BF16),
            v((E, T, DZ), BF16), v((E, T, DZ), BF16), v((E, T, D), BF16), v((E, T, DZ), BF16),
            v((E, T, DZ), BF16),
        ]
        + [v(p, BF16) for p in p_shapes]
        + [v((p[0], 4) + p[3:], BF16) for p in p_shapes]
        + [v((3, p[0]) + p[3:], BF16) for p in p_shapes]
        + [v((E,) + p[3:], BF16) for p in p_shapes[:3]]
        + [
            sem(4, 2), sem(4, 2), sem(4, 3, 2), sem(4, 3, 2), sem(4, E - 1, 2), sem(4, E - 1, 2), sem(4, 3, 2),
            sem(4, 3, 2), sem(4, 4, 2), sem(4, 4, 2), sem(4),
            sem(24), sem(E - 1), sem(E - 1), sem(S - 1), sem(S - 1),
            pltpu.SemaphoreType.DMA, pltpu.SemaphoreType.DMA,
            sem(E - 1), sem(E - 1), sem(E - 1), sem(E - 1), sem(chain_slots), sem(chain_slots),
            sem(6), sem(6), sem(E - 1), sem(E - 1),
        ],
        compiler_params=pltpu.CompilerParams(
            collective_id=cid, has_side_effects=True, vmem_limit_bytes=60 * 1024 * 1024
        ),
    )(*ins)


def finish(z, gr, plane, pg, pc, pm, po, tg, mid, chances, choose, table, back, up, down):
    T, D, DI, N, J, E = z.T, z.D, z.DI, z.N, z.J, z.E
    DZ, NZ, FB = DI // E, D // E, z.FF // 8
    U = up.shape[1]

    def body(pg, pc, pm, po, tg, mid, ch, cho, tb, bk, up, dn, *outs):
        dwi, dwo, out, tgo, cw, cb, xw, dw, db, al, sk, na, nb, ro = outs[:14]
        for g in range(NZ // 16):
            chunk, off = group_place(NZ // 16, g)
            for h, src in enumerate((pc, pg)):
                for e in range(E):
                    dwi[16 * g : 16 * g + 16, h * DI + e * DZ : h * DI + (e + 1) * DZ] = src[
                        chunk, e, off : off + 16, :
                    ].astype(F32)
        for g in range(DZ // 16):
            chunk, off = group_place(DZ // 16, g)
            dwo[16 * g : 16 * g + 16, :] = po[chunk, off : off + 16, :].astype(F32)
        sm = pm[...].astype(F32)
        cw[...] = sm[CONV_W : CONV_W + 4]
        for ref, row in ((cb, CONV_B), (db, DT_B), (sk, SKIP)):
            ref[...] = sm[row : row + 1].reshape(DZ)
        al[...] = sm[A_LOG : A_LOG + N]
        dw[...] = sm[z.DT0 : z.X0]
        xw[...] = sm[z.X0 : z.SMALL]
        na[...] = sm[z.SMALL : z.SMALL + 1, 0:NZ].reshape(NZ)
        nb[...] = sm[z.SMALL + 1 : z.SMALL + 2, 0:NZ].reshape(NZ)
        ro[...] = sm[z.SMALL + 2 : z.SMALL + 2 + E, 0:NZ]
        lane = lax.broadcasted_iota(jnp.int32, (T, T), 1)
        prow = lax.broadcasted_iota(jnp.int32, (T, T), 0)
        order = (lane == (prow % SUB) * J + prow // SUB).astype(F32).astype(BF16)
        gating = jnp.sum(ch[...] * cho[...], axis=-1, keepdims=True)
        low = (mid[...] + gating * mm(tb[...], bk[...])).astype(BF16)
        out[...] = mm_tn(order, low).astype(BF16)
        v = tg[...]
        hi, rest = v.astype(BF16), v - v.astype(BF16).astype(F32)
        lo, end = split_hi_lo(rest)
        tgo[...] = mm_tn(order, hi) + (mm_tn(order, lo) + mm_tn(order, end))
        if plane:
            upo, dno = outs[14:]
            for c in range(2):
                for i in range(4):
                    at = (2 * i + c) * FB
                    upo[:, at : at + FB] = up[c, :, i * FB : (i + 1) * FB].astype(F32)
            dno[...] = dn[...].astype(F32)

    vm = pl.BlockSpec(memory_space=pltpu.VMEM)
    shapes = [
        sds((NZ, 2 * DI), F32), sds((DZ, D), F32), sds((T, D), BF16), sds((T, D), F32), sds((4, DZ), F32),
        sds((DZ,), F32), sds((z.XW, DZ), F32), sds((z.R, DZ), F32), sds((DZ,), F32), sds((N, DZ), F32),
        sds((DZ,), F32), sds((NZ,), F32), sds((NZ,), F32), sds((E, NZ), F32),
    ]
    if plane:
        shapes += [sds((U, z.FF), F32), sds(down.shape, F32)]
    return pl.pallas_call(
        body,
        name="finish",
        in_specs=[vm] * 12,
        out_specs=[vm] * len(shapes),
        out_shape=shapes,
        compiler_params=pltpu.CompilerParams(vmem_limit_bytes=VMEM_LIMIT),
    )(pg, pc, pm, po, tg, mid, chances, choose, table, back, up, down)


def on_device(
    tokens, segment_ids, routes, cotangent, norm_gain, in_proj, conv_weight, conv_bias, x_proj,
    dt_proj, dt_bias, a_log, d_skip, out_proj, moe_gain, router, up_proj, down_proj,
):
    E = lax.axis_size("exp")
    S = lax.axis_size("seq")
    z = Sizes(tokens, in_proj, dt_proj, x_proj, a_log, up_proj, E)
    T, D, DI, N, J, CAP = z.T, z.D, z.DI, z.N, z.J, z.CAP
    me_s, me_e = lax.axis_index("seq"), lax.axis_index("exp")
    core = lax.rem(me_s, 2)
    cw = dt_proj.shape[1]
    dw = norm_gain.shape[0]
    plane = S == 8 and dw % 32 == 0
    line = lambda v: v.reshape(1, -1)
    if plane:
        params = [conv_weight, conv_bias, dt_bias, d_skip, a_log, dt_proj, x_proj.T, norm_gain, moe_gain, router.T]
        w_in, w_out = in_proj, out_proj
    else:
        small_own = jnp.concatenate(
            [conv_weight, line(conv_bias), line(dt_bias), line(d_skip), jnp.zeros((1, cw), BF16), a_log, dt_proj,
             x_proj.T, jnp.zeros((small_rows(z) - z.SMALL, cw), BF16)], axis=0
        )
        g_own = jnp.concatenate(
            [line(norm_gain), line(moe_gain), router.T, jnp.zeros((32 - 2 - E, dw), BF16)], axis=0
        )
        gathered = [lax.all_gather(a, "exp", tiled=True) for a in (in_proj, out_proj, small_own, g_own)]
        w_in, w_out, params = gathered[0], gathered[1], gathered[2:]
    gr = 8 * -(-(2 + E) // 8)
    (
        small, gpack, router_t, table, choose_wide, masks, hconv, mixed, mid, moe, chances, s_all, tok, cot, normed,
        states, w_in, w_out, arrived, cot_pair, conv_in, gate, sig, dt, y,
    ) = forward(
        z, S, plane, tokens[0], cotangent[0], segment_ids, routes.reshape(1, T), params, w_in, w_out, gr, 1
    )
    dx_z, expert_out, dwu, dwd, normed_all = expert(
        z, arrived.reshape(2 * E * CAP, D), cot_pair.reshape(2 * E * CAP, D), router_t, normed, up_proj[0],
        down_proj[0], 3
    )
    token_grad, _, _, back_out, pg, pc, pm, po, up_sum, down_sum = backward(
        z, S, plane, expert_out, dx_z, dwu, dwd, states, w_out, w_in, table, choose_wide, chances, mid, moe, cot, gpack, router_t,
        gate, y, sig, small, mixed, dt, masks, conv_in, hconv, s_all, tok, normed_all.reshape(E * T, D), 4
    )
    if not plane:
        pg, pc, pm, po = [lax.psum(a, "seq") for a in (pg, pc, pm, po)]
        pg, pc = [
            lax.all_to_all(a, "exp", split_axis=0, concat_axis=0, tiled=True).transpose(1, 2, 0, 3, 4)
            for a in (pg, pc)
        ]
        pm = lax.psum_scatter(pm, "exp", scatter_dimension=0, tiled=True)[0]
        po = po[0]
    eight = lambda a: a.reshape((8,) + a.shape[2:])
    dw_in, dw_out, output, token_grad, g_cw, g_cb, g_xw, g_dw, g_db, g_al, g_sk, g_na, g_nb, g_ro, *rest = finish(
        z, gr, plane, eight(pg), eight(pc), pm.reshape(-1, pm.shape[-1]), po.reshape(8, -1, D), token_grad, mid,
        chances, choose_wide, table, back_out, up_sum, down_sum
    )
    if plane:
        up_part, down_part = rest
    else:
        fb = z.FF // 8
        up_full = jnp.zeros((D, 4, 2, fb), BF16)
        up_full = lax.dynamic_update_slice_in_dim(up_full, dwu.reshape(D, 4, 1, fb), core, axis=2)
        down_full = jnp.zeros((4, 2, fb, D), BF16)
        down_full = lax.dynamic_update_slice_in_dim(down_full, dwd.reshape(4, 1, fb, D), core, axis=1)
        up_part, down_part = [
            lax.psum_scatter(v, "seq", scatter_dimension=0, tiled=True).astype(F32)
            for v in (up_full.reshape(D, z.FF), down_full.reshape(z.FF, D))
        ]
    return (
        output[None], token_grad[None], g_na, dw_in, g_cw, g_cb, g_xw.T, g_dw, g_db, g_al, g_sk, dw_out,
        g_nb, g_ro.T, up_part[None], down_part[None],
    )


def solution(mesh):
    row = P("exp", "seq", None)
    in_specs = (
        row, P("exp", "seq"), row, row, P("exp"), P("exp", None), P(None, "exp"), P("exp"), P("exp", None),
        P(None, "exp"), P("exp"), P(None, "exp"), P("exp"), P("exp", None), P("exp"), P("exp", None),
        P("exp", None, None), P("exp", None, None),
    )
    out_specs = (
        row, row, P("exp"), P("exp", None), P(None, "exp"), P("exp"), P("exp", None), P(None, "exp"), P("exp"),
        P(None, "exp"), P("exp"), P("exp", None), P("exp"), P("exp", None), row, row,
    )
    return jax.shard_map(on_device, mesh=mesh, in_specs=in_specs, out_specs=out_specs, check_vma=False)
```
